32 devices in a mesh: dp: 8 (over y, x, core), expert: 4 (over z).
Axes of the slice: x: 2, y: 2, z: 4, core: 2. Of those that a mesh axis runs over, the one named last changes fastest.
Arguments:
- expert_master: float32 [4, 7168, 2048], P('expert', 'dp'), may hold values from -6 to 6
- expert_first: bfloat16 [4, 7168, 2048], P('expert', 'dp'), may hold values from -0.29882812 to 0.29882812
- expert_second: bfloat16 [4, 7168, 2048], P('expert', 'dp'), may hold values from 9.9658966e-05 to 0.0099487305
- expert_grad: bfloat16 [4, 7168, 2048], P('expert', 'dp'), may hold values from -0.29882812 to 0.29882812
- latent_master: float32 [7168, 1536], P(('dp', 'expert')), may hold values from -6 to 6
- latent_first: bfloat16 [7168, 1536], P(('dp', 'expert')), may hold values from -0.29882812 to 0.29882812
- latent_second: bfloat16 [7168, 1536], P(('dp', 'expert')), may hold values from 9.9658966e-05 to 0.0099487305
- latent_grad: bfloat16 [7168, 1536], P(('dp', 'expert')), may hold values from -0.29882812 to 0.29882812
- step_count: int32 [1], replicated, may hold values from 1 to 11
- column_owner: int32 [16], replicated, may hold values from 0 to 15, each once
Outputs:
- expert_master_new: float32 [4, 7168, 2048], P('expert', 'dp')
- expert_first_new: bfloat16 [4, 7168, 2048], P('expert', 'dp')
- expert_second_new: bfloat16 [4, 7168, 2048], P('expert', 'dp')
- expert_served: bfloat16 [4, 114688, 128], P('expert', 'dp')
- expert_scales: float32 [4, 896], P('expert', 'dp')
- latent_master_new: float32 [7168, 1536], P(('dp', 'expert'))
- latent_first_new: bfloat16 [7168, 1536], P(('dp', 'expert'))
- latent_second_new: bfloat16 [7168, 1536], P(('dp', 'expert'))
- latent_served: bfloat16 [7168, 1536], P('dp')
- latent_scales: float32 [56, 12], replicated
The draws below stay inside these ranges and needn't reach their ends.
Inputs may be any that keep to these rules, and one draw needn't show every extreme that they name: column_owner names each serving position of the 16 column blocks exactly once.
All inputs are finite; a program needn't handle non-finite values. Where the reference program divides by a largest or mean magnitude, that divisor is 1e-20 or more.
Results may differ from the reference program's by a relative error of at most 0.0017.
Values may be sent and summed in bfloat16 or wider, within the bound.
No kernel may reach another device: no remote copies, remote signals or barrier semaphores. Data moves between devices by JAX's collectives and lax.ppermute only.
A program may use at most 128 MiB of HBM per device.

```python
import math
import jax
import jax.numpy as jnp
from jax import lax

D = 7168
F = 2048
FM = 1536
TILE = 128
EXPERTS = 4


def shard_levels(stream_key, shape, shards, smallest, high):
    def one(axis_at, blocks):
        heights = jax.random.uniform(jax.random.fold_in(jax.random.fold_in(stream_key, 6), axis_at), (blocks,), jnp.float32, smallest / len(shards), high / len(shards))
        return jnp.repeat(jnp.exp(heights), shape[axis_at] // blocks).reshape((-1,) + (1,) * (len(shape) - axis_at - 1))

    factor_of = one(*shards[0])
    for cut in shards[1:]:
        factor_of = factor_of * one(*cut)
    return factor_of


def noise(own_key, extent, width, bound, split=(), kind=jnp.bfloat16):
    loudness = shard_levels(own_key, extent, split, -0.22, 0.18) if split else 1.0
    entries = jax.random.normal(own_key, extent, jnp.float32) * width * loudness
    return jnp.minimum(jnp.maximum(entries, -bound), bound).astype(kind)


def setup_inputs(seed: int = 0) -> dict:
    key_list = jax.random.split(jax.random.key(seed), 11)
    return {
        "expert_master": noise(key_list[0], (EXPERTS, D, F), 1.0, 6.0, ((0, 4), (1, 8)), jnp.float32),
        "expert_first": noise(key_list[1], (EXPERTS, D, F), 0.05, 0.29882812, ((0, 4), (1, 8))),
        "expert_second": jnp.clip(jnp.exp(math.log(0.0099487305) - 4.603446 * jax.random.uniform(key_list[2], (EXPERTS, D, F), jnp.float32) ** shard_levels(key_list[2], (EXPERTS, D, F), ((0, 4), (1, 8)), -0.2, 0.2)), 9.965896606445312e-05, 0.0099487305).astype(jnp.bfloat16),
        "expert_grad": noise(key_list[3], (EXPERTS, D, F), 0.05, 0.29882812, ((0, 4), (1, 8))),
        "latent_master": noise(key_list[4], (D, FM), 1.0, 6.0, ((0, 32),), jnp.float32),
        "latent_first": noise(key_list[5], (D, FM), 0.05, 0.29882812, ((0, 32),)),
        "latent_second": jnp.clip(jnp.exp(math.log(0.0099487305) - 4.603446 * jax.random.uniform(key_list[6], (D, FM), jnp.float32) ** shard_levels(key_list[6], (D, FM), ((0, 32),), -0.2, 0.2)), 9.965896606445312e-05, 0.0099487305).astype(jnp.bfloat16),
        "latent_grad": noise(key_list[7], (D, FM), 0.05, 0.29882812, ((0, 32),)),
        "step_count": jax.random.randint(key_list[8], (1,), 1, 12).astype(jnp.int32),
        "column_owner": jax.random.permutation(key_list[9], F // TILE).astype(jnp.int32),
    }


BETA_ONE = 0.9
BETA_TWO = 0.95
LEARN_RATE = 0.2
DECAY_RATE = 0.1
ADAM_EPS = 1e-08
SCALE_EPS = 1e-06

def adamw_step(master, moment_one, moment_two, gradient, step_count):
    grad_value = gradient.astype(jnp.float32)
    first_new = BETA_ONE * moment_one.astype(jnp.float32) + (1.0 - BETA_ONE) * grad_value
    second_new = BETA_TWO * moment_two.astype(jnp.float32) + (1.0 - BETA_TWO) * grad_value * grad_value
    step_value = step_count[0].astype(jnp.float32)
    corr_one = 1.0 - jnp.power(jnp.float32(BETA_ONE), step_value)
    corr_two = 1.0 - jnp.power(jnp.float32(BETA_TWO), step_value)
    update = first_new / corr_one / (jnp.sqrt(second_new / corr_two) + ADAM_EPS)
    master_new = master - LEARN_RATE * (update + DECAY_RATE * master)
    return (master_new, first_new.astype(jnp.bfloat16), second_new.astype(jnp.bfloat16))

def quantize_full(weights):
    row_count, col_count = weights.shape
    blocks = weights.reshape(row_count // TILE, TILE, col_count // TILE, TILE)
    block_max = lax.optimization_barrier(jnp.max(jnp.abs(blocks), axis=(1, 3)))
    scaled = blocks / (block_max[:, None, :, None] + SCALE_EPS)
    return (scaled.reshape(row_count, col_count).astype(jnp.bfloat16), block_max)

def reference(expert_master, expert_first, expert_second, expert_grad, latent_master, latent_first, latent_second, latent_grad, step_count, column_owner):

    def per_expert(items):
        master, moment_one, moment_two, gradient = items
        master_new, first_new, second_new = adamw_step(master, moment_one, moment_two, gradient, step_count)
        scaled, block_max = quantize_full(master_new)
        return (master_new, first_new, second_new, scaled, block_max)
    master_out, first_out, second_out, scaled_all, maxima_all = lax.map(per_expert, (expert_master, expert_first, expert_second, expert_grad))
    block_count = F // TILE
    positions = jnp.arange(block_count, dtype=jnp.int32)
    inverse = lax.optimization_barrier(jnp.sum(positions[:, None] * (column_owner[:, None] == positions[None, :]).astype(jnp.int32), axis=0)).astype(jnp.int32)
    served = jnp.take(scaled_all.reshape(EXPERTS, D, block_count, TILE), inverse, axis=2)
    served = jnp.transpose(served, (0, 2, 1, 3)).reshape(EXPERTS, block_count * D, TILE)
    scales = jnp.take(maxima_all, inverse, axis=2)
    scales = jnp.transpose(scales, (0, 2, 1)).reshape(EXPERTS, block_count * (D // TILE))
    latent_new, latent_one, latent_two = adamw_step(latent_master, latent_first, latent_second, latent_grad, step_count)
    latent_out, latent_scales = quantize_full(latent_new)
    return (master_out, first_out, second_out, served, scales, latent_new, latent_one, latent_two, latent_out, latent_scales)
```

```python
import functools
import math

import jax
import jax.numpy as jnp
from jax import lax
from jax.experimental import pallas as pl
from jax.experimental.pallas import tpu as pltpu
from jax.sharding import PartitionSpec as P

D = 7168
TILE = 128


BETA_ONE = 0.9
BETA_TWO = 0.95
LEARN_RATE = 0.2
DECAY_RATE = 0.1
ADAM_EPS = 1e-08
SCALE_EPS = 1e-06


def adamw_step(master, moment_one, moment_two, gradient, step_count):
    grad_value = gradient.astype(jnp.float32)
    first_new = BETA_ONE * moment_one.astype(jnp.float32) + (1.0 - BETA_ONE) * grad_value
    second_new = (
        BETA_TWO * moment_two.astype(jnp.float32) + (1.0 - BETA_TWO) * grad_value * grad_value
    )
    step_value = step_count[0].astype(jnp.float32)
    corr_one = 1.0 - jnp.power(jnp.float32(BETA_ONE), step_value)
    corr_two = 1.0 - jnp.power(jnp.float32(BETA_TWO), step_value)
    update = first_new / corr_one / (jnp.sqrt(second_new / corr_two) + ADAM_EPS)
    master_new = master - LEARN_RATE * (update + DECAY_RATE * master)
    return (master_new, first_new.astype(jnp.bfloat16), second_new.astype(jnp.bfloat16))


def row_maxima(weights):
    leading = weights.shape[:-1]
    tile_count = weights.shape[-1] // TILE
    return jnp.max(jnp.abs(weights).reshape(leading + (tile_count, TILE)), axis=-1)


def local_tiles(row_max, lead_rows):
    exp_count, row_count, tile_count = row_max.shape
    tile_span = row_count // TILE + 2
    buffer = jnp.zeros((exp_count, tile_span * TILE, tile_count), jnp.float32)
    buffer = lax.dynamic_update_slice(buffer, row_max, (jnp.int32(0), lead_rows, jnp.int32(0)))
    return jnp.max(buffer.reshape(exp_count, tile_span, TILE, tile_count), axis=2)


def place_tiles(tile_max, first_tile):
    exp_count, tile_span, tile_count = tile_max.shape
    global_map = jnp.zeros((exp_count, D // TILE + tile_span, tile_count), jnp.float32)
    return lax.dynamic_update_slice(global_map, tile_max, (jnp.int32(0), first_tile, jnp.int32(0)))


def quantized_rows(weights, tile_max, lead_rows):
    exp_count, row_count, col_count = weights.shape
    repeated = jnp.repeat(tile_max, TILE, axis=1)
    row_scale = lax.dynamic_slice_in_dim(repeated, lead_rows, row_count, 1)
    blocks = weights.reshape(exp_count, row_count, col_count // TILE, TILE)
    return (blocks / (row_scale[..., None] + SCALE_EPS)).reshape(weights.shape).astype(jnp.bfloat16)


def general_body(
    expert_master,
    expert_first,
    expert_second,
    expert_grad,
    latent_master,
    latent_first,
    latent_second,
    latent_grad,
    step_count,
    column_owner,
):
    master_new, first_new, second_new = adamw_step(
        expert_master, expert_first, expert_second, expert_grad, step_count
    )
    latent_new, latent_one, latent_two = adamw_step(
        latent_master, latent_first, latent_second, latent_grad, step_count
    )
    dp_count = lax.axis_size("dp")
    dp_pos = lax.axis_index("dp")
    exp_count, row_count, col_count = master_new.shape
    block_count = col_count // TILE
    slot_count = max(1, block_count // dp_count)
    total_tiles = D // TILE
    recv_rows = block_count * row_count
    recv_tiles = recv_rows // TILE
    positions = jnp.arange(block_count, dtype=jnp.int32)
    inverse = jnp.sum(
        positions[:, None] * (column_owner[:, None] == positions[None, :]).astype(jnp.int32), axis=0
    )
    receiver_ids = jnp.arange(dp_count, dtype=jnp.int32)[:, None]
    slot_ids = jnp.arange(slot_count, dtype=jnp.int32)[None, :]
    segment = (
        receiver_ids * block_count
        + jnp.mod(dp_pos - receiver_ids * block_count, dp_count)
        + slot_ids * dp_count
    )
    usable_slot = (segment < (receiver_ids + 1) * block_count).reshape(-1)
    send_block = jnp.take(inverse, jnp.minimum(segment // dp_count, block_count - 1)).reshape(-1)
    local_segments = jnp.arange(block_count, dtype=jnp.int32)
    source_dev = jnp.mod(dp_pos * block_count + local_segments, dp_count)
    pick_index = source_dev * slot_count + local_segments // dp_count
    blocks = master_new.reshape(exp_count, row_count, block_count, TILE)
    picked = jnp.take(blocks, send_block, axis=2)
    received = lax.all_to_all(
        jnp.where(usable_slot[None, None, :, None], picked, jnp.zeros((), picked.dtype)),
        "dp",
        split_axis=2,
        concat_axis=2,
        tiled=True,
    )
    ordered = jnp.take(received, pick_index, axis=2)
    tall = (
        jnp.transpose(ordered, (0, 2, 1, 3))
        .reshape(exp_count, recv_rows, TILE)
        .reshape(exp_count, recv_tiles, TILE, TILE)
    )
    expert_scales = jnp.max(jnp.abs(tall), axis=(2, 3))
    expert_served = (
        (tall / (expert_scales[:, :, None, None] + SCALE_EPS))
        .reshape(exp_count, recv_rows, TILE)
        .astype(jnp.bfloat16)
    )
    latent_block = lax.all_gather(latent_new, "expert", axis=0, tiled=True)
    block_rows = latent_block.shape[0]
    block_offset = dp_pos * block_rows
    block_lead = block_offset % TILE
    block_tiles = local_tiles(row_maxima(latent_block)[None], block_lead)
    block_map = lax.pmax(place_tiles(block_tiles, block_offset // TILE), "dp")
    latent_scales = block_map[0, :total_tiles]
    block_tiles = lax.dynamic_slice_in_dim(block_map, block_offset // TILE, block_tiles.shape[1], 1)
    latent_served = quantized_rows(latent_block[None], block_tiles, block_lead)[0]
    return (
        master_new,
        first_new,
        second_new,
        expert_served,
        expert_scales,
        latent_new,
        latent_one,
        latent_two,
        latent_served,
        latent_scales,
    )


CHUNK = 32
F32 = jnp.float32
BF16 = jnp.bfloat16
VMEM_LIMIT = 40 * 1024 * 1024


def adamw_tile(w, m, v, g, rate, corr):
    g = g.astype(F32)
    m1 = BETA_ONE * m.astype(F32) + (1.0 - BETA_ONE) * g
    v1 = BETA_TWO * v.astype(F32) + (1.0 - BETA_TWO) * g * g
    w1 = (1.0 - LEARN_RATE * DECAY_RATE) * w - rate * m1 / (jnp.sqrt(v1 * corr) + ADAM_EPS)
    return w1, m1.astype(BF16), v1.astype(BF16)


def sub_max(w1):
    return jnp.max(jnp.abs(w1).reshape(w1.shape[0] // 8, 8, TILE), axis=0)


def stack_max(parts):
    rows = [jnp.max(p, axis=0, keepdims=True) for p in parts]
    return jnp.max(jnp.concatenate(rows, axis=0), axis=1, keepdims=True)


def expert_kernel(per_dest, n_dest, tiles, n_alias, blk_ref, scal_ref, *refs):
    w_ref, m_ref, v_ref, g_ref = refs[:4]
    w1_ref, m1_ref, v1_ref, s_ref = refs[4 + n_alias : 8 + n_alias]
    q_refs = refs[8 + n_alias :]
    rate, corr = scal_ref[0], scal_ref[1]
    parts = []
    for t in range(tiles):
        rows = pl.ds(t * TILE, TILE)
        w1, m1, v1 = adamw_tile(
            w_ref[rows, :], m_ref[rows, :], v_ref[rows, :], g_ref[rows, :], rate, corr
        )
        w1_ref[rows, :] = w1
        m1_ref[rows, :] = m1
        v1_ref[rows, :] = v1
        parts.append(sub_max(w1))
    top = stack_max(parts)
    s_ref[0] = jnp.broadcast_to(top, (tiles, TILE))
    inv = 1.0 / (top + SCALE_EPS)
    step = pl.program_id(0)
    for d in range(n_dest):

        @pl.when(step // per_dest == d)
        def _(d=d):
            for t in range(tiles):
                rows = pl.ds(t * TILE, TILE)
                q_refs[d][0, rows, :] = (w1_ref[rows, :] * inv[t : t + 1, :]).astype(BF16)


def expert_group(arrays, state, blk, scal, n_dest, per_dest):
    rows, cols = arrays[0].shape
    tiles = rows // TILE
    steps = n_dest * per_dest
    column = lambda i, blk: (0, blk[i])
    spec = pl.BlockSpec((rows, TILE), column)
    any_spec = pl.BlockSpec(memory_space=pl.ANY)
    n_alias = len(state)

    def q_map(d):
        return lambda i, blk: (jnp.clip(i - d * per_dest, 0, per_dest - 1), 0, 0)

    out_shape = [
        jax.ShapeDtypeStruct((rows, cols), F32),
        jax.ShapeDtypeStruct((rows, cols), BF16),
        jax.ShapeDtypeStruct((rows, cols), BF16),
        jax.ShapeDtypeStruct((steps, tiles, TILE), F32),
    ] + [jax.ShapeDtypeStruct((per_dest, rows, TILE), BF16)] * n_dest
    out_specs = [spec, spec, spec, pl.BlockSpec((1, tiles, TILE), lambda i, blk: (i, 0, 0))] + [
        pl.BlockSpec((1, rows, TILE), q_map(d)) for d in range(n_dest)
    ]
    elems = rows * TILE * steps
    out = pl.pallas_call(
        functools.partial(expert_kernel, per_dest, n_dest, tiles, n_alias),
        grid_spec=pltpu.PrefetchScalarGridSpec(
            num_scalar_prefetch=1,
            grid=(steps,),
            in_specs=[pl.BlockSpec(memory_space=pltpu.SMEM)] + [spec] * 4 + [any_spec] * n_alias,
            out_specs=out_specs,
        ),
        out_shape=out_shape,
        input_output_aliases={6 + i: i for i in range(n_alias)},
        compiler_params=pltpu.CompilerParams(vmem_limit_bytes=VMEM_LIMIT),
        cost_estimate=pl.CostEstimate(
            flops=30 * elems, bytes_accessed=20 * elems, transcendentals=2 * elems
        ),
        name="expert_adamw",
    )(blk, scal, *arrays, *state)
    return out[:3], out[3], out[4:]


def place_kernel(n_alias, src_ref, q_ref, *refs):
    refs[n_alias][0, 0] = q_ref[0]


def place_rows(served, src, q, dp_count):
    per_dest, rows, _ = q.shape
    n_alias = 0 if served is None else 1
    any_spec = pl.BlockSpec(memory_space=pl.ANY)
    return pl.pallas_call(
        functools.partial(place_kernel, n_alias),
        grid_spec=pltpu.PrefetchScalarGridSpec(
            num_scalar_prefetch=1,
            grid=(per_dest,),
            in_specs=[pl.BlockSpec((1, rows, TILE), lambda j, src: (j, 0, 0))] + [any_spec] * n_alias,
            out_specs=pl.BlockSpec((1, 1, rows, TILE), lambda j, src: (j, src[0], 0, 0)),
        ),
        out_shape=jax.ShapeDtypeStruct((per_dest, dp_count, rows, TILE), BF16),
        input_output_aliases={2: 0} if n_alias else {},
        compiler_params=pltpu.CompilerParams(vmem_limit_bytes=VMEM_LIMIT),
        cost_estimate=pl.CostEstimate(
            flops=0, bytes_accessed=4 * per_dest * rows * TILE, transcendentals=0
        ),
        name="place_served",
    )(src, q, *(() if served is None else (served,)))


def latent_kernel(chunks, width, scal_ref, w_ref, m_ref, v_ref, g_ref, w1_ref, m1_ref, v1_ref, top_ref):
    rate, corr = scal_ref[0], scal_ref[1]
    step = pl.program_id(0)
    lane = lax.broadcasted_iota(jnp.int32, (8, TILE), 1)

    @pl.when(step == 0)
    def _():
        top_ref[...] = jnp.zeros_like(top_ref)

    tops = top_ref[...]
    for b in range(width):
        cols = pl.ds(b * TILE, TILE)
        w1, m1, v1 = adamw_tile(
            w_ref[:, cols], m_ref[:, cols], v_ref[:, cols], g_ref[:, cols], rate, corr
        )
        w1_ref[:, cols] = w1
        m1_ref[:, cols] = m1
        v1_ref[:, cols] = v1
        parts = [sub_max(w1[c * CHUNK : (c + 1) * CHUNK]) for c in range(chunks)]
        parts += [parts[-1]] * (8 - chunks)
        tops = jnp.where(lane == step * width + b, stack_max(parts), tops)
    top_ref[...] = tops


def latent_update(arrays, scal):
    rows, cols = arrays[0].shape
    width = 4
    spec = pl.BlockSpec((rows, width * TILE), lambda i: (0, i))
    elems = rows * cols
    return pl.pallas_call(
        functools.partial(latent_kernel, rows // CHUNK, width),
        grid=(cols // (width * TILE),),
        in_specs=[pl.BlockSpec(memory_space=pltpu.SMEM)] + [spec] * 4,
        out_specs=[spec] * 3 + [pl.BlockSpec((8, TILE), lambda i: (0, 0))],
        out_shape=[
            jax.ShapeDtypeStruct((rows, cols), F32),
            jax.ShapeDtypeStruct((rows, cols), BF16),
            jax.ShapeDtypeStruct((rows, cols), BF16),
            jax.ShapeDtypeStruct((8, TILE), F32),
        ],
        compiler_params=pltpu.CompilerParams(vmem_limit_bytes=VMEM_LIMIT),
        cost_estimate=pl.CostEstimate(
            flops=30 * elems, bytes_accessed=18 * elems, transcendentals=2 * elems
        ),
        name="latent_adamw",
    )(scal, *arrays)


def latent_quant_kernel(chunks, width, off_ref, w1_ref, own_ref, prev_ref, next_ref, q_ref, ext):
    per_tile = TILE // CHUNK
    step = pl.program_id(0)
    ext[0:chunks, :] = prev_ref[0:chunks, :]
    ext[chunks : 2 * chunks, :] = own_ref[0:chunks, :]
    ext[2 * chunks : 3 * chunks, :] = next_ref[0:chunks, :]
    lane = lax.broadcasted_iota(jnp.int32, (8, TILE), 1)
    off = off_ref[0]
    rows = []
    for c in range(chunks):
        first = chunks + c - lax.rem(off + c, per_tile)
        rows.append(jnp.max(ext[pl.ds(first, per_tile), :], axis=0, keepdims=True))
    rows += [rows[-1]] * (8 - chunks)
    tops = jnp.concatenate(rows, axis=0)
    for b in range(width):
        mine = jnp.where(lane == step * width + b, tops, 0.0)
        inv = 1.0 / (jnp.max(mine, axis=1, keepdims=True) + SCALE_EPS)
        cols = pl.ds(b * TILE, TILE)
        for c in range(chunks):
            span = pl.ds(c * CHUNK, CHUNK)
            q_ref[span, cols] = (w1_ref[span, cols] * inv[c : c + 1, :]).astype(BF16)


def latent_quant(w1, own, prev, nxt, off):
    rows, cols = w1.shape
    width = 4
    chunks = rows // CHUNK
    spec = pl.BlockSpec((rows, width * TILE), lambda i: (0, i))
    small = pl.BlockSpec((8, TILE), lambda i: (0, 0))
    return pl.pallas_call(
        functools.partial(latent_quant_kernel, chunks, width),
        grid=(cols // (width * TILE),),
        in_specs=[pl.BlockSpec(memory_space=pltpu.SMEM), spec] + [small] * 3,
        out_specs=spec,
        out_shape=jax.ShapeDtypeStruct((rows, cols), BF16),
        scratch_shapes=[pltpu.VMEM((3 * 8, TILE), F32)],
        compiler_params=pltpu.CompilerParams(vmem_limit_bytes=VMEM_LIMIT),
        cost_estimate=pl.CostEstimate(
            flops=2 * rows * cols, bytes_accessed=6 * rows * cols, transcendentals=0
        ),
        name="latent_quant",
    )(off, w1, own, prev, nxt)


def fast_fits(expert_shape, latent_shape, dp_count, exp_axis):
    exp_count, rows, cols = expert_shape
    latent_rows, latent_cols = latent_shape
    return (
        exp_count == 1
        and rows % TILE == 0
        and (cols // TILE) % dp_count == 0
        and dp_count & (dp_count - 1) == 0
        and latent_rows % CHUNK == 0
        and TILE <= latent_rows <= 8 * CHUNK
        and latent_rows * exp_axis % TILE == 0
        and latent_cols % (4 * TILE) == 0
        and latent_cols <= TILE * TILE
    )


def fast_body(
    expert_master,
    expert_first,
    expert_second,
    expert_grad,
    latent_master,
    latent_first,
    latent_second,
    latent_grad,
    step_count,
    column_owner,
):
    dp_count = lax.axis_size("dp")
    dp_pos = lax.axis_index("dp")
    exp_axis = lax.axis_size("expert")
    exp_pos = lax.axis_index("expert")
    _, rows, cols = expert_master.shape
    block_count = cols // TILE
    per_dest = block_count // dp_count
    tiles = rows // TILE

    step_value = step_count[0].astype(F32)
    corr_one = 1.0 - jnp.power(F32(BETA_ONE), step_value)
    corr_two = 1.0 - jnp.power(F32(BETA_TWO), step_value)
    scal = jnp.stack([LEARN_RATE / corr_one, 1.0 / corr_two])

    latent_new, latent_one, latent_two, chunk_top = latent_update(
        (latent_master, latent_first, latent_second, latent_grad), scal
    )
    latent_rows = latent_new.shape[0]
    chunks = latent_rows // CHUNK
    off = lax.rem((dp_pos * exp_axis + exp_pos) * chunks, TILE // CHUNK).astype(jnp.int32)
    top_prev = lax.ppermute(chunk_top, "expert", [(i, i + 1) for i in range(exp_axis - 1)])
    top_next = lax.ppermute(chunk_top, "expert", [(i + 1, i) for i in range(exp_axis - 1)])
    latent_q = latent_quant(latent_new, chunk_top, top_prev, top_next, off.reshape(1))
    latent_served = lax.all_gather(latent_q, "expert", axis=0, tiled=True)

    positions = jnp.arange(block_count, dtype=jnp.int32)
    inverse = jnp.sum(
        positions[:, None] * (column_owner[:, None] == positions[None, :]).astype(jnp.int32), axis=0
    )
    order = sorted(range(1, dp_count), key=lambda k: (-bin(k >> 1).count("1"), k & 1, k)) + [0]
    dests = dp_pos ^ jnp.array(order, jnp.int32)
    slots = dests[:, None] * per_dest + jnp.arange(per_dest, dtype=jnp.int32)[None, :]
    blk = jnp.take(inverse, slots.reshape(-1))
    arrays = tuple(
        a.reshape(rows, cols) for a in (expert_master, expert_first, expert_second, expert_grad)
    )
    group = max(1, dp_count // 4)
    state, tops, sent = (), [], []
    for at in range(0, dp_count, group):
        part = blk[at * per_dest : (at + group) * per_dest]
        state, top, q = expert_group(arrays, state, part, scal, group, per_dest)
        tops.append(top[:, :, 0])
        sent.extend(q)
    got = [
        q if k == 0 else lax.ppermute(q, "dp", [(i, i ^ k) for i in range(dp_count)])
        for k, q in zip(order, sent)
    ]
    served = place_rows(None, dests[-1:], got[-1], dp_count)
    for i in range(dp_count - 1):
        served = place_rows(served, dests[i : i + 1], got[i], dp_count)
    expert_served = served.reshape(1, block_count * rows, TILE)

    small = jnp.concatenate(
        [
            jnp.concatenate(tops, axis=0).reshape(-1),
            chunk_top[:chunks, : latent_new.shape[1] // TILE].reshape(-1),
        ]
    )
    everyone = lax.all_gather(small, ("dp", "expert"), axis=0)
    n_top = block_count * tiles
    latent_chunks = everyone[:, n_top:].reshape(-1, TILE // CHUNK, latent_new.shape[1] // TILE)
    latent_scales = jnp.max(latent_chunks, axis=1)
    peers = everyone.reshape(dp_count, exp_axis, -1)
    peers = lax.dynamic_index_in_dim(peers, exp_pos, 1, keepdims=False)[:, :n_top]
    peers = peers.reshape(dp_count, dp_count, per_dest, tiles)
    place = [order.index(k) for k in range(dp_count)]
    sel = jnp.take(jnp.array(place, jnp.int32), dp_pos ^ jnp.arange(dp_count, dtype=jnp.int32))
    hit = sel[:, None] == jnp.arange(dp_count, dtype=jnp.int32)[None, :]
    mine = jnp.max(jnp.where(hit[:, :, None, None], peers, 0.0), axis=1)
    expert_scales = jnp.transpose(mine, (1, 0, 2)).reshape(1, block_count * tiles)

    return (
        state[0][None],
        state[1][None],
        state[2][None],
        expert_served,
        expert_scales,
        latent_new,
        latent_one,
        latent_two,
        latent_served,
        latent_scales,
    )


def body(*args):
    if fast_fits(args[0].shape, args[4].shape, lax.axis_size("dp"), lax.axis_size("expert")):
        return fast_body(*args)
    return general_body(*args)


def solution(mesh):
    placed = (
        P("expert", "dp", None),
        P("expert", "dp", None),
        P("expert", "dp", None),
        P("expert", "dp", None),
        P(("dp", "expert"), None),
        P(("dp", "expert"), None),
        P(("dp", "expert"), None),
        P(("dp", "expert"), None),
        P(),
        P(),
    )
    return jax.shard_map(
        body,
        mesh=mesh,
        in_specs=placed,
        out_specs=(
            P("expert", "dp", None),
            P("expert", "dp", None),
            P("expert", "dp", None),
            P("expert", "dp", None),
            P("expert", "dp"),
            P(("dp", "expert"), None),
            P(("dp", "expert"), None),
            P(("dp", "expert"), None),
            P("dp", None),
            P(),
        ),
        check_vma=False,
    )
```

```python
import functools
import math

import jax
import jax.numpy as jnp
from jax import lax
from jax.experimental import pallas as pl
from jax.experimental.pallas import tpu as pltpu
from jax.sharding import PartitionSpec as P

D = 7168
TILE = 128


BETA_ONE = 0.9
BETA_TWO = 0.95
LEARN_RATE = 0.2
DECAY_RATE = 0.1
ADAM_EPS = 1e-08
SCALE_EPS = 1e-06


def adamw_step(master, moment_one, moment_two, gradient, step_count):
    grad_value = gradient.astype(jnp.float32)
    first_new = BETA_ONE * moment_one.astype(jnp.float32) + (1.0 - BETA_ONE) * grad_value
    second_new = (
        BETA_TWO * moment_two.astype(jnp.float32) + (1.0 - BETA_TWO) * grad_value * grad_value
    )
    step_value = step_count[0].astype(jnp.float32)
    corr_one = 1.0 - jnp.power(jnp.float32(BETA_ONE), step_value)
    corr_two = 1.0 - jnp.power(jnp.float32(BETA_TWO), step_value)
    update = first_new / corr_one / (jnp.sqrt(second_new / corr_two) + ADAM_EPS)
    master_new = master - LEARN_RATE * (update + DECAY_RATE * master)
    return (master_new, first_new.astype(jnp.bfloat16), second_new.astype(jnp.bfloat16))


def row_maxima(weights):
    leading = weights.shape[:-1]
    tile_count = weights.shape[-1] // TILE
    return jnp.max(jnp.abs(weights).reshape(leading + (tile_count, TILE)), axis=-1)


def local_tiles(row_max, lead_rows):
    exp_count, row_count, tile_count = row_max.shape
    tile_span = row_count // TILE + 2
    buffer = jnp.zeros((exp_count, tile_span * TILE, tile_count), jnp.float32)
    buffer = lax.dynamic_update_slice(buffer, row_max, (jnp.int32(0), lead_rows, jnp.int32(0)))
    return jnp.max(buffer.reshape(exp_count, tile_span, TILE, tile_count), axis=2)


def place_tiles(tile_max, first_tile):
    exp_count, tile_span, tile_count = tile_max.shape
    global_map = jnp.zeros((exp_count, D // TILE + tile_span, tile_count), jnp.float32)
    return lax.dynamic_update_slice(global_map, tile_max, (jnp.int32(0), first_tile, jnp.int32(0)))


def quantized_rows(weights, tile_max, lead_rows):
    exp_count, row_count, col_count = weights.shape
    repeated = jnp.repeat(tile_max, TILE, axis=1)
    row_scale = lax.dynamic_slice_in_dim(repeated, lead_rows, row_count, 1)
    blocks = weights.reshape(exp_count, row_count, col_count // TILE, TILE)
    return (blocks / (row_scale[..., None] + SCALE_EPS)).reshape(weights.shape).astype(jnp.bfloat16)


def general_body(
    expert_master,
    expert_first,
    expert_second,
    expert_grad,
    latent_master,
    latent_first,
    latent_second,
    latent_grad,
    step_count,
    column_owner,
):
    master_new, first_new, second_new = adamw_step(
        expert_master, expert_first, expert_second, expert_grad, step_count
    )
    latent_new, latent_one, latent_two = adamw_step(
        latent_master, latent_first, latent_second, latent_grad, step_count
    )
    dp_count = lax.axis_size("dp")
    dp_pos = lax.axis_index("dp")
    exp_count, row_count, col_count = master_new.shape
    block_count = col_count // TILE
    slot_count = max(1, block_count // dp_count)
    total_tiles = D // TILE
    recv_rows = block_count * row_count
    recv_tiles = recv_rows // TILE
    positions = jnp.arange(block_count, dtype=jnp.int32)
    inverse = jnp.sum(
        positions[:, None] * (column_owner[:, None] == positions[None, :]).astype(jnp.int32), axis=0
    )
    receiver_ids = jnp.arange(dp_count, dtype=jnp.int32)[:, None]
    slot_ids = jnp.arange(slot_count, dtype=jnp.int32)[None, :]
    segment = (
        receiver_ids * block_count
        + jnp.mod(dp_pos - receiver_ids * block_count, dp_count)
        + slot_ids * dp_count
    )
    usable_slot = (segment < (receiver_ids + 1) * block_count).reshape(-1)
    send_block = jnp.take(inverse, jnp.minimum(segment // dp_count, block_count - 1)).reshape(-1)
    local_segments = jnp.arange(block_count, dtype=jnp.int32)
    source_dev = jnp.mod(dp_pos * block_count + local_segments, dp_count)
    pick_index = source_dev * slot_count + local_segments // dp_count
    blocks = master_new.reshape(exp_count, row_count, block_count, TILE)
    picked = jnp.take(blocks, send_block, axis=2)
    received = lax.all_to_all(
        jnp.where(usable_slot[None, None, :, None], picked, jnp.zeros((), picked.dtype)),
        "dp",
        split_axis=2,
        concat_axis=2,
        tiled=True,
    )
    ordered = jnp.take(received, pick_index, axis=2)
    tall = (
        jnp.transpose(ordered, (0, 2, 1, 3))
        .reshape(exp_count, recv_rows, TILE)
        .reshape(exp_count, recv_tiles, TILE, TILE)
    )
    expert_scales = jnp.max(jnp.abs(tall), axis=(2, 3))
    expert_served = (
        (tall / (expert_scales[:, :, None, None] + SCALE_EPS))
        .reshape(exp_count, recv_rows, TILE)
        .astype(jnp.bfloat16)
    )
    latent_block = lax.all_gather(latent_new, "expert", axis=0, tiled=True)
    block_rows = latent_block.shape[0]
    block_offset = dp_pos * block_rows
    block_lead = block_offset % TILE
    block_tiles = local_tiles(row_maxima(latent_block)[None], block_lead)
    block_map = lax.pmax(place_tiles(block_tiles, block_offset // TILE), "dp")
    latent_scales = block_map[0, :total_tiles]
    block_tiles = lax.dynamic_slice_in_dim(block_map, block_offset // TILE, block_tiles.shape[1], 1)
    latent_served = quantized_rows(latent_block[None], block_tiles, block_lead)[0]
    return (
        master_new,
        first_new,
        second_new,
        expert_served,
        expert_scales,
        latent_new,
        latent_one,
        latent_two,
        latent_served,
        latent_scales,
    )


CHUNK = 32
F32 = jnp.float32
BF16 = jnp.bfloat16
VMEM_LIMIT = 60 * 1024 * 1024


def adamw_tile(w, m, v, g, rate, corr):
    g = g.astype(F32)
    m1 = BETA_ONE * m.astype(F32) + (1.0 - BETA_ONE) * g
    v1 = BETA_TWO * v.astype(F32) + (1.0 - BETA_TWO) * g * g
    x = v1 * corr
    inv = pl.reciprocal(x * lax.rsqrt(x) + ADAM_EPS, approx=True)
    w1 = (1.0 - LEARN_RATE * DECAY_RATE) * w - rate * m1 * inv
    return w1, m1.astype(BF16), v1.astype(BF16)


def sub_max(w1):
    return jnp.max(jnp.abs(w1).reshape(w1.shape[0] // 8, 8, TILE), axis=0)


def stack_max(parts):
    rows = [jnp.max(p, axis=0, keepdims=True) for p in parts]
    return jnp.max(jnp.concatenate(rows, axis=0), axis=1, keepdims=True)


def expert_kernel(first, blocks, lat_blocks, owner_ref, scal_ref, w_ref, m_ref, v_ref, g_ref, *refs):
    w1_ref, m1_ref, v1_ref, q_ref, s_ref = refs[-5:]
    step = pl.program_id(0)
    rate, corr = scal_ref[0], scal_ref[1]

    @pl.when(step == 0)
    def _():
        s_ref[...] = jnp.zeros_like(s_ref) if first == 0 else refs[0][...]

    parts = []
    for b in range(blocks):
        cols = pl.ds(b * TILE, TILE)
        w1, m1, v1 = adamw_tile(
            w_ref[:, cols], m_ref[:, cols], v_ref[:, cols], g_ref[:, cols], rate, corr
        )
        w1_ref[:, cols] = w1
        m1_ref[:, cols] = m1
        v1_ref[:, cols] = v1
        parts.append(sub_max(w1))
    top = stack_max(parts)
    inv = 1.0 / (top + SCALE_EPS)
    for b in range(blocks):
        slot = owner_ref[b]
        cols = pl.ds(b * TILE, TILE)
        q_ref[slot, 0] = (w1_ref[:, cols] * inv[b : b + 1, :]).astype(BF16)
        s_ref[slot, pl.ds(first + step, 1), :] = jnp.broadcast_to(top[b : b + 1, :], (1, TILE))

    if first > 0:
        @pl.when(step == pl.num_programs(0) - 1)
        def _():
            lane = lax.broadcasted_iota(jnp.int32, (8, TILE), 1)
            for b in range(blocks):
                s_ref[b] = jnp.where(lane < lat_blocks, refs[1][...], s_ref[b])


def expert_rows(arrays, owner, scal, first, count, state, tops, lat_tops, lat_blocks):
    rows, cols = arrays[0].shape
    blocks = cols // TILE
    spec = pl.BlockSpec((TILE, cols), lambda i, own: (first + i, 0))
    any_spec = pl.BlockSpec(memory_space=pl.ANY)
    small = pl.BlockSpec((blocks, 8, TILE), lambda i, own: (0, 0, 0))
    flat = pl.BlockSpec((8, TILE), lambda i, own: (0, 0))
    extra = () if first == 0 else (tops, lat_tops, *state)
    extra_specs = [] if first == 0 else [small, flat, any_spec, any_spec, any_spec]
    elems = TILE * cols * count
    out = pl.pallas_call(
        functools.partial(expert_kernel, first, blocks, lat_blocks),
        grid_spec=pltpu.PrefetchScalarGridSpec(
            num_scalar_prefetch=1,
            grid=(count,),
            in_specs=[pl.BlockSpec(memory_space=pltpu.SMEM)] + [spec] * 4 + extra_specs,
            out_specs=[spec] * 3
            + [pl.BlockSpec((blocks, 1, TILE, TILE), lambda i, own: (0, i, 0, 0)), small],
        ),
        out_shape=[
            jax.ShapeDtypeStruct((rows, cols), F32),
            jax.ShapeDtypeStruct((rows, cols), BF16),
            jax.ShapeDtypeStruct((rows, cols), BF16),
            jax.ShapeDtypeStruct((blocks, count, TILE, TILE), BF16),
            jax.ShapeDtypeStruct((blocks, 8, TILE), F32),
        ],
        input_output_aliases={} if first == 0 else {8: 0, 9: 1, 10: 2},
        compiler_params=pltpu.CompilerParams(vmem_limit_bytes=VMEM_LIMIT),
        cost_estimate=pl.CostEstimate(
            flops=30 * elems, bytes_accessed=20 * elems, transcendentals=2 * elems
        ),
        name="expert_adamw",
    )(owner, scal, *arrays, *extra)
    return out[:3], out[3], out[4]


def place_kernel(q_ref, *refs):
    out_ref = refs[-1]
    srcs, slots = q_ref.shape[:2]
    for s in range(srcs):
        for j in range(slots):
            out_ref[j, s, 0] = q_ref[s, j, 0]


def place_rows(served, q, first, tiles):
    srcs, slots, count = q.shape[:3]
    any_spec = pl.BlockSpec(memory_space=pl.ANY)
    have = served is not None
    return pl.pallas_call(
        place_kernel,
        grid=(count,),
        in_specs=[pl.BlockSpec((srcs, slots, 1, TILE, TILE), lambda i: (0, 0, i, 0, 0))]
        + [any_spec] * have,
        out_specs=pl.BlockSpec((slots, srcs, 1, TILE, TILE), lambda i: (0, 0, first + i, 0, 0)),
        out_shape=jax.ShapeDtypeStruct((slots, srcs, tiles, TILE, TILE), BF16),
        input_output_aliases={1: 0} if have else {},
        compiler_params=pltpu.CompilerParams(vmem_limit_bytes=VMEM_LIMIT),
        cost_estimate=pl.CostEstimate(flops=0, bytes_accessed=4 * q.size, transcendentals=0),
        name="place_served",
    )(q, *((served,) if have else ()))


def latent_kernel(chunks, width, scal_ref, w_ref, m_ref, v_ref, g_ref, w1_ref, m1_ref, v1_ref, top_ref):
    rate, corr = scal_ref[0], scal_ref[1]
    step = pl.program_id(0)
    lane = lax.broadcasted_iota(jnp.int32, (8, TILE), 1)

    @pl.when(step == 0)
    def _():
        top_ref[...] = jnp.zeros_like(top_ref)

    tops = top_ref[...]
    for b in range(width):
        cols = pl.ds(b * TILE, TILE)
        w1, m1, v1 = adamw_tile(
            w_ref[:, cols], m_ref[:, cols], v_ref[:, cols], g_ref[:, cols], rate, corr
        )
        w1_ref[:, cols] = w1
        m1_ref[:, cols] = m1
        v1_ref[:, cols] = v1
        parts = [sub_max(w1[c * CHUNK : (c + 1) * CHUNK]) for c in range(chunks)]
        parts += [parts[-1]] * (8 - chunks)
        tops = jnp.where(lane == step * width + b, stack_max(parts), tops)
    top_ref[...] = tops


def latent_update(arrays, scal):
    rows, cols = arrays[0].shape
    width = 3
    spec = pl.BlockSpec((rows, width * TILE), lambda i: (0, i))
    elems = rows * cols
    return pl.pallas_call(
        functools.partial(latent_kernel, rows // CHUNK, width),
        grid=(cols // (width * TILE),),
        in_specs=[pl.BlockSpec(memory_space=pltpu.SMEM)] + [spec] * 4,
        out_specs=[spec] * 3 + [pl.BlockSpec((8, TILE), lambda i: (0, 0))],
        out_shape=[
            jax.ShapeDtypeStruct((rows, cols), F32),
            jax.ShapeDtypeStruct((rows, cols), BF16),
            jax.ShapeDtypeStruct((rows, cols), BF16),
            jax.ShapeDtypeStruct((8, TILE), F32),
        ],
        compiler_params=pltpu.CompilerParams(vmem_limit_bytes=VMEM_LIMIT),
        cost_estimate=pl.CostEstimate(
            flops=30 * elems, bytes_accessed=18 * elems, transcendentals=2 * elems
        ),
        name="latent_adamw",
    )(scal, *arrays)


def latent_quant_kernel(chunks, peers, width, pos_ref, w1_ref, *refs):
    q_ref, tops_ref, ext = refs[-3:]
    per_tile = TILE // CHUNK
    step = pl.program_id(0)
    pos = pos_ref[0]

    @pl.when(step == 0)
    def _():
        for s in range(peers):
            at = lax.rem(pos + peers - s, peers) * chunks
            ext[pl.ds(at, chunks), :] = refs[s][0:chunks, :]
        tops_ref[...] = jnp.zeros_like(tops_ref)
        for t in range(peers * chunks // per_tile):
            tops_ref[t : t + 1, :] = jnp.max(
                ext[t * per_tile : (t + 1) * per_tile, :], axis=0, keepdims=True
            )

    lane = lax.broadcasted_iota(jnp.int32, (8, TILE), 1)
    rows = [tops_ref[pl.ds((pos * chunks + c) // per_tile, 1), :] for c in range(chunks)]
    rows += [rows[-1]] * (8 - chunks)
    mine = jnp.concatenate(rows, axis=0)
    for b in range(width):
        top = jnp.max(jnp.where(lane == step * width + b, mine, 0.0), axis=1, keepdims=True)
        inv = 1.0 / (top + SCALE_EPS)
        cols = pl.ds(b * TILE, TILE)
        for c in range(chunks):
            span = pl.ds(c * CHUNK, CHUNK)
            q_ref[span, cols] = (w1_ref[span, cols] * inv[c : c + 1, :]).astype(BF16)


def latent_quant(w1, maxima, pos):
    rows, cols = w1.shape
    width = 3
    chunks = rows // CHUNK
    peers = len(maxima)
    spec = pl.BlockSpec((rows, width * TILE), lambda i: (0, i))
    small = pl.BlockSpec((8, TILE), lambda i: (0, 0))
    return pl.pallas_call(
        functools.partial(latent_quant_kernel, chunks, peers, width),
        grid=(cols // (width * TILE),),
        in_specs=[pl.BlockSpec(memory_space=pltpu.SMEM), spec] + [small] * peers,
        out_specs=[spec, small],
        out_shape=[
            jax.ShapeDtypeStruct((rows, cols), BF16),
            jax.ShapeDtypeStruct((8, TILE), F32),
        ],
        scratch_shapes=[pltpu.VMEM((8 * peers, TILE), F32)],
        compiler_params=pltpu.CompilerParams(vmem_limit_bytes=VMEM_LIMIT),
        cost_estimate=pl.CostEstimate(
            flops=2 * rows * cols, bytes_accessed=6 * rows * cols, transcendentals=0
        ),
        name="latent_quant",
    )(pos, w1, *maxima)


def fast_fits(expert_shape, latent_shape, dp_count, exp_axis):
    exp_count, rows, cols = expert_shape
    latent_rows, latent_cols = latent_shape
    return (
        exp_count == 1
        and rows % TILE == 0
        and 2 * TILE <= rows <= 8 * TILE
        and cols % (TILE * dp_count) == 0
        and latent_rows % CHUNK == 0
        and latent_rows <= 8 * CHUNK
        and latent_rows * exp_axis % TILE == 0
        and latent_rows * exp_axis <= 8 * TILE
        and latent_cols % (3 * TILE) == 0
        and latent_cols < TILE * TILE
    )


def fast_body(
    expert_master,
    expert_first,
    expert_second,
    expert_grad,
    latent_master,
    latent_first,
    latent_second,
    latent_grad,
    step_count,
    column_owner,
):
    dp_count = lax.axis_size("dp")
    exp_axis = lax.axis_size("expert")
    exp_pos = lax.axis_index("expert")
    _, rows, cols = expert_master.shape
    block_count = cols // TILE
    per_dest = block_count // dp_count
    tiles = rows // TILE

    step_value = step_count[0].astype(F32)
    corr_one = 1.0 - jnp.power(F32(BETA_ONE), step_value)
    corr_two = 1.0 - jnp.power(F32(BETA_TWO), step_value)
    scal = jnp.stack([LEARN_RATE / corr_one, 1.0 / corr_two])

    latent_new, latent_one, latent_two, chunk_top = latent_update(
        (latent_master, latent_first, latent_second, latent_grad), scal
    )
    maxima = [chunk_top] + [
        lax.ppermute(chunk_top, "expert", [(i, (i + s) % exp_axis) for i in range(exp_axis)])
        for s in range(1, exp_axis)
    ]
    lat_blocks = latent_new.shape[1] // TILE
    latent_q, lat_tops = latent_quant(latent_new, maxima, exp_pos.astype(jnp.int32).reshape(1))
    latent_served = lax.all_gather(latent_q, "expert", axis=0, tiled=True)

    arrays = tuple(
        a.reshape(rows, cols) for a in (expert_master, expert_first, expert_second, expert_grad)
    )

    def exchange(x):
        x = x.reshape((dp_count, per_dest) + x.shape[1:])
        return lax.all_to_all(x, "dp", split_axis=0, concat_axis=0, tiled=True)

    half = (tiles + 1) // 2
    state, q, tops = expert_rows(
        arrays, column_owner, scal, 0, half, (), None, None, lat_blocks
    )
    got_one = exchange(q)
    state, q, tops = expert_rows(
        arrays, column_owner, scal, half, tiles - half, state, tops, lat_tops, lat_blocks
    )
    got_two = exchange(q)
    small = exchange(tops)
    served = place_rows(None, got_one, 0, tiles)
    served = place_rows(served, got_two, half, tiles)
    expert_served = served.reshape(1, block_count * rows, TILE)

    lat_tiles = latent_served.shape[0] // TILE
    latent_scales = small[:, 0, :lat_tiles, :lat_blocks].reshape(dp_count * lat_tiles, lat_blocks)
    expert_scales = jnp.transpose(small[:, :, :tiles, TILE - 1], (1, 0, 2))
    expert_scales = expert_scales.reshape(1, block_count * tiles)

    return (
        state[0][None],
        state[1][None],
        state[2][None],
        expert_served,
        expert_scales,
        latent_new,
        latent_one,
        latent_two,
        latent_served,
        latent_scales,
    )


def body(*args):
    if fast_fits(args[0].shape, args[4].shape, lax.axis_size("dp"), lax.axis_size("expert")):
        return fast_body(*args)
    return general_body(*args)


def solution(mesh):
    placed = (
        P("expert", "dp", None),
        P("expert", "dp", None),
        P("expert", "dp", None),
        P("expert", "dp", None),
        P(("dp", "expert"), None),
        P(("dp", "expert"), None),
        P(("dp", "expert"), None),
        P(("dp", "expert"), None),
        P(),
        P(),
    )
    return jax.shard_map(
        body,
        mesh=mesh,
        in_specs=placed,
        out_specs=(
            P("expert", "dp", None),
            P("expert", "dp", None),
            P("expert", "dp", None),
            P("expert", "dp", None),
            P("expert", "dp"),
            P(("dp", "expert"), None),
            P(("dp", "expert"), None),
            P(("dp", "expert"), None),
            P("dp", None),
            P(),
        ),
        check_vma=False,
    )
```

```python
import functools
import math

import jax
import jax.numpy as jnp
from jax import lax
from jax.experimental import pallas as pl
from jax.experimental.pallas import tpu as pltpu
from jax.sharding import PartitionSpec as P

D = 7168
TILE = 128


BETA_ONE = 0.9
BETA_TWO = 0.95
LEARN_RATE = 0.2
DECAY_RATE = 0.1
ADAM_EPS = 1e-08
SCALE_EPS = 1e-06


def adamw_step(master, moment_one, moment_two, gradient, step_count):
    grad_value = gradient.astype(jnp.float32)
    first_new = BETA_ONE * moment_one.astype(jnp.float32) + (1.0 - BETA_ONE) * grad_value
    second_new = (
        BETA_TWO * moment_two.astype(jnp.float32) + (1.0 - BETA_TWO) * grad_value * grad_value
    )
    step_value = step_count[0].astype(jnp.float32)
    corr_one = 1.0 - jnp.power(jnp.float32(BETA_ONE), step_value)
    corr_two = 1.0 - jnp.power(jnp.float32(BETA_TWO), step_value)
    update = first_new / corr_one / (jnp.sqrt(second_new / corr_two) + ADAM_EPS)
    master_new = master - LEARN_RATE * (update + DECAY_RATE * master)
    return (master_new, first_new.astype(jnp.bfloat16), second_new.astype(jnp.bfloat16))


def row_maxima(weights):
    leading = weights.shape[:-1]
    tile_count = weights.shape[-1] // TILE
    return jnp.max(jnp.abs(weights).reshape(leading + (tile_count, TILE)), axis=-1)


def local_tiles(row_max, lead_rows):
    exp_count, row_count, tile_count = row_max.shape
    tile_span = row_count // TILE + 2
    buffer = jnp.zeros((exp_count, tile_span * TILE, tile_count), jnp.float32)
    buffer = lax.dynamic_update_slice(buffer, row_max, (jnp.int32(0), lead_rows, jnp.int32(0)))
    return jnp.max(buffer.reshape(exp_count, tile_span, TILE, tile_count), axis=2)


def place_tiles(tile_max, first_tile):
    exp_count, tile_span, tile_count = tile_max.shape
    global_map = jnp.zeros((exp_count, D // TILE + tile_span, tile_count), jnp.float32)
    return lax.dynamic_update_slice(global_map, tile_max, (jnp.int32(0), first_tile, jnp.int32(0)))


def quantized_rows(weights, tile_max, lead_rows):
    exp_count, row_count, col_count = weights.shape
    repeated = jnp.repeat(tile_max, TILE, axis=1)
    row_scale = lax.dynamic_slice_in_dim(repeated, lead_rows, row_count, 1)
    blocks = weights.reshape(exp_count, row_count, col_count // TILE, TILE)
    return (blocks / (row_scale[..., None] + SCALE_EPS)).reshape(weights.shape).astype(jnp.bfloat16)


def general_body(
    expert_master,
    expert_first,
    expert_second,
    expert_grad,
    latent_master,
    latent_first,
    latent_second,
    latent_grad,
    step_count,
    column_owner,
):
    master_new, first_new, second_new = adamw_step(
        expert_master, expert_first, expert_second, expert_grad, step_count
    )
    latent_new, latent_one, latent_two = adamw_step(
        latent_master, latent_first, latent_second, latent_grad, step_count
    )
    dp_count = lax.axis_size("dp")
    dp_pos = lax.axis_index("dp")
    exp_count, row_count, col_count = master_new.shape
    block_count = col_count // TILE
    slot_count = max(1, block_count // dp_count)
    total_tiles = D // TILE
    recv_rows = block_count * row_count
    recv_tiles = recv_rows // TILE
    positions = jnp.arange(block_count, dtype=jnp.int32)
    inverse = jnp.sum(
        positions[:, None] * (column_owner[:, None] == positions[None, :]).astype(jnp.int32), axis=0
    )
    receiver_ids = jnp.arange(dp_count, dtype=jnp.int32)[:, None]
    slot_ids = jnp.arange(slot_count, dtype=jnp.int32)[None, :]
    segment = (
        receiver_ids * block_count
        + jnp.mod(dp_pos - receiver_ids * block_count, dp_count)
        + slot_ids * dp_count
    )
    usable_slot = (segment < (receiver_ids + 1) * block_count).reshape(-1)
    send_block = jnp.take(inverse, jnp.minimum(segment // dp_count, block_count - 1)).reshape(-1)
    local_segments = jnp.arange(block_count, dtype=jnp.int32)
    source_dev = jnp.mod(dp_pos * block_count + local_segments, dp_count)
    pick_index = source_dev * slot_count + local_segments // dp_count
    blocks = master_new.reshape(exp_count, row_count, block_count, TILE)
    picked = jnp.take(blocks, send_block, axis=2)
    received = lax.all_to_all(
        jnp.where(usable_slot[None, None, :, None], picked, jnp.zeros((), picked.dtype)),
        "dp",
        split_axis=2,
        concat_axis=2,
        tiled=True,
    )
    ordered = jnp.take(received, pick_index, axis=2)
    tall = (
        jnp.transpose(ordered, (0, 2, 1, 3))
        .reshape(exp_count, recv_rows, TILE)
        .reshape(exp_count, recv_tiles, TILE, TILE)
    )
    expert_scales = jnp.max(jnp.abs(tall), axis=(2, 3))
    expert_served = (
        (tall / (expert_scales[:, :, None, None] + SCALE_EPS))
        .reshape(exp_count, recv_rows, TILE)
        .astype(jnp.bfloat16)
    )
    latent_block = lax.all_gather(latent_new, "expert", axis=0, tiled=True)
    block_rows = latent_block.shape[0]
    block_offset = dp_pos * block_rows
    block_lead = block_offset % TILE
    block_tiles = local_tiles(row_maxima(latent_block)[None], block_lead)
    block_map = lax.pmax(place_tiles(block_tiles, block_offset // TILE), "dp")
    latent_scales = block_map[0, :total_tiles]
    block_tiles = lax.dynamic_slice_in_dim(block_map, block_offset // TILE, block_tiles.shape[1], 1)
    latent_served = quantized_rows(latent_block[None], block_tiles, block_lead)[0]
    return (
        master_new,
        first_new,
        second_new,
        expert_served,
        expert_scales,
        latent_new,
        latent_one,
        latent_two,
        latent_served,
        latent_scales,
    )


CHUNK = 32
EXTRA = 16
SPARE = 64
F32 = jnp.float32
BF16 = jnp.bfloat16
VMEM_LIMIT = 56 * 1024 * 1024
ANY = pl.BlockSpec(memory_space=pl.ANY)
SMEM = pl.BlockSpec(memory_space=pltpu.SMEM)
VMEM = pl.BlockSpec(memory_space=pltpu.VMEM)
PARAMS = pltpu.CompilerParams(vmem_limit_bytes=VMEM_LIMIT)
LIGHT = pltpu.CompilerParams(vmem_limit_bytes=1024 * 1024)


def corrections(step_ref):
    one, two = lax.fori_loop(
        0, step_ref[0], lambda _, p: (p[0] * BETA_ONE, p[1] * BETA_TWO), (F32(1.0), F32(1.0))
    )
    rate = LEARN_RATE / (1.0 - jnp.full((1, TILE), one, F32))
    corr = 1.0 / (1.0 - jnp.full((1, TILE), two, F32))
    return rate, corr


def adamw_tile(w, m, v, g, rate, corr):
    g = g.astype(F32)
    m1 = BETA_ONE * m.astype(F32) + (1.0 - BETA_ONE) * g
    v1 = BETA_TWO * v.astype(F32) + (1.0 - BETA_TWO) * g * g
    x = v1 * corr
    inv = pl.reciprocal(x * lax.rsqrt(x) + ADAM_EPS, approx=True)
    w1 = (1.0 - LEARN_RATE * DECAY_RATE) * w - rate * m1 * inv
    return w1, m1.astype(BF16), v1.astype(BF16)


def sub_max(w1):
    return jnp.max(jnp.abs(w1).reshape(w1.shape[0] // 8, 8, TILE), axis=0)


def stack_max(parts):
    parts = parts + [parts[-1]] * (8 - len(parts))
    rows = [jnp.max(p, axis=0, keepdims=True) for p in parts]
    return jnp.max(jnp.concatenate(rows, axis=0), axis=1, keepdims=True)


def three_parts(x):
    high = x.astype(BF16).astype(F32)
    rest = x - high
    middle = rest.astype(BF16).astype(F32)
    return high, middle, rest - middle


def copy_all(copies):
    for c in copies:
        c.start()


def wait_all(copies):
    for c in copies:
        c.wait()


def expert_kernel(partners, per_dest, n_alias, owner_ref, pos_ref, step_ref, lat_ref, *refs):
    hbm = refs[:4]
    outs = refs[4 + n_alias : 7 + n_alias]
    n_dest = len(partners)
    q_refs = refs[7 + n_alias : 7 + n_alias + n_dest]
    w, m, v, g, extra, in_sem, out_sem, extra_sem = refs[7 + n_alias + n_dest :]
    bufs = (w, m, v, g)
    blocks = owner_ref.shape[0]
    rows = w.shape[1]
    tiles = rows // TILE
    pos = pos_ref[0]

    loads, stores = [], []
    for d, k in enumerate(partners):
        for j in range(per_dest):
            i = d * per_dest + j
            slot = (pos ^ k) * per_dest + j
            block = jnp.int32(0)
            for b in range(blocks):
                block = jnp.where(owner_ref[b] == slot, b, block)
            cols = pl.ds(pl.multiple_of(block * TILE, TILE), TILE)
            loads.append(
                [
                    pltpu.make_async_copy(hbm[a].at[:, cols], bufs[a].at[i], in_sem.at[i, a])
                    for a in range(4)
                ]
            )
            stores.append(
                [
                    pltpu.make_async_copy(bufs[a].at[i], outs[a].at[:, cols], out_sem.at[i, a])
                    for a in range(3)
                ]
                + [
                    pltpu.make_async_copy(
                        g.at[i], q_refs[d].at[pl.ds(j * rows, rows), :], out_sem.at[i, 3]
                    )
                ]
            )
            copy_all(loads[-1])
    rate, corr = corrections(step_ref)
    lane = lax.broadcasted_iota(jnp.int32, (8, TILE), 1)
    extras = []
    for d in range(n_dest):
        side = lat_ref[...]
        for j in range(per_dest):
            i = d * per_dest + j
            wait_all(loads[i])
            parts = []
            for t in range(tiles):
                at = pl.ds(t * TILE, TILE)
                w1, m1, v1 = adamw_tile(w[i, at, :], m[i, at, :], v[i, at, :], g[i, at, :], rate, corr)
                w[i, at, :] = w1
                m[i, at, :] = m1
                v[i, at, :] = v1
                parts.append(sub_max(w1))
            copy_all(stores[i][:3])
            top = stack_max(parts)
            inv = 1.0 / (top + SCALE_EPS)
            for t in range(tiles):
                at = pl.ds(t * TILE, TILE)
                g[i, at, :] = (w[i, at, :] * inv[t : t + 1, :]).astype(BF16)
            stores[i][3].start()
            for p, value in enumerate(three_parts(top)):
                side = jnp.where(lane == SPARE + 3 * j + p, value, side)
        extra[d] = jnp.concatenate([side, jnp.zeros_like(side)], axis=0).astype(BF16)
        extras.append(
            pltpu.make_async_copy(
                extra.at[d], q_refs[d].at[pl.ds(per_dest * rows, EXTRA), :], extra_sem.at[d]
            )
        )
        extras[-1].start()
    for group in stores:
        wait_all(group)
    wait_all(extras)


def expert_group(arrays, state, owner, pos, step, lat, partners, per_dest):
    rows, cols = arrays[0].shape
    n_alias = len(state)
    n = len(partners) * per_dest
    elems = rows * TILE * n
    out = pl.pallas_call(
        functools.partial(expert_kernel, partners, per_dest, n_alias),
        in_specs=[SMEM] * 3 + [VMEM] + [ANY] * (4 + n_alias),
        out_specs=[ANY] * (3 + len(partners)),
        out_shape=[
            jax.ShapeDtypeStruct((rows, cols), F32),
            jax.ShapeDtypeStruct((rows, cols), BF16),
            jax.ShapeDtypeStruct((rows, cols), BF16),
        ]
        + [jax.ShapeDtypeStruct((per_dest * rows + EXTRA, TILE), BF16)] * len(partners),
        scratch_shapes=[
            pltpu.VMEM((n, rows, TILE), F32),
            pltpu.VMEM((n, rows, TILE), BF16),
            pltpu.VMEM((n, rows, TILE), BF16),
            pltpu.VMEM((n, rows, TILE), BF16),
            pltpu.VMEM((len(partners), EXTRA, TILE), BF16),
            pltpu.SemaphoreType.DMA((n, 4)),
            pltpu.SemaphoreType.DMA((n, 4)),
            pltpu.SemaphoreType.DMA((len(partners),)),
        ],
        input_output_aliases={8 + i: i for i in range(n_alias)},
        compiler_params=PARAMS,
        cost_estimate=pl.CostEstimate(
            flops=30 * elems, bytes_accessed=20 * elems, transcendentals=2 * elems
        ),
        name="expert_adamw",
    )(owner, pos, step, lat, *arrays, *state)
    return out[:3], out[3:]


def place_kernel(src_ref, q_ref, *refs):
    served, sem = refs[-2:]
    per_dest, _, rows, _ = served.shape
    src = src_ref[0]
    copies = [
        pltpu.make_async_copy(q_ref.at[pl.ds(j * rows, rows), :], served.at[j, src], sem.at[j])
        for j in range(per_dest)
    ]
    copy_all(copies)
    wait_all(copies)


def place_rows(placed, src, q, dp_count, per_dest):
    rows = (q.shape[0] - EXTRA) // per_dest
    return pl.pallas_call(
        place_kernel,
        in_specs=[SMEM] + [ANY] * (1 + len(placed)),
        out_specs=ANY,
        out_shape=jax.ShapeDtypeStruct((per_dest, dp_count, rows, TILE), BF16),
        scratch_shapes=[pltpu.SemaphoreType.DMA((per_dest,))],
        input_output_aliases={2: 0} if placed else {},
        compiler_params=LIGHT,
        cost_estimate=pl.CostEstimate(flops=0, bytes_accessed=4 * q.size, transcendentals=0),
        name="place_served",
    )(src, q, *placed)


def scales_kernel(order, tiles, lat_tiles, pos_ref, *refs):
    n = len(order)
    q_refs = refs[:n]
    exp_ref, lat_ref, extra, rows_ref, sem = refs[n:]
    at = q_refs[0].shape[0] - EXTRA
    per_dest = at // (tiles * TILE)
    copies = [
        pltpu.make_async_copy(q.at[pl.ds(at, EXTRA), :], extra.at[i], sem.at[i])
        for i, q in enumerate(q_refs)
    ]
    copy_all(copies)
    rows_ref[...] = jnp.zeros_like(rows_ref)
    lane = lax.broadcasted_iota(jnp.int32, (8, TILE), 1)
    sub = lax.broadcasted_iota(jnp.int32, (8, TILE), 0)
    flat = jnp.zeros((8, exp_ref.shape[1]), F32)
    wide = lax.broadcasted_iota(jnp.int32, flat.shape, 1)
    deep = lax.broadcasted_iota(jnp.int32, flat.shape, 0)
    for i, k in enumerate(order):
        copies[i].wait()
        src = pos_ref[0] ^ k
        x = extra[i].astype(F32)[0:8, :]
        lat = x + pltpu.roll(x, TILE - 16, 1) + pltpu.roll(x, TILE - 32, 1)
        rows_ref[pl.ds(src * lat_tiles, lat_tiles), :] = lat[0:lat_tiles, :]
        for j in range(per_dest):
            first = SPARE + 3 * j
            top = x[:, first : first + 1] + x[:, first + 1 : first + 2] + x[:, first + 2 : first + 3]
            hit = (wide == (j * n + src) * tiles + deep) & (deep < tiles)
            flat = jnp.where(hit, top, flat)
    exp_ref[...] = jnp.max(flat, axis=0, keepdims=True)
    blocks, height = lat_ref.shape
    lat_ref[...] = jnp.transpose(rows_ref[...])[0:blocks, 0:height]


def all_scales(pos, received, order, tiles, lat_tiles, lat_blocks):
    n = len(order)
    per_dest = (received[0].shape[0] - EXTRA) // (tiles * TILE)
    expert, latent = pl.pallas_call(
        functools.partial(scales_kernel, order, tiles, lat_tiles),
        in_specs=[SMEM] + [ANY] * n,
        out_specs=[VMEM, VMEM],
        out_shape=[
            jax.ShapeDtypeStruct((1, per_dest * n * tiles), F32),
            jax.ShapeDtypeStruct((lat_blocks, n * lat_tiles), F32),
        ],
        scratch_shapes=[
            pltpu.VMEM((n, EXTRA, TILE), BF16),
            pltpu.VMEM((TILE, TILE), F32),
            pltpu.SemaphoreType.DMA((n,)),
        ],
        compiler_params=LIGHT,
        cost_estimate=pl.CostEstimate(
            flops=1000000, bytes_accessed=100000, transcendentals=0
        ),
        name="all_scales",
    )(pos, *received)
    return expert, latent.T


def spread_copy_kernel(pieces, x_ref, o_ref, sem):
    rows = x_ref.shape[0] // pieces
    copies = [
        pltpu.make_async_copy(
            x_ref.at[pl.ds(i * rows, rows), :], o_ref.at[pl.ds(i * rows, rows), :], sem.at[i]
        )
        for i in range(pieces)
    ]
    copy_all(copies)
    wait_all(copies)


def spread_copy(x):
    pieces = x.shape[0] // TILE
    return pl.pallas_call(
        functools.partial(spread_copy_kernel, pieces),
        in_specs=[ANY],
        out_specs=ANY,
        out_shape=jax.ShapeDtypeStruct(x.shape, x.dtype),
        scratch_shapes=[pltpu.SemaphoreType.DMA((pieces,))],
        compiler_params=pltpu.CompilerParams(vmem_limit_bytes=VMEM_LIMIT + 4 * 1024 * 1024),
        cost_estimate=pl.CostEstimate(flops=0, bytes_accessed=4 * x.size, transcendentals=0),
        name="latent_copy",
    )(x)


SLABS = 4


def latent_kernel(chunks, step_ref, *refs):
    hbm, outs, top_ref = refs[:4], refs[4:7], refs[7]
    w, m, v, g, in_sem, out_sem = refs[8:]
    bufs = (w, m, v, g)
    width = w.shape[1] // SLABS
    loads, stores = [], []
    for i in range(SLABS):
        cols = pl.ds(i * width, width)
        loads.append(
            [
                pltpu.make_async_copy(hbm[a].at[:, cols], bufs[a].at[:, cols], in_sem.at[i, a])
                for a in range(4)
            ]
        )
        stores.append(
            [
                pltpu.make_async_copy(bufs[a].at[:, cols], outs[a].at[:, cols], out_sem.at[i, a])
                for a in range(3)
            ]
        )
        copy_all(loads[i])
    rate, corr = corrections(step_ref)
    lane = lax.broadcasted_iota(jnp.int32, (8, TILE), 1)
    tops = jnp.zeros((8, TILE), F32)
    for i in range(SLABS):
        wait_all(loads[i])
        for b in range(i * width // TILE, (i + 1) * width // TILE):
            cols = pl.ds(b * TILE, TILE)
            w1, m1, v1 = adamw_tile(w[:, cols], m[:, cols], v[:, cols], g[:, cols], rate, corr)
            w[:, cols] = w1
            m[:, cols] = m1
            v[:, cols] = v1
            parts = [sub_max(w1[c * CHUNK : (c + 1) * CHUNK]) for c in range(chunks)]
            tops = jnp.where(lane == b, stack_max(parts), tops)
        copy_all(stores[i])
    top_ref[...] = tops
    for group in stores:
        wait_all(group)


def latent_update(arrays, step):
    rows, cols = arrays[0].shape
    elems = rows * cols
    return pl.pallas_call(
        functools.partial(latent_kernel, rows // CHUNK),
        in_specs=[SMEM] + [ANY] * 4,
        out_specs=[ANY] * 3 + [VMEM],
        out_shape=[
            jax.ShapeDtypeStruct((rows, cols), F32),
            jax.ShapeDtypeStruct((rows, cols), BF16),
            jax.ShapeDtypeStruct((rows, cols), BF16),
            jax.ShapeDtypeStruct((8, TILE), F32),
        ],
        scratch_shapes=[
            pltpu.VMEM((rows, cols), F32),
            pltpu.VMEM((rows, cols), BF16),
            pltpu.VMEM((rows, cols), BF16),
            pltpu.VMEM((rows, cols), BF16),
            pltpu.SemaphoreType.DMA((SLABS, 4)),
            pltpu.SemaphoreType.DMA((SLABS, 3)),
        ],
        compiler_params=PARAMS,
        cost_estimate=pl.CostEstimate(
            flops=30 * elems, bytes_accessed=18 * elems, transcendentals=2 * elems
        ),
        name="latent_adamw",
    )(step, *arrays)


def latent_quant_kernel(chunks, peers, pos_ref, w1_ref, *refs):
    q_ref, side_ref, w, q, ext, tops_ref, in_sem, out_sem = refs[peers:]
    per_tile = TILE // CHUNK
    width = w.shape[1] // SLABS
    pos = pos_ref[0]
    slabs = [pl.ds(i * width, width) for i in range(SLABS)]
    loads = [
        pltpu.make_async_copy(w1_ref.at[:, c], w.at[:, c], in_sem.at[i]) for i, c in enumerate(slabs)
    ]
    stores = [
        pltpu.make_async_copy(q.at[:, c], q_ref.at[:, c], out_sem.at[i]) for i, c in enumerate(slabs)
    ]
    copy_all(loads)
    for s in range(peers):
        at = lax.rem(pos + peers - s, peers) * chunks
        ext[pl.ds(at, chunks), :] = refs[s][0:chunks, :]
    tops_ref[...] = jnp.zeros_like(tops_ref)
    for t in range(peers * chunks // per_tile):
        tops_ref[t : t + 1, :] = jnp.max(
            ext[t * per_tile : (t + 1) * per_tile, :], axis=0, keepdims=True
        )
    lane = lax.broadcasted_iota(jnp.int32, (8, TILE), 1)
    side = jnp.zeros((8, TILE), F32)
    for p, value in enumerate(three_parts(tops_ref[...])):
        value = pltpu.roll(value, 16 * p, 1) if p else value
        side = jnp.where((lane >= 16 * p) & (lane < 16 * p + 16), value, side)
    side_ref[...] = side

    rows = [tops_ref[pl.ds((pos * chunks + c) // per_tile, 1), :] for c in range(chunks)]
    rows += [rows[-1]] * (8 - chunks)
    mine = jnp.concatenate(rows, axis=0)
    for i in range(SLABS):
        loads[i].wait()
        for b in range(i * width // TILE, (i + 1) * width // TILE):
            top = jnp.max(jnp.where(lane == b, mine, 0.0), axis=1, keepdims=True)
            inv = 1.0 / (top + SCALE_EPS)
            cols = pl.ds(b * TILE, TILE)
            for c in range(chunks):
                span = pl.ds(c * CHUNK, CHUNK)
                q[span, cols] = (w[span, cols] * inv[c : c + 1, :]).astype(BF16)
        stores[i].start()
    wait_all(stores)


def latent_quant(w1, maxima, pos):
    rows, cols = w1.shape
    chunks = rows // CHUNK
    peers = len(maxima)
    return pl.pallas_call(
        functools.partial(latent_quant_kernel, chunks, peers),
        in_specs=[SMEM, ANY] + [VMEM] * peers,
        out_specs=[ANY, VMEM],
        out_shape=[
            jax.ShapeDtypeStruct((rows, cols), BF16),
            jax.ShapeDtypeStruct((8, TILE), F32),
        ],
        scratch_shapes=[
            pltpu.VMEM((rows, cols), F32),
            pltpu.VMEM((rows, cols), BF16),
            pltpu.VMEM((8 * peers, TILE), F32),
            pltpu.VMEM((8, TILE), F32),
            pltpu.SemaphoreType.DMA((SLABS,)),
            pltpu.SemaphoreType.DMA((SLABS,)),
        ],
        compiler_params=PARAMS,
        cost_estimate=pl.CostEstimate(
            flops=2 * rows * cols, bytes_accessed=6 * rows * cols, transcendentals=0
        ),
        name="latent_quant",
    )(pos, w1, *maxima)


def fast_fits(expert_shape, latent_shape, dp_count, exp_axis):
    exp_count, rows, cols = expert_shape
    latent_rows, latent_cols = latent_shape
    return (
        exp_count == 1
        and rows % TILE == 0
        and rows <= 8 * TILE
        and cols % (TILE * dp_count) == 0
        and cols // TILE // dp_count <= 20
        and dp_count >= 4
        and dp_count & (dp_count - 1) == 0
        and dp_count * latent_rows * exp_axis <= TILE * TILE
        and latent_rows % CHUNK == 0
        and latent_rows <= 8 * CHUNK
        and latent_rows * exp_axis % TILE == 0
        and latent_rows * exp_axis <= 8 * TILE
        and latent_cols % (SLABS * TILE) == 0
        and latent_cols <= 16 * TILE
    )


def partner_groups(dp_count):
    hops = lambda k: bin(k >> 1).count("1")
    stage = lambda k: 3 if k < 2 else (1 if hops(k) > 1 else (2 if k & 1 else 0))
    order = sorted(range(dp_count), key=lambda k: (stage(k), -k))
    first = [k for k in order if stage(k) == 0]
    second = [k for k in order if stage(k) == 1]
    return [g for g in (first, second, [k for k in order if stage(k) > 1]) if g]


def fast_body(
    expert_master,
    expert_first,
    expert_second,
    expert_grad,
    latent_master,
    latent_first,
    latent_second,
    latent_grad,
    step_count,
    column_owner,
):
    dp_count = lax.axis_size("dp")
    dp_pos = lax.axis_index("dp").astype(jnp.int32)
    exp_axis = lax.axis_size("expert")
    exp_pos = lax.axis_index("expert").astype(jnp.int32)
    _, rows, cols = expert_master.shape
    block_count = cols // TILE
    per_dest = block_count // dp_count
    tiles = rows // TILE

    latent_new, latent_one, latent_two, chunk_top = latent_update(
        (latent_master, latent_first, latent_second, latent_grad), step_count
    )
    maxima = [chunk_top] + [
        lax.ppermute(chunk_top, "expert", [(i, (i + s) % exp_axis) for i in range(exp_axis)])
        for s in range(1, exp_axis)
    ]
    latent_q, side = latent_quant(latent_new, maxima, exp_pos.reshape(1))
    latent_served = spread_copy(lax.all_gather(latent_q, "expert", axis=0, tiled=True))

    arrays = tuple(
        a.reshape(rows, cols) for a in (expert_master, expert_first, expert_second, expert_grad)
    )
    state, arrived = (), []
    for partners in partner_groups(dp_count):
        state, sent = expert_group(
            arrays, state, column_owner, dp_pos.reshape(1), step_count, side, partners, per_dest
        )
        for k, q in zip(partners, sent):
            pairs = [(i, i ^ k) for i in range(dp_count)]
            arrived.append((k, lax.ppermute(q, "dp", pairs) if k else q))
    placed = ()
    for k, q in arrived[-1:] + arrived[:-1]:
        placed = (place_rows(placed, (dp_pos ^ k).reshape(1), q, dp_count, per_dest),)
    expert_served = placed[0].reshape(1, block_count * rows, TILE)
    expert_scales, latent_scales = all_scales(
        dp_pos.reshape(1),
        [q for _, q in arrived],
        [k for k, _ in arrived],
        tiles,
        latent_served.shape[0] // TILE,
        latent_new.shape[1] // TILE,
    )

    return (
        state[0][None],
        state[1][None],
        state[2][None],
        expert_served,
        expert_scales,
        latent_new,
        latent_one,
        latent_two,
        latent_served,
        latent_scales,
    )


def body(*args):
    if fast_fits(args[0].shape, args[4].shape, lax.axis_size("dp"), lax.axis_size("expert")):
        return fast_body(*args)
    return general_body(*args)


def solution(mesh):
    placed = (
        P("expert", "dp", None),
        P("expert", "dp", None),
        P("expert", "dp", None),
        P("expert", "dp", None),
        P(("dp", "expert"), None),
        P(("dp", "expert"), None),
        P(("dp", "expert"), None),
        P(("dp", "expert"), None),
        P(),
        P(),
    )
    return jax.shard_map(
        body,
        mesh=mesh,
        in_specs=placed,
        out_specs=(
            P("expert", "dp", None),
            P("expert", "dp", None),
            P("expert", "dp", None),
            P("expert", "dp", None),
            P("expert", "dp"),
            P(("dp", "expert"), None),
            P(("dp", "expert"), None),
            P(("dp", "expert"), None),
            P("dp", None),
            P(),
        ),
        check_vma=False,
    )
```

```python
import functools
import math

import jax
import jax.numpy as jnp
from jax import lax
from jax.experimental import pallas as pl
from jax.experimental.pallas import tpu as pltpu
from jax.sharding import PartitionSpec as P

D = 7168
TILE = 128


BETA_ONE = 0.9
BETA_TWO = 0.95
LEARN_RATE = 0.2
DECAY_RATE = 0.1
ADAM_EPS = 1e-08
SCALE_EPS = 1e-06


def adamw_step(master, moment_one, moment_two, gradient, step_count):
    grad_value = gradient.astype(jnp.float32)
    first_new = BETA_ONE * moment_one.astype(jnp.float32) + (1.0 - BETA_ONE) * grad_value
    second_new = (
        BETA_TWO * moment_two.astype(jnp.float32) + (1.0 - BETA_TWO) * grad_value * grad_value
    )
    step_value = step_count[0].astype(jnp.float32)
    corr_one = 1.0 - jnp.power(jnp.float32(BETA_ONE), step_value)
    corr_two = 1.0 - jnp.power(jnp.float32(BETA_TWO), step_value)
    update = first_new / corr_one / (jnp.sqrt(second_new / corr_two) + ADAM_EPS)
    master_new = master - LEARN_RATE * (update + DECAY_RATE * master)
    return (master_new, first_new.astype(jnp.bfloat16), second_new.astype(jnp.bfloat16))


def row_maxima(weights):
    leading = weights.shape[:-1]
    tile_count = weights.shape[-1] // TILE
    return jnp.max(jnp.abs(weights).reshape(leading + (tile_count, TILE)), axis=-1)


def local_tiles(row_max, lead_rows):
    exp_count, row_count, tile_count = row_max.shape
    tile_span = row_count // TILE + 2
    buffer = jnp.zeros((exp_count, tile_span * TILE, tile_count), jnp.float32)
    buffer = lax.dynamic_update_slice(buffer, row_max, (jnp.int32(0), lead_rows, jnp.int32(0)))
    return jnp.max(buffer.reshape(exp_count, tile_span, TILE, tile_count), axis=2)


def place_tiles(tile_max, first_tile):
    exp_count, tile_span, tile_count = tile_max.shape
    global_map = jnp.zeros((exp_count, D // TILE + tile_span, tile_count), jnp.float32)
    return lax.dynamic_update_slice(global_map, tile_max, (jnp.int32(0), first_tile, jnp.int32(0)))


def quantized_rows(weights, tile_max, lead_rows):
    exp_count, row_count, col_count = weights.shape
    repeated = jnp.repeat(tile_max, TILE, axis=1)
    row_scale = lax.dynamic_slice_in_dim(repeated, lead_rows, row_count, 1)
    blocks = weights.reshape(exp_count, row_count, col_count // TILE, TILE)
    return (blocks / (row_scale[..., None] + SCALE_EPS)).reshape(weights.shape).astype(jnp.bfloat16)


def general_body(
    expert_master,
    expert_first,
    expert_second,
    expert_grad,
    latent_master,
    latent_first,
    latent_second,
    latent_grad,
    step_count,
    column_owner,
):
    master_new, first_new, second_new = adamw_step(
        expert_master, expert_first, expert_second, expert_grad, step_count
    )
    latent_new, latent_one, latent_two = adamw_step(
        latent_master, latent_first, latent_second, latent_grad, step_count
    )
    dp_count = lax.axis_size("dp")
    dp_pos = lax.axis_index("dp")
    exp_count, row_count, col_count = master_new.shape
    block_count = col_count // TILE
    slot_count = max(1, block_count // dp_count)
    total_tiles = D // TILE
    recv_rows = block_count * row_count
    recv_tiles = recv_rows // TILE
    positions = jnp.arange(block_count, dtype=jnp.int32)
    inverse = jnp.sum(
        positions[:, None] * (column_owner[:, None] == positions[None, :]).astype(jnp.int32), axis=0
    )
    receiver_ids = jnp.arange(dp_count, dtype=jnp.int32)[:, None]
    slot_ids = jnp.arange(slot_count, dtype=jnp.int32)[None, :]
    segment = (
        receiver_ids * block_count
        + jnp.mod(dp_pos - receiver_ids * block_count, dp_count)
        + slot_ids * dp_count
    )
    usable_slot = (segment < (receiver_ids + 1) * block_count).reshape(-1)
    send_block = jnp.take(inverse, jnp.minimum(segment // dp_count, block_count - 1)).reshape(-1)
    local_segments = jnp.arange(block_count, dtype=jnp.int32)
    source_dev = jnp.mod(dp_pos * block_count + local_segments, dp_count)
    pick_index = source_dev * slot_count + local_segments // dp_count
    blocks = master_new.reshape(exp_count, row_count, block_count, TILE)
    picked = jnp.take(blocks, send_block, axis=2)
    received = lax.all_to_all(
        jnp.where(usable_slot[None, None, :, None], picked, jnp.zeros((), picked.dtype)),
        "dp",
        split_axis=2,
        concat_axis=2,
        tiled=True,
    )
    ordered = jnp.take(received, pick_index, axis=2)
    tall = (
        jnp.transpose(ordered, (0, 2, 1, 3))
        .reshape(exp_count, recv_rows, TILE)
        .reshape(exp_count, recv_tiles, TILE, TILE)
    )
    expert_scales = jnp.max(jnp.abs(tall), axis=(2, 3))
    expert_served = (
        (tall / (expert_scales[:, :, None, None] + SCALE_EPS))
        .reshape(exp_count, recv_rows, TILE)
        .astype(jnp.bfloat16)
    )
    latent_block = lax.all_gather(latent_new, "expert", axis=0, tiled=True)
    block_rows = latent_block.shape[0]
    block_offset = dp_pos * block_rows
    block_lead = block_offset % TILE
    block_tiles = local_tiles(row_maxima(latent_block)[None], block_lead)
    block_map = lax.pmax(place_tiles(block_tiles, block_offset // TILE), "dp")
    latent_scales = block_map[0, :total_tiles]
    block_tiles = lax.dynamic_slice_in_dim(block_map, block_offset // TILE, block_tiles.shape[1], 1)
    latent_served = quantized_rows(latent_block[None], block_tiles, block_lead)[0]
    return (
        master_new,
        first_new,
        second_new,
        expert_served,
        expert_scales,
        latent_new,
        latent_one,
        latent_two,
        latent_served,
        latent_scales,
    )


CHUNK = 32
EXTRA = 16
F32 = jnp.float32
BF16 = jnp.bfloat16
VMEM_LIMIT = 56 * 1024 * 1024
ANY = pl.BlockSpec(memory_space=pl.ANY)
SMEM = pl.BlockSpec(memory_space=pltpu.SMEM)
VMEM = pl.BlockSpec(memory_space=pltpu.VMEM)
PARAMS = pltpu.CompilerParams(vmem_limit_bytes=VMEM_LIMIT)
LIGHT = pltpu.CompilerParams(vmem_limit_bytes=1024 * 1024)


def corrections(step_ref):
    one, two = lax.fori_loop(
        0, step_ref[0], lambda _, p: (p[0] * BETA_ONE, p[1] * BETA_TWO), (F32(1.0), F32(1.0))
    )
    rate = LEARN_RATE / (1.0 - jnp.full((1, TILE), one, F32))
    corr = 1.0 / (1.0 - jnp.full((1, TILE), two, F32))
    return rate, corr


def adamw_tile(w, m, v, g, rate, corr):
    g = g.astype(F32)
    m1 = BETA_ONE * m.astype(F32) + (1.0 - BETA_ONE) * g
    v1 = BETA_TWO * v.astype(F32) + (1.0 - BETA_TWO) * g * g
    x = v1 * corr
    inv = pl.reciprocal(x * lax.rsqrt(x) + ADAM_EPS, approx=True)
    w1 = (1.0 - LEARN_RATE * DECAY_RATE) * w - rate * m1 * inv
    return w1, m1.astype(BF16), v1.astype(BF16)


def sub_max(w1):
    return jnp.max(jnp.abs(w1).reshape(w1.shape[0] // 8, 8, TILE), axis=0)


def stack_max(parts):
    parts = parts + [parts[-1]] * (8 - len(parts))
    rows = [jnp.max(p, axis=0, keepdims=True) for p in parts]
    return jnp.max(jnp.concatenate(rows, axis=0), axis=1, keepdims=True)


def three_parts(x):
    high = x.astype(BF16).astype(F32)
    rest = x - high
    middle = rest.astype(BF16).astype(F32)
    return high, middle, rest - middle


def copy_all(copies):
    for c in copies:
        c.start()


def wait_all(copies):
    for c in copies:
        c.wait()


def expert_kernel(partners, per_dest, n_alias, n_after, owner_ref, pos_ref, step_ref, *refs):
    refs = refs[: 4 + n_alias] + refs[4 + n_alias + n_after :]
    hbm = refs[:4]
    outs = refs[4 + n_alias : 7 + n_alias]
    n_dest = len(partners)
    q_refs = refs[7 + n_alias : 7 + n_alias + n_dest]
    w, m, v, g, extra, in_sem, out_sem, extra_sem = refs[7 + n_alias + n_dest :]
    bufs = (w, m, v, g)
    blocks = owner_ref.shape[0]
    rows = w.shape[1]
    tiles = rows // TILE
    pos = pos_ref[0]

    loads, stores = [], []
    for d, k in enumerate(partners):
        for j in range(per_dest):
            i = d * per_dest + j
            slot = (pos ^ k) * per_dest + j
            block = jnp.int32(0)
            for b in range(blocks):
                block = jnp.where(owner_ref[b] == slot, b, block)
            cols = pl.ds(pl.multiple_of(block * TILE, TILE), TILE)
            loads.append(
                [
                    pltpu.make_async_copy(hbm[a].at[:, cols], bufs[a].at[i], in_sem.at[i, a])
                    for a in range(4)
                ]
            )
            stores.append(
                [
                    pltpu.make_async_copy(bufs[a].at[i], outs[a].at[:, cols], out_sem.at[i, a])
                    for a in range(3)
                ]
                + [
                    pltpu.make_async_copy(
                        g.at[i], q_refs[d].at[pl.ds(j * rows, rows), :], out_sem.at[i, 3]
                    )
                ]
            )
            copy_all(loads[-1])
    rate, corr = corrections(step_ref)
    lane = lax.broadcasted_iota(jnp.int32, (8, TILE), 1)
    extras = []
    for d in range(n_dest):
        side = jnp.zeros((8, TILE), F32)
        for j in range(per_dest):
            i = d * per_dest + j
            wait_all(loads[i])
            parts = []
            for t in range(tiles):
                at = pl.ds(t * TILE, TILE)
                w1, m1, v1 = adamw_tile(w[i, at, :], m[i, at, :], v[i, at, :], g[i, at, :], rate, corr)
                w[i, at, :] = w1
                m[i, at, :] = m1
                v[i, at, :] = v1
                parts.append(sub_max(w1))
            copy_all(stores[i][:3])
            top = stack_max(parts)
            inv = 1.0 / (top + SCALE_EPS)
            for t in range(tiles):
                at = pl.ds(t * TILE, TILE)
                g[i, at, :] = (w[i, at, :] * inv[t : t + 1, :]).astype(BF16)
            stores[i][3].start()
            for p, value in enumerate(three_parts(top)):
                side = jnp.where(lane == 3 * j + p, value, side)
        extra[d] = jnp.concatenate([side, jnp.zeros_like(side)], axis=0).astype(BF16)
        extras.append(
            pltpu.make_async_copy(
                extra.at[d], q_refs[d].at[pl.ds(per_dest * rows, EXTRA), :], extra_sem.at[d]
            )
        )
        extras[-1].start()
    for group in stores:
        wait_all(group)
    wait_all(extras)


def expert_group(arrays, state, owner, pos, step, after, partners, per_dest):
    rows, cols = arrays[0].shape
    n_alias = len(state)
    n = len(partners) * per_dest
    elems = rows * TILE * n
    out = pl.pallas_call(
        functools.partial(expert_kernel, partners, per_dest, n_alias, len(after)),
        in_specs=[SMEM] * 3 + [ANY] * (4 + n_alias + len(after)),
        out_specs=[ANY] * (3 + len(partners)),
        out_shape=[
            jax.ShapeDtypeStruct((rows, cols), F32),
            jax.ShapeDtypeStruct((rows, cols), BF16),
            jax.ShapeDtypeStruct((rows, cols), BF16),
        ]
        + [jax.ShapeDtypeStruct((per_dest * rows + EXTRA, TILE), BF16)] * len(partners),
        scratch_shapes=[
            pltpu.VMEM((n, rows, TILE), F32),
            pltpu.VMEM((n, rows, TILE), BF16),
            pltpu.VMEM((n, rows, TILE), BF16),
            pltpu.VMEM((n, rows, TILE), BF16),
            pltpu.VMEM((len(partners), EXTRA, TILE), BF16),
            pltpu.SemaphoreType.DMA((n, 4)),
            pltpu.SemaphoreType.DMA((n, 4)),
            pltpu.SemaphoreType.DMA((len(partners),)),
        ],
        input_output_aliases={7 + i: i for i in range(n_alias)},
        compiler_params=PARAMS,
        cost_estimate=pl.CostEstimate(flops=elems, bytes_accessed=elems, transcendentals=0),
        name="expert_adamw",
    )(owner, pos, step, *arrays, *state, *after)
    return out[:3], out[3:]


def place_kernel(src_ref, q_ref, *refs):
    served, sem = refs[-2:]
    per_dest, _, rows, _ = served.shape
    src = src_ref[0]
    copies = [
        pltpu.make_async_copy(q_ref.at[pl.ds(j * rows, rows), :], served.at[j, src], sem.at[j])
        for j in range(per_dest)
    ]
    copy_all(copies)
    wait_all(copies)


def place_rows(placed, src, q, dp_count, per_dest):
    rows = (q.shape[0] - EXTRA) // per_dest
    return pl.pallas_call(
        place_kernel,
        in_specs=[SMEM] + [ANY] * (1 + len(placed)),
        out_specs=ANY,
        out_shape=jax.ShapeDtypeStruct((per_dest, dp_count, rows, TILE), BF16),
        scratch_shapes=[pltpu.SemaphoreType.DMA((per_dest,))],
        input_output_aliases={2: 0} if placed else {},
        compiler_params=LIGHT,
        cost_estimate=pl.CostEstimate(flops=0, bytes_accessed=4 * q.size, transcendentals=0),
        name="place_served",
    )(src, q, *placed)


def scales_kernel(order, tiles, chunks, pos_ref, maxima_ref, *refs):
    n = len(order)
    q_refs = refs[:n]
    exp_ref, lat_ref, extra, rows_ref, tops_ref, sem = refs[n:]
    at = q_refs[0].shape[0] - EXTRA
    per_dest = at // (tiles * TILE)
    per_tile = TILE // CHUNK
    copies = [
        pltpu.make_async_copy(q.at[pl.ds(at, EXTRA), :], extra.at[i], sem.at[i])
        for i, q in enumerate(q_refs)
    ]
    copy_all(copies)
    for d in range(maxima_ref.shape[0] // 8):
        rows_ref[d * chunks : (d + 1) * chunks, :] = maxima_ref[8 * d : 8 * d + chunks, :]
    blocks, height = lat_ref.shape
    tops = rows_ref[pl.ds(0, height, stride=per_tile), :]
    for r in range(1, per_tile):
        tops = jnp.maximum(tops, rows_ref[pl.ds(r, height, stride=per_tile), :])
    tops_ref[...] = jnp.zeros_like(tops_ref)
    tops_ref[0:height, :] = tops
    lat_ref[...] = jnp.transpose(tops_ref[...])[0:blocks, 0:height]
    flat = jnp.zeros((8, exp_ref.shape[1]), F32)
    wide = lax.broadcasted_iota(jnp.int32, flat.shape, 1)
    deep = lax.broadcasted_iota(jnp.int32, flat.shape, 0)
    for i, k in enumerate(order):
        copies[i].wait()
        src = pos_ref[0] ^ k
        x = extra[i].astype(F32)[0:8, :]
        for j in range(per_dest):
            first = 3 * j
            top = x[:, first : first + 1] + x[:, first + 1 : first + 2] + x[:, first + 2 : first + 3]
            hit = (wide == (j * n + src) * tiles + deep) & (deep < tiles)
            flat = jnp.where(hit, top, flat)
    exp_ref[...] = jnp.max(flat, axis=0, keepdims=True)


def all_scales(pos, maxima, received, order, tiles, chunks, lat_blocks):
    n = len(order)
    per_dest = (received[0].shape[0] - EXTRA) // (tiles * TILE)
    lat_rows = maxima.shape[0] // 8 * chunks
    expert, latent = pl.pallas_call(
        functools.partial(scales_kernel, order, tiles, chunks),
        in_specs=[SMEM, VMEM] + [ANY] * n,
        out_specs=[VMEM, VMEM],
        out_shape=[
            jax.ShapeDtypeStruct((1, per_dest * n * tiles), F32),
            jax.ShapeDtypeStruct((lat_blocks, lat_rows * CHUNK // TILE), F32),
        ],
        scratch_shapes=[
            pltpu.VMEM((n, EXTRA, TILE), BF16),
            pltpu.VMEM((lat_rows, TILE), F32),
            pltpu.VMEM((TILE, TILE), F32),
            pltpu.SemaphoreType.DMA((n,)),
        ],
        compiler_params=LIGHT,
        cost_estimate=pl.CostEstimate(flops=1000000, bytes_accessed=100000, transcendentals=0),
        name="all_scales",
    )(pos, maxima, *received)
    return expert, latent.T


def whole_tile(pos, rows):
    return pl.multiple_of(lax.rem(pos * (TILE - rows % TILE), TILE), CHUNK)


def full_kernel(pieces, rows, x_ref, tops_ref, *refs):
    out_ref, tops_out, buf, in_sem, out_sem = refs[-5:]
    tops_out[...] = tops_ref[...]
    loads, stores = [], []
    for i in range(pieces):
        lead = i * (TILE - rows % TILE) % TILE
        at = pl.ds(i * TILE, TILE)
        loads.append(pltpu.make_async_copy(x_ref.at[at, :], buf.at[at, :], in_sem.at[i]))
        stores.append(
            pltpu.make_async_copy(
                buf.at[at, :], out_ref.at[pl.ds(i * rows + lead, TILE), :], out_sem.at[i]
            )
        )
    copy_all(loads)
    for i in range(pieces):
        loads[i].wait()
        stores[i].start()
    wait_all(stores)


def place_full(out, x, tops, rows):
    pieces = x.shape[0] // TILE
    return pl.pallas_call(
        functools.partial(full_kernel, pieces, rows),
        in_specs=[ANY, VMEM] + [ANY] * len(out),
        out_specs=[ANY, VMEM],
        out_shape=[
            jax.ShapeDtypeStruct((pieces * rows, x.shape[1]), BF16),
            jax.ShapeDtypeStruct(tops.shape, tops.dtype),
        ],
        scratch_shapes=[
            pltpu.VMEM(x.shape, BF16),
            pltpu.SemaphoreType.DMA((pieces,)),
            pltpu.SemaphoreType.DMA((pieces,)),
        ],
        input_output_aliases={2: 0} if out else {},
        compiler_params=PARAMS,
        cost_estimate=pl.CostEstimate(flops=0, bytes_accessed=4 * x.size, transcendentals=0),
        name="place_whole",
    )(x, tops, *out)


def rest_kernel(deltas, rows, pos_ref, *refs):
    x_refs = refs[: len(deltas)]
    out_ref, buf, in_sem, out_sem = refs[-4:]
    span = rows - TILE
    loads = [
        pltpu.make_async_copy(x_refs[i], buf.at[i], in_sem.at[i]) for i in range(len(deltas))
    ]
    copy_all(loads)
    stores = []
    for i, delta in enumerate(deltas):
        peer = pos_ref[0] ^ delta
        lead = whole_tile(peer, rows)
        loads[i].wait()
        for c in range(span // CHUNK):
            at = peer * rows + c * CHUNK + jnp.where(c * CHUNK < lead, 0, TILE)
            stores.append(
                pltpu.make_async_copy(
                    buf.at[i, pl.ds(c * CHUNK, CHUNK), :],
                    out_ref.at[pl.ds(pl.multiple_of(at, CHUNK), CHUNK), :],
                    out_sem.at[i, c],
                )
            )
            stores[-1].start()
    wait_all(stores)


def place_rest(out, pos, xs, deltas, rows, peers):
    span, cols = xs[0].shape
    n = len(xs)
    return pl.pallas_call(
        functools.partial(rest_kernel, deltas, rows),
        in_specs=[SMEM] + [ANY] * (n + len(out)),
        out_specs=ANY,
        out_shape=jax.ShapeDtypeStruct((peers * rows, cols), BF16),
        scratch_shapes=[
            pltpu.VMEM((n, span, cols), BF16),
            pltpu.SemaphoreType.DMA((n,)),
            pltpu.SemaphoreType.DMA((n, span // CHUNK)),
        ],
        input_output_aliases={1 + n: 0} if out else {},
        compiler_params=pltpu.CompilerParams(vmem_limit_bytes=4 * 1024 * 1024),
        cost_estimate=pl.CostEstimate(flops=0, bytes_accessed=4 * n * span * cols, transcendentals=0),
        name="place_rest",
    )(pos, *xs, *out)


SLABS = 4


def latent_kernel(chunks, step_ref, pos_ref, *refs):
    hbm, outs, top_ref = refs[:4], refs[4:8], refs[8]
    w, m, v, g, q, in_sem, out_sem = refs[9:]
    bufs = (w, m, v, g)
    width = w.shape[1] // SLABS
    loads, stores = [], []
    for i in range(SLABS):
        cols = pl.ds(i * width, width)
        loads.append(
            [
                pltpu.make_async_copy(hbm[a].at[:, cols], bufs[a].at[:, cols], in_sem.at[i, a])
                for a in range(4)
            ]
        )
        stores.append(
            [
                pltpu.make_async_copy(src.at[:, cols], outs[a].at[:, cols], out_sem.at[i, a])
                for a, src in enumerate((w, m, v, q))
            ]
        )
        copy_all(loads[i])
    rate, corr = corrections(step_ref)
    lane = lax.broadcasted_iota(jnp.int32, (8, TILE), 1)
    lead = whole_tile(pos_ref[0], w.shape[0])
    sub = lax.broadcasted_iota(jnp.int32, (8, 1), 0) * CHUNK
    inside = (sub >= lead) & (sub < lead + TILE)
    tops = jnp.zeros((8, TILE), F32)
    for i in range(SLABS):
        wait_all(loads[i])
        blocks = range(i * width // TILE, (i + 1) * width // TILE)
        slab_tops = []
        for b in blocks:
            cols = pl.ds(b * TILE, TILE)
            w1, m1, v1 = adamw_tile(w[:, cols], m[:, cols], v[:, cols], g[:, cols], rate, corr)
            w[:, cols] = w1
            m[:, cols] = m1
            v[:, cols] = v1
            slab_tops.append(stack_max([sub_max(w1[c * CHUNK : (c + 1) * CHUNK]) for c in range(chunks)]))
        for b, top in zip(blocks, slab_tops):
            cols = pl.ds(b * TILE, TILE)
            tops = jnp.where(lane == b, top, tops)
            whole = jnp.max(jnp.where(inside, top, 0.0), axis=0, keepdims=True)
            q[:, cols] = (w[pl.ds(lead, TILE), cols] * (1.0 / (whole + SCALE_EPS))).astype(BF16)
        copy_all(stores[i])
    top_ref[...] = tops
    for group in stores:
        wait_all(group)


def latent_update(arrays, step, pos):
    rows, cols = arrays[0].shape
    elems = rows * cols
    return pl.pallas_call(
        functools.partial(latent_kernel, rows // CHUNK),
        in_specs=[SMEM] * 2 + [ANY] * 4,
        out_specs=[ANY] * 4 + [VMEM],
        out_shape=[
            jax.ShapeDtypeStruct((rows, cols), F32),
            jax.ShapeDtypeStruct((rows, cols), BF16),
            jax.ShapeDtypeStruct((rows, cols), BF16),
            jax.ShapeDtypeStruct((TILE, cols), BF16),
            jax.ShapeDtypeStruct((8, TILE), F32),
        ],
        scratch_shapes=[
            pltpu.VMEM((rows, cols), F32),
            pltpu.VMEM((rows, cols), BF16),
            pltpu.VMEM((rows, cols), BF16),
            pltpu.VMEM((rows, cols), BF16),
            pltpu.VMEM((TILE, cols), BF16),
            pltpu.SemaphoreType.DMA((SLABS, 4)),
            pltpu.SemaphoreType.DMA((SLABS, 4)),
        ],
        compiler_params=PARAMS,
        cost_estimate=pl.CostEstimate(
            flops=30 * elems, bytes_accessed=18 * elems, transcendentals=2 * elems
        ),
        name="latent_adamw",
    )(step, pos, *arrays)


def latent_rest_kernel(chunks, pos_ref, w1_ref, own_ref, prev_ref, next_ref, after_ref, *refs):
    q_ref, w, q, ext, in_sem, out_sem = refs
    per_tile = TILE // CHUNK
    rows, cols = w1_ref.shape
    width = cols // SLABS
    lead = whole_tile(pos_ref[0], rows)
    loads, stores = [], []
    for i in range(SLABS):
        at = pl.ds(i * width, width)
        group = []
        for c in range(chunks - per_tile):
            first = pl.multiple_of(c * CHUNK + jnp.where(c * CHUNK < lead, 0, TILE), CHUNK)
            group.append(
                pltpu.make_async_copy(
                    w1_ref.at[pl.ds(first, CHUNK), at],
                    w.at[pl.ds(c * CHUNK, CHUNK), at],
                    in_sem.at[i, c],
                )
            )
        copy_all(group)
        loads.append(group)
        stores.append(pltpu.make_async_copy(q.at[:, at], q_ref.at[:, at], out_sem.at[i]))
    ext[0:chunks, :] = prev_ref[0:chunks, :]
    ext[chunks : 2 * chunks, :] = own_ref[0:chunks, :]
    ext[2 * chunks : 3 * chunks, :] = next_ref[0:chunks, :]
    first = chunks + lead // CHUNK
    above = jnp.max(ext[pl.ds(first - per_tile, per_tile), :], axis=0, keepdims=True)
    below = jnp.max(ext[pl.ds(first + per_tile, per_tile), :], axis=0, keepdims=True)
    both = jnp.concatenate([above] * 4 + [below] * 4, axis=0)
    lane = lax.broadcasted_iota(jnp.int32, (8, TILE), 1)
    tops = [
        jnp.max(jnp.where(lane == b, both, 0.0), axis=1, keepdims=True) for b in range(cols // TILE)
    ]
    invs = [1.0 / (top + SCALE_EPS) for top in tops]
    for i in range(SLABS):
        wait_all(loads[i])
        for b in range(i * width // TILE, (i + 1) * width // TILE):
            at = pl.ds(b * TILE, TILE)
            for c in range(chunks - per_tile):
                span = pl.ds(c * CHUNK, CHUNK)
                inv = jnp.where(c * CHUNK < lead, invs[b][0:1, :], invs[b][4:5, :])
                q[span, at] = (w[span, at] * inv).astype(BF16)
        stores[i].start()
    wait_all(stores)


def latent_rest(w1, own, above, below, pos, after):
    rows, cols = w1.shape
    chunks = rows // CHUNK
    return pl.pallas_call(
        functools.partial(latent_rest_kernel, chunks),
        in_specs=[SMEM, ANY] + [VMEM] * 3 + [ANY],
        out_specs=ANY,
        out_shape=jax.ShapeDtypeStruct((rows - TILE, cols), BF16),
        scratch_shapes=[
            pltpu.VMEM((rows - TILE, cols), F32),
            pltpu.VMEM((rows - TILE, cols), BF16),
            pltpu.VMEM((24, TILE), F32),
            pltpu.SemaphoreType.DMA((SLABS, chunks)),
            pltpu.SemaphoreType.DMA((SLABS,)),
        ],
        compiler_params=PARAMS,
        cost_estimate=pl.CostEstimate(
            flops=rows * cols, bytes_accessed=3 * rows * cols, transcendentals=0
        ),
        name="latent_rest",
    )(pos, w1, own, above, below, after)


def fast_fits(expert_shape, latent_shape, dp_count, exp_axis):
    exp_count, rows, cols = expert_shape
    latent_rows, latent_cols = latent_shape
    return (
        exp_count == 1
        and rows % TILE == 0
        and rows <= 8 * TILE
        and cols % (TILE * dp_count) == 0
        and cols // TILE // dp_count <= 20
        and dp_count >= 4
        and dp_count & (dp_count - 1) == 0
        and dp_count * latent_rows * exp_axis <= TILE * TILE
        and latent_rows % CHUNK == 0
        and 2 * TILE - CHUNK <= latent_rows < 2 * TILE
        and latent_rows * exp_axis % TILE == 0
        and exp_axis & (exp_axis - 1) == 0
        and latent_cols % (SLABS * TILE) == 0
        and latent_cols <= TILE * TILE
    )


def partner_groups(dp_count):
    hops = lambda k: bin(k >> 1).count("1")
    stage = lambda k: 3 if k < 2 else (1 if hops(k) > 1 else (2 if k & 1 else 0))
    order = sorted(range(dp_count), key=lambda k: (stage(k), -k))
    return [g for g in ([k for k in order if stage(k) == n] for n in range(4)) if g]


def fast_body(
    expert_master,
    expert_first,
    expert_second,
    expert_grad,
    latent_master,
    latent_first,
    latent_second,
    latent_grad,
    step_count,
    column_owner,
):
    dp_count = lax.axis_size("dp")
    dp_pos = lax.axis_index("dp").astype(jnp.int32)
    exp_axis = lax.axis_size("expert")
    exp_pos = lax.axis_index("expert").astype(jnp.int32)
    _, rows, cols = expert_master.shape
    block_count = cols // TILE
    per_dest = block_count // dp_count
    tiles = rows // TILE

    expert_at = exp_pos.reshape(1)
    latent_new, latent_one, latent_two, whole, chunk_top = latent_update(
        (latent_master, latent_first, latent_second, latent_grad), step_count, expert_at
    )
    latent_rows = latent_new.shape[0]
    whole = lax.all_gather(whole, "expert", axis=0, tiled=True)
    above = lax.ppermute(chunk_top, "expert", [(i, i + 1) for i in range(exp_axis - 1)])
    below = lax.ppermute(chunk_top, "expert", [(i + 1, i) for i in range(exp_axis - 1)])
    arrays = tuple(
        a.reshape(rows, cols) for a in (expert_master, expert_first, expert_second, expert_grad)
    )
    state, arrived, after = (), [], ()
    for n, partners in enumerate(partner_groups(dp_count)):
        state, sent = expert_group(
            arrays, state, column_owner, dp_pos.reshape(1), step_count, after, partners, per_dest
        )
        if n == 0:
            rest = {
                0: latent_rest(latent_new, chunk_top, above, below, expert_at, sent[0])
            }
            bit = exp_axis // 2
            while bit:
                pairs = [(i, i ^ bit) for i in range(exp_axis)]
                moved = {d ^ bit: lax.ppermute(x, "expert", pairs) for d, x in rest.items()}
                rest.update(moved)
                bit //= 2
        for k, q in zip(partners, sent):
            pairs = [(i, i ^ k) for i in range(dp_count)]
            arrived.append((k, lax.ppermute(q, "dp", pairs) if k else q))
        if n == 0:
            after = (rest[0],)
        elif n == 1:
            after = tuple(q[-EXTRA:] for _, q in arrived[: len(partners)])
        else:
            after = (rest[exp_axis - 1][:EXTRA, :TILE],)
    placed = ()
    for k, q in arrived[-1:] + arrived[:-1]:
        placed = (place_rows(placed, (dp_pos ^ k).reshape(1), q, dp_count, per_dest),)
    expert_served = placed[0].reshape(1, block_count * rows, TILE)
    deltas = list(rest)
    near, last = deltas[:-1], deltas[-1:]
    latent_served = place_rest(
        (), expert_at, [rest[d] for d in near], near, latent_rows, exp_axis
    )
    latent_served, tops = place_full((latent_served,), whole, chunk_top, latent_rows)
    latent_served = place_rest(
        (latent_served,), expert_at, [rest[d] for d in last], last, latent_rows, exp_axis
    )
    maxima = lax.all_gather(tops, ("dp", "expert"), axis=0, tiled=True)
    expert_scales, latent_scales = all_scales(
        dp_pos.reshape(1),
        maxima,
        [q for _, q in arrived],
        [k for k, _ in arrived],
        tiles,
        latent_rows // CHUNK,
        latent_new.shape[1] // TILE,
    )

    return (
        state[0][None],
        state[1][None],
        state[2][None],
        expert_served,
        expert_scales,
        latent_new,
        latent_one,
        latent_two,
        latent_served,
        latent_scales,
    )


def body(*args):
    if fast_fits(args[0].shape, args[4].shape, lax.axis_size("dp"), lax.axis_size("expert")):
        return fast_body(*args)
    return general_body(*args)


def solution(mesh):
    placed = (
        P("expert", "dp", None),
        P("expert", "dp", None),
        P("expert", "dp", None),
        P("expert", "dp", None),
        P(("dp", "expert"), None),
        P(("dp", "expert"), None),
        P(("dp", "expert"), None),
        P(("dp", "expert"), None),
        P(),
        P(),
    )
    return jax.shard_map(
        body,
        mesh=mesh,
        in_specs=placed,
        out_specs=(
            P("expert", "dp", None),
            P("expert", "dp", None),
            P("expert", "dp", None),
            P("expert", "dp", None),
            P("expert", "dp"),
            P(("dp", "expert"), None),
            P(("dp", "expert"), None),
            P(("dp", "expert"), None),
            P("dp", None),
            P(),
        ),
        check_vma=False,
    )
```

```python
import functools
import math

import jax
import jax.numpy as jnp
from jax import lax
from jax.experimental import pallas as pl
from jax.experimental.pallas import tpu as pltpu
from jax.sharding import PartitionSpec as P

D = 7168
TILE = 128


BETA_ONE = 0.9
BETA_TWO = 0.95
LEARN_RATE = 0.2
DECAY_RATE = 0.1
ADAM_EPS = 1e-08
SCALE_EPS = 1e-06


def adamw_step(master, moment_one, moment_two, gradient, step_count):
    grad_value = gradient.astype(jnp.float32)
    first_new = BETA_ONE * moment_one.astype(jnp.float32) + (1.0 - BETA_ONE) * grad_value
    second_new = (
        BETA_TWO * moment_two.astype(jnp.float32) + (1.0 - BETA_TWO) * grad_value * grad_value
    )
    step_value = step_count[0].astype(jnp.float32)
    corr_one = 1.0 - jnp.power(jnp.float32(BETA_ONE), step_value)
    corr_two = 1.0 - jnp.power(jnp.float32(BETA_TWO), step_value)
    update = first_new / corr_one / (jnp.sqrt(second_new / corr_two) + ADAM_EPS)
    master_new = master - LEARN_RATE * (update + DECAY_RATE * master)
    return (master_new, first_new.astype(jnp.bfloat16), second_new.astype(jnp.bfloat16))


def row_maxima(weights):
    leading = weights.shape[:-1]
    tile_count = weights.shape[-1] // TILE
    return jnp.max(jnp.abs(weights).reshape(leading + (tile_count, TILE)), axis=-1)


def local_tiles(row_max, lead_rows):
    exp_count, row_count, tile_count = row_max.shape
    tile_span = row_count // TILE + 2
    buffer = jnp.zeros((exp_count, tile_span * TILE, tile_count), jnp.float32)
    buffer = lax.dynamic_update_slice(buffer, row_max, (jnp.int32(0), lead_rows, jnp.int32(0)))
    return jnp.max(buffer.reshape(exp_count, tile_span, TILE, tile_count), axis=2)


def place_tiles(tile_max, first_tile):
    exp_count, tile_span, tile_count = tile_max.shape
    global_map = jnp.zeros((exp_count, D // TILE + tile_span, tile_count), jnp.float32)
    return lax.dynamic_update_slice(global_map, tile_max, (jnp.int32(0), first_tile, jnp.int32(0)))


def quantized_rows(weights, tile_max, lead_rows):
    exp_count, row_count, col_count = weights.shape
    repeated = jnp.repeat(tile_max, TILE, axis=1)
    row_scale = lax.dynamic_slice_in_dim(repeated, lead_rows, row_count, 1)
    blocks = weights.reshape(exp_count, row_count, col_count // TILE, TILE)
    return (blocks / (row_scale[..., None] + SCALE_EPS)).reshape(weights.shape).astype(jnp.bfloat16)


def general_body(
    expert_master,
    expert_first,
    expert_second,
    expert_grad,
    latent_master,
    latent_first,
    latent_second,
    latent_grad,
    step_count,
    column_owner,
):
    master_new, first_new, second_new = adamw_step(
        expert_master, expert_first, expert_second, expert_grad, step_count
    )
    latent_new, latent_one, latent_two = adamw_step(
        latent_master, latent_first, latent_second, latent_grad, step_count
    )
    dp_count = lax.axis_size("dp")
    dp_pos = lax.axis_index("dp")
    exp_count, row_count, col_count = master_new.shape
    block_count = col_count // TILE
    slot_count = max(1, block_count // dp_count)
    total_tiles = D // TILE
    recv_rows = block_count * row_count
    recv_tiles = recv_rows // TILE
    positions = jnp.arange(block_count, dtype=jnp.int32)
    inverse = jnp.sum(
        positions[:, None] * (column_owner[:, None] == positions[None, :]).astype(jnp.int32), axis=0
    )
    receiver_ids = jnp.arange(dp_count, dtype=jnp.int32)[:, None]
    slot_ids = jnp.arange(slot_count, dtype=jnp.int32)[None, :]
    segment = (
        receiver_ids * block_count
        + jnp.mod(dp_pos - receiver_ids * block_count, dp_count)
        + slot_ids * dp_count
    )
    usable_slot = (segment < (receiver_ids + 1) * block_count).reshape(-1)
    send_block = jnp.take(inverse, jnp.minimum(segment // dp_count, block_count - 1)).reshape(-1)
    local_segments = jnp.arange(block_count, dtype=jnp.int32)
    source_dev = jnp.mod(dp_pos * block_count + local_segments, dp_count)
    pick_index = source_dev * slot_count + local_segments // dp_count
    blocks = master_new.reshape(exp_count, row_count, block_count, TILE)
    picked = jnp.take(blocks, send_block, axis=2)
    received = lax.all_to_all(
        jnp.where(usable_slot[None, None, :, None], picked, jnp.zeros((), picked.dtype)),
        "dp",
        split_axis=2,
        concat_axis=2,
        tiled=True,
    )
    ordered = jnp.take(received, pick_index, axis=2)
    tall = (
        jnp.transpose(ordered, (0, 2, 1, 3))
        .reshape(exp_count, recv_rows, TILE)
        .reshape(exp_count, recv_tiles, TILE, TILE)
    )
    expert_scales = jnp.max(jnp.abs(tall), axis=(2, 3))
    expert_served = (
        (tall / (expert_scales[:, :, None, None] + SCALE_EPS))
        .reshape(exp_count, recv_rows, TILE)
        .astype(jnp.bfloat16)
    )
    latent_block = lax.all_gather(latent_new, "expert", axis=0, tiled=True)
    block_rows = latent_block.shape[0]
    block_offset = dp_pos * block_rows
    block_lead = block_offset % TILE
    block_tiles = local_tiles(row_maxima(latent_block)[None], block_lead)
    block_map = lax.pmax(place_tiles(block_tiles, block_offset // TILE), "dp")
    latent_scales = block_map[0, :total_tiles]
    block_tiles = lax.dynamic_slice_in_dim(block_map, block_offset // TILE, block_tiles.shape[1], 1)
    latent_served = quantized_rows(latent_block[None], block_tiles, block_lead)[0]
    return (
        master_new,
        first_new,
        second_new,
        expert_served,
        expert_scales,
        latent_new,
        latent_one,
        latent_two,
        latent_served,
        latent_scales,
    )


CHUNK = 32
EXTRA = 16
SPARE = 64
F32 = jnp.float32
BF16 = jnp.bfloat16
VMEM_LIMIT = 56 * 1024 * 1024
ANY = pl.BlockSpec(memory_space=pl.ANY)
SMEM = pl.BlockSpec(memory_space=pltpu.SMEM)
VMEM = pl.BlockSpec(memory_space=pltpu.VMEM)
PARAMS = pltpu.CompilerParams(vmem_limit_bytes=VMEM_LIMIT)
LIGHT = pltpu.CompilerParams(vmem_limit_bytes=1024 * 1024)


def corrections(step_ref):
    one, two = lax.fori_loop(
        0, step_ref[0], lambda _, p: (p[0] * BETA_ONE, p[1] * BETA_TWO), (F32(1.0), F32(1.0))
    )
    rate = LEARN_RATE / (1.0 - jnp.full((1, TILE), one, F32))
    corr = 1.0 / (1.0 - jnp.full((1, TILE), two, F32))
    return rate, corr


def adamw_tile(w, m, v, g, rate, corr):
    g = g.astype(F32)
    m1 = BETA_ONE * m.astype(F32) + (1.0 - BETA_ONE) * g
    v1 = BETA_TWO * v.astype(F32) + (1.0 - BETA_TWO) * g * g
    x = v1 * corr
    inv = pl.reciprocal(x * lax.rsqrt(x) + ADAM_EPS, approx=True)
    w1 = (1.0 - LEARN_RATE * DECAY_RATE) * w - rate * m1 * inv
    return w1, m1.astype(BF16), v1.astype(BF16)


def sub_max(w1):
    return jnp.max(jnp.abs(w1).reshape(w1.shape[0] // 8, 8, TILE), axis=0)


def stack_max(parts):
    parts = parts + [parts[-1]] * (8 - len(parts))
    rows = [jnp.max(p, axis=0, keepdims=True) for p in parts]
    return jnp.max(jnp.concatenate(rows, axis=0), axis=1, keepdims=True)


def three_parts(x):
    high = x.astype(BF16).astype(F32)
    rest = x - high
    middle = rest.astype(BF16).astype(F32)
    return high, middle, rest - middle


def copy_all(copies):
    for c in copies:
        c.start()


def wait_all(copies):
    for c in copies:
        c.wait()


def expert_kernel(partners, per_dest, n_alias, n_after, owner_ref, pos_ref, step_ref, side_ref, *refs):
    refs = refs[: 4 + n_alias] + refs[4 + n_alias + n_after :]
    hbm = refs[:4]
    outs = refs[4 + n_alias : 7 + n_alias]
    n_dest = len(partners)
    q_refs = refs[7 + n_alias : 7 + n_alias + n_dest]
    w, m, v, g, extra, in_sem, out_sem, extra_sem = refs[7 + n_alias + n_dest :]
    bufs = (w, m, v, g)
    blocks = owner_ref.shape[0]
    rows = w.shape[1]
    tiles = rows // TILE
    pos = pos_ref[0]

    loads, stores = [], []
    for d, k in enumerate(partners):
        for j in range(per_dest):
            i = d * per_dest + j
            slot = (pos ^ k) * per_dest + j
            block = jnp.int32(0)
            for b in range(blocks):
                block = jnp.where(owner_ref[b] == slot, b, block)
            cols = pl.ds(pl.multiple_of(block * TILE, TILE), TILE)
            loads.append(
                [
                    pltpu.make_async_copy(hbm[a].at[:, cols], bufs[a].at[i], in_sem.at[i, a])
                    for a in range(4)
                ]
            )
            stores.append(
                [
                    pltpu.make_async_copy(bufs[a].at[i], outs[a].at[:, cols], out_sem.at[i, a])
                    for a in range(3)
                ]
                + [
                    pltpu.make_async_copy(
                        g.at[i], q_refs[d].at[pl.ds(j * rows, rows), :], out_sem.at[i, 3]
                    )
                ]
            )
            copy_all(loads[-1])
    rate, corr = corrections(step_ref)
    lane = lax.broadcasted_iota(jnp.int32, (8, TILE), 1)
    extras = []
    for d in range(n_dest):
        side = side_ref[...]
        for j in range(per_dest):
            i = d * per_dest + j
            wait_all(loads[i])
            parts = []
            for t in range(tiles):
                at = pl.ds(t * TILE, TILE)
                w1, m1, v1 = adamw_tile(w[i, at, :], m[i, at, :], v[i, at, :], g[i, at, :], rate, corr)
                w[i, at, :] = w1
                m[i, at, :] = m1
                v[i, at, :] = v1
                parts.append(sub_max(w1))
            copy_all(stores[i][:3])
            top = stack_max(parts)
            inv = 1.0 / (top + SCALE_EPS)
            for t in range(tiles):
                at = pl.ds(t * TILE, TILE)
                g[i, at, :] = (w[i, at, :] * inv[t : t + 1, :]).astype(BF16)
            stores[i][3].start()
            for p, value in enumerate(three_parts(top)):
                side = jnp.where(lane == 3 * j + p, value, side)
        extra[d] = jnp.concatenate([side, jnp.zeros_like(side)], axis=0).astype(BF16)
        extras.append(
            pltpu.make_async_copy(
                extra.at[d], q_refs[d].at[pl.ds(per_dest * rows, EXTRA), :], extra_sem.at[d]
            )
        )
        extras[-1].start()
    for group in stores:
        wait_all(group)
    wait_all(extras)


def expert_group(arrays, state, owner, pos, step, side, after, partners, per_dest):
    rows, cols = arrays[0].shape
    n_alias = len(state)
    n = len(partners) * per_dest
    elems = rows * TILE * n
    out = pl.pallas_call(
        functools.partial(expert_kernel, partners, per_dest, n_alias, len(after)),
        in_specs=[SMEM] * 3 + [VMEM] + [ANY] * (4 + n_alias + len(after)),
        out_specs=[ANY] * (3 + len(partners)),
        out_shape=[
            jax.ShapeDtypeStruct((rows, cols), F32),
            jax.ShapeDtypeStruct((rows, cols), BF16),
            jax.ShapeDtypeStruct((rows, cols), BF16),
        ]
        + [jax.ShapeDtypeStruct((per_dest * rows + EXTRA, TILE), BF16)] * len(partners),
        scratch_shapes=[
            pltpu.VMEM((n, rows, TILE), F32),
            pltpu.VMEM((n, rows, TILE), BF16),
            pltpu.VMEM((n, rows, TILE), BF16),
            pltpu.VMEM((n, rows, TILE), BF16),
            pltpu.VMEM((len(partners), EXTRA, TILE), BF16),
            pltpu.SemaphoreType.DMA((n, 4)),
            pltpu.SemaphoreType.DMA((n, 4)),
            pltpu.SemaphoreType.DMA((len(partners),)),
        ],
        input_output_aliases={8 + i: i for i in range(n_alias)},
        compiler_params=PARAMS,
        cost_estimate=pl.CostEstimate(flops=elems, bytes_accessed=elems, transcendentals=0),
        name="expert_adamw",
    )(owner, pos, step, side, *arrays, *state, *after)
    return out[:3], out[3:]


def place_kernel(src_ref, q_ref, *refs):
    served, sem = refs[-2:]
    per_dest, _, rows, _ = served.shape
    src = src_ref[0]
    copies = [
        pltpu.make_async_copy(q_ref.at[pl.ds(j * rows, rows), :], served.at[j, src], sem.at[j])
        for j in range(per_dest)
    ]
    copy_all(copies)
    wait_all(copies)


def place_rows(placed, src, q, dp_count, per_dest):
    rows = (q.shape[0] - EXTRA) // per_dest
    return pl.pallas_call(
        place_kernel,
        in_specs=[SMEM] + [ANY] * (1 + len(placed)),
        out_specs=ANY,
        out_shape=jax.ShapeDtypeStruct((per_dest, dp_count, rows, TILE), BF16),
        scratch_shapes=[pltpu.SemaphoreType.DMA((per_dest,))],
        input_output_aliases={2: 0} if placed else {},
        compiler_params=LIGHT,
        cost_estimate=pl.CostEstimate(flops=0, bytes_accessed=4 * q.size, transcendentals=0),
        name="place_served",
    )(src, q, *placed)


def scales_kernel(order, tiles, lat_tiles, n_late, pos_ref, *refs):
    n = len(order)
    late, q_refs = refs[:n_late], refs[n_late : n_late + n]
    exp_ref, lat_ref, extra, rows_ref, sem = refs[n_late + n :]
    at = q_refs[0].shape[0] - EXTRA
    per_dest = at // (tiles * TILE)
    copies = [
        pltpu.make_async_copy(q.at[pl.ds(at, EXTRA), :], extra.at[i], sem.at[i])
        for i, q in enumerate(q_refs)
    ]
    copy_all(copies)
    rows_ref[...] = jnp.zeros_like(rows_ref)
    flat = jnp.zeros((8, exp_ref.shape[1]), F32)
    wide = lax.broadcasted_iota(jnp.int32, flat.shape, 1)
    deep = lax.broadcasted_iota(jnp.int32, flat.shape, 0)
    for i, k in enumerate(order):
        copies[i].wait()
        src = pos_ref[0] ^ k
        x = extra[i].astype(F32)[0:8, :]
        side = late[i][...] if i < n_late else x
        lat = sum(pltpu.roll(side, TILE - SPARE - 16 * p, 1) for p in range(3))
        rows_ref[pl.ds(src * lat_tiles, lat_tiles), :] = lat[0:lat_tiles, :]
        for j in range(per_dest):
            first = 3 * j
            top = x[:, first : first + 1] + x[:, first + 1 : first + 2] + x[:, first + 2 : first + 3]
            hit = (wide == (j * n + src) * tiles + deep) & (deep < tiles)
            flat = jnp.where(hit, top, flat)
    exp_ref[...] = jnp.max(flat, axis=0, keepdims=True)
    blocks, height = lat_ref.shape
    lat_ref[...] = jnp.transpose(rows_ref[...])[0:blocks, 0:height]


def all_scales(pos, late, received, order, tiles, lat_tiles, lat_blocks):
    n = len(order)
    per_dest = (received[0].shape[0] - EXTRA) // (tiles * TILE)
    expert, latent = pl.pallas_call(
        functools.partial(scales_kernel, order, tiles, lat_tiles, len(late)),
        in_specs=[SMEM] + [VMEM] * len(late) + [ANY] * n,
        out_specs=[VMEM, VMEM],
        out_shape=[
            jax.ShapeDtypeStruct((1, per_dest * n * tiles), F32),
            jax.ShapeDtypeStruct((lat_blocks, n * lat_tiles), F32),
        ],
        scratch_shapes=[
            pltpu.VMEM((n, EXTRA, TILE), BF16),
            pltpu.VMEM((TILE, TILE), F32),
            pltpu.SemaphoreType.DMA((n,)),
        ],
        compiler_params=LIGHT,
        cost_estimate=pl.CostEstimate(flops=1000000, bytes_accessed=100000, transcendentals=0),
        name="all_scales",
    )(pos, *late, *received)
    return expert, latent.T


def whole_tile(pos, rows):
    return pl.multiple_of(lax.rem(pos * (TILE - rows % TILE), TILE), CHUNK)


def full_kernel(pieces, rows, x_ref, *refs):
    out_ref, buf, in_sem, out_sem = refs[-4:]
    loads, stores = [], []
    for i in range(pieces):
        lead = i * (TILE - rows % TILE) % TILE
        at = pl.ds(i * TILE, TILE)
        loads.append(pltpu.make_async_copy(x_ref.at[at, :], buf.at[at, :], in_sem.at[i]))
        stores.append(
            pltpu.make_async_copy(
                buf.at[at, :], out_ref.at[pl.ds(i * rows + lead, TILE), :], out_sem.at[i]
            )
        )
    copy_all(loads)
    for i in range(pieces):
        loads[i].wait()
        stores[i].start()
    wait_all(stores)


def place_full(out, x, rows):
    pieces = x.shape[0] // TILE
    return pl.pallas_call(
        functools.partial(full_kernel, pieces, rows),
        in_specs=[ANY] * (1 + len(out)),
        out_specs=ANY,
        out_shape=jax.ShapeDtypeStruct((pieces * rows, x.shape[1]), BF16),
        scratch_shapes=[
            pltpu.VMEM(x.shape, BF16),
            pltpu.SemaphoreType.DMA((pieces,)),
            pltpu.SemaphoreType.DMA((pieces,)),
        ],
        input_output_aliases={1: 0} if out else {},
        compiler_params=PARAMS,
        cost_estimate=pl.CostEstimate(flops=0, bytes_accessed=4 * x.size, transcendentals=0),
        name="place_whole",
    )(x, *out)


def rest_kernel(deltas, rows, n_after, forward, pos_ref, *refs):
    n = len(deltas)
    x_refs, out_ref = refs[:n], refs[-4 - forward]
    buf, in_sem, out_sem = refs[-3:]
    span = rows - TILE
    loads = [pltpu.make_async_copy(x_refs[i], buf.at[i], in_sem.at[i]) for i in range(n)]
    copy_all(loads)
    stores = []
    for i in reversed(range(n)):
        peer = pos_ref[0] ^ deltas[i]
        lead = whole_tile(peer, rows)
        loads[i].wait()
        if forward and i == n - 1:
            stores.append(pltpu.make_async_copy(buf.at[i], refs[-4], out_sem.at[n, 0]))
            stores[-1].start()
        for c in range(span // CHUNK):
            at = peer * rows + c * CHUNK + jnp.where(c * CHUNK < lead, 0, TILE)
            stores.append(
                pltpu.make_async_copy(
                    buf.at[i, pl.ds(c * CHUNK, CHUNK), :],
                    out_ref.at[pl.ds(pl.multiple_of(at, CHUNK), CHUNK), :],
                    out_sem.at[i, c],
                )
            )
            stores[-1].start()
    wait_all(stores)


def place_rest(out, pos, xs, deltas, rows, peers, after=(), forward=False):
    span, cols = xs[0].shape
    n = len(xs)
    shapes = [jax.ShapeDtypeStruct((peers * rows, cols), BF16)]
    shapes += [jax.ShapeDtypeStruct((span, cols), BF16)] * forward
    return pl.pallas_call(
        functools.partial(rest_kernel, deltas, rows, len(after), int(forward)),
        in_specs=[SMEM] + [ANY] * (n + len(out) + len(after)),
        out_specs=[ANY] * len(shapes),
        out_shape=shapes,
        scratch_shapes=[
            pltpu.VMEM((n, span, cols), BF16),
            pltpu.SemaphoreType.DMA((n,)),
            pltpu.SemaphoreType.DMA((n + 1, span // CHUNK)),
        ],
        input_output_aliases={1 + n: 0} if out else {},
        compiler_params=pltpu.CompilerParams(vmem_limit_bytes=4 * 1024 * 1024),
        cost_estimate=pl.CostEstimate(flops=0, bytes_accessed=4 * n * span * cols, transcendentals=0),
        name="place_rest",
    )(pos, *xs, *out, *after)


SLABS = 4


def latent_kernel(chunks, step_ref, pos_ref, *refs):
    hbm, outs, top_ref = refs[:4], refs[4:8], refs[8]
    w, m, v, g, q, in_sem, out_sem = refs[9:]
    bufs = (w, m, v, g)
    width = w.shape[1] // SLABS
    loads, stores = [], []
    for i in range(SLABS):
        cols = pl.ds(i * width, width)
        loads.append(
            [
                pltpu.make_async_copy(hbm[a].at[:, cols], bufs[a].at[:, cols], in_sem.at[i, a])
                for a in range(4)
            ]
        )
        stores.append(
            [
                pltpu.make_async_copy(src.at[:, cols], outs[a].at[:, cols], out_sem.at[i, a])
                for a, src in enumerate((w, m, v, q))
            ]
        )
        copy_all(loads[i])
    rate, corr = corrections(step_ref)
    lane = lax.broadcasted_iota(jnp.int32, (8, TILE), 1)
    lead = whole_tile(pos_ref[0], w.shape[0])
    sub = lax.broadcasted_iota(jnp.int32, (8, 1), 0) * CHUNK
    inside = (sub >= lead) & (sub < lead + TILE)
    tops = jnp.zeros((8, TILE), F32)
    for i in range(SLABS):
        wait_all(loads[i])
        blocks = range(i * width // TILE, (i + 1) * width // TILE)
        slab_tops = []
        for b in blocks:
            cols = pl.ds(b * TILE, TILE)
            w1, m1, v1 = adamw_tile(w[:, cols], m[:, cols], v[:, cols], g[:, cols], rate, corr)
            w[:, cols] = w1
            m[:, cols] = m1
            v[:, cols] = v1
            slab_tops.append(stack_max([sub_max(w1[c * CHUNK : (c + 1) * CHUNK]) for c in range(chunks)]))
        for b, top in zip(blocks, slab_tops):
            cols = pl.ds(b * TILE, TILE)
            tops = jnp.where(lane == b, top, tops)
            whole = jnp.max(jnp.where(inside, top, 0.0), axis=0, keepdims=True)
            q[:, cols] = (w[pl.ds(lead, TILE), cols] * (1.0 / (whole + SCALE_EPS))).astype(BF16)
        copy_all(stores[i])
    top_ref[...] = tops
    for group in stores:
        wait_all(group)


def latent_update(arrays, step, pos):
    rows, cols = arrays[0].shape
    elems = rows * cols
    return pl.pallas_call(
        functools.partial(latent_kernel, rows // CHUNK),
        in_specs=[SMEM] * 2 + [ANY] * 4,
        out_specs=[ANY] * 4 + [VMEM],
        out_shape=[
            jax.ShapeDtypeStruct((rows, cols), F32),
            jax.ShapeDtypeStruct((rows, cols), BF16),
            jax.ShapeDtypeStruct((rows, cols), BF16),
            jax.ShapeDtypeStruct((TILE, cols), BF16),
            jax.ShapeDtypeStruct((8, TILE), F32),
        ],
        scratch_shapes=[
            pltpu.VMEM((rows, cols), F32),
            pltpu.VMEM((rows, cols), BF16),
            pltpu.VMEM((rows, cols), BF16),
            pltpu.VMEM((rows, cols), BF16),
            pltpu.VMEM((TILE, cols), BF16),
            pltpu.SemaphoreType.DMA((SLABS, 4)),
            pltpu.SemaphoreType.DMA((SLABS, 4)),
        ],
        compiler_params=PARAMS,
        cost_estimate=pl.CostEstimate(
            flops=30 * elems, bytes_accessed=18 * elems, transcendentals=2 * elems
        ),
        name="latent_adamw",
    )(step, pos, *arrays)


def latent_rest_kernel(chunks, peers, pos_ref, w1_ref, *refs):
    q_ref, side_ref, w, q, ext, tops_ref, in_sem, out_sem = refs[-8:]
    per_tile = TILE // CHUNK
    rows, cols = w1_ref.shape
    width = cols // SLABS
    pos = pos_ref[0]
    lead = whole_tile(pos, rows)
    loads, stores = [], []
    for i in range(SLABS):
        at = pl.ds(i * width, width)
        group = []
        for c in range(chunks - per_tile):
            first = pl.multiple_of(c * CHUNK + jnp.where(c * CHUNK < lead, 0, TILE), CHUNK)
            group.append(
                pltpu.make_async_copy(
                    w1_ref.at[pl.ds(first, CHUNK), at],
                    w.at[pl.ds(c * CHUNK, CHUNK), at],
                    in_sem.at[i, c],
                )
            )
        copy_all(group)
        loads.append(group)
        stores.append(pltpu.make_async_copy(q.at[:, at], q_ref.at[:, at], out_sem.at[i]))
    for s in range(peers):
        peer = lax.rem(pos + peers - s, peers)
        ext[pl.ds(peer * chunks, chunks), :] = refs[s][0:chunks, :]
    tops_ref[...] = jnp.zeros_like(tops_ref)
    for t in range(peers * chunks // per_tile):
        tops_ref[t : t + 1, :] = jnp.max(
            ext[t * per_tile : (t + 1) * per_tile, :], axis=0, keepdims=True
        )
    lane = lax.broadcasted_iota(jnp.int32, (8, TILE), 1)
    side = jnp.zeros((8, TILE), F32)
    for p, value in enumerate(three_parts(tops_ref[...])):
        at = SPARE + 16 * p
        side = jnp.where((lane >= at) & (lane < at + 16), pltpu.roll(value, at, 1), side)
    side_ref[...] = side
    start = pos * chunks
    above = tops_ref[pl.ds(start // per_tile, 1), :]
    below = tops_ref[pl.ds((start + lead // CHUNK + per_tile) // per_tile, 1), :]
    both = jnp.concatenate([above] * 4 + [below] * 4, axis=0)
    tops = [
        jnp.max(jnp.where(lane == b, both, 0.0), axis=1, keepdims=True) for b in range(cols // TILE)
    ]
    invs = [1.0 / (top + SCALE_EPS) for top in tops]
    for i in range(SLABS):
        wait_all(loads[i])
        for b in range(i * width // TILE, (i + 1) * width // TILE):
            at = pl.ds(b * TILE, TILE)
            for c in range(chunks - per_tile):
                span = pl.ds(c * CHUNK, CHUNK)
                inv = jnp.where(c * CHUNK < lead, invs[b][0:1, :], invs[b][4:5, :])
                q[span, at] = (w[span, at] * inv).astype(BF16)
        stores[i].start()
    wait_all(stores)


def latent_rest(w1, maxima, pos, after):
    rows, cols = w1.shape
    chunks = rows // CHUNK
    peers = len(maxima)
    return pl.pallas_call(
        functools.partial(latent_rest_kernel, chunks, peers),
        in_specs=[SMEM, ANY] + [VMEM] * peers + [ANY],
        out_specs=[ANY, VMEM],
        out_shape=[
            jax.ShapeDtypeStruct((rows - TILE, cols), BF16),
            jax.ShapeDtypeStruct((8, TILE), F32),
        ],
        scratch_shapes=[
            pltpu.VMEM((rows - TILE, cols), F32),
            pltpu.VMEM((rows - TILE, cols), BF16),
            pltpu.VMEM((8 * peers, TILE), F32),
            pltpu.VMEM((8, TILE), F32),
            pltpu.SemaphoreType.DMA((SLABS, chunks)),
            pltpu.SemaphoreType.DMA((SLABS,)),
        ],
        compiler_params=PARAMS,
        cost_estimate=pl.CostEstimate(
            flops=rows * cols, bytes_accessed=3 * rows * cols, transcendentals=0
        ),
        name="latent_rest",
    )(pos, w1, *maxima, after)


def fast_fits(expert_shape, latent_shape, dp_count, exp_axis):
    exp_count, rows, cols = expert_shape
    latent_rows, latent_cols = latent_shape
    return (
        exp_count == 1
        and rows % TILE == 0
        and rows <= 8 * TILE
        and cols % (TILE * dp_count) == 0
        and cols // TILE // dp_count <= 16
        and dp_count >= 4
        and dp_count & (dp_count - 1) == 0
        and dp_count * latent_rows * exp_axis <= TILE * TILE
        and latent_rows % CHUNK == 0
        and 2 * TILE - CHUNK <= latent_rows < 2 * TILE
        and latent_rows * exp_axis % TILE == 0
        and latent_rows * exp_axis <= 8 * TILE
        and exp_axis == 4
        and latent_cols % (SLABS * TILE) == 0
        and latent_cols <= 16 * TILE
    )


def partner_groups(dp_count):
    hops = lambda k: bin(k >> 1).count("1")
    stage = lambda k: 3 if k < 2 else (1 if hops(k) > 1 else (2 if k & 1 else 0))
    order = sorted(range(dp_count), key=lambda k: (stage(k), -k))
    return [g for g in ([k for k in order if stage(k) == n] for n in range(4)) if g]


def fast_body(
    expert_master,
    expert_first,
    expert_second,
    expert_grad,
    latent_master,
    latent_first,
    latent_second,
    latent_grad,
    step_count,
    column_owner,
):
    dp_count = lax.axis_size("dp")
    dp_pos = lax.axis_index("dp").astype(jnp.int32)
    exp_axis = lax.axis_size("expert")
    exp_pos = lax.axis_index("expert").astype(jnp.int32)
    _, rows, cols = expert_master.shape
    block_count = cols // TILE
    per_dest = block_count // dp_count
    tiles = rows // TILE

    expert_at = exp_pos.reshape(1)
    latent_new, latent_one, latent_two, whole, chunk_top = latent_update(
        (latent_master, latent_first, latent_second, latent_grad), step_count, expert_at
    )
    latent_rows = latent_new.shape[0]
    whole = lax.all_gather(whole, "expert", axis=0, tiled=True)
    maxima = [chunk_top] + [
        lax.ppermute(chunk_top, "expert", [(i, (i + s) % exp_axis) for i in range(exp_axis)])
        for s in range(1, exp_axis)
    ]

    arrays = tuple(
        a.reshape(rows, cols) for a in (expert_master, expert_first, expert_second, expert_grad)
    )
    def swap(x, axis, k):
        return lax.ppermute(x, axis, [(i, i ^ k) for i in range(lax.axis_size(axis))])

    state, arrived, after = (), [], ()
    side = jnp.zeros((8, TILE), F32)
    groups = partner_groups(dp_count)
    for n, partners in enumerate(groups):
        state, sent = expert_group(
            arrays, state, column_owner, dp_pos.reshape(1), step_count, side, after, partners, per_dest
        )
        arrived += [(k, swap(q, "dp", k) if k else q) for k, q in zip(partners, sent)]
        if n == 0:
            rest, side = latent_rest(latent_new, maxima, expert_at, sent[0])
            far, near = swap(rest, "expert", 2), swap(rest, "expert", 1)
            late = [swap(side, "dp", k) for k in partners]
            after = ()
        elif n == 1:
            after = tuple(q[-EXTRA:] for _, q in arrived[: len(groups[0])])
        else:
            after = ()
    latent_served, far_again = place_rest(
        (), expert_at, [rest, far], [0, 2], latent_rows, exp_axis, (sent[-1][-EXTRA:],), True
    )
    last = swap(far_again, "expert", 1)
    (latent_served,) = place_rest((latent_served,), expert_at, [near], [1], latent_rows, exp_axis)
    latent_served = place_full((latent_served,), whole, latent_rows)
    (latent_served,) = place_rest((latent_served,), expert_at, [last], [3], latent_rows, exp_axis)

    placed = ()
    for k, q in arrived[-1:] + arrived[:-1]:
        placed = (place_rows(placed, (dp_pos ^ k).reshape(1), q, dp_count, per_dest),)
    expert_served = placed[0].reshape(1, block_count * rows, TILE)
    expert_scales, latent_scales = all_scales(
        dp_pos.reshape(1),
        late,
        [q for _, q in arrived],
        [k for k, _ in arrived],
        tiles,
        latent_rows * exp_axis // TILE,
        latent_new.shape[1] // TILE,
    )

    return (
        state[0][None],
        state[1][None],
        state[2][None],
        expert_served,
        expert_scales,
        latent_new,
        latent_one,
        latent_two,
        latent_served,
        latent_scales,
    )


def body(*args):
    if fast_fits(args[0].shape, args[4].shape, lax.axis_size("dp"), lax.axis_size("expert")):
        return fast_body(*args)
    return general_body(*args)


def solution(mesh):
    placed = (
        P("expert", "dp", None),
        P("expert", "dp", None),
        P("expert", "dp", None),
        P("expert", "dp", None),
        P(("dp", "expert"), None),
        P(("dp", "expert"), None),
        P(("dp", "expert"), None),
        P(("dp", "expert"), None),
        P(),
        P(),
    )
    return jax.shard_map(
        body,
        mesh=mesh,
        in_specs=placed,
        out_specs=(
            P("expert", "dp", None),
            P("expert", "dp", None),
            P("expert", "dp", None),
            P("expert", "dp", None),
            P("expert", "dp"),
            P(("dp", "expert"), None),
            P(("dp", "expert"), None),
            P(("dp", "expert"), None),
            P("dp", None),
            P(),
        ),
        check_vma=False,
    )
```

```python
import functools
import math

import jax
import jax.numpy as jnp
from jax import lax
from jax.experimental import pallas as pl
from jax.experimental.pallas import tpu as pltpu
from jax.sharding import PartitionSpec as P

D = 7168
TILE = 128


BETA_ONE = 0.9
BETA_TWO = 0.95
LEARN_RATE = 0.2
DECAY_RATE = 0.1
ADAM_EPS = 1e-08
SCALE_EPS = 1e-06


def adamw_step(master, moment_one, moment_two, gradient, step_count):
    grad_value = gradient.astype(jnp.float32)
    first_new = BETA_ONE * moment_one.astype(jnp.float32) + (1.0 - BETA_ONE) * grad_value
    second_new = (
        BETA_TWO * moment_two.astype(jnp.float32) + (1.0 - BETA_TWO) * grad_value * grad_value
    )
    step_value = step_count[0].astype(jnp.float32)
    corr_one = 1.0 - jnp.power(jnp.float32(BETA_ONE), step_value)
    corr_two = 1.0 - jnp.power(jnp.float32(BETA_TWO), step_value)
    update = first_new / corr_one / (jnp.sqrt(second_new / corr_two) + ADAM_EPS)
    master_new = master - LEARN_RATE * (update + DECAY_RATE * master)
    return (master_new, first_new.astype(jnp.bfloat16), second_new.astype(jnp.bfloat16))


def row_maxima(weights):
    leading = weights.shape[:-1]
    tile_count = weights.shape[-1] // TILE
    return jnp.max(jnp.abs(weights).reshape(leading + (tile_count, TILE)), axis=-1)


def local_tiles(row_max, lead_rows):
    exp_count, row_count, tile_count = row_max.shape
    tile_span = row_count // TILE + 2
    buffer = jnp.zeros((exp_count, tile_span * TILE, tile_count), jnp.float32)
    buffer = lax.dynamic_update_slice(buffer, row_max, (jnp.int32(0), lead_rows, jnp.int32(0)))
    return jnp.max(buffer.reshape(exp_count, tile_span, TILE, tile_count), axis=2)


def place_tiles(tile_max, first_tile):
    exp_count, tile_span, tile_count = tile_max.shape
    global_map = jnp.zeros((exp_count, D // TILE + tile_span, tile_count), jnp.float32)
    return lax.dynamic_update_slice(global_map, tile_max, (jnp.int32(0), first_tile, jnp.int32(0)))


def quantized_rows(weights, tile_max, lead_rows):
    exp_count, row_count, col_count = weights.shape
    repeated = jnp.repeat(tile_max, TILE, axis=1)
    row_scale = lax.dynamic_slice_in_dim(repeated, lead_rows, row_count, 1)
    blocks = weights.reshape(exp_count, row_count, col_count // TILE, TILE)
    return (blocks / (row_scale[..., None] + SCALE_EPS)).reshape(weights.shape).astype(jnp.bfloat16)


def general_body(
    expert_master,
    expert_first,
    expert_second,
    expert_grad,
    latent_master,
    latent_first,
    latent_second,
    latent_grad,
    step_count,
    column_owner,
):
    master_new, first_new, second_new = adamw_step(
        expert_master, expert_first, expert_second, expert_grad, step_count
    )
    latent_new, latent_one, latent_two = adamw_step(
        latent_master, latent_first, latent_second, latent_grad, step_count
    )
    dp_count = lax.axis_size("dp")
    dp_pos = lax.axis_index("dp")
    exp_count, row_count, col_count = master_new.shape
    block_count = col_count // TILE
    slot_count = max(1, block_count // dp_count)
    total_tiles = D // TILE
    recv_rows = block_count * row_count
    recv_tiles = recv_rows // TILE
    positions = jnp.arange(block_count, dtype=jnp.int32)
    inverse = jnp.sum(
        positions[:, None] * (column_owner[:, None] == positions[None, :]).astype(jnp.int32), axis=0
    )
    receiver_ids = jnp.arange(dp_count, dtype=jnp.int32)[:, None]
    slot_ids = jnp.arange(slot_count, dtype=jnp.int32)[None, :]
    segment = (
        receiver_ids * block_count
        + jnp.mod(dp_pos - receiver_ids * block_count, dp_count)
        + slot_ids * dp_count
    )
    usable_slot = (segment < (receiver_ids + 1) * block_count).reshape(-1)
    send_block = jnp.take(inverse, jnp.minimum(segment // dp_count, block_count - 1)).reshape(-1)
    local_segments = jnp.arange(block_count, dtype=jnp.int32)
    source_dev = jnp.mod(dp_pos * block_count + local_segments, dp_count)
    pick_index = source_dev * slot_count + local_segments // dp_count
    blocks = master_new.reshape(exp_count, row_count, block_count, TILE)
    picked = jnp.take(blocks, send_block, axis=2)
    received = lax.all_to_all(
        jnp.where(usable_slot[None, None, :, None], picked, jnp.zeros((), picked.dtype)),
        "dp",
        split_axis=2,
        concat_axis=2,
        tiled=True,
    )
    ordered = jnp.take(received, pick_index, axis=2)
    tall = (
        jnp.transpose(ordered, (0, 2, 1, 3))
        .reshape(exp_count, recv_rows, TILE)
        .reshape(exp_count, recv_tiles, TILE, TILE)
    )
    expert_scales = jnp.max(jnp.abs(tall), axis=(2, 3))
    expert_served = (
        (tall / (expert_scales[:, :, None, None] + SCALE_EPS))
        .reshape(exp_count, recv_rows, TILE)
        .astype(jnp.bfloat16)
    )
    latent_block = lax.all_gather(latent_new, "expert", axis=0, tiled=True)
    block_rows = latent_block.shape[0]
    block_offset = dp_pos * block_rows
    block_lead = block_offset % TILE
    block_tiles = local_tiles(row_maxima(latent_block)[None], block_lead)
    block_map = lax.pmax(place_tiles(block_tiles, block_offset // TILE), "dp")
    latent_scales = block_map[0, :total_tiles]
    block_tiles = lax.dynamic_slice_in_dim(block_map, block_offset // TILE, block_tiles.shape[1], 1)
    latent_served = quantized_rows(latent_block[None], block_tiles, block_lead)[0]
    return (
        master_new,
        first_new,
        second_new,
        expert_served,
        expert_scales,
        latent_new,
        latent_one,
        latent_two,
        latent_served,
        latent_scales,
    )


CHUNK = 32
EXTRA = 16
SPARE = 64
F32 = jnp.float32
BF16 = jnp.bfloat16
VMEM_LIMIT = 56 * 1024 * 1024
ANY = pl.BlockSpec(memory_space=pl.ANY)
SMEM = pl.BlockSpec(memory_space=pltpu.SMEM)
VMEM = pl.BlockSpec(memory_space=pltpu.VMEM)
PARAMS = pltpu.CompilerParams(vmem_limit_bytes=VMEM_LIMIT)
LIGHT = pltpu.CompilerParams(vmem_limit_bytes=1024 * 1024)


def corrections(step_ref):
    one, two = lax.fori_loop(
        0, step_ref[0], lambda _, p: (p[0] * BETA_ONE, p[1] * BETA_TWO), (F32(1.0), F32(1.0))
    )
    rate = LEARN_RATE / (1.0 - jnp.full((1, TILE), one, F32))
    corr = 1.0 / (1.0 - jnp.full((1, TILE), two, F32))
    return rate, corr


def adamw_tile(w, m, v, g, rate, corr):
    g = g.astype(F32)
    m1 = BETA_ONE * m.astype(F32) + (1.0 - BETA_ONE) * g
    v1 = BETA_TWO * v.astype(F32) + (1.0 - BETA_TWO) * g * g
    x = v1 * corr
    inv = pl.reciprocal(x * lax.rsqrt(x) + ADAM_EPS, approx=True)
    w1 = (1.0 - LEARN_RATE * DECAY_RATE) * w - rate * m1 * inv
    return w1, m1.astype(BF16), v1.astype(BF16)


def sub_max(w1):
    return jnp.max(jnp.abs(w1).reshape(w1.shape[0] // 8, 8, TILE), axis=0)


def stack_max(parts):
    parts = parts + [parts[-1]] * (8 - len(parts))
    rows = [jnp.max(p, axis=0, keepdims=True) for p in parts]
    return jnp.max(jnp.concatenate(rows, axis=0), axis=1, keepdims=True)


def three_parts(x):
    high = x.astype(BF16).astype(F32)
    rest = x - high
    middle = rest.astype(BF16).astype(F32)
    return high, middle, rest - middle


def copy_all(copies):
    for c in copies:
        c.start()


def wait_all(copies):
    for c in copies:
        c.wait()


def expert_kernel(partners, per_dest, n_alias, n_skip, has_side, owner_ref, pos_ref, step_ref, side_ref, *refs):
    hbm, refs = refs[:4], refs[4 + n_alias + n_skip :]
    n_dest = len(partners)
    outs, q_refs, served_ref = refs[:3], refs[3 : 3 + n_dest], refs[3 + n_dest]
    w, m, v, g, extra, in_sem, out_sem, extra_sem = refs[-8:]
    bufs = (w, m, v, g)
    blocks = owner_ref.shape[0]
    rows = w.shape[1]
    tiles = rows // TILE
    pos = pos_ref[0]
    if has_side:
        refs[-9][...] = side_ref[...]

    loads, stores = [], []
    for d, k in enumerate(partners):
        for j in range(per_dest):
            i = d * per_dest + j
            slot = (pos ^ k) * per_dest + j
            block = jnp.int32(0)
            for b in range(blocks):
                block = jnp.where(owner_ref[b] == slot, b, block)
            cols = pl.ds(pl.multiple_of(block * TILE, TILE), TILE)
            loads.append(
                [
                    pltpu.make_async_copy(hbm[a].at[:, cols], bufs[a].at[i], in_sem.at[i, a])
                    for a in range(4)
                ]
            )
            target = q_refs[d].at[pl.ds(j * rows, rows), :] if k else served_ref.at[j, pos]
            stores.append(
                [
                    pltpu.make_async_copy(bufs[a].at[i], outs[a].at[:, cols], out_sem.at[i, a])
                    for a in range(3)
                ]
                + [pltpu.make_async_copy(g.at[i], target, out_sem.at[i, 3])]
            )
            copy_all(loads[-1])
    rate, corr = corrections(step_ref)
    lane = lax.broadcasted_iota(jnp.int32, (8, TILE), 1)
    extras = []
    for d, k in enumerate(partners):
        side = side_ref[...]
        for j in range(per_dest):
            i = d * per_dest + j
            wait_all(loads[i])
            parts = []
            for t in range(tiles):
                at = pl.ds(t * TILE, TILE)
                w1, m1, v1 = adamw_tile(w[i, at, :], m[i, at, :], v[i, at, :], g[i, at, :], rate, corr)
                w[i, at, :] = w1
                m[i, at, :] = m1
                v[i, at, :] = v1
                parts.append(sub_max(w1))
            copy_all(stores[i][:3])
            top = stack_max(parts)
            inv = 1.0 / (top + SCALE_EPS)
            for t in range(tiles):
                at = pl.ds(t * TILE, TILE)
                g[i, at, :] = (w[i, at, :] * inv[t : t + 1, :]).astype(BF16)
            stores[i][3].start()
            for p, value in enumerate(three_parts(top)):
                side = jnp.where(lane == 3 * j + p, value, side)
        extra[d] = jnp.concatenate([side, jnp.zeros_like(side)], axis=0).astype(BF16)
        first = per_dest * rows if k else 0
        extras.append(
            pltpu.make_async_copy(
                extra.at[d], q_refs[d].at[pl.ds(first, EXTRA), :], extra_sem.at[d]
            )
        )
        extras[-1].start()
    for group in stores:
        wait_all(group)
    wait_all(extras)


def expert_group(arrays, state, owner, pos, step, side, carry, after, partners, per_dest):
    rows, cols = arrays[0].shape
    n_alias = len(state)
    n = len(partners) * per_dest
    elems = rows * TILE * n
    sides = [jax.ShapeDtypeStruct(side.shape, side.dtype)] * (len(carry) > 0)
    aliases = {8 + i: i for i in range(n_alias)}
    aliases.update({8 + n_alias + i: 3 + len(partners) + i for i in range(len(carry))})
    out = pl.pallas_call(
        functools.partial(
            expert_kernel, partners, per_dest, n_alias, len(carry) + len(after), len(sides)
        ),
        in_specs=[SMEM] * 3 + [VMEM] + [ANY] * (4 + n_alias + len(carry) + len(after)),
        out_specs=[ANY] * (3 + len(partners) + len(carry)) + [VMEM] * len(sides),
        out_shape=[
            jax.ShapeDtypeStruct((rows, cols), F32),
            jax.ShapeDtypeStruct((rows, cols), BF16),
            jax.ShapeDtypeStruct((rows, cols), BF16),
        ]
        + [
            jax.ShapeDtypeStruct((per_dest * rows * (k > 0) + EXTRA, TILE), BF16)
            for k in partners
        ]
        + [jax.ShapeDtypeStruct(x.shape, x.dtype) for x in carry]
        + sides,
        scratch_shapes=[
            pltpu.VMEM((n, rows, TILE), F32),
            pltpu.VMEM((n, rows, TILE), BF16),
            pltpu.VMEM((n, rows, TILE), BF16),
            pltpu.VMEM((n, rows, TILE), BF16),
            pltpu.VMEM((len(partners), EXTRA, TILE), BF16),
            pltpu.SemaphoreType.DMA((n, 4)),
            pltpu.SemaphoreType.DMA((n, 4)),
            pltpu.SemaphoreType.DMA((len(partners),)),
        ],
        input_output_aliases=aliases,
        compiler_params=PARAMS,
        cost_estimate=pl.CostEstimate(flops=elems, bytes_accessed=elems, transcendentals=0),
        name="expert_adamw",
    )(owner, pos, step, side, *arrays, *state, *carry, *after)
    return out[:3], out[3 : 3 + len(partners)], out[3 + len(partners) :]


def block_copies(served, payloads, srcs, sem):
    per_dest, _, rows, _ = served.shape
    return [
        pltpu.make_async_copy(q.at[pl.ds(j * rows, rows), :], served.at[j, src], sem.at[i, j])
        for i, (q, src) in enumerate(zip(payloads, srcs))
        for j in range(per_dest)
    ]


def place_kernel(partners, pos_ref, *refs):
    n = len(partners)
    served, sem = refs[-2:]
    copies = block_copies(served, refs[:n], [pos_ref[0] ^ k for k in partners], sem)
    copy_all(copies)
    wait_all(copies)


def place_blocks(served, pos, payloads, partners, shape):
    n = len(partners)
    return pl.pallas_call(
        functools.partial(place_kernel, partners),
        in_specs=[SMEM] + [ANY] * (n + len(served)),
        out_specs=ANY,
        out_shape=jax.ShapeDtypeStruct(shape, BF16),
        scratch_shapes=[pltpu.SemaphoreType.DMA((n, shape[0]))],
        input_output_aliases={1 + n: 0} if served else {},
        compiler_params=LIGHT,
        cost_estimate=pl.CostEstimate(
            flops=0, bytes_accessed=4 * n * payloads[0].size, transcendentals=0
        ),
        name="place_served",
    )(pos, *payloads, *served)


def finish_kernel(order, tiles, lat_tiles, n_late, to_place, deltas, rows, pos_ref, line_ref, *refs):
    n = len(order)
    late, q_refs = refs[:n_late], refs[n_late : n_late + n]
    n_rest = len(deltas)
    rest = refs[n_late + n : n_late + n + n_rest]
    outs = refs[n_late + n + n_rest + 2 :]
    served, latent, exp_ref, lat_ref, extra, rows_ref, buf, place_sem, sem, in_sem, out_sem = outs
    pos = pos_ref[0]
    per_dest = served.shape[0]
    blocks_copies = block_copies(
        served, [q_refs[i] for i in to_place], [pos ^ order[i] for i in to_place], place_sem
    )
    copies = [
        pltpu.make_async_copy(
            q.at[pl.ds(q.shape[0] - EXTRA, EXTRA), :], extra.at[i], sem.at[i]
        )
        for i, q in enumerate(q_refs)
    ]
    rest_loads = [pltpu.make_async_copy(rest[i], buf.at[i], in_sem.at[i]) for i in range(n_rest)]
    copy_all(rest_loads)
    copy_all(copies)
    copy_all(blocks_copies)
    rest_copies = []
    for i, delta in enumerate(deltas):
        rest_loads[i].wait()
        group = rest_stores(buf, i, line_ref[0] ^ delta, rows, latent, out_sem)
        copy_all(group)
        rest_copies += group
    rows_ref[...] = jnp.zeros_like(rows_ref)
    flat = jnp.zeros((8, exp_ref.shape[1]), F32)
    wide = lax.broadcasted_iota(jnp.int32, flat.shape, 1)
    deep = lax.broadcasted_iota(jnp.int32, flat.shape, 0)
    for i, k in enumerate(order):
        copies[i].wait()
        src = pos ^ k
        x = extra[i].astype(F32)[0:8, :]
        side = late[i][...] if i < n_late else x
        lat = sum(pltpu.roll(side, TILE - SPARE - 16 * p, 1) for p in range(3))
        rows_ref[pl.ds(src * lat_tiles, lat_tiles), :] = lat[0:lat_tiles, :]
        for j in range(per_dest):
            first = 3 * j
            top = x[:, first : first + 1] + x[:, first + 1 : first + 2] + x[:, first + 2 : first + 3]
            hit = (wide == (j * n + src) * tiles + deep) & (deep < tiles)
            flat = jnp.where(hit, top, flat)
    exp_ref[...] = jnp.max(flat, axis=0, keepdims=True)
    blocks, height = lat_ref.shape
    lat_ref[...] = jnp.transpose(rows_ref[...])[0:blocks, 0:height]
    wait_all(blocks_copies)
    wait_all(rest_copies)


def finish(
    served, latent, pos, line, late, received, rest, order, to_place, deltas, tiles, lat_tiles, lat_blocks
):
    n = len(order)
    per_dest = served.shape[0]
    span, cols = rest[0].shape
    rows = TILE + span
    ins = 2 + len(late) + n + len(rest)
    served, latent, expert, scales = pl.pallas_call(
        functools.partial(
            finish_kernel, order, tiles, lat_tiles, len(late), to_place, deltas, rows
        ),
        in_specs=[SMEM] * 2 + [VMEM] * len(late) + [ANY] * (n + len(rest) + 2),
        out_specs=[ANY, ANY, VMEM, VMEM],
        out_shape=[
            jax.ShapeDtypeStruct(served.shape, served.dtype),
            jax.ShapeDtypeStruct(latent.shape, latent.dtype),
            jax.ShapeDtypeStruct((1, per_dest * n * tiles), F32),
            jax.ShapeDtypeStruct((lat_blocks, n * lat_tiles), F32),
        ],
        scratch_shapes=[
            pltpu.VMEM((n, EXTRA, TILE), BF16),
            pltpu.VMEM((TILE, TILE), F32),
            pltpu.VMEM((len(rest), span, cols), BF16),
            pltpu.SemaphoreType.DMA((len(to_place), per_dest)),
            pltpu.SemaphoreType.DMA((n,)),
            pltpu.SemaphoreType.DMA((len(rest),)),
            pltpu.SemaphoreType.DMA((len(rest), span // CHUNK)),
        ],
        input_output_aliases={ins: 0, ins + 1: 1},
        compiler_params=pltpu.CompilerParams(vmem_limit_bytes=4 * 1024 * 1024),
        cost_estimate=pl.CostEstimate(flops=1000000, bytes_accessed=1000000, transcendentals=0),
        name="place_last",
    )(pos, line, *late, *received, *rest, served, latent)
    return served, latent, expert, scales.T


def whole_tile(pos, rows):
    return pl.multiple_of(lax.rem(pos * (TILE - rows % TILE), TILE), CHUNK)


def full_kernel(pieces, rows, x_ref, *refs):
    out_ref, buf, in_sem, out_sem = refs[-4:]
    loads, stores = [], []
    for i in range(pieces):
        lead = i * (TILE - rows % TILE) % TILE
        at = pl.ds(i * TILE, TILE)
        loads.append(pltpu.make_async_copy(x_ref.at[at, :], buf.at[at, :], in_sem.at[i]))
        stores.append(
            pltpu.make_async_copy(
                buf.at[at, :], out_ref.at[pl.ds(i * rows + lead, TILE), :], out_sem.at[i]
            )
        )
    copy_all(loads)
    for i in range(pieces):
        loads[i].wait()
        stores[i].start()
    wait_all(stores)


def place_full(out, x, rows):
    pieces = x.shape[0] // TILE
    return pl.pallas_call(
        functools.partial(full_kernel, pieces, rows),
        in_specs=[ANY] * (1 + len(out)),
        out_specs=ANY,
        out_shape=jax.ShapeDtypeStruct((pieces * rows, x.shape[1]), BF16),
        scratch_shapes=[
            pltpu.VMEM(x.shape, BF16),
            pltpu.SemaphoreType.DMA((pieces,)),
            pltpu.SemaphoreType.DMA((pieces,)),
        ],
        input_output_aliases={1: 0} if out else {},
        compiler_params=PARAMS,
        cost_estimate=pl.CostEstimate(flops=0, bytes_accessed=4 * x.size, transcendentals=0),
        name="place_whole",
    )(x, *out)


def rest_stores(buf, i, peer, rows, out_ref, sem):
    lead = whole_tile(peer, rows)
    copies = []
    for c in range((rows - TILE) // CHUNK):
        at = peer * rows + c * CHUNK + jnp.where(c * CHUNK < lead, 0, TILE)
        copies.append(
            pltpu.make_async_copy(
                buf.at[i, pl.ds(c * CHUNK, CHUNK), :],
                out_ref.at[pl.ds(pl.multiple_of(at, CHUNK), CHUNK), :],
                sem.at[i, c],
            )
        )
    return copies


def rest_kernel(deltas, rows, pos_ref, *refs):
    n = len(deltas)
    x_refs = refs[:n]
    out_ref, again_ref, side_ref, buf, in_sem, out_sem = refs[-6:]
    side_ref[...] = refs[n][...]
    loads = [pltpu.make_async_copy(x_refs[i], buf.at[i], in_sem.at[i]) for i in range(n)]
    copy_all(loads)
    stores = []
    for i in reversed(range(n)):
        loads[i].wait()
        if i == n - 1:
            stores.append(pltpu.make_async_copy(buf.at[i], again_ref, out_sem.at[n, 0]))
            stores[-1].start()
        group = rest_stores(buf, i, pos_ref[0] ^ deltas[i], rows, out_ref, out_sem)
        copy_all(group)
        stores += group
    wait_all(stores)


def place_rest(pos, xs, deltas, side, after, rows, peers):
    span, cols = xs[0].shape
    n = len(xs)
    return pl.pallas_call(
        functools.partial(rest_kernel, deltas, rows),
        in_specs=[SMEM] + [ANY] * n + [VMEM, ANY],
        out_specs=[ANY, ANY, VMEM],
        out_shape=[
            jax.ShapeDtypeStruct((peers * rows, cols), BF16),
            jax.ShapeDtypeStruct((span, cols), BF16),
            jax.ShapeDtypeStruct(side.shape, side.dtype),
        ],
        scratch_shapes=[
            pltpu.VMEM((n, span, cols), BF16),
            pltpu.SemaphoreType.DMA((n,)),
            pltpu.SemaphoreType.DMA((n + 1, span // CHUNK)),
        ],
        compiler_params=pltpu.CompilerParams(vmem_limit_bytes=4 * 1024 * 1024),
        cost_estimate=pl.CostEstimate(flops=0, bytes_accessed=4 * n * span * cols, transcendentals=0),
        name="place_rest",
    )(pos, *xs, side, after)


SLABS = 4


def latent_kernel(chunks, step_ref, pos_ref, *refs):
    hbm, outs, top_ref = refs[:4], refs[4:8], refs[8]
    w, m, v, g, q, in_sem, out_sem = refs[9:]
    bufs = (w, m, v, g)
    width = w.shape[1] // SLABS
    loads, stores = [], []
    for i in range(SLABS):
        cols = pl.ds(i * width, width)
        loads.append(
            [
                pltpu.make_async_copy(hbm[a].at[:, cols], bufs[a].at[:, cols], in_sem.at[i, a])
                for a in range(4)
            ]
        )
        stores.append(
            [
                pltpu.make_async_copy(src.at[:, cols], outs[a].at[:, cols], out_sem.at[i, a])
                for a, src in enumerate((w, m, v, q))
            ]
        )
        copy_all(loads[i])
    rate, corr = corrections(step_ref)
    lane = lax.broadcasted_iota(jnp.int32, (8, TILE), 1)
    lead = whole_tile(pos_ref[0], w.shape[0])
    sub = lax.broadcasted_iota(jnp.int32, (8, 1), 0) * CHUNK
    inside = (sub >= lead) & (sub < lead + TILE)
    tops = jnp.zeros((8, TILE), F32)
    for i in range(SLABS):
        wait_all(loads[i])
        blocks = range(i * width // TILE, (i + 1) * width // TILE)
        slab_tops = []
        for b in blocks:
            cols = pl.ds(b * TILE, TILE)
            w1, m1, v1 = adamw_tile(w[:, cols], m[:, cols], v[:, cols], g[:, cols], rate, corr)
            w[:, cols] = w1
            m[:, cols] = m1
            v[:, cols] = v1
            slab_tops.append(stack_max([sub_max(w1[c * CHUNK : (c + 1) * CHUNK]) for c in range(chunks)]))
        for b, top in zip(blocks, slab_tops):
            cols = pl.ds(b * TILE, TILE)
            tops = jnp.where(lane == b, top, tops)
            whole = jnp.max(jnp.where(inside, top, 0.0), axis=0, keepdims=True)
            q[:, cols] = (w[pl.ds(lead, TILE), cols] * (1.0 / (whole + SCALE_EPS))).astype(BF16)
        copy_all(stores[i])
    top_ref[...] = tops
    for group in stores:
        wait_all(group)


def latent_update(arrays, step, pos):
    rows, cols = arrays[0].shape
    elems = rows * cols
    return pl.pallas_call(
        functools.partial(latent_kernel, rows // CHUNK),
        in_specs=[SMEM] * 2 + [ANY] * 4,
        out_specs=[ANY] * 4 + [VMEM],
        out_shape=[
            jax.ShapeDtypeStruct((rows, cols), F32),
            jax.ShapeDtypeStruct((rows, cols), BF16),
            jax.ShapeDtypeStruct((rows, cols), BF16),
            jax.ShapeDtypeStruct((TILE, cols), BF16),
            jax.ShapeDtypeStruct((8, TILE), F32),
        ],
        scratch_shapes=[
            pltpu.VMEM((rows, cols), F32),
            pltpu.VMEM((rows, cols), BF16),
            pltpu.VMEM((rows, cols), BF16),
            pltpu.VMEM((rows, cols), BF16),
            pltpu.VMEM((TILE, cols), BF16),
            pltpu.SemaphoreType.DMA((SLABS, 4)),
            pltpu.SemaphoreType.DMA((SLABS, 4)),
        ],
        compiler_params=PARAMS,
        cost_estimate=pl.CostEstimate(
            flops=30 * elems, bytes_accessed=18 * elems, transcendentals=2 * elems
        ),
        name="latent_adamw",
    )(step, pos, *arrays)


def latent_rest_kernel(chunks, peers, pos_ref, w1_ref, *refs):
    q_ref, again_ref, side_ref, w, q, ext, tops_ref, in_sem, out_sem = refs[-9:]
    per_tile = TILE // CHUNK
    rows, cols = w1_ref.shape
    width = cols // SLABS
    pos = pos_ref[0]
    lead = whole_tile(pos, rows)
    loads, stores = [], []
    for i in range(SLABS):
        at = pl.ds(i * width, width)
        group = []
        for c in range(chunks - per_tile):
            first = pl.multiple_of(c * CHUNK + jnp.where(c * CHUNK < lead, 0, TILE), CHUNK)
            group.append(
                pltpu.make_async_copy(
                    w1_ref.at[pl.ds(first, CHUNK), at],
                    w.at[pl.ds(c * CHUNK, CHUNK), at],
                    in_sem.at[i, c],
                )
            )
        copy_all(group)
        loads.append(group)
        stores.append(
            [
                pltpu.make_async_copy(q.at[:, at], out.at[:, at], out_sem.at[i, n])
                for n, out in enumerate((q_ref, again_ref))
            ]
        )
    for s in range(peers):
        peer = lax.rem(pos + peers - s, peers)
        ext[pl.ds(peer * chunks, chunks), :] = refs[s][0:chunks, :]
    tops_ref[...] = jnp.zeros_like(tops_ref)
    for t in range(peers * chunks // per_tile):
        tops_ref[t : t + 1, :] = jnp.max(
            ext[t * per_tile : (t + 1) * per_tile, :], axis=0, keepdims=True
        )
    lane = lax.broadcasted_iota(jnp.int32, (8, TILE), 1)
    side = jnp.zeros((8, TILE), F32)
    for p, value in enumerate(three_parts(tops_ref[...])):
        at = SPARE + 16 * p
        side = jnp.where((lane >= at) & (lane < at + 16), pltpu.roll(value, at, 1), side)
    side_ref[...] = side
    start = pos * chunks
    above = tops_ref[pl.ds(start // per_tile, 1), :]
    below = tops_ref[pl.ds((start + lead // CHUNK + per_tile) // per_tile, 1), :]
    both = jnp.concatenate([above] * 4 + [below] * 4, axis=0)
    tops = [
        jnp.max(jnp.where(lane == b, both, 0.0), axis=1, keepdims=True) for b in range(cols // TILE)
    ]
    invs = [1.0 / (top + SCALE_EPS) for top in tops]
    for i in range(SLABS):
        wait_all(loads[i])
        for b in range(i * width // TILE, (i + 1) * width // TILE):
            at = pl.ds(b * TILE, TILE)
            for c in range(chunks - per_tile):
                span = pl.ds(c * CHUNK, CHUNK)
                inv = jnp.where(c * CHUNK < lead, invs[b][0:1, :], invs[b][4:5, :])
                q[span, at] = (w[span, at] * inv).astype(BF16)
        copy_all(stores[i])
    for group in stores:
        wait_all(group)


def latent_rest(w1, maxima, pos, after):
    rows, cols = w1.shape
    chunks = rows // CHUNK
    peers = len(maxima)
    return pl.pallas_call(
        functools.partial(latent_rest_kernel, chunks, peers),
        in_specs=[SMEM, ANY] + [VMEM] * peers + [ANY],
        out_specs=[ANY, ANY, VMEM],
        out_shape=[
            jax.ShapeDtypeStruct((rows - TILE, cols), BF16),
            jax.ShapeDtypeStruct((rows - TILE, cols), BF16),
            jax.ShapeDtypeStruct((8, TILE), F32),
        ],
        scratch_shapes=[
            pltpu.VMEM((rows - TILE, cols), F32),
            pltpu.VMEM((rows - TILE, cols), BF16),
            pltpu.VMEM((8 * peers, TILE), F32),
            pltpu.VMEM((8, TILE), F32),
            pltpu.SemaphoreType.DMA((SLABS, chunks)),
            pltpu.SemaphoreType.DMA((SLABS, 2)),
        ],
        compiler_params=PARAMS,
        cost_estimate=pl.CostEstimate(
            flops=rows * cols, bytes_accessed=3 * rows * cols, transcendentals=0
        ),
        name="latent_rest",
    )(pos, w1, *maxima, after)


def fast_fits(expert_shape, latent_shape, dp_count, exp_axis):
    exp_count, rows, cols = expert_shape
    latent_rows, latent_cols = latent_shape
    return (
        exp_count == 1
        and rows % TILE == 0
        and rows <= 8 * TILE
        and cols % (TILE * dp_count) == 0
        and cols // TILE // dp_count <= 16
        and dp_count == 8
        and dp_count * latent_rows * exp_axis <= TILE * TILE
        and latent_rows % CHUNK == 0
        and 2 * TILE - CHUNK <= latent_rows < 2 * TILE
        and latent_rows * exp_axis % TILE == 0
        and latent_rows * exp_axis <= 8 * TILE
        and exp_axis == 4
        and latent_cols % (SLABS * TILE) == 0
        and latent_cols <= 16 * TILE
    )


def partner_groups(dp_count):
    hops = lambda k: bin(k >> 1).count("1")
    stage = lambda k: 3 if k < 2 else (1 if hops(k) > 1 else (2 if k & 1 else 0))
    order = sorted(range(dp_count), key=lambda k: (stage(k), -k))
    return [[k for k in order if stage(k) in n] for n in ((0,), (1,), (2, 3))]


def fast_body(
    expert_master,
    expert_first,
    expert_second,
    expert_grad,
    latent_master,
    latent_first,
    latent_second,
    latent_grad,
    step_count,
    column_owner,
):
    dp_count = lax.axis_size("dp")
    dp_pos = lax.axis_index("dp").astype(jnp.int32)
    exp_axis = lax.axis_size("expert")
    exp_pos = lax.axis_index("expert").astype(jnp.int32)
    _, rows, cols = expert_master.shape
    block_count = cols // TILE
    per_dest = block_count // dp_count
    tiles = rows // TILE

    expert_at, dp_at = exp_pos.reshape(1), dp_pos.reshape(1)
    latent_new, latent_one, latent_two, whole, chunk_top = latent_update(
        (latent_master, latent_first, latent_second, latent_grad), step_count, expert_at
    )
    latent_rows = latent_new.shape[0]
    whole = lax.all_gather(whole, "expert", axis=0, tiled=True)
    maxima = [chunk_top] + [
        lax.ppermute(chunk_top, "expert", [(i, (i + s) % exp_axis) for i in range(exp_axis)])
        for s in range(1, exp_axis)
    ]

    arrays = tuple(
        a.reshape(rows, cols) for a in (expert_master, expert_first, expert_second, expert_grad)
    )
    def swap(x, axis, k):
        return lax.ppermute(x, axis, [(i, i ^ k) for i in range(lax.axis_size(axis))])

    groups = partner_groups(dp_count)
    order = [k for partners in groups for k in partners]
    state, received, carry = (), [], ()
    side = jnp.zeros((8, TILE), F32)
    for n, partners in enumerate(groups):
        state, sent, carried = expert_group(
            arrays, state, column_owner, dp_at, step_count, side, carry, (), partners, per_dest
        )
        received += [swap(q, "dp", k) if k else q for k, q in zip(partners, sent)]
        if n == 1:
            rest, again, side = latent_rest(latent_new, maxima, expert_at, sent[0])
            far = swap(rest, "expert", 2)
            served = place_blocks(
                (), dp_at, received[: len(groups[0])], groups[0], (per_dest, dp_count, rows, TILE)
            )
            carry = (served, again)
    served, again, side = carried
    near = swap(again, "expert", 1)
    first, count = len(groups[0]), len(groups[0]) + len(groups[1])
    served = place_blocks((served,), dp_at, received[first:count], groups[1], served.shape)
    latent_served, far_again, side = place_rest(
        expert_at, [rest, far], [0, 2], side, sent[-1], latent_rows, exp_axis
    )
    last = swap(far_again, "expert", 1)
    late = [swap(side, "dp", k) for k in groups[0] + groups[1]]
    latent_served = place_full((latent_served,), whole, latent_rows)
    served, latent_served, expert_scales, latent_scales = finish(
        served,
        latent_served,
        dp_at,
        expert_at,
        late,
        received,
        [near, last],
        order,
        range(count, dp_count - 1),
        [1, 3],
        tiles,
        latent_rows * exp_axis // TILE,
        latent_new.shape[1] // TILE,
    )
    expert_served = served.reshape(1, block_count * rows, TILE)

    return (
        state[0][None],
        state[1][None],
        state[2][None],
        expert_served,
        expert_scales,
        latent_new,
        latent_one,
        latent_two,
        latent_served,
        latent_scales,
    )


def body(*args):
    if fast_fits(args[0].shape, args[4].shape, lax.axis_size("dp"), lax.axis_size("expert")):
        return fast_body(*args)
    return general_body(*args)


def solution(mesh):
    placed = (
        P("expert", "dp", None),
        P("expert", "dp", None),
        P("expert", "dp", None),
        P("expert", "dp", None),
        P(("dp", "expert"), None),
        P(("dp", "expert"), None),
        P(("dp", "expert"), None),
        P(("dp", "expert"), None),
        P(),
        P(),
    )
    return jax.shard_map(
        body,
        mesh=mesh,
        in_specs=placed,
        out_specs=(
            P("expert", "dp", None),
            P("expert", "dp", None),
            P("expert", "dp", None),
            P("expert", "dp", None),
            P("expert", "dp"),
            P(("dp", "expert"), None),
            P(("dp", "expert"), None),
            P(("dp", "expert"), None),
            P("dp", None),
            P(),
        ),
        check_vma=False,
    )
```

```python
import functools
import math

import jax
import jax.numpy as jnp
from jax import lax
from jax.experimental import pallas as pl
from jax.experimental.pallas import tpu as pltpu
from jax.sharding import PartitionSpec as P

D = 7168
TILE = 128


BETA_ONE = 0.9
BETA_TWO = 0.95
LEARN_RATE = 0.2
DECAY_RATE = 0.1
ADAM_EPS = 1e-08
SCALE_EPS = 1e-06


def adamw_step(master, moment_one, moment_two, gradient, step_count):
    grad_value = gradient.astype(jnp.float32)
    first_new = BETA_ONE * moment_one.astype(jnp.float32) + (1.0 - BETA_ONE) * grad_value
    second_new = (
        BETA_TWO * moment_two.astype(jnp.float32) + (1.0 - BETA_TWO) * grad_value * grad_value
    )
    step_value = step_count[0].astype(jnp.float32)
    corr_one = 1.0 - jnp.power(jnp.float32(BETA_ONE), step_value)
    corr_two = 1.0 - jnp.power(jnp.float32(BETA_TWO), step_value)
    update = first_new / corr_one / (jnp.sqrt(second_new / corr_two) + ADAM_EPS)
    master_new = master - LEARN_RATE * (update + DECAY_RATE * master)
    return (master_new, first_new.astype(jnp.bfloat16), second_new.astype(jnp.bfloat16))


def row_maxima(weights):
    leading = weights.shape[:-1]
    tile_count = weights.shape[-1] // TILE
    return jnp.max(jnp.abs(weights).reshape(leading + (tile_count, TILE)), axis=-1)


def local_tiles(row_max, lead_rows):
    exp_count, row_count, tile_count = row_max.shape
    tile_span = row_count // TILE + 2
    buffer = jnp.zeros((exp_count, tile_span * TILE, tile_count), jnp.float32)
    buffer = lax.dynamic_update_slice(buffer, row_max, (jnp.int32(0), lead_rows, jnp.int32(0)))
    return jnp.max(buffer.reshape(exp_count, tile_span, TILE, tile_count), axis=2)


def place_tiles(tile_max, first_tile):
    exp_count, tile_span, tile_count = tile_max.shape
    global_map = jnp.zeros((exp_count, D // TILE + tile_span, tile_count), jnp.float32)
    return lax.dynamic_update_slice(global_map, tile_max, (jnp.int32(0), first_tile, jnp.int32(0)))


def quantized_rows(weights, tile_max, lead_rows):
    exp_count, row_count, col_count = weights.shape
    repeated = jnp.repeat(tile_max, TILE, axis=1)
    row_scale = lax.dynamic_slice_in_dim(repeated, lead_rows, row_count, 1)
    blocks = weights.reshape(exp_count, row_count, col_count // TILE, TILE)
    return (blocks / (row_scale[..., None] + SCALE_EPS)).reshape(weights.shape).astype(jnp.bfloat16)


def general_body(
    expert_master,
    expert_first,
    expert_second,
    expert_grad,
    latent_master,
    latent_first,
    latent_second,
    latent_grad,
    step_count,
    column_owner,
):
    master_new, first_new, second_new = adamw_step(
        expert_master, expert_first, expert_second, expert_grad, step_count
    )
    latent_new, latent_one, latent_two = adamw_step(
        latent_master, latent_first, latent_second, latent_grad, step_count
    )
    dp_count = lax.axis_size("dp")
    dp_pos = lax.axis_index("dp")
    exp_count, row_count, col_count = master_new.shape
    block_count = col_count // TILE
    slot_count = max(1, block_count // dp_count)
    total_tiles = D // TILE
    recv_rows = block_count * row_count
    recv_tiles = recv_rows // TILE
    positions = jnp.arange(block_count, dtype=jnp.int32)
    inverse = jnp.sum(
        positions[:, None] * (column_owner[:, None] == positions[None, :]).astype(jnp.int32), axis=0
    )
    receiver_ids = jnp.arange(dp_count, dtype=jnp.int32)[:, None]
    slot_ids = jnp.arange(slot_count, dtype=jnp.int32)[None, :]
    segment = (
        receiver_ids * block_count
        + jnp.mod(dp_pos - receiver_ids * block_count, dp_count)
        + slot_ids * dp_count
    )
    usable_slot = (segment < (receiver_ids + 1) * block_count).reshape(-1)
    send_block = jnp.take(inverse, jnp.minimum(segment // dp_count, block_count - 1)).reshape(-1)
    local_segments = jnp.arange(block_count, dtype=jnp.int32)
    source_dev = jnp.mod(dp_pos * block_count + local_segments, dp_count)
    pick_index = source_dev * slot_count + local_segments // dp_count
    blocks = master_new.reshape(exp_count, row_count, block_count, TILE)
    picked = jnp.take(blocks, send_block, axis=2)
    received = lax.all_to_all(
        jnp.where(usable_slot[None, None, :, None], picked, jnp.zeros((), picked.dtype)),
        "dp",
        split_axis=2,
        concat_axis=2,
        tiled=True,
    )
    ordered = jnp.take(received, pick_index, axis=2)
    tall = (
        jnp.transpose(ordered, (0, 2, 1, 3))
        .reshape(exp_count, recv_rows, TILE)
        .reshape(exp_count, recv_tiles, TILE, TILE)
    )
    expert_scales = jnp.max(jnp.abs(tall), axis=(2, 3))
    expert_served = (
        (tall / (expert_scales[:, :, None, None] + SCALE_EPS))
        .reshape(exp_count, recv_rows, TILE)
        .astype(jnp.bfloat16)
    )
    latent_block = lax.all_gather(latent_new, "expert", axis=0, tiled=True)
    block_rows = latent_block.shape[0]
    block_offset = dp_pos * block_rows
    block_lead = block_offset % TILE
    block_tiles = local_tiles(row_maxima(latent_block)[None], block_lead)
    block_map = lax.pmax(place_tiles(block_tiles, block_offset // TILE), "dp")
    latent_scales = block_map[0, :total_tiles]
    block_tiles = lax.dynamic_slice_in_dim(block_map, block_offset // TILE, block_tiles.shape[1], 1)
    latent_served = quantized_rows(latent_block[None], block_tiles, block_lead)[0]
    return (
        master_new,
        first_new,
        second_new,
        expert_served,
        expert_scales,
        latent_new,
        latent_one,
        latent_two,
        latent_served,
        latent_scales,
    )


CHUNK = 32
EXTRA = 16
SPARE = 64
F32 = jnp.float32
BF16 = jnp.bfloat16
VMEM_LIMIT = 56 * 1024 * 1024
ANY = pl.BlockSpec(memory_space=pl.ANY)
SMEM = pl.BlockSpec(memory_space=pltpu.SMEM)
VMEM = pl.BlockSpec(memory_space=pltpu.VMEM)
PARAMS = pltpu.CompilerParams(vmem_limit_bytes=VMEM_LIMIT)
LIGHT = pltpu.CompilerParams(vmem_limit_bytes=1024 * 1024)


def corrections(step_ref):
    one, two = lax.fori_loop(
        0, step_ref[0], lambda _, p: (p[0] * BETA_ONE, p[1] * BETA_TWO), (F32(1.0), F32(1.0))
    )
    rate = LEARN_RATE / (1.0 - jnp.full((1, TILE), one, F32))
    corr = 1.0 / (1.0 - jnp.full((1, TILE), two, F32))
    return rate, corr


def adamw_tile(w, m, v, g, rate, corr):
    g = g.astype(F32)
    m1 = BETA_ONE * m.astype(F32) + (1.0 - BETA_ONE) * g
    v1 = BETA_TWO * v.astype(F32) + (1.0 - BETA_TWO) * g * g
    x = v1 * corr
    inv = pl.reciprocal(x * lax.rsqrt(x) + ADAM_EPS, approx=True)
    w1 = (1.0 - LEARN_RATE * DECAY_RATE) * w - rate * m1 * inv
    return w1, m1.astype(BF16), v1.astype(BF16)


def sub_max(w1):
    return jnp.max(jnp.abs(w1).reshape(w1.shape[0] // 8, 8, TILE), axis=0)


def stack_max(parts):
    parts = parts + [parts[-1]] * (8 - len(parts))
    rows = [jnp.max(p, axis=0, keepdims=True) for p in parts]
    return jnp.max(jnp.concatenate(rows, axis=0), axis=1, keepdims=True)


def three_parts(x):
    high = x.astype(BF16).astype(F32)
    rest = x - high
    middle = rest.astype(BF16).astype(F32)
    return high, middle, rest - middle


def copy_all(copies):
    for c in copies:
        c.start()


def wait_all(copies):
    for c in copies:
        c.wait()


def expert_kernel(partners, per_dest, n_alias, n_skip, has_side, owner_ref, pos_ref, step_ref, side_ref, *refs):
    hbm, refs = refs[:4], refs[4 + n_alias + n_skip :]
    n_dest = len(partners)
    outs, q_refs, served_ref = refs[:3], refs[3 : 3 + n_dest], refs[3 + n_dest]
    w, m, v, g, extra, in_sem, out_sem, extra_sem = refs[-8:]
    bufs = (w, m, v, g)
    blocks = owner_ref.shape[0]
    rows = w.shape[1]
    tiles = rows // TILE
    pos = pos_ref[0]
    if has_side:
        refs[-9][...] = side_ref[...]

    loads, stores = [], []
    for d, k in enumerate(partners):
        for j in range(per_dest):
            i = d * per_dest + j
            slot = (pos ^ k) * per_dest + j
            block = jnp.int32(0)
            for b in range(blocks):
                block = jnp.where(owner_ref[b] == slot, b, block)
            cols = pl.ds(pl.multiple_of(block * TILE, TILE), TILE)
            loads.append(
                [
                    pltpu.make_async_copy(hbm[a].at[:, cols], bufs[a].at[i], in_sem.at[i, a])
                    for a in range(4)
                ]
            )
            target = q_refs[d].at[pl.ds(j * rows, rows), :] if k else served_ref.at[j, pos]
            stores.append(
                [
                    pltpu.make_async_copy(bufs[a].at[i], outs[a].at[:, cols], out_sem.at[i, a])
                    for a in range(3)
                ]
                + [pltpu.make_async_copy(g.at[i], target, out_sem.at[i, 3])]
            )
            copy_all(loads[-1])
    rate, corr = corrections(step_ref)
    lane = lax.broadcasted_iota(jnp.int32, (8, TILE), 1)
    parts_of_maxima = jnp.zeros((8, TILE), F32)
    for p, value in enumerate(three_parts(side_ref[...])):
        at = SPARE + 16 * p
        parts_of_maxima = jnp.where(
            (lane >= at) & (lane < at + 16), pltpu.roll(value, at, 1), parts_of_maxima
        )
    extras = []
    for d, k in enumerate(partners):
        side = parts_of_maxima
        for j in range(per_dest):
            i = d * per_dest + j
            wait_all(loads[i])
            parts = []
            for t in range(tiles):
                at = pl.ds(t * TILE, TILE)
                w1, m1, v1 = adamw_tile(w[i, at, :], m[i, at, :], v[i, at, :], g[i, at, :], rate, corr)
                w[i, at, :] = w1
                m[i, at, :] = m1
                v[i, at, :] = v1
                parts.append(sub_max(w1))
            copy_all(stores[i][:3])
            top = stack_max(parts)
            inv = 1.0 / (top + SCALE_EPS)
            for t in range(tiles):
                at = pl.ds(t * TILE, TILE)
                g[i, at, :] = (w[i, at, :] * inv[t : t + 1, :]).astype(BF16)
            stores[i][3].start()
            for p, value in enumerate(three_parts(top)):
                side = jnp.where(lane == 3 * j + p, value, side)
        extra[d] = jnp.concatenate([side, jnp.zeros_like(side)], axis=0).astype(BF16)
        first = per_dest * rows if k else 0
        extras.append(
            pltpu.make_async_copy(
                extra.at[d], q_refs[d].at[pl.ds(first, EXTRA), :], extra_sem.at[d]
            )
        )
        extras[-1].start()
    for group in stores:
        wait_all(group)
    wait_all(extras)


def expert_group(arrays, state, owner, pos, step, side, carry, after, partners, per_dest):
    rows, cols = arrays[0].shape
    n_alias = len(state)
    n = len(partners) * per_dest
    elems = rows * TILE * n
    sides = [jax.ShapeDtypeStruct(side.shape, side.dtype)] * (len(carry) > 0)
    aliases = {8 + i: i for i in range(n_alias)}
    aliases.update({8 + n_alias + i: 3 + len(partners) + i for i in range(len(carry))})
    out = pl.pallas_call(
        functools.partial(
            expert_kernel, partners, per_dest, n_alias, len(carry) + len(after), len(sides)
        ),
        in_specs=[SMEM] * 3 + [VMEM] + [ANY] * (4 + n_alias + len(carry) + len(after)),
        out_specs=[ANY] * (3 + len(partners) + len(carry)) + [VMEM] * len(sides),
        out_shape=[
            jax.ShapeDtypeStruct((rows, cols), F32),
            jax.ShapeDtypeStruct((rows, cols), BF16),
            jax.ShapeDtypeStruct((rows, cols), BF16),
        ]
        + [
            jax.ShapeDtypeStruct((per_dest * rows * (k > 0) + EXTRA, TILE), BF16)
            for k in partners
        ]
        + [jax.ShapeDtypeStruct(x.shape, x.dtype) for x in carry]
        + sides,
        scratch_shapes=[
            pltpu.VMEM((n, rows, TILE), F32),
            pltpu.VMEM((n, rows, TILE), BF16),
            pltpu.VMEM((n, rows, TILE), BF16),
            pltpu.VMEM((n, rows, TILE), BF16),
            pltpu.VMEM((len(partners), EXTRA, TILE), BF16),
            pltpu.SemaphoreType.DMA((n, 4)),
            pltpu.SemaphoreType.DMA((n, 4)),
            pltpu.SemaphoreType.DMA((len(partners),)),
        ],
        input_output_aliases=aliases,
        compiler_params=PARAMS,
        cost_estimate=pl.CostEstimate(flops=elems, bytes_accessed=elems, transcendentals=0),
        name="expert_adamw",
    )(owner, pos, step, side, *arrays, *state, *carry, *after)
    return out[:3], out[3 : 3 + len(partners)], out[3 + len(partners) :]


def block_copies(served, payloads, srcs, sem):
    per_dest, _, rows, _ = served.shape
    return [
        pltpu.make_async_copy(q.at[pl.ds(j * rows, rows), :], served.at[j, src], sem.at[i, j])
        for i, (q, src) in enumerate(zip(payloads, srcs))
        for j in range(per_dest)
    ]


def place_kernel(partners, pos_ref, *refs):
    n = len(partners)
    served, token, sem = refs[-3:]
    token[...] = jnp.zeros_like(token)
    copies = block_copies(served, refs[:n], [pos_ref[0] ^ k for k in partners], sem)
    copy_all(copies)
    wait_all(copies)


def place_blocks(served, pos, payloads, partners, shape):
    n = len(partners)
    return pl.pallas_call(
        functools.partial(place_kernel, partners),
        in_specs=[SMEM] + [ANY] * (n + len(served)),
        out_specs=[ANY, VMEM],
        out_shape=[jax.ShapeDtypeStruct(shape, BF16), jax.ShapeDtypeStruct((8, TILE), F32)],
        scratch_shapes=[pltpu.SemaphoreType.DMA((n, shape[0]))],
        input_output_aliases={1 + n: 0} if served else {},
        compiler_params=LIGHT,
        cost_estimate=pl.CostEstimate(
            flops=0, bytes_accessed=4 * n * payloads[0].size, transcendentals=0
        ),
        name="place_served",
    )(pos, *payloads, *served)


def collect_kernel(order, tiles, to_place, pos_ref, *refs):
    n = len(order)
    q_refs = refs[:n]
    served, exp_ref, maxima_ref, extra, place_sem, sem = refs[n + 1 :]
    pos = pos_ref[0]
    per_dest = served.shape[0]
    blocks_copies = block_copies(
        served, [q_refs[i] for i in to_place], [pos ^ order[i] for i in to_place], place_sem
    )
    copies = [
        pltpu.make_async_copy(
            q.at[pl.ds(q.shape[0] - EXTRA, EXTRA), :], extra.at[i], sem.at[i]
        )
        for i, q in enumerate(q_refs)
    ]
    copy_all(copies)
    copy_all(blocks_copies)
    flat = jnp.zeros((8, exp_ref.shape[1]), F32)
    wide = lax.broadcasted_iota(jnp.int32, flat.shape, 1)
    deep = lax.broadcasted_iota(jnp.int32, flat.shape, 0)
    for i, k in enumerate(order):
        copies[i].wait()
        src = pos ^ k
        x = extra[i].astype(F32)[0:8, :]
        lat = sum(pltpu.roll(x, TILE - SPARE - 16 * p, 1) for p in range(3))
        maxima_ref[pl.ds(pl.multiple_of(8 * src, 8), 8), :] = lat
        for j in range(per_dest):
            first = 3 * j
            top = x[:, first : first + 1] + x[:, first + 1 : first + 2] + x[:, first + 2 : first + 3]
            hit = (wide == (j * n + src) * tiles + deep) & (deep < tiles)
            flat = jnp.where(hit, top, flat)
    exp_ref[...] = jnp.max(flat, axis=0, keepdims=True)
    wait_all(blocks_copies)


def collect(served, pos, received, order, to_place, tiles):
    n = len(order)
    per_dest = served.shape[0]
    return pl.pallas_call(
        functools.partial(collect_kernel, order, tiles, to_place),
        in_specs=[SMEM] + [ANY] * (n + 1),
        out_specs=[ANY, VMEM, VMEM],
        out_shape=[
            jax.ShapeDtypeStruct(served.shape, served.dtype),
            jax.ShapeDtypeStruct((1, per_dest * n * tiles), F32),
            jax.ShapeDtypeStruct((8 * n, TILE), F32),
        ],
        scratch_shapes=[
            pltpu.VMEM((n, EXTRA, TILE), BF16),
            pltpu.SemaphoreType.DMA((len(to_place), per_dest)),
            pltpu.SemaphoreType.DMA((n,)),
        ],
        input_output_aliases={1 + n: 0},
        compiler_params=LIGHT,
        cost_estimate=pl.CostEstimate(flops=1000000, bytes_accessed=1000000, transcendentals=0),
        name="place_last",
    )(pos, *received, served)


def finish_kernel(deltas, chunks, lanes, rows, pos_ref, *refs):
    n, peers = len(deltas), len(refs) - len(deltas) - 8
    rest, maxima = refs[:n], refs[n : n + peers]
    latent, scale_ref, buf, ext, tops_ref, in_sem, out_sem = refs[n + peers + 1 :]
    per_tile = TILE // CHUNK
    pos = pos_ref[0]
    loads = [pltpu.make_async_copy(rest[i], buf.at[i], in_sem.at[i]) for i in range(n)]
    copy_all(loads)
    copies = []
    for i, delta in enumerate(deltas):
        loads[i].wait()
        group = rest_stores(buf, i, pos ^ delta, rows, latent, out_sem)
        copy_all(group)
        copies += group
    count = maxima[0].shape[0] // 8
    for s in range(peers):
        peer = lax.rem(pos + peers - s, peers)
        for d in range(count):
            ext[pl.ds((d * peers + peer) * chunks, chunks), :] = maxima[s][8 * d : 8 * d + chunks, :]
    blocks, height = scale_ref.shape
    tops = ext[pl.ds(0, height, stride=per_tile), :]
    for r in range(1, per_tile):
        tops = jnp.maximum(tops, ext[pl.ds(r, height, stride=per_tile), :])
    tops_ref[...] = jnp.zeros_like(tops_ref)
    tops_ref[0:height, :] = tops
    scale_ref[...] = jnp.transpose(tops_ref[...])[0:blocks, 0:height]
    wait_all(copies)


def finish(latent, pos, rest, deltas, maxima, chunks, lat_blocks):
    n, peers = len(rest), len(maxima)
    span, cols = rest[0].shape
    lat_rows = maxima[0].shape[0] // 8 * peers * chunks
    latent, scales = pl.pallas_call(
        functools.partial(finish_kernel, deltas, chunks, lat_blocks, TILE + span),
        in_specs=[SMEM] + [ANY] * n + [VMEM] * peers + [ANY],
        out_specs=[ANY, VMEM],
        out_shape=[
            jax.ShapeDtypeStruct(latent.shape, latent.dtype),
            jax.ShapeDtypeStruct((lat_blocks, lat_rows * CHUNK // TILE), F32),
        ],
        scratch_shapes=[
            pltpu.VMEM((n, span, cols), BF16),
            pltpu.VMEM((lat_rows, TILE), F32),
            pltpu.VMEM((TILE, TILE), F32),
            pltpu.SemaphoreType.DMA((n,)),
            pltpu.SemaphoreType.DMA((n, span // CHUNK)),
        ],
        input_output_aliases={1 + n + peers: 0},
        compiler_params=pltpu.CompilerParams(vmem_limit_bytes=4 * 1024 * 1024),
        cost_estimate=pl.CostEstimate(flops=1000000, bytes_accessed=1000000, transcendentals=0),
        name="place_finish",
    )(pos, *rest, *maxima, latent)
    return latent, scales.T


def whole_tile(pos, rows):
    return pl.multiple_of(lax.rem(pos * (TILE - rows % TILE), TILE), CHUNK)


def full_kernel(pieces, rows, pos_ref, x_ref, own_ref, *refs):
    out_ref, buf, own, in_sem, out_sem, own_in, own_out = refs[1:]
    loads, stores = [], []
    for i in range(pieces):
        lead = i * (TILE - rows % TILE) % TILE
        at = pl.ds(i * TILE, TILE)
        loads.append(pltpu.make_async_copy(x_ref.at[at, :], buf.at[at, :], in_sem.at[i]))
        stores.append(
            pltpu.make_async_copy(
                buf.at[at, :], out_ref.at[pl.ds(i * rows + lead, TILE), :], out_sem.at[i]
            )
        )
    loads.append(pltpu.make_async_copy(own_ref, own.at[0], own_in.at[0]))
    copy_all(loads)
    for i in range(pieces):
        loads[i].wait()
        stores[i].start()
    loads[pieces].wait()
    rest = rest_stores(own, 0, pos_ref[0], rows, out_ref, own_out)
    copy_all(rest)
    wait_all(stores + rest)


def place_full(out, pos, x, own, rows):
    pieces = x.shape[0] // TILE
    return pl.pallas_call(
        functools.partial(full_kernel, pieces, rows),
        in_specs=[SMEM] + [ANY] * 3,
        out_specs=ANY,
        out_shape=jax.ShapeDtypeStruct((pieces * rows, x.shape[1]), BF16),
        scratch_shapes=[
            pltpu.VMEM(x.shape, BF16),
            pltpu.VMEM((1,) + own.shape, BF16),
            pltpu.SemaphoreType.DMA((pieces,)),
            pltpu.SemaphoreType.DMA((pieces,)),
            pltpu.SemaphoreType.DMA((1,)),
            pltpu.SemaphoreType.DMA((1, own.shape[0] // CHUNK)),
        ],
        input_output_aliases={3: 0},
        compiler_params=PARAMS,
        cost_estimate=pl.CostEstimate(flops=0, bytes_accessed=4 * x.size, transcendentals=0),
        name="place_whole",
    )(pos, x, own, out)


def rest_stores(buf, i, peer, rows, out_ref, sem):
    lead = whole_tile(peer, rows)
    copies = []
    for c in range((rows - TILE) // CHUNK):
        at = peer * rows + c * CHUNK + jnp.where(c * CHUNK < lead, 0, TILE)
        copies.append(
            pltpu.make_async_copy(
                buf.at[i, pl.ds(c * CHUNK, CHUNK), :],
                out_ref.at[pl.ds(pl.multiple_of(at, CHUNK), CHUNK), :],
                sem.at[i, c],
            )
        )
    return copies


def hop_kernel(delta, rows, n_after, pos_ref, x_ref, *refs):
    out_ref, again_ref, buf, in_sem, out_sem = refs[n_after:]
    load = pltpu.make_async_copy(x_ref, buf.at[0], in_sem.at[0])
    load.start()
    load.wait()
    copies = [pltpu.make_async_copy(buf.at[0], again_ref, in_sem.at[1])]
    copies += rest_stores(buf, 0, pos_ref[0] ^ delta, rows, out_ref, out_sem)
    copy_all(copies)
    wait_all(copies)


def place_and_pass(pos, x, delta, after, rows, peers):
    span, cols = x.shape
    return pl.pallas_call(
        functools.partial(hop_kernel, delta, rows, len(after)),
        in_specs=[SMEM, ANY] + [VMEM] * len(after),
        out_specs=[ANY, ANY],
        out_shape=[
            jax.ShapeDtypeStruct((peers * rows, cols), BF16),
            jax.ShapeDtypeStruct((span, cols), BF16),
        ],
        scratch_shapes=[
            pltpu.VMEM((1, span, cols), BF16),
            pltpu.SemaphoreType.DMA((2,)),
            pltpu.SemaphoreType.DMA((1, span // CHUNK)),
        ],
        compiler_params=pltpu.CompilerParams(vmem_limit_bytes=4 * 1024 * 1024),
        cost_estimate=pl.CostEstimate(flops=0, bytes_accessed=6 * span * cols, transcendentals=0),
        name="place_hop",
    )(pos, x, *after)


SLABS = 4


def latent_kernel(chunks, step_ref, pos_ref, *refs):
    hbm, outs, top_ref = refs[:4], refs[4:8], refs[8]
    w, m, v, g, q, in_sem, out_sem = refs[9:]
    bufs = (w, m, v, g)
    width = w.shape[1] // SLABS
    loads, stores = [], []
    for i in range(SLABS):
        cols = pl.ds(i * width, width)
        loads.append(
            [
                pltpu.make_async_copy(hbm[a].at[:, cols], bufs[a].at[:, cols], in_sem.at[i, a])
                for a in range(4)
            ]
        )
        stores.append(
            [
                pltpu.make_async_copy(src.at[:, cols], outs[a].at[:, cols], out_sem.at[i, a])
                for a, src in enumerate((w, m, v, q))
            ]
        )
        copy_all(loads[i])
    rate, corr = corrections(step_ref)
    lane = lax.broadcasted_iota(jnp.int32, (8, TILE), 1)
    lead = whole_tile(pos_ref[0], w.shape[0])
    sub = lax.broadcasted_iota(jnp.int32, (8, 1), 0) * CHUNK
    inside = (sub >= lead) & (sub < lead + TILE)
    tops = jnp.zeros((8, TILE), F32)
    for i in range(SLABS):
        wait_all(loads[i])
        blocks = range(i * width // TILE, (i + 1) * width // TILE)
        slab_tops = []
        for b in blocks:
            cols = pl.ds(b * TILE, TILE)
            w1, m1, v1 = adamw_tile(w[:, cols], m[:, cols], v[:, cols], g[:, cols], rate, corr)
            w[:, cols] = w1
            m[:, cols] = m1
            v[:, cols] = v1
            slab_tops.append(stack_max([sub_max(w1[c * CHUNK : (c + 1) * CHUNK]) for c in range(chunks)]))
        for b, top in zip(blocks, slab_tops):
            cols = pl.ds(b * TILE, TILE)
            tops = jnp.where(lane == b, top, tops)
            whole = jnp.max(jnp.where(inside, top, 0.0), axis=0, keepdims=True)
            q[:, cols] = (w[pl.ds(lead, TILE), cols] * (1.0 / (whole + SCALE_EPS))).astype(BF16)
        copy_all(stores[i])
    top_ref[...] = tops
    for group in stores:
        wait_all(group)


def latent_update(arrays, step, pos):
    rows, cols = arrays[0].shape
    elems = rows * cols
    return pl.pallas_call(
        functools.partial(latent_kernel, rows // CHUNK),
        in_specs=[SMEM] * 2 + [ANY] * 4,
        out_specs=[ANY] * 4 + [VMEM],
        out_shape=[
            jax.ShapeDtypeStruct((rows, cols), F32),
            jax.ShapeDtypeStruct((rows, cols), BF16),
            jax.ShapeDtypeStruct((rows, cols), BF16),
            jax.ShapeDtypeStruct((TILE, cols), BF16),
            jax.ShapeDtypeStruct((8, TILE), F32),
        ],
        scratch_shapes=[
            pltpu.VMEM((rows, cols), F32),
            pltpu.VMEM((rows, cols), BF16),
            pltpu.VMEM((rows, cols), BF16),
            pltpu.VMEM((rows, cols), BF16),
            pltpu.VMEM((TILE, cols), BF16),
            pltpu.SemaphoreType.DMA((SLABS, 4)),
            pltpu.SemaphoreType.DMA((SLABS, 4)),
        ],
        compiler_params=PARAMS,
        cost_estimate=pl.CostEstimate(
            flops=30 * elems, bytes_accessed=18 * elems, transcendentals=2 * elems
        ),
        name="latent_adamw",
    )(step, pos, *arrays)


def latent_rest_kernel(
    chunks, pos_ref, w1_ref, own_ref, prev_ref, next_ref, after_ref, q_ref, w, q, ext, in_sem, out_sem
):
    per_tile = TILE // CHUNK
    rows, cols = w1_ref.shape
    width = cols // SLABS
    lead = whole_tile(pos_ref[0], rows)
    loads, stores = [], []
    for i in range(SLABS):
        at = pl.ds(i * width, width)
        group = []
        for c in range(chunks - per_tile):
            first = pl.multiple_of(c * CHUNK + jnp.where(c * CHUNK < lead, 0, TILE), CHUNK)
            group.append(
                pltpu.make_async_copy(
                    w1_ref.at[pl.ds(first, CHUNK), at],
                    w.at[pl.ds(c * CHUNK, CHUNK), at],
                    in_sem.at[i, c],
                )
            )
        copy_all(group)
        loads.append(group)
        stores.append(pltpu.make_async_copy(q.at[:, at], q_ref.at[:, at], out_sem.at[i]))
    ext[0:chunks, :] = prev_ref[0:chunks, :]
    ext[chunks : 2 * chunks, :] = own_ref[0:chunks, :]
    ext[2 * chunks : 3 * chunks, :] = next_ref[0:chunks, :]
    first = chunks + lead // CHUNK
    above = jnp.max(ext[pl.ds(first - per_tile, per_tile), :], axis=0, keepdims=True)
    below = jnp.max(ext[pl.ds(first + per_tile, per_tile), :], axis=0, keepdims=True)
    both = jnp.concatenate([above] * 4 + [below] * 4, axis=0)
    lane = lax.broadcasted_iota(jnp.int32, (8, TILE), 1)
    tops = [
        jnp.max(jnp.where(lane == b, both, 0.0), axis=1, keepdims=True) for b in range(cols // TILE)
    ]
    invs = [1.0 / (top + SCALE_EPS) for top in tops]
    for i in range(SLABS):
        wait_all(loads[i])
        for b in range(i * width // TILE, (i + 1) * width // TILE):
            at = pl.ds(b * TILE, TILE)
            for c in range(chunks - per_tile):
                span = pl.ds(c * CHUNK, CHUNK)
                inv = jnp.where(c * CHUNK < lead, invs[b][0:1, :], invs[b][4:5, :])
                q[span, at] = (w[span, at] * inv).astype(BF16)
        stores[i].start()
    wait_all(stores)


def latent_rest(w1, own, above, below, pos, after):
    rows, cols = w1.shape
    chunks = rows // CHUNK
    return pl.pallas_call(
        functools.partial(latent_rest_kernel, chunks),
        in_specs=[SMEM, ANY] + [VMEM] * 3 + [ANY],
        out_specs=ANY,
        out_shape=jax.ShapeDtypeStruct((rows - TILE, cols), BF16),
        scratch_shapes=[
            pltpu.VMEM((rows - TILE, cols), F32),
            pltpu.VMEM((rows - TILE, cols), BF16),
            pltpu.VMEM((24, TILE), F32),
            pltpu.SemaphoreType.DMA((SLABS, chunks)),
            pltpu.SemaphoreType.DMA((SLABS,)),
        ],
        compiler_params=PARAMS,
        cost_estimate=pl.CostEstimate(
            flops=rows * cols, bytes_accessed=3 * rows * cols, transcendentals=0
        ),
        name="latent_rest",
    )(pos, w1, own, above, below, after)


def fast_fits(expert_shape, latent_shape, dp_count, exp_axis):
    exp_count, rows, cols = expert_shape
    latent_rows, latent_cols = latent_shape
    return (
        exp_count == 1
        and rows % TILE == 0
        and rows <= 8 * TILE
        and cols % (TILE * dp_count) == 0
        and cols // TILE // dp_count <= 16
        and dp_count == 8
        and dp_count * latent_rows * exp_axis <= TILE * TILE
        and latent_rows % CHUNK == 0
        and 2 * TILE - CHUNK <= latent_rows < 2 * TILE
        and latent_rows * exp_axis % TILE == 0
        and latent_rows * exp_axis * dp_count <= TILE * TILE
        and exp_axis == 4
        and latent_cols % (SLABS * TILE) == 0
        and latent_cols <= 16 * TILE
    )


def partner_groups(dp_count):
    hops = lambda k: bin(k >> 1).count("1")
    stage = lambda k: 3 if k < 2 else (1 if hops(k) > 1 else (2 if k & 1 else 0))
    order = sorted(range(dp_count), key=lambda k: (stage(k), -k))
    return [[k for k in order if stage(k) in n] for n in ((0,), (1,), (2, 3))]


def fast_body(
    expert_master,
    expert_first,
    expert_second,
    expert_grad,
    latent_master,
    latent_first,
    latent_second,
    latent_grad,
    step_count,
    column_owner,
):
    dp_count = lax.axis_size("dp")
    dp_pos = lax.axis_index("dp").astype(jnp.int32)
    exp_axis = lax.axis_size("expert")
    exp_pos = lax.axis_index("expert").astype(jnp.int32)
    _, rows, cols = expert_master.shape
    block_count = cols // TILE
    per_dest = block_count // dp_count
    tiles = rows // TILE

    expert_at, dp_at = exp_pos.reshape(1), dp_pos.reshape(1)
    latent_new, latent_one, latent_two, whole, chunk_top = latent_update(
        (latent_master, latent_first, latent_second, latent_grad), step_count, expert_at
    )
    latent_rows = latent_new.shape[0]
    whole = lax.all_gather(whole, "expert", axis=0, tiled=True)
    above = lax.ppermute(chunk_top, "expert", [(i, i + 1) for i in range(exp_axis - 1)])
    below = lax.ppermute(chunk_top, "expert", [(i + 1, i) for i in range(exp_axis - 1)])

    arrays = tuple(
        a.reshape(rows, cols) for a in (expert_master, expert_first, expert_second, expert_grad)
    )
    def swap(x, axis, k):
        return lax.ppermute(x, axis, [(i, i ^ k) for i in range(lax.axis_size(axis))])

    groups = partner_groups(dp_count)
    order = [k for partners in groups for k in partners]
    state, received, carry, tops = (), [], (), chunk_top
    for n, partners in enumerate(groups):
        state, sent, carried = expert_group(
            arrays, state, column_owner, dp_at, step_count, tops, carry, (), partners, per_dest
        )
        received += [swap(q, "dp", k) if k else q for k, q in zip(partners, sent)]
        if n == 1:
            rest = latent_rest(latent_new, chunk_top, above, below, expert_at, sent[0])
            far, near = swap(rest, "expert", 2), swap(rest, "expert", 1)
            served, _ = place_blocks(
                (), dp_at, received[: len(groups[0])], groups[0], (per_dest, dp_count, rows, TILE)
            )
            carry = (served,)
    served, tops = carried
    first, count = len(groups[0]), len(groups[0]) + len(groups[1])
    served, token = place_blocks(
        (served,), dp_at, received[first:count], groups[1], served.shape
    )
    latent_served, far_again = place_and_pass(
        expert_at, far, 2, (tops, token), latent_rows, exp_axis
    )
    last = swap(far_again, "expert", 1)
    latent_served = place_full(latent_served, expert_at, whole, rest, latent_rows)
    served, expert_scales, maxima = collect(
        served, dp_at, received, order, range(count, dp_count - 1), tiles
    )
    maxima = [maxima] + [
        lax.ppermute(maxima, "expert", [(i, (i + s) % exp_axis) for i in range(exp_axis)])
        for s in range(1, exp_axis)
    ]
    latent_served, latent_scales = finish(
        latent_served,
        expert_at,
        [near, last],
        [1, 3],
        maxima,
        latent_rows // CHUNK,
        latent_new.shape[1] // TILE,
    )
    expert_served = served.reshape(1, block_count * rows, TILE)

    return (
        state[0][None],
        state[1][None],
        state[2][None],
        expert_served,
        expert_scales,
        latent_new,
        latent_one,
        latent_two,
        latent_served,
        latent_scales,
    )


def body(*args):
    if fast_fits(args[0].shape, args[4].shape, lax.axis_size("dp"), lax.axis_size("expert")):
        return fast_body(*args)
    return general_body(*args)


def solution(mesh):
    placed = (
        P("expert", "dp", None),
        P("expert", "dp", None),
        P("expert", "dp", None),
        P("expert", "dp", None),
        P(("dp", "expert"), None),
        P(("dp", "expert"), None),
        P(("dp", "expert"), None),
        P(("dp", "expert"), None),
        P(),
        P(),
    )
    return jax.shard_map(
        body,
        mesh=mesh,
        in_specs=placed,
        out_specs=(
            P("expert", "dp", None),
            P("expert", "dp", None),
            P("expert", "dp", None),
            P("expert", "dp", None),
            P("expert", "dp"),
            P(("dp", "expert"), None),
            P(("dp", "expert"), None),
            P(("dp", "expert"), None),
            P("dp", None),
            P(),
        ),
        check_vma=False,
    )
```

```python
import functools
import math

import jax
import jax.numpy as jnp
from jax import lax
from jax.experimental import pallas as pl
from jax.experimental.pallas import tpu as pltpu
from jax.sharding import PartitionSpec as P

D = 7168
TILE = 128


BETA_ONE = 0.9
BETA_TWO = 0.95
LEARN_RATE = 0.2
DECAY_RATE = 0.1
ADAM_EPS = 1e-08
SCALE_EPS = 1e-06


def adamw_step(master, moment_one, moment_two, gradient, step_count):
    grad_value = gradient.astype(jnp.float32)
    first_new = BETA_ONE * moment_one.astype(jnp.float32) + (1.0 - BETA_ONE) * grad_value
    second_new = (
        BETA_TWO * moment_two.astype(jnp.float32) + (1.0 - BETA_TWO) * grad_value * grad_value
    )
    step_value = step_count[0].astype(jnp.float32)
    corr_one = 1.0 - jnp.power(jnp.float32(BETA_ONE), step_value)
    corr_two = 1.0 - jnp.power(jnp.float32(BETA_TWO), step_value)
    update = first_new / corr_one / (jnp.sqrt(second_new / corr_two) + ADAM_EPS)
    master_new = master - LEARN_RATE * (update + DECAY_RATE * master)
    return (master_new, first_new.astype(jnp.bfloat16), second_new.astype(jnp.bfloat16))


def row_maxima(weights):
    leading = weights.shape[:-1]
    tile_count = weights.shape[-1] // TILE
    return jnp.max(jnp.abs(weights).reshape(leading + (tile_count, TILE)), axis=-1)


def local_tiles(row_max, lead_rows):
    exp_count, row_count, tile_count = row_max.shape
    tile_span = row_count // TILE + 2
    buffer = jnp.zeros((exp_count, tile_span * TILE, tile_count), jnp.float32)
    buffer = lax.dynamic_update_slice(buffer, row_max, (jnp.int32(0), lead_rows, jnp.int32(0)))
    return jnp.max(buffer.reshape(exp_count, tile_span, TILE, tile_count), axis=2)


def place_tiles(tile_max, first_tile):
    exp_count, tile_span, tile_count = tile_max.shape
    global_map = jnp.zeros((exp_count, D // TILE + tile_span, tile_count), jnp.float32)
    return lax.dynamic_update_slice(global_map, tile_max, (jnp.int32(0), first_tile, jnp.int32(0)))


def quantized_rows(weights, tile_max, lead_rows):
    exp_count, row_count, col_count = weights.shape
    repeated = jnp.repeat(tile_max, TILE, axis=1)
    row_scale = lax.dynamic_slice_in_dim(repeated, lead_rows, row_count, 1)
    blocks = weights.reshape(exp_count, row_count, col_count // TILE, TILE)
    return (blocks / (row_scale[..., None] + SCALE_EPS)).reshape(weights.shape).astype(jnp.bfloat16)


def general_body(
    expert_master,
    expert_first,
    expert_second,
    expert_grad,
    latent_master,
    latent_first,
    latent_second,
    latent_grad,
    step_count,
    column_owner,
):
    master_new, first_new, second_new = adamw_step(
        expert_master, expert_first, expert_second, expert_grad, step_count
    )
    latent_new, latent_one, latent_two = adamw_step(
        latent_master, latent_first, latent_second, latent_grad, step_count
    )
    dp_count = lax.axis_size("dp")
    dp_pos = lax.axis_index("dp")
    exp_count, row_count, col_count = master_new.shape
    block_count = col_count // TILE
    slot_count = max(1, block_count // dp_count)
    total_tiles = D // TILE
    recv_rows = block_count * row_count
    recv_tiles = recv_rows // TILE
    positions = jnp.arange(block_count, dtype=jnp.int32)
    inverse = jnp.sum(
        positions[:, None] * (column_owner[:, None] == positions[None, :]).astype(jnp.int32), axis=0
    )
    receiver_ids = jnp.arange(dp_count, dtype=jnp.int32)[:, None]
    slot_ids = jnp.arange(slot_count, dtype=jnp.int32)[None, :]
    segment = (
        receiver_ids * block_count
        + jnp.mod(dp_pos - receiver_ids * block_count, dp_count)
        + slot_ids * dp_count
    )
    usable_slot = (segment < (receiver_ids + 1) * block_count).reshape(-1)
    send_block = jnp.take(inverse, jnp.minimum(segment // dp_count, block_count - 1)).reshape(-1)
    local_segments = jnp.arange(block_count, dtype=jnp.int32)
    source_dev = jnp.mod(dp_pos * block_count + local_segments, dp_count)
    pick_index = source_dev * slot_count + local_segments // dp_count
    blocks = master_new.reshape(exp_count, row_count, block_count, TILE)
    picked = jnp.take(blocks, send_block, axis=2)
    received = lax.all_to_all(
        jnp.where(usable_slot[None, None, :, None], picked, jnp.zeros((), picked.dtype)),
        "dp",
        split_axis=2,
        concat_axis=2,
        tiled=True,
    )
    ordered = jnp.take(received, pick_index, axis=2)
    tall = (
        jnp.transpose(ordered, (0, 2, 1, 3))
        .reshape(exp_count, recv_rows, TILE)
        .reshape(exp_count, recv_tiles, TILE, TILE)
    )
    expert_scales = jnp.max(jnp.abs(tall), axis=(2, 3))
    expert_served = (
        (tall / (expert_scales[:, :, None, None] + SCALE_EPS))
        .reshape(exp_count, recv_rows, TILE)
        .astype(jnp.bfloat16)
    )
    latent_block = lax.all_gather(latent_new, "expert", axis=0, tiled=True)
    block_rows = latent_block.shape[0]
    block_offset = dp_pos * block_rows
    block_lead = block_offset % TILE
    block_tiles = local_tiles(row_maxima(latent_block)[None], block_lead)
    block_map = lax.pmax(place_tiles(block_tiles, block_offset // TILE), "dp")
    latent_scales = block_map[0, :total_tiles]
    block_tiles = lax.dynamic_slice_in_dim(block_map, block_offset // TILE, block_tiles.shape[1], 1)
    latent_served = quantized_rows(latent_block[None], block_tiles, block_lead)[0]
    return (
        master_new,
        first_new,
        second_new,
        expert_served,
        expert_scales,
        latent_new,
        latent_one,
        latent_two,
        latent_served,
        latent_scales,
    )


CHUNK = 32
EXTRA = 16
SPARE = 64
F32 = jnp.float32
BF16 = jnp.bfloat16
VMEM_LIMIT = 56 * 1024 * 1024
ANY = pl.BlockSpec(memory_space=pl.ANY)
SMEM = pl.BlockSpec(memory_space=pltpu.SMEM)
VMEM = pl.BlockSpec(memory_space=pltpu.VMEM)
PARAMS = pltpu.CompilerParams(vmem_limit_bytes=VMEM_LIMIT)
LIGHT = pltpu.CompilerParams(vmem_limit_bytes=1024 * 1024)


def corrections(step_ref):
    one, two = lax.fori_loop(
        0, step_ref[0], lambda _, p: (p[0] * BETA_ONE, p[1] * BETA_TWO), (F32(1.0), F32(1.0))
    )
    rate = LEARN_RATE / (1.0 - jnp.full((1, TILE), one, F32))
    corr = 1.0 / (1.0 - jnp.full((1, TILE), two, F32))
    return rate, corr


def adamw_tile(w, m, v, g, rate, corr):
    g = g.astype(F32)
    m1 = BETA_ONE * m.astype(F32) + (1.0 - BETA_ONE) * g
    v1 = BETA_TWO * v.astype(F32) + (1.0 - BETA_TWO) * g * g
    x = v1 * corr
    inv = pl.reciprocal(x * lax.rsqrt(x) + ADAM_EPS, approx=True)
    w1 = (1.0 - LEARN_RATE * DECAY_RATE) * w - rate * m1 * inv
    return w1, m1.astype(BF16), v1.astype(BF16)


def sub_max(w1):
    return jnp.max(jnp.abs(w1).reshape(w1.shape[0] // 8, 8, TILE), axis=0)


def stack_max(parts):
    parts = parts + [parts[-1]] * (8 - len(parts))
    rows = [jnp.max(p, axis=0, keepdims=True) for p in parts]
    return jnp.max(jnp.concatenate(rows, axis=0), axis=1, keepdims=True)


def three_parts(x):
    high = x.astype(BF16).astype(F32)
    rest = x - high
    middle = rest.astype(BF16).astype(F32)
    return high, middle, rest - middle


def copy_all(copies):
    for c in copies:
        c.start()


def wait_all(copies):
    for c in copies:
        c.wait()


def expert_kernel(partners, per_dest, n_alias, n_skip, has_side, owner_ref, pos_ref, step_ref, side_ref, *refs):
    hbm, refs = refs[:4], refs[4 + n_alias + n_skip :]
    n_dest = len(partners)
    outs, q_refs, served_ref = refs[:3], refs[3 : 3 + n_dest], refs[3 + n_dest]
    w, m, v, g, extra, in_sem, out_sem, extra_sem = refs[-8:]
    bufs = (w, m, v, g)
    blocks = owner_ref.shape[0]
    rows = w.shape[1]
    tiles = rows // TILE
    pos = pos_ref[0]
    if has_side:
        refs[-9][...] = side_ref[...]

    loads, stores = [], []
    for d, k in enumerate(partners):
        for j in range(per_dest):
            i = d * per_dest + j
            slot = (pos ^ k) * per_dest + j
            block = jnp.int32(0)
            for b in range(blocks):
                block = jnp.where(owner_ref[b] == slot, b, block)
            cols = pl.ds(pl.multiple_of(block * TILE, TILE), TILE)
            loads.append(
                [
                    pltpu.make_async_copy(hbm[a].at[:, cols], bufs[a].at[i], in_sem.at[i, a])
                    for a in range(4)
                ]
            )
            target = q_refs[d].at[pl.ds(j * rows, rows), :] if k else served_ref.at[j, pos]
            stores.append(
                [
                    pltpu.make_async_copy(bufs[a].at[i], outs[a].at[:, cols], out_sem.at[i, a])
                    for a in range(3)
                ]
                + [pltpu.make_async_copy(g.at[i], target, out_sem.at[i, 3])]
            )
            copy_all(loads[-1])
    rate, corr = corrections(step_ref)
    lane = lax.broadcasted_iota(jnp.int32, (8, TILE), 1)
    parts_of_maxima = jnp.zeros((8, TILE), F32)
    for p, value in enumerate(three_parts(side_ref[...])):
        at = SPARE + 16 * p
        parts_of_maxima = jnp.where(
            (lane >= at) & (lane < at + 16), pltpu.roll(value, at, 1), parts_of_maxima
        )
    extras = []
    for d, k in enumerate(partners):
        side = parts_of_maxima
        for j in range(per_dest):
            i = d * per_dest + j
            wait_all(loads[i])
            parts = []
            for t in range(tiles):
                at = pl.ds(t * TILE, TILE)
                w1, m1, v1 = adamw_tile(w[i, at, :], m[i, at, :], v[i, at, :], g[i, at, :], rate, corr)
                w[i, at, :] = w1
                m[i, at, :] = m1
                v[i, at, :] = v1
                parts.append(sub_max(w1))
            copy_all(stores[i][:3])
            top = stack_max(parts)
            inv = 1.0 / (top + SCALE_EPS)
            for t in range(tiles):
                at = pl.ds(t * TILE, TILE)
                g[i, at, :] = (w[i, at, :] * inv[t : t + 1, :]).astype(BF16)
            stores[i][3].start()
            for p, value in enumerate(three_parts(top)):
                side = jnp.where(lane == 3 * j + p, value, side)
        extra[d] = jnp.concatenate([side, jnp.zeros_like(side)], axis=0).astype(BF16)
        first = per_dest * rows if k else 0
        extras.append(
            pltpu.make_async_copy(
                extra.at[d], q_refs[d].at[pl.ds(first, EXTRA), :], extra_sem.at[d]
            )
        )
        extras[-1].start()
    for group in stores:
        wait_all(group)
    wait_all(extras)


def expert_group(arrays, state, owner, pos, step, side, carry, after, partners, per_dest):
    rows, cols = arrays[0].shape
    n_alias = len(state)
    n = len(partners) * per_dest
    elems = rows * TILE * n
    sides = [jax.ShapeDtypeStruct(side.shape, side.dtype)] * (len(carry) > 0)
    aliases = {8 + i: i for i in range(n_alias)}
    aliases.update({8 + n_alias + i: 3 + len(partners) + i for i in range(len(carry))})
    out = pl.pallas_call(
        functools.partial(
            expert_kernel, partners, per_dest, n_alias, len(carry) + len(after), len(sides)
        ),
        in_specs=[SMEM] * 3 + [VMEM] + [ANY] * (4 + n_alias + len(carry) + len(after)),
        out_specs=[ANY] * (3 + len(partners) + len(carry)) + [VMEM] * len(sides),
        out_shape=[
            jax.ShapeDtypeStruct((rows, cols), F32),
            jax.ShapeDtypeStruct((rows, cols), BF16),
            jax.ShapeDtypeStruct((rows, cols), BF16),
        ]
        + [
            jax.ShapeDtypeStruct((per_dest * rows * (k > 0) + EXTRA, TILE), BF16)
            for k in partners
        ]
        + [jax.ShapeDtypeStruct(x.shape, x.dtype) for x in carry]
        + sides,
        scratch_shapes=[
            pltpu.VMEM((n, rows, TILE), F32),
            pltpu.VMEM((n, rows, TILE), BF16),
            pltpu.VMEM((n, rows, TILE), BF16),
            pltpu.VMEM((n, rows, TILE), BF16),
            pltpu.VMEM((len(partners), EXTRA, TILE), BF16),
            pltpu.SemaphoreType.DMA((n, 4)),
            pltpu.SemaphoreType.DMA((n, 4)),
            pltpu.SemaphoreType.DMA((len(partners),)),
        ],
        input_output_aliases=aliases,
        compiler_params=PARAMS,
        cost_estimate=pl.CostEstimate(flops=elems, bytes_accessed=elems, transcendentals=0),
        name="expert_adamw",
    )(owner, pos, step, side, *arrays, *state, *carry, *after)
    return out[:3], out[3 : 3 + len(partners)], out[3 + len(partners) :]


def block_copies(served, payloads, srcs, sem):
    per_dest, _, rows, _ = served.shape
    return [
        pltpu.make_async_copy(q.at[pl.ds(j * rows, rows), :], served.at[j, src], sem.at[i, j])
        for i, (q, src) in enumerate(zip(payloads, srcs))
        for j in range(per_dest)
    ]


def place_kernel(partners, pos_ref, *refs):
    n = len(partners)
    served, token, sem = refs[-3:]
    token[...] = jnp.zeros_like(token)
    copies = block_copies(served, refs[:n], [pos_ref[0] ^ k for k in partners], sem)
    copy_all(copies)
    wait_all(copies)


def place_blocks(served, pos, payloads, partners, shape):
    n = len(partners)
    return pl.pallas_call(
        functools.partial(place_kernel, partners),
        in_specs=[SMEM] + [ANY] * (n + len(served)),
        out_specs=[ANY, VMEM],
        out_shape=[jax.ShapeDtypeStruct(shape, BF16), jax.ShapeDtypeStruct((8, TILE), F32)],
        scratch_shapes=[pltpu.SemaphoreType.DMA((n, shape[0]))],
        input_output_aliases={1 + n: 0} if served else {},
        compiler_params=LIGHT,
        cost_estimate=pl.CostEstimate(
            flops=0, bytes_accessed=4 * n * payloads[0].size, transcendentals=0
        ),
        name="place_served",
    )(pos, *payloads, *served)


def collect_kernel(order, tiles, to_place, pos_ref, *refs):
    n = len(order)
    q_refs = refs[:n]
    served, exp_ref, maxima_ref, extra, place_sem, sem = refs[n + 1 :]
    pos = pos_ref[0]
    per_dest = served.shape[0]
    blocks_copies = block_copies(
        served, [q_refs[i] for i in to_place], [pos ^ order[i] for i in to_place], place_sem
    )
    copies = [
        pltpu.make_async_copy(
            q.at[pl.ds(q.shape[0] - EXTRA, EXTRA), :], extra.at[i], sem.at[i]
        )
        for i, q in enumerate(q_refs)
    ]
    copy_all(copies)
    copy_all(blocks_copies)
    flat = jnp.zeros((8, exp_ref.shape[1]), F32)
    wide = lax.broadcasted_iota(jnp.int32, flat.shape, 1)
    deep = lax.broadcasted_iota(jnp.int32, flat.shape, 0)
    for i, k in enumerate(order):
        copies[i].wait()
        src = pos ^ k
        x = extra[i].astype(F32)[0:8, :]
        lat = sum(pltpu.roll(x, TILE - SPARE - 16 * p, 1) for p in range(3))
        maxima_ref[pl.ds(pl.multiple_of(8 * src, 8), 8), :] = lat
        for j in range(per_dest):
            first = 3 * j
            top = x[:, first : first + 1] + x[:, first + 1 : first + 2] + x[:, first + 2 : first + 3]
            hit = (wide == (j * n + src) * tiles + deep) & (deep < tiles)
            flat = jnp.where(hit, top, flat)
    exp_ref[...] = jnp.max(flat, axis=0, keepdims=True)
    wait_all(blocks_copies)


def collect(served, pos, received, order, to_place, tiles):
    n = len(order)
    per_dest = served.shape[0]
    return pl.pallas_call(
        functools.partial(collect_kernel, order, tiles, to_place),
        in_specs=[SMEM] + [ANY] * (n + 1),
        out_specs=[ANY, VMEM, VMEM],
        out_shape=[
            jax.ShapeDtypeStruct(served.shape, served.dtype),
            jax.ShapeDtypeStruct((1, per_dest * n * tiles), F32),
            jax.ShapeDtypeStruct((8 * n, TILE), F32),
        ],
        scratch_shapes=[
            pltpu.VMEM((n, EXTRA, TILE), BF16),
            pltpu.SemaphoreType.DMA((len(to_place), per_dest)),
            pltpu.SemaphoreType.DMA((n,)),
        ],
        input_output_aliases={1 + n: 0},
        compiler_params=LIGHT,
        cost_estimate=pl.CostEstimate(flops=1000000, bytes_accessed=1000000, transcendentals=0),
        name="place_last",
    )(pos, *received, served)


def finish_kernel(deltas, chunks, lanes, rows, pos_ref, *refs):
    n, peers = len(deltas), len(refs) - len(deltas) - 8
    rest, maxima = refs[:n], refs[n : n + peers]
    latent, scale_ref, buf, ext, tops_ref, in_sem, out_sem = refs[n + peers + 1 :]
    per_tile = TILE // CHUNK
    pos = pos_ref[0]
    loads = [pltpu.make_async_copy(rest[i], buf.at[i], in_sem.at[i]) for i in range(n)]
    copy_all(loads)
    copies = []
    for i, delta in enumerate(deltas):
        loads[i].wait()
        group = rest_stores(buf, i, pos ^ delta, rows, latent, out_sem)
        copy_all(group)
        copies += group
    count = maxima[0].shape[0] // 8
    for s in range(peers):
        peer = lax.rem(pos + peers - s, peers)
        for d in range(count):
            ext[pl.ds((d * peers + peer) * chunks, chunks), :] = maxima[s][8 * d : 8 * d + chunks, :]
    blocks, height = scale_ref.shape
    tops = ext[pl.ds(0, height, stride=per_tile), :]
    for r in range(1, per_tile):
        tops = jnp.maximum(tops, ext[pl.ds(r, height, stride=per_tile), :])
    tops_ref[...] = jnp.zeros_like(tops_ref)
    tops_ref[0:height, :] = tops
    scale_ref[...] = jnp.transpose(tops_ref[...])[0:blocks, 0:height]
    wait_all(copies)


def finish(latent, pos, rest, deltas, maxima, chunks, lat_blocks):
    n, peers = len(rest), len(maxima)
    span, cols = rest[0].shape
    lat_rows = maxima[0].shape[0] // 8 * peers * chunks
    latent, scales = pl.pallas_call(
        functools.partial(finish_kernel, deltas, chunks, lat_blocks, TILE + span),
        in_specs=[SMEM] + [ANY] * n + [VMEM] * peers + [ANY],
        out_specs=[ANY, VMEM],
        out_shape=[
            jax.ShapeDtypeStruct(latent.shape, latent.dtype),
            jax.ShapeDtypeStruct((lat_blocks, lat_rows * CHUNK // TILE), F32),
        ],
        scratch_shapes=[
            pltpu.VMEM((n, span, cols), BF16),
            pltpu.VMEM((lat_rows, TILE), F32),
            pltpu.VMEM((TILE, TILE), F32),
            pltpu.SemaphoreType.DMA((n,)),
            pltpu.SemaphoreType.DMA((n, span // CHUNK)),
        ],
        input_output_aliases={1 + n + peers: 0},
        compiler_params=pltpu.CompilerParams(vmem_limit_bytes=4 * 1024 * 1024),
        cost_estimate=pl.CostEstimate(flops=1000000, bytes_accessed=1000000, transcendentals=0),
        name="place_finish",
    )(pos, *rest, *maxima, latent)
    return latent, scales.T


def whole_tile(pos, rows):
    return pl.multiple_of(lax.rem(pos * (TILE - rows % TILE), TILE), CHUNK)


def full_kernel(pieces, rows, pos_ref, x_ref, own_ref, *refs):
    out_ref, buf, own, in_sem, out_sem, own_in, own_out = refs[1:]
    loads, stores = [], []
    for i in range(pieces):
        lead = i * (TILE - rows % TILE) % TILE
        at = pl.ds(i * TILE, TILE)
        loads.append(pltpu.make_async_copy(x_ref.at[at, :], buf.at[at, :], in_sem.at[i]))
        stores.append(
            pltpu.make_async_copy(
                buf.at[at, :], out_ref.at[pl.ds(i * rows + lead, TILE), :], out_sem.at[i]
            )
        )
    loads.append(pltpu.make_async_copy(own_ref, own.at[0], own_in.at[0]))
    copy_all(loads)
    for i in range(pieces):
        loads[i].wait()
        stores[i].start()
    loads[pieces].wait()
    rest = rest_stores(own, 0, pos_ref[0], rows, out_ref, own_out)
    copy_all(rest)
    wait_all(stores + rest)


def place_full(out, pos, x, own, rows):
    pieces = x.shape[0] // TILE
    return pl.pallas_call(
        functools.partial(full_kernel, pieces, rows),
        in_specs=[SMEM] + [ANY] * 3,
        out_specs=ANY,
        out_shape=jax.ShapeDtypeStruct((pieces * rows, x.shape[1]), BF16),
        scratch_shapes=[
            pltpu.VMEM(x.shape, BF16),
            pltpu.VMEM((1,) + own.shape, BF16),
            pltpu.SemaphoreType.DMA((pieces,)),
            pltpu.SemaphoreType.DMA((pieces,)),
            pltpu.SemaphoreType.DMA((1,)),
            pltpu.SemaphoreType.DMA((1, own.shape[0] // CHUNK)),
        ],
        input_output_aliases={3: 0},
        compiler_params=PARAMS,
        cost_estimate=pl.CostEstimate(flops=0, bytes_accessed=4 * x.size, transcendentals=0),
        name="place_whole",
    )(pos, x, own, out)


def rest_stores(buf, i, peer, rows, out_ref, sem):
    lead = whole_tile(peer, rows)
    copies = []
    for c in range((rows - TILE) // CHUNK):
        at = peer * rows + c * CHUNK + jnp.where(c * CHUNK < lead, 0, TILE)
        copies.append(
            pltpu.make_async_copy(
                buf.at[i, pl.ds(c * CHUNK, CHUNK), :],
                out_ref.at[pl.ds(pl.multiple_of(at, CHUNK), CHUNK), :],
                sem.at[i, c],
            )
        )
    return copies


def hop_kernel(deltas, rows, pos_ref, *refs):
    n = len(deltas)
    out_ref, again_ref, buf, in_sem, out_sem = refs[-5:]
    loads = [pltpu.make_async_copy(refs[i], buf.at[i], in_sem.at[i]) for i in range(n)]
    copy_all(loads)
    copies = [pltpu.make_async_copy(buf.at[n - 1], again_ref, in_sem.at[n])]
    for i in reversed(range(n)):
        loads[i].wait()
        group = rest_stores(buf, i, pos_ref[0] ^ deltas[i], rows, out_ref, out_sem)
        copy_all(copies + group if i == n - 1 else group)
        copies += group
    wait_all(copies)


def place_and_pass(pos, xs, deltas, after, rows, peers):
    span, cols = xs[0].shape
    n = len(xs)
    return pl.pallas_call(
        functools.partial(hop_kernel, deltas, rows),
        in_specs=[SMEM] + [ANY] * n + [VMEM] * len(after),
        out_specs=[ANY, ANY],
        out_shape=[
            jax.ShapeDtypeStruct((peers * rows, cols), BF16),
            jax.ShapeDtypeStruct((span, cols), BF16),
        ],
        scratch_shapes=[
            pltpu.VMEM((n, span, cols), BF16),
            pltpu.SemaphoreType.DMA((n + 1,)),
            pltpu.SemaphoreType.DMA((n, span // CHUNK)),
        ],
        compiler_params=pltpu.CompilerParams(vmem_limit_bytes=4 * 1024 * 1024),
        cost_estimate=pl.CostEstimate(flops=0, bytes_accessed=6 * span * cols, transcendentals=0),
        name="place_hop",
    )(pos, *xs, *after)


SLABS = 6


def latent_kernel(chunks, step_ref, pos_ref, *refs):
    hbm, outs, top_ref = refs[:4], refs[4:8], refs[8]
    w, m, v, g, q, in_sem, out_sem = refs[9:]
    bufs = (w, m, v, g)
    width = w.shape[1] // SLABS
    loads, stores = [], []
    for i in range(SLABS):
        cols = pl.ds(i * width, width)
        loads.append(
            [
                pltpu.make_async_copy(hbm[a].at[:, cols], bufs[a].at[:, cols], in_sem.at[i, a])
                for a in range(4)
            ]
        )
        stores.append(
            [
                pltpu.make_async_copy(src.at[:, cols], outs[a].at[:, cols], out_sem.at[i, a])
                for a, src in enumerate((w, m, v, q))
            ]
        )
        copy_all(loads[i])
    rate, corr = corrections(step_ref)
    lane = lax.broadcasted_iota(jnp.int32, (8, TILE), 1)
    lead = whole_tile(pos_ref[0], w.shape[0])
    sub = lax.broadcasted_iota(jnp.int32, (8, 1), 0) * CHUNK
    inside = (sub >= lead) & (sub < lead + TILE)
    tops = jnp.zeros((8, TILE), F32)
    for i in range(SLABS):
        wait_all(loads[i])
        blocks = range(i * width // TILE, (i + 1) * width // TILE)
        slab_tops = []
        for b in blocks:
            cols = pl.ds(b * TILE, TILE)
            w1, m1, v1 = adamw_tile(w[:, cols], m[:, cols], v[:, cols], g[:, cols], rate, corr)
            w[:, cols] = w1
            m[:, cols] = m1
            v[:, cols] = v1
            slab_tops.append(stack_max([sub_max(w1[c * CHUNK : (c + 1) * CHUNK]) for c in range(chunks)]))
        for b, top in zip(blocks, slab_tops):
            cols = pl.ds(b * TILE, TILE)
            tops = jnp.where(lane == b, top, tops)
            whole = jnp.max(jnp.where(inside, top, 0.0), axis=0, keepdims=True)
            q[:, cols] = (w[pl.ds(lead, TILE), cols] * (1.0 / (whole + SCALE_EPS))).astype(BF16)
        copy_all(stores[i])
    top_ref[...] = tops
    for group in stores:
        wait_all(group)


def latent_update(arrays, step, pos):
    rows, cols = arrays[0].shape
    elems = rows * cols
    return pl.pallas_call(
        functools.partial(latent_kernel, rows // CHUNK),
        in_specs=[SMEM] * 2 + [ANY] * 4,
        out_specs=[ANY] * 4 + [VMEM],
        out_shape=[
            jax.ShapeDtypeStruct((rows, cols), F32),
            jax.ShapeDtypeStruct((rows, cols), BF16),
            jax.ShapeDtypeStruct((rows, cols), BF16),
            jax.ShapeDtypeStruct((TILE, cols), BF16),
            jax.ShapeDtypeStruct((8, TILE), F32),
        ],
        scratch_shapes=[
            pltpu.VMEM((rows, cols), F32),
            pltpu.VMEM((rows, cols), BF16),
            pltpu.VMEM((rows, cols), BF16),
            pltpu.VMEM((rows, cols), BF16),
            pltpu.VMEM((TILE, cols), BF16),
            pltpu.SemaphoreType.DMA((SLABS, 4)),
            pltpu.SemaphoreType.DMA((SLABS, 4)),
        ],
        compiler_params=PARAMS,
        cost_estimate=pl.CostEstimate(
            flops=30 * elems, bytes_accessed=18 * elems, transcendentals=2 * elems
        ),
        name="latent_adamw",
    )(step, pos, *arrays)


def latent_rest_kernel(
    chunks, pos_ref, w1_ref, own_ref, prev_ref, next_ref, after_ref, q_ref, w, q, ext, in_sem, out_sem
):
    per_tile = TILE // CHUNK
    rows, cols = w1_ref.shape
    width = cols // SLABS
    lead = whole_tile(pos_ref[0], rows)
    loads, stores = [], []
    for i in range(SLABS):
        at = pl.ds(i * width, width)
        group = []
        for c in range(chunks - per_tile):
            first = pl.multiple_of(c * CHUNK + jnp.where(c * CHUNK < lead, 0, TILE), CHUNK)
            group.append(
                pltpu.make_async_copy(
                    w1_ref.at[pl.ds(first, CHUNK), at],
                    w.at[pl.ds(c * CHUNK, CHUNK), at],
                    in_sem.at[i, c],
                )
            )
        copy_all(group)
        loads.append(group)
        stores.append(pltpu.make_async_copy(q.at[:, at], q_ref.at[:, at], out_sem.at[i]))
    ext[0:chunks, :] = prev_ref[0:chunks, :]
    ext[chunks : 2 * chunks, :] = own_ref[0:chunks, :]
    ext[2 * chunks : 3 * chunks, :] = next_ref[0:chunks, :]
    first = chunks + lead // CHUNK
    above = jnp.max(ext[pl.ds(first - per_tile, per_tile), :], axis=0, keepdims=True)
    below = jnp.max(ext[pl.ds(first + per_tile, per_tile), :], axis=0, keepdims=True)
    both = jnp.concatenate([above] * 4 + [below] * 4, axis=0)
    lane = lax.broadcasted_iota(jnp.int32, (8, TILE), 1)
    tops = [
        jnp.max(jnp.where(lane == b, both, 0.0), axis=1, keepdims=True) for b in range(cols // TILE)
    ]
    invs = [1.0 / (top + SCALE_EPS) for top in tops]
    for i in range(SLABS):
        wait_all(loads[i])
        for b in range(i * width // TILE, (i + 1) * width // TILE):
            at = pl.ds(b * TILE, TILE)
            for c in range(chunks - per_tile):
                span = pl.ds(c * CHUNK, CHUNK)
                inv = jnp.where(c * CHUNK < lead, invs[b][0:1, :], invs[b][4:5, :])
                q[span, at] = (w[span, at] * inv).astype(BF16)
        stores[i].start()
    wait_all(stores)


def latent_rest(w1, own, above, below, pos, after):
    rows, cols = w1.shape
    chunks = rows // CHUNK
    return pl.pallas_call(
        functools.partial(latent_rest_kernel, chunks),
        in_specs=[SMEM, ANY] + [VMEM] * 3 + [ANY],
        out_specs=ANY,
        out_shape=jax.ShapeDtypeStruct((rows - TILE, cols), BF16),
        scratch_shapes=[
            pltpu.VMEM((rows - TILE, cols), F32),
            pltpu.VMEM((rows - TILE, cols), BF16),
            pltpu.VMEM((24, TILE), F32),
            pltpu.SemaphoreType.DMA((SLABS, chunks)),
            pltpu.SemaphoreType.DMA((SLABS,)),
        ],
        compiler_params=PARAMS,
        cost_estimate=pl.CostEstimate(
            flops=rows * cols, bytes_accessed=3 * rows * cols, transcendentals=0
        ),
        name="latent_rest",
    )(pos, w1, own, above, below, after)


def fast_fits(expert_shape, latent_shape, dp_count, exp_axis):
    exp_count, rows, cols = expert_shape
    latent_rows, latent_cols = latent_shape
    return (
        exp_count == 1
        and rows % TILE == 0
        and rows <= 8 * TILE
        and cols % (TILE * dp_count) == 0
        and cols // TILE // dp_count <= 16
        and dp_count == 8
        and dp_count * latent_rows * exp_axis <= TILE * TILE
        and latent_rows % CHUNK == 0
        and 2 * TILE - CHUNK <= latent_rows < 2 * TILE
        and latent_rows * exp_axis % TILE == 0
        and latent_rows * exp_axis * dp_count <= TILE * TILE
        and exp_axis == 4
        and latent_cols % (SLABS * TILE) == 0
        and latent_cols <= 16 * TILE
    )


def partner_groups(dp_count):
    hops = lambda k: bin(k >> 1).count("1")
    stage = lambda k: 3 if k < 2 else (1 if hops(k) > 1 else (2 if k & 1 else 0))
    order = sorted(range(dp_count), key=lambda k: (stage(k), -k))
    return [[k for k in order if stage(k) in n] for n in ((0,), (1,), (2, 3))]


def fast_body(
    expert_master,
    expert_first,
    expert_second,
    expert_grad,
    latent_master,
    latent_first,
    latent_second,
    latent_grad,
    step_count,
    column_owner,
):
    dp_count = lax.axis_size("dp")
    dp_pos = lax.axis_index("dp").astype(jnp.int32)
    exp_axis = lax.axis_size("expert")
    exp_pos = lax.axis_index("expert").astype(jnp.int32)
    _, rows, cols = expert_master.shape
    block_count = cols // TILE
    per_dest = block_count // dp_count
    tiles = rows // TILE

    expert_at, dp_at = exp_pos.reshape(1), dp_pos.reshape(1)
    latent_new, latent_one, latent_two, whole, chunk_top = latent_update(
        (latent_master, latent_first, latent_second, latent_grad), step_count, expert_at
    )
    latent_rows = latent_new.shape[0]
    whole = lax.all_gather(whole, "expert", axis=0, tiled=True)
    above = lax.ppermute(chunk_top, "expert", [(i, i + 1) for i in range(exp_axis - 1)])
    below = lax.ppermute(chunk_top, "expert", [(i + 1, i) for i in range(exp_axis - 1)])

    arrays = tuple(
        a.reshape(rows, cols) for a in (expert_master, expert_first, expert_second, expert_grad)
    )
    def swap(x, axis, k):
        return lax.ppermute(x, axis, [(i, i ^ k) for i in range(lax.axis_size(axis))])

    groups = partner_groups(dp_count)
    order = [k for partners in groups for k in partners]
    state, received, carry, after, tops = (), [], (), (), chunk_top
    for n, partners in enumerate(groups):
        state, sent, carried = expert_group(
            arrays, state, column_owner, dp_at, step_count, tops, carry, after, partners, per_dest
        )
        received += [swap(q, "dp", k) if k else q for k, q in zip(partners, sent)]
        after = (above, below) if n == 0 else ()
        if n == 1:
            rest = latent_rest(latent_new, chunk_top, above, below, expert_at, sent[0])
            far, near = swap(rest, "expert", 2), swap(rest, "expert", 1)
            served, _ = place_blocks(
                (), dp_at, received[: len(groups[0])], groups[0], (per_dest, dp_count, rows, TILE)
            )
            carry = (served,)
    served, tops = carried
    first, count = len(groups[0]), len(groups[0]) + len(groups[1])
    served, token = place_blocks(
        (served,), dp_at, received[first:count], groups[1], served.shape
    )
    latent_served, far_again = place_and_pass(
        expert_at, [near, far], [1, 2], (tops, token), latent_rows, exp_axis
    )
    last = swap(far_again, "expert", 1)
    latent_served = place_full(latent_served, expert_at, whole, rest, latent_rows)
    served, expert_scales, maxima = collect(
        served, dp_at, received, order, range(count, dp_count - 1), tiles
    )
    maxima = [maxima] + [
        lax.ppermute(maxima, "expert", [(i, (i + s) % exp_axis) for i in range(exp_axis)])
        for s in range(1, exp_axis)
    ]
    latent_served, latent_scales = finish(
        latent_served,
        expert_at,
        [last],
        [3],
        maxima,
        latent_rows // CHUNK,
        latent_new.shape[1] // TILE,
    )
    expert_served = served.reshape(1, block_count * rows, TILE)

    return (
        state[0][None],
        state[1][None],
        state[2][None],
        expert_served,
        expert_scales,
        latent_new,
        latent_one,
        latent_two,
        latent_served,
        latent_scales,
    )


def body(*args):
    if fast_fits(args[0].shape, args[4].shape, lax.axis_size("dp"), lax.axis_size("expert")):
        return fast_body(*args)
    return general_body(*args)


def solution(mesh):
    placed = (
        P("expert", "dp", None),
        P("expert", "dp", None),
        P("expert", "dp", None),
        P("expert", "dp", None),
        P(("dp", "expert"), None),
        P(("dp", "expert"), None),
        P(("dp", "expert"), None),
        P(("dp", "expert"), None),
        P(),
        P(),
    )
    return jax.shard_map(
        body,
        mesh=mesh,
        in_specs=placed,
        out_specs=(
            P("expert", "dp", None),
            P("expert", "dp", None),
            P("expert", "dp", None),
            P("expert", "dp", None),
            P("expert", "dp"),
            P(("dp", "expert"), None),
            P(("dp", "expert"), None),
            P(("dp", "expert"), None),
            P("dp", None),
            P(),
        ),
        check_vma=False,
    )
```

```python
import functools
import math

import jax
import jax.numpy as jnp
from jax import lax
from jax.experimental import pallas as pl
from jax.experimental.pallas import tpu as pltpu
from jax.sharding import PartitionSpec as P

D = 7168
TILE = 128


BETA_ONE = 0.9
BETA_TWO = 0.95
LEARN_RATE = 0.2
DECAY_RATE = 0.1
ADAM_EPS = 1e-08
SCALE_EPS = 1e-06


def adamw_step(master, moment_one, moment_two, gradient, step_count):
    grad_value = gradient.astype(jnp.float32)
    first_new = BETA_ONE * moment_one.astype(jnp.float32) + (1.0 - BETA_ONE) * grad_value
    second_new = (
        BETA_TWO * moment_two.astype(jnp.float32) + (1.0 - BETA_TWO) * grad_value * grad_value
    )
    step_value = step_count[0].astype(jnp.float32)
    corr_one = 1.0 - jnp.power(jnp.float32(BETA_ONE), step_value)
    corr_two = 1.0 - jnp.power(jnp.float32(BETA_TWO), step_value)
    update = first_new / corr_one / (jnp.sqrt(second_new / corr_two) + ADAM_EPS)
    master_new = master - LEARN_RATE * (update + DECAY_RATE * master)
    return (master_new, first_new.astype(jnp.bfloat16), second_new.astype(jnp.bfloat16))


def row_maxima(weights):
    leading = weights.shape[:-1]
    tile_count = weights.shape[-1] // TILE
    return jnp.max(jnp.abs(weights).reshape(leading + (tile_count, TILE)), axis=-1)


def local_tiles(row_max, lead_rows):
    exp_count, row_count, tile_count = row_max.shape
    tile_span = row_count // TILE + 2
    buffer = jnp.zeros((exp_count, tile_span * TILE, tile_count), jnp.float32)
    buffer = lax.dynamic_update_slice(buffer, row_max, (jnp.int32(0), lead_rows, jnp.int32(0)))
    return jnp.max(buffer.reshape(exp_count, tile_span, TILE, tile_count), axis=2)


def place_tiles(tile_max, first_tile):
    exp_count, tile_span, tile_count = tile_max.shape
    global_map = jnp.zeros((exp_count, D // TILE + tile_span, tile_count), jnp.float32)
    return lax.dynamic_update_slice(global_map, tile_max, (jnp.int32(0), first_tile, jnp.int32(0)))


def quantized_rows(weights, tile_max, lead_rows):
    exp_count, row_count, col_count = weights.shape
    repeated = jnp.repeat(tile_max, TILE, axis=1)
    row_scale = lax.dynamic_slice_in_dim(repeated, lead_rows, row_count, 1)
    blocks = weights.reshape(exp_count, row_count, col_count // TILE, TILE)
    return (blocks / (row_scale[..., None] + SCALE_EPS)).reshape(weights.shape).astype(jnp.bfloat16)


def general_body(
    expert_master,
    expert_first,
    expert_second,
    expert_grad,
    latent_master,
    latent_first,
    latent_second,
    latent_grad,
    step_count,
    column_owner,
):
    master_new, first_new, second_new = adamw_step(
        expert_master, expert_first, expert_second, expert_grad, step_count
    )
    latent_new, latent_one, latent_two = adamw_step(
        latent_master, latent_first, latent_second, latent_grad, step_count
    )
    dp_count = lax.axis_size("dp")
    dp_pos = lax.axis_index("dp")
    exp_count, row_count, col_count = master_new.shape
    block_count = col_count // TILE
    slot_count = max(1, block_count // dp_count)
    total_tiles = D // TILE
    recv_rows = block_count * row_count
    recv_tiles = recv_rows // TILE
    positions = jnp.arange(block_count, dtype=jnp.int32)
    inverse = jnp.sum(
        positions[:, None] * (column_owner[:, None] == positions[None, :]).astype(jnp.int32), axis=0
    )
    receiver_ids = jnp.arange(dp_count, dtype=jnp.int32)[:, None]
    slot_ids = jnp.arange(slot_count, dtype=jnp.int32)[None, :]
    segment = (
        receiver_ids * block_count
        + jnp.mod(dp_pos - receiver_ids * block_count, dp_count)
        + slot_ids * dp_count
    )
    usable_slot = (segment < (receiver_ids + 1) * block_count).reshape(-1)
    send_block = jnp.take(inverse, jnp.minimum(segment // dp_count, block_count - 1)).reshape(-1)
    local_segments = jnp.arange(block_count, dtype=jnp.int32)
    source_dev = jnp.mod(dp_pos * block_count + local_segments, dp_count)
    pick_index = source_dev * slot_count + local_segments // dp_count
    blocks = master_new.reshape(exp_count, row_count, block_count, TILE)
    picked = jnp.take(blocks, send_block, axis=2)
    received = lax.all_to_all(
        jnp.where(usable_slot[None, None, :, None], picked, jnp.zeros((), picked.dtype)),
        "dp",
        split_axis=2,
        concat_axis=2,
        tiled=True,
    )
    ordered = jnp.take(received, pick_index, axis=2)
    tall = (
        jnp.transpose(ordered, (0, 2, 1, 3))
        .reshape(exp_count, recv_rows, TILE)
        .reshape(exp_count, recv_tiles, TILE, TILE)
    )
    expert_scales = jnp.max(jnp.abs(tall), axis=(2, 3))
    expert_served = (
        (tall / (expert_scales[:, :, None, None] + SCALE_EPS))
        .reshape(exp_count, recv_rows, TILE)
        .astype(jnp.bfloat16)
    )
    latent_block = lax.all_gather(latent_new, "expert", axis=0, tiled=True)
    block_rows = latent_block.shape[0]
    block_offset = dp_pos * block_rows
    block_lead = block_offset % TILE
    block_tiles = local_tiles(row_maxima(latent_block)[None], block_lead)
    block_map = lax.pmax(place_tiles(block_tiles, block_offset // TILE), "dp")
    latent_scales = block_map[0, :total_tiles]
    block_tiles = lax.dynamic_slice_in_dim(block_map, block_offset // TILE, block_tiles.shape[1], 1)
    latent_served = quantized_rows(latent_block[None], block_tiles, block_lead)[0]
    return (
        master_new,
        first_new,
        second_new,
        expert_served,
        expert_scales,
        latent_new,
        latent_one,
        latent_two,
        latent_served,
        latent_scales,
    )


CHUNK = 32
EXTRA = 16
MAXIMA_AT = (64, 16)
F32 = jnp.float32
BF16 = jnp.bfloat16
VMEM_LIMIT = 56 * 1024 * 1024
ANY = pl.BlockSpec(memory_space=pl.ANY)
SMEM = pl.BlockSpec(memory_space=pltpu.SMEM)
VMEM = pl.BlockSpec(memory_space=pltpu.VMEM)
PARAMS = pltpu.CompilerParams(vmem_limit_bytes=VMEM_LIMIT)
LIGHT = pltpu.CompilerParams(vmem_limit_bytes=1024 * 1024)


def corrections(step_ref):
    one, two = lax.fori_loop(
        0, step_ref[0], lambda _, p: (p[0] * BETA_ONE, p[1] * BETA_TWO), (F32(1.0), F32(1.0))
    )
    rate = LEARN_RATE / (1.0 - jnp.full((1, TILE), one, F32))
    corr = 1.0 / (1.0 - jnp.full((1, TILE), two, F32))
    return rate, corr


def adamw_tile(w, m, v, g, rate, corr):
    g = g.astype(F32)
    m1 = BETA_ONE * m.astype(F32) + (1.0 - BETA_ONE) * g
    v1 = BETA_TWO * v.astype(F32) + (1.0 - BETA_TWO) * g * g
    x = v1 * corr
    inv = pl.reciprocal(x * lax.rsqrt(x) + ADAM_EPS, approx=True)
    w1 = (1.0 - LEARN_RATE * DECAY_RATE) * w - rate * m1 * inv
    return w1, m1.astype(BF16), v1.astype(BF16)


def sub_max(w1):
    return jnp.max(jnp.abs(w1).reshape(w1.shape[0] // 8, 8, TILE), axis=0)


def stack_max(parts):
    parts = parts + [parts[-1]] * (8 - len(parts))
    rows = [jnp.max(p, axis=0, keepdims=True) for p in parts]
    return jnp.max(jnp.concatenate(rows, axis=0), axis=1, keepdims=True)


def three_parts(x):
    high = x.astype(BF16).astype(F32)
    rest = x - high
    middle = rest.astype(BF16).astype(F32)
    return high, middle, rest - middle


def copy_all(copies):
    for c in copies:
        c.start()


def wait_all(copies):
    for c in copies:
        c.wait()


def expert_kernel(
    partners, per_dest, n_alias, n_carry, chunks, n_maxima, owner_ref, pos_ref, step_ref, *refs
):
    maxima, refs = refs[:n_maxima], refs[n_maxima:]
    hbm, refs = refs[:4], refs[4 + n_alias + n_carry :]
    n_dest = len(partners)
    outs, q_refs, served_ref = refs[:3], refs[3 : 3 + n_dest], refs[3 + n_dest]
    w, m, v, g, extra, in_sem, out_sem, extra_sem = refs[-8:]
    bufs = (w, m, v, g)
    blocks = owner_ref.shape[0]
    rows = w.shape[1]
    tiles = rows // TILE
    pos = pos_ref[0]

    loads, stores = [], []
    for d, k in enumerate(partners):
        for j in range(per_dest):
            i = d * per_dest + j
            slot = (pos ^ k) * per_dest + j
            block = jnp.int32(0)
            for b in range(blocks):
                block = jnp.where(owner_ref[b] == slot, b, block)
            cols = pl.ds(pl.multiple_of(block * TILE, TILE), TILE)
            loads.append(
                [
                    pltpu.make_async_copy(hbm[a].at[:, cols], bufs[a].at[i], in_sem.at[i, a])
                    for a in range(4)
                ]
            )
            target = q_refs[d].at[pl.ds(j * rows, rows), :] if k else served_ref.at[j, pos]
            stores.append(
                [
                    pltpu.make_async_copy(bufs[a].at[i], outs[a].at[:, cols], out_sem.at[i, a])
                    for a in range(3)
                ]
                + [pltpu.make_async_copy(g.at[i], target, out_sem.at[i, 3])]
            )
            copy_all(loads[-1])
    rate, corr = corrections(step_ref)
    lane = lax.broadcasted_iota(jnp.int32, (8, TILE), 1)
    if chunks:
        tops_ref, ext = refs[3 + n_dest + n_carry], refs[-9]
        per_tile = TILE // CHUNK
        for s in range(n_maxima):
            peer = lax.rem(pos_ref[1] + n_maxima - s, n_maxima)
            ext[pl.ds(peer * chunks, chunks), :] = maxima[s][0:chunks, :]
        tops_ref[...] = jnp.zeros_like(tops_ref)
        for t in range(n_maxima * chunks // per_tile):
            tops_ref[t : t + 1, :] = jnp.max(
                ext[t * per_tile : (t + 1) * per_tile, :], axis=0, keepdims=True
            )
        maxima = (tops_ref,)
    carried = jnp.zeros((8, TILE), F32)
    for first, x_ref in zip(MAXIMA_AT, maxima):
        for p, value in enumerate(three_parts(x_ref[...])):
            at = first + 16 * p
            carried = jnp.where((lane >= at) & (lane < at + 16), pltpu.roll(value, at, 1), carried)
    extras = []
    for d, k in enumerate(partners):
        side = carried
        for j in range(per_dest):
            i = d * per_dest + j
            wait_all(loads[i])
            parts = []
            for t in range(tiles):
                at = pl.ds(t * TILE, TILE)
                w1, m1, v1 = adamw_tile(w[i, at, :], m[i, at, :], v[i, at, :], g[i, at, :], rate, corr)
                w[i, at, :] = w1
                m[i, at, :] = m1
                v[i, at, :] = v1
                parts.append(sub_max(w1))
            copy_all(stores[i][:3])
            top = stack_max(parts)
            inv = 1.0 / (top + SCALE_EPS)
            for t in range(tiles):
                at = pl.ds(t * TILE, TILE)
                g[i, at, :] = (w[i, at, :] * inv[t : t + 1, :]).astype(BF16)
            stores[i][3].start()
            for p, value in enumerate(three_parts(top)):
                side = jnp.where(lane == 3 * j + p, value, side)
        extra[d] = jnp.concatenate([side, jnp.zeros_like(side)], axis=0).astype(BF16)
        first = per_dest * rows if k else 0
        extras.append(
            pltpu.make_async_copy(
                extra.at[d], q_refs[d].at[pl.ds(first, EXTRA), :], extra_sem.at[d]
            )
        )
        extras[-1].start()
    for group in stores:
        wait_all(group)
    wait_all(extras)


def expert_group(arrays, state, owner, pos, step, maxima, chunks, carry, partners, per_dest):
    rows, cols = arrays[0].shape
    n_alias, n_maxima = len(state), len(maxima)
    n = len(partners) * per_dest
    elems = rows * TILE * n
    flat = [jax.ShapeDtypeStruct((8, TILE), F32)] * (chunks > 0)
    first = 7 + n_maxima
    aliases = {first + i: i for i in range(n_alias)}
    aliases.update({first + n_alias + i: 3 + len(partners) + i for i in range(len(carry))})
    out = pl.pallas_call(
        functools.partial(
            expert_kernel, partners, per_dest, n_alias, len(carry), chunks, n_maxima
        ),
        in_specs=[SMEM] * 3 + [VMEM] * n_maxima + [ANY] * (4 + n_alias + len(carry)),
        out_specs=[ANY] * (3 + len(partners) + len(carry)) + [VMEM] * len(flat),
        out_shape=[
            jax.ShapeDtypeStruct((rows, cols), F32),
            jax.ShapeDtypeStruct((rows, cols), BF16),
            jax.ShapeDtypeStruct((rows, cols), BF16),
        ]
        + [
            jax.ShapeDtypeStruct((per_dest * rows * (k > 0) + EXTRA, TILE), BF16)
            for k in partners
        ]
        + [jax.ShapeDtypeStruct(x.shape, x.dtype) for x in carry]
        + flat,
        scratch_shapes=[
            pltpu.VMEM((32, TILE), F32),
            pltpu.VMEM((n, rows, TILE), F32),
            pltpu.VMEM((n, rows, TILE), BF16),
            pltpu.VMEM((n, rows, TILE), BF16),
            pltpu.VMEM((n, rows, TILE), BF16),
            pltpu.VMEM((len(partners), EXTRA, TILE), BF16),
            pltpu.SemaphoreType.DMA((n, 4)),
            pltpu.SemaphoreType.DMA((n, 4)),
            pltpu.SemaphoreType.DMA((len(partners),)),
        ],
        input_output_aliases=aliases,
        compiler_params=PARAMS,
        cost_estimate=pl.CostEstimate(flops=elems, bytes_accessed=elems, transcendentals=0),
        name="expert_adamw",
    )(owner, pos, step, *maxima, *arrays, *state, *carry)
    return out[:3], out[3 : 3 + len(partners)], out[3 + len(partners) :]


def block_copies(served, payloads, srcs, sem):
    per_dest, _, rows, _ = served.shape
    return [
        pltpu.make_async_copy(q.at[pl.ds(j * rows, rows), :], served.at[j, src], sem.at[i, j])
        for i, (q, src) in enumerate(zip(payloads, srcs))
        for j in range(per_dest)
    ]


def place_kernel(partners, pos_ref, *refs):
    n = len(partners)
    served, token, sem = refs[-3:]
    token[...] = jnp.zeros_like(token)
    copies = block_copies(served, refs[:n], [pos_ref[0] ^ k for k in partners], sem)
    copy_all(copies)
    wait_all(copies)


def place_blocks(served, pos, payloads, partners, shape):
    n = len(partners)
    return pl.pallas_call(
        functools.partial(place_kernel, partners),
        in_specs=[SMEM] + [ANY] * (n + len(served)),
        out_specs=[ANY, VMEM],
        out_shape=[jax.ShapeDtypeStruct(shape, BF16), jax.ShapeDtypeStruct((8, TILE), F32)],
        scratch_shapes=[pltpu.SemaphoreType.DMA((n, shape[0]))],
        input_output_aliases={1 + n: 0} if served else {},
        compiler_params=LIGHT,
        cost_estimate=pl.CostEstimate(
            flops=0, bytes_accessed=4 * n * payloads[0].size, transcendentals=0
        ),
        name="place_served",
    )(pos, *payloads, *served)


def collect_kernel(order, tiles, lat_tiles, to_place, groups, pos_ref, after_ref, *refs):
    n = len(order)
    q_refs = refs[:n]
    served, exp_ref, lat_ref, extra, rows_ref, place_sem, sem = refs[n + 1 :]
    pos = pos_ref[0]
    per_dest = served.shape[0]
    blocks_copies = block_copies(
        served, [q_refs[i] for i in to_place], [pos ^ order[i] for i in to_place], place_sem
    )
    copies = [
        pltpu.make_async_copy(
            q.at[pl.ds(q.shape[0] - EXTRA, EXTRA), :], extra.at[i], sem.at[i]
        )
        for i, q in enumerate(q_refs)
    ]
    copy_all(copies)
    copy_all(blocks_copies)
    rows_ref[...] = jnp.zeros_like(rows_ref)
    flat = jnp.zeros((8, exp_ref.shape[1]), F32)
    wide = lax.broadcasted_iota(jnp.int32, flat.shape, 1)
    deep = lax.broadcasted_iota(jnp.int32, flat.shape, 0)
    for i, k in enumerate(order):
        copies[i].wait()
        src = pos ^ k
        x = extra[i].astype(F32)[0:8, :]
        known = (src, src ^ 1) if k in groups[2] else (src,) if k in groups[1] else ()
        for first, peer in zip(MAXIMA_AT, known):
            lat = sum(pltpu.roll(x, TILE - first - 16 * p, 1) for p in range(3))
            rows_ref[pl.ds(peer * lat_tiles, lat_tiles), :] = lat[0:lat_tiles, :]
        for j in range(per_dest):
            first = 3 * j
            top = x[:, first : first + 1] + x[:, first + 1 : first + 2] + x[:, first + 2 : first + 3]
            hit = (wide == (j * n + src) * tiles + deep) & (deep < tiles)
            flat = jnp.where(hit, top, flat)
    exp_ref[...] = jnp.max(flat, axis=0, keepdims=True)
    blocks, height = lat_ref.shape
    lat_ref[...] = jnp.transpose(rows_ref[...])[0:blocks, 0:height]
    wait_all(blocks_copies)


def collect(served, pos, after, received, groups, tiles, lat_tiles, lat_blocks):
    order = [k for partners in groups for k in partners]
    n = len(order)
    per_dest = served.shape[0]
    to_place = [i for i, k in enumerate(order) if k in groups[2] and k]
    served, expert, latent = pl.pallas_call(
        functools.partial(collect_kernel, order, tiles, lat_tiles, to_place, groups),
        in_specs=[SMEM, VMEM] + [ANY] * (n + 1),
        out_specs=[ANY, VMEM, VMEM],
        out_shape=[
            jax.ShapeDtypeStruct(served.shape, served.dtype),
            jax.ShapeDtypeStruct((1, per_dest * n * tiles), F32),
            jax.ShapeDtypeStruct((lat_blocks, n * lat_tiles), F32),
        ],
        scratch_shapes=[
            pltpu.VMEM((n, EXTRA, TILE), BF16),
            pltpu.VMEM((TILE, TILE), F32),
            pltpu.SemaphoreType.DMA((len(to_place), per_dest)),
            pltpu.SemaphoreType.DMA((n,)),
        ],
        input_output_aliases={2 + n: 0},
        compiler_params=LIGHT,
        cost_estimate=pl.CostEstimate(flops=1000000, bytes_accessed=1000000, transcendentals=0),
        name="place_last",
    )(pos, after, *received, served)
    return served, expert, latent.T


def finish_kernel(deltas, rows, pos_ref, *refs):
    n = len(deltas)
    latent, buf, in_sem, out_sem = refs[n + 2 :]
    loads = [pltpu.make_async_copy(refs[i], buf.at[i], in_sem.at[i]) for i in range(n)]
    copy_all(loads)
    copies = []
    for i, delta in enumerate(deltas):
        loads[i].wait()
        group = rest_stores(buf, i, pos_ref[0] ^ delta, rows, latent, out_sem)
        copy_all(group)
        copies += group
    wait_all(copies)


def finish(latent, pos, rest, deltas, after):
    n = len(rest)
    span, cols = rest[0].shape
    return pl.pallas_call(
        functools.partial(finish_kernel, deltas, TILE + span),
        in_specs=[SMEM] + [ANY] * (n + 2),
        out_specs=ANY,
        out_shape=jax.ShapeDtypeStruct(latent.shape, latent.dtype),
        scratch_shapes=[
            pltpu.VMEM((n, span, cols), BF16),
            pltpu.SemaphoreType.DMA((n,)),
            pltpu.SemaphoreType.DMA((n, span // CHUNK)),
        ],
        input_output_aliases={1 + n: 0},
        compiler_params=pltpu.CompilerParams(vmem_limit_bytes=4 * 1024 * 1024),
        cost_estimate=pl.CostEstimate(flops=0, bytes_accessed=1000000, transcendentals=0),
        name="place_finish",
    )(pos, *rest, latent, after)


def whole_tile(pos, rows):
    return pl.multiple_of(lax.rem(pos * (TILE - rows % TILE), TILE), CHUNK)


def full_kernel(pieces, rows, pos_ref, x_ref, own_ref, *refs):
    out_ref, token, buf, own, in_sem, out_sem, own_in, own_out = refs[1:]
    token[...] = jnp.zeros_like(token)
    loads, stores = [], []
    for i in range(pieces):
        lead = i * (TILE - rows % TILE) % TILE
        at = pl.ds(i * TILE, TILE)
        loads.append(pltpu.make_async_copy(x_ref.at[at, :], buf.at[at, :], in_sem.at[i]))
        stores.append(
            pltpu.make_async_copy(
                buf.at[at, :], out_ref.at[pl.ds(i * rows + lead, TILE), :], out_sem.at[i]
            )
        )
    loads.append(pltpu.make_async_copy(own_ref, own.at[0], own_in.at[0]))
    copy_all(loads)
    for i in range(pieces):
        loads[i].wait()
        stores[i].start()
    loads[pieces].wait()
    rest = rest_stores(own, 0, pos_ref[0], rows, out_ref, own_out)
    copy_all(rest)
    wait_all(stores + rest)


def place_full(out, pos, x, own, rows):
    pieces = x.shape[0] // TILE
    return pl.pallas_call(
        functools.partial(full_kernel, pieces, rows),
        in_specs=[SMEM] + [ANY] * 3,
        out_specs=[ANY, VMEM],
        out_shape=[
            jax.ShapeDtypeStruct((pieces * rows, x.shape[1]), BF16),
            jax.ShapeDtypeStruct((8, TILE), F32),
        ],
        scratch_shapes=[
            pltpu.VMEM(x.shape, BF16),
            pltpu.VMEM((1,) + own.shape, BF16),
            pltpu.SemaphoreType.DMA((pieces,)),
            pltpu.SemaphoreType.DMA((pieces,)),
            pltpu.SemaphoreType.DMA((1,)),
            pltpu.SemaphoreType.DMA((1, own.shape[0] // CHUNK)),
        ],
        input_output_aliases={3: 0},
        compiler_params=PARAMS,
        cost_estimate=pl.CostEstimate(flops=0, bytes_accessed=4 * x.size, transcendentals=0),
        name="place_whole",
    )(pos, x, own, out)


def rest_stores(buf, i, peer, rows, out_ref, sem):
    lead = whole_tile(peer, rows)
    copies = []
    for c in range((rows - TILE) // CHUNK):
        at = peer * rows + c * CHUNK + jnp.where(c * CHUNK < lead, 0, TILE)
        copies.append(
            pltpu.make_async_copy(
                buf.at[i, pl.ds(c * CHUNK, CHUNK), :],
                out_ref.at[pl.ds(pl.multiple_of(at, CHUNK), CHUNK), :],
                sem.at[i, c],
            )
        )
    return copies


def hop_kernel(deltas, rows, pos_ref, *refs):
    n = len(deltas)
    out_ref, again_ref, buf, in_sem, out_sem = refs[-5:]
    loads = [pltpu.make_async_copy(refs[i], buf.at[i], in_sem.at[i]) for i in range(n)]
    copy_all(loads)
    copies = [pltpu.make_async_copy(buf.at[n - 1], again_ref, in_sem.at[n])]
    for i in reversed(range(n)):
        loads[i].wait()
        group = rest_stores(buf, i, pos_ref[0] ^ deltas[i], rows, out_ref, out_sem)
        copy_all(copies + group if i == n - 1 else group)
        copies += group
    wait_all(copies)


def place_and_pass(pos, xs, deltas, after, rows, peers):
    span, cols = xs[0].shape
    n = len(xs)
    return pl.pallas_call(
        functools.partial(hop_kernel, deltas, rows),
        in_specs=[SMEM] + [ANY] * n + [VMEM] * len(after),
        out_specs=[ANY, ANY],
        out_shape=[
            jax.ShapeDtypeStruct((peers * rows, cols), BF16),
            jax.ShapeDtypeStruct((span, cols), BF16),
        ],
        scratch_shapes=[
            pltpu.VMEM((n, span, cols), BF16),
            pltpu.SemaphoreType.DMA((n + 1,)),
            pltpu.SemaphoreType.DMA((n, span // CHUNK)),
        ],
        compiler_params=pltpu.CompilerParams(vmem_limit_bytes=4 * 1024 * 1024),
        cost_estimate=pl.CostEstimate(flops=0, bytes_accessed=6 * span * cols, transcendentals=0),
        name="place_hop",
    )(pos, *xs, *after)


SLABS = 6


def latent_kernel(chunks, step_ref, pos_ref, *refs):
    hbm, outs, top_ref = refs[:4], refs[4:8], refs[8]
    w, m, v, g, q, in_sem, out_sem = refs[9:]
    bufs = (w, m, v, g)
    width = w.shape[1] // SLABS
    loads, stores = [], []
    for i in range(SLABS):
        cols = pl.ds(i * width, width)
        loads.append(
            [
                pltpu.make_async_copy(hbm[a].at[:, cols], bufs[a].at[:, cols], in_sem.at[i, a])
                for a in range(4)
            ]
        )
        stores.append(
            [
                pltpu.make_async_copy(src.at[:, cols], outs[a].at[:, cols], out_sem.at[i, a])
                for a, src in enumerate((w, m, v, q))
            ]
        )
        copy_all(loads[i])
    rate, corr = corrections(step_ref)
    lane = lax.broadcasted_iota(jnp.int32, (8, TILE), 1)
    lead = whole_tile(pos_ref[0], w.shape[0])
    sub = lax.broadcasted_iota(jnp.int32, (8, 1), 0) * CHUNK
    inside = (sub >= lead) & (sub < lead + TILE)
    tops = jnp.zeros((8, TILE), F32)
    for i in range(SLABS):
        wait_all(loads[i])
        blocks = range(i * width // TILE, (i + 1) * width // TILE)
        slab_tops = []
        for b in blocks:
            cols = pl.ds(b * TILE, TILE)
            w1, m1, v1 = adamw_tile(w[:, cols], m[:, cols], v[:, cols], g[:, cols], rate, corr)
            w[:, cols] = w1
            m[:, cols] = m1
            v[:, cols] = v1
            slab_tops.append(stack_max([sub_max(w1[c * CHUNK : (c + 1) * CHUNK]) for c in range(chunks)]))
        for b, top in zip(blocks, slab_tops):
            cols = pl.ds(b * TILE, TILE)
            tops = jnp.where(lane == b, top, tops)
            whole = jnp.max(jnp.where(inside, top, 0.0), axis=0, keepdims=True)
            q[:, cols] = (w[pl.ds(lead, TILE), cols] * (1.0 / (whole + SCALE_EPS))).astype(BF16)
        copy_all(stores[i])
    top_ref[...] = tops
    for group in stores:
        wait_all(group)


def latent_update(arrays, step, pos):
    rows, cols = arrays[0].shape
    elems = rows * cols
    return pl.pallas_call(
        functools.partial(latent_kernel, rows // CHUNK),
        in_specs=[SMEM] * 2 + [ANY] * 4,
        out_specs=[ANY] * 4 + [VMEM],
        out_shape=[
            jax.ShapeDtypeStruct((rows, cols), F32),
            jax.ShapeDtypeStruct((rows, cols), BF16),
            jax.ShapeDtypeStruct((rows, cols), BF16),
            jax.ShapeDtypeStruct((TILE, cols), BF16),
            jax.ShapeDtypeStruct((8, TILE), F32),
        ],
        scratch_shapes=[
            pltpu.VMEM((rows, cols), F32),
            pltpu.VMEM((rows, cols), BF16),
            pltpu.VMEM((rows, cols), BF16),
            pltpu.VMEM((rows, cols), BF16),
            pltpu.VMEM((TILE, cols), BF16),
            pltpu.SemaphoreType.DMA((SLABS, 4)),
            pltpu.SemaphoreType.DMA((SLABS, 4)),
        ],
        compiler_params=PARAMS,
        cost_estimate=pl.CostEstimate(
            flops=30 * elems, bytes_accessed=18 * elems, transcendentals=2 * elems
        ),
        name="latent_adamw",
    )(step, pos, *arrays)


def latent_rest_kernel(
    chunks, pos_ref, w1_ref, own_ref, prev_ref, next_ref, after_ref, q_ref, w, q, ext, in_sem, out_sem
):
    per_tile = TILE // CHUNK
    rows, cols = w1_ref.shape
    width = cols // SLABS
    lead = whole_tile(pos_ref[0], rows)
    loads, stores = [], []
    for i in range(SLABS):
        at = pl.ds(i * width, width)
        group = []
        for c in range(chunks - per_tile):
            first = pl.multiple_of(c * CHUNK + jnp.where(c * CHUNK < lead, 0, TILE), CHUNK)
            group.append(
                pltpu.make_async_copy(
                    w1_ref.at[pl.ds(first, CHUNK), at],
                    w.at[pl.ds(c * CHUNK, CHUNK), at],
                    in_sem.at[i, c],
                )
            )
        copy_all(group)
        loads.append(group)
        stores.append(pltpu.make_async_copy(q.at[:, at], q_ref.at[:, at], out_sem.at[i]))
    ext[0:chunks, :] = prev_ref[0:chunks, :]
    ext[chunks : 2 * chunks, :] = own_ref[0:chunks, :]
    ext[2 * chunks : 3 * chunks, :] = next_ref[0:chunks, :]
    first = chunks + lead // CHUNK
    above = jnp.max(ext[pl.ds(first - per_tile, per_tile), :], axis=0, keepdims=True)
    below = jnp.max(ext[pl.ds(first + per_tile, per_tile), :], axis=0, keepdims=True)
    both = jnp.concatenate([above] * 4 + [below] * 4, axis=0)
    lane = lax.broadcasted_iota(jnp.int32, (8, TILE), 1)
    tops = [
        jnp.max(jnp.where(lane == b, both, 0.0), axis=1, keepdims=True) for b in range(cols // TILE)
    ]
    invs = [1.0 / (top + SCALE_EPS) for top in tops]
    for i in range(SLABS):
        wait_all(loads[i])
        for b in range(i * width // TILE, (i + 1) * width // TILE):
            at = pl.ds(b * TILE, TILE)
            for c in range(chunks - per_tile):
                span = pl.ds(c * CHUNK, CHUNK)
                inv = jnp.where(c * CHUNK < lead, invs[b][0:1, :], invs[b][4:5, :])
                q[span, at] = (w[span, at] * inv).astype(BF16)
        stores[i].start()
    wait_all(stores)


def latent_rest(w1, own, above, below, pos, after):
    rows, cols = w1.shape
    chunks = rows // CHUNK
    return pl.pallas_call(
        functools.partial(latent_rest_kernel, chunks),
        in_specs=[SMEM, ANY] + [VMEM] * 3 + [ANY],
        out_specs=ANY,
        out_shape=jax.ShapeDtypeStruct((rows - TILE, cols), BF16),
        scratch_shapes=[
            pltpu.VMEM((rows - TILE, cols), F32),
            pltpu.VMEM((rows - TILE, cols), BF16),
            pltpu.VMEM((24, TILE), F32),
            pltpu.SemaphoreType.DMA((SLABS, chunks)),
            pltpu.SemaphoreType.DMA((SLABS,)),
        ],
        compiler_params=PARAMS,
        cost_estimate=pl.CostEstimate(
            flops=rows * cols, bytes_accessed=3 * rows * cols, transcendentals=0
        ),
        name="latent_rest",
    )(pos, w1, own, above, below, after)


def fast_fits(expert_shape, latent_shape, dp_count, exp_axis):
    exp_count, rows, cols = expert_shape
    latent_rows, latent_cols = latent_shape
    return (
        exp_count == 1
        and rows % TILE == 0
        and rows <= 8 * TILE
        and cols % (TILE * dp_count) == 0
        and cols // TILE // dp_count <= 5
        and dp_count == 8
        and dp_count * latent_rows * exp_axis <= TILE * TILE
        and latent_rows % CHUNK == 0
        and 2 * TILE - CHUNK <= latent_rows < 2 * TILE
        and latent_rows * exp_axis % TILE == 0
        and latent_rows * exp_axis <= 8 * TILE
        and exp_axis == 4
        and latent_cols % (SLABS * TILE) == 0
        and latent_cols <= 16 * TILE
    )


def partner_groups(dp_count):
    hops = lambda k: bin(k >> 1).count("1")
    stage = lambda k: 3 if k < 2 else (1 if hops(k) > 1 else (2 if k & 1 else 0))
    order = sorted(range(dp_count), key=lambda k: (stage(k), -k))
    return [[k for k in order if stage(k) in n] for n in ((0,), (1,), (2, 3))]


def fast_body(
    expert_master,
    expert_first,
    expert_second,
    expert_grad,
    latent_master,
    latent_first,
    latent_second,
    latent_grad,
    step_count,
    column_owner,
):
    dp_count = lax.axis_size("dp")
    dp_pos = lax.axis_index("dp").astype(jnp.int32)
    exp_axis = lax.axis_size("expert")
    exp_pos = lax.axis_index("expert").astype(jnp.int32)
    _, rows, cols = expert_master.shape
    block_count = cols // TILE
    per_dest = block_count // dp_count
    tiles = rows // TILE

    expert_at, dp_at = exp_pos.reshape(1), dp_pos.reshape(1)
    latent_new, latent_one, latent_two, whole, chunk_top = latent_update(
        (latent_master, latent_first, latent_second, latent_grad), step_count, expert_at
    )
    latent_rows = latent_new.shape[0]
    whole = lax.all_gather(whole, "expert", axis=0, tiled=True)
    maxima = [chunk_top] + [
        lax.ppermute(chunk_top, "expert", [(i, (i + s) % exp_axis) for i in range(exp_axis)])
        for s in range(1, exp_axis)
    ]

    arrays = tuple(
        a.reshape(rows, cols) for a in (expert_master, expert_first, expert_second, expert_grad)
    )
    def swap(x, axis, k):
        return lax.ppermute(x, axis, [(i, i ^ k) for i in range(lax.axis_size(axis))])

    groups = partner_groups(dp_count)
    order = [k for partners in groups for k in partners]
    both_at = jnp.concatenate([dp_at, expert_at])
    send = lambda sent, partners: [swap(q, "dp", k) if k else q for k, q in zip(partners, sent)]
    group = functools.partial(expert_group, arrays, owner=column_owner, pos=both_at, step=step_count)
    chunks = latent_rows // CHUNK
    state, sent, _ = group(
        state=(), maxima=(), chunks=0, carry=(), partners=groups[0], per_dest=per_dest
    )
    received = send(sent, groups[0])
    state, sent, (tops,) = group(
        state=state, maxima=maxima, chunks=chunks, carry=(), partners=groups[1], per_dest=per_dest
    )
    received += send(sent, groups[1])
    rest = latent_rest(latent_new, chunk_top, maxima[1], maxima[-1], expert_at, sent[0])
    far, near = swap(rest, "expert", 2), swap(rest, "expert", 1)
    served, _ = place_blocks(
        (), dp_at, received[: len(groups[0])], groups[0], (per_dest, dp_count, rows, TILE)
    )
    state, sent, (served,) = group(
        state=state,
        maxima=[tops, swap(tops, "dp", 1)],
        chunks=0,
        carry=(served,),
        partners=groups[2],
        per_dest=per_dest,
    )
    received += send(sent, groups[2])
    first, count = len(groups[0]), len(groups[0]) + len(groups[1])
    served, token = place_blocks(
        (served,), dp_at, received[first:count], groups[1], served.shape
    )
    latent_served, far_again = place_and_pass(
        expert_at, [near, far], [1, 2], (tops, token), latent_rows, exp_axis
    )
    last = swap(far_again, "expert", 1)
    latent_served, token = place_full(latent_served, expert_at, whole, rest, latent_rows)
    served, expert_scales, latent_scales = collect(
        served,
        dp_at,
        token,
        received,
        groups,
        tiles,
        latent_rows * exp_axis // TILE,
        latent_new.shape[1] // TILE,
    )
    latent_served = finish(latent_served, expert_at, [last], [3], expert_scales)
    expert_served = served.reshape(1, block_count * rows, TILE)

    return (
        state[0][None],
        state[1][None],
        state[2][None],
        expert_served,
        expert_scales,
        latent_new,
        latent_one,
        latent_two,
        latent_served,
        latent_scales,
    )


def body(*args):
    if fast_fits(args[0].shape, args[4].shape, lax.axis_size("dp"), lax.axis_size("expert")):
        return fast_body(*args)
    return general_body(*args)


def solution(mesh):
    placed = (
        P("expert", "dp", None),
        P("expert", "dp", None),
        P("expert", "dp", None),
        P("expert", "dp", None),
        P(("dp", "expert"), None),
        P(("dp", "expert"), None),
        P(("dp", "expert"), None),
        P(("dp", "expert"), None),
        P(),
        P(),
    )
    return jax.shard_map(
        body,
        mesh=mesh,
        in_specs=placed,
        out_specs=(
            P("expert", "dp", None),
            P("expert", "dp", None),
            P("expert", "dp", None),
            P("expert", "dp", None),
            P("expert", "dp"),
            P(("dp", "expert"), None),
            P(("dp", "expert"), None),
            P(("dp", "expert"), None),
            P("dp", None),
            P(),
        ),
        check_vma=False,
    )
```

```python
import functools
import math

import jax
import jax.numpy as jnp
from jax import lax
from jax.experimental import pallas as pl
from jax.experimental.pallas import tpu as pltpu
from jax.sharding import PartitionSpec as P

D = 7168
TILE = 128


BETA_ONE = 0.9
BETA_TWO = 0.95
LEARN_RATE = 0.2
DECAY_RATE = 0.1
ADAM_EPS = 1e-08
SCALE_EPS = 1e-06


def adamw_step(master, moment_one, moment_two, gradient, step_count):
    grad_value = gradient.astype(jnp.float32)
    first_new = BETA_ONE * moment_one.astype(jnp.float32) + (1.0 - BETA_ONE) * grad_value
    second_new = (
        BETA_TWO * moment_two.astype(jnp.float32) + (1.0 - BETA_TWO) * grad_value * grad_value
    )
    step_value = step_count[0].astype(jnp.float32)
    corr_one = 1.0 - jnp.power(jnp.float32(BETA_ONE), step_value)
    corr_two = 1.0 - jnp.power(jnp.float32(BETA_TWO), step_value)
    update = first_new / corr_one / (jnp.sqrt(second_new / corr_two) + ADAM_EPS)
    master_new = master - LEARN_RATE * (update + DECAY_RATE * master)
    return (master_new, first_new.astype(jnp.bfloat16), second_new.astype(jnp.bfloat16))


def row_maxima(weights):
    leading = weights.shape[:-1]
    tile_count = weights.shape[-1] // TILE
    return jnp.max(jnp.abs(weights).reshape(leading + (tile_count, TILE)), axis=-1)


def local_tiles(row_max, lead_rows):
    exp_count, row_count, tile_count = row_max.shape
    tile_span = row_count // TILE + 2
    buffer = jnp.zeros((exp_count, tile_span * TILE, tile_count), jnp.float32)
    buffer = lax.dynamic_update_slice(buffer, row_max, (jnp.int32(0), lead_rows, jnp.int32(0)))
    return jnp.max(buffer.reshape(exp_count, tile_span, TILE, tile_count), axis=2)


def place_tiles(tile_max, first_tile):
    exp_count, tile_span, tile_count = tile_max.shape
    global_map = jnp.zeros((exp_count, D // TILE + tile_span, tile_count), jnp.float32)
    return lax.dynamic_update_slice(global_map, tile_max, (jnp.int32(0), first_tile, jnp.int32(0)))


def quantized_rows(weights, tile_max, lead_rows):
    exp_count, row_count, col_count = weights.shape
    repeated = jnp.repeat(tile_max, TILE, axis=1)
    row_scale = lax.dynamic_slice_in_dim(repeated, lead_rows, row_count, 1)
    blocks = weights.reshape(exp_count, row_count, col_count // TILE, TILE)
    return (blocks / (row_scale[..., None] + SCALE_EPS)).reshape(weights.shape).astype(jnp.bfloat16)


def general_body(
    expert_master,
    expert_first,
    expert_second,
    expert_grad,
    latent_master,
    latent_first,
    latent_second,
    latent_grad,
    step_count,
    column_owner,
):
    master_new, first_new, second_new = adamw_step(
        expert_master, expert_first, expert_second, expert_grad, step_count
    )
    latent_new, latent_one, latent_two = adamw_step(
        latent_master, latent_first, latent_second, latent_grad, step_count
    )
    dp_count = lax.axis_size("dp")
    dp_pos = lax.axis_index("dp")
    exp_count, row_count, col_count = master_new.shape
    block_count = col_count // TILE
    slot_count = max(1, block_count // dp_count)
    total_tiles = D // TILE
    recv_rows = block_count * row_count
    recv_tiles = recv_rows // TILE
    positions = jnp.arange(block_count, dtype=jnp.int32)
    inverse = jnp.sum(
        positions[:, None] * (column_owner[:, None] == positions[None, :]).astype(jnp.int32), axis=0
    )
    receiver_ids = jnp.arange(dp_count, dtype=jnp.int32)[:, None]
    slot_ids = jnp.arange(slot_count, dtype=jnp.int32)[None, :]
    segment = (
        receiver_ids * block_count
        + jnp.mod(dp_pos - receiver_ids * block_count, dp_count)
        + slot_ids * dp_count
    )
    usable_slot = (segment < (receiver_ids + 1) * block_count).reshape(-1)
    send_block = jnp.take(inverse, jnp.minimum(segment // dp_count, block_count - 1)).reshape(-1)
    local_segments = jnp.arange(block_count, dtype=jnp.int32)
    source_dev = jnp.mod(dp_pos * block_count + local_segments, dp_count)
    pick_index = source_dev * slot_count + local_segments // dp_count
    blocks = master_new.reshape(exp_count, row_count, block_count, TILE)
    picked = jnp.take(blocks, send_block, axis=2)
    received = lax.all_to_all(
        jnp.where(usable_slot[None, None, :, None], picked, jnp.zeros((), picked.dtype)),
        "dp",
        split_axis=2,
        concat_axis=2,
        tiled=True,
    )
    ordered = jnp.take(received, pick_index, axis=2)
    tall = (
        jnp.transpose(ordered, (0, 2, 1, 3))
        .reshape(exp_count, recv_rows, TILE)
        .reshape(exp_count, recv_tiles, TILE, TILE)
    )
    expert_scales = jnp.max(jnp.abs(tall), axis=(2, 3))
    expert_served = (
        (tall / (expert_scales[:, :, None, None] + SCALE_EPS))
        .reshape(exp_count, recv_rows, TILE)
        .astype(jnp.bfloat16)
    )
    latent_block = lax.all_gather(latent_new, "expert", axis=0, tiled=True)
    block_rows = latent_block.shape[0]
    block_offset = dp_pos * block_rows
    block_lead = block_offset % TILE
    block_tiles = local_tiles(row_maxima(latent_block)[None], block_lead)
    block_map = lax.pmax(place_tiles(block_tiles, block_offset // TILE), "dp")
    latent_scales = block_map[0, :total_tiles]
    block_tiles = lax.dynamic_slice_in_dim(block_map, block_offset // TILE, block_tiles.shape[1], 1)
    latent_served = quantized_rows(latent_block[None], block_tiles, block_lead)[0]
    return (
        master_new,
        first_new,
        second_new,
        expert_served,
        expert_scales,
        latent_new,
        latent_one,
        latent_two,
        latent_served,
        latent_scales,
    )


CHUNK = 32
EXTRA = 16
MAXIMA_AT = 64
F32 = jnp.float32
BF16 = jnp.bfloat16
VMEM_LIMIT = 56 * 1024 * 1024
ANY = pl.BlockSpec(memory_space=pl.ANY)
SMEM = pl.BlockSpec(memory_space=pltpu.SMEM)
VMEM = pl.BlockSpec(memory_space=pltpu.VMEM)
PARAMS = pltpu.CompilerParams(vmem_limit_bytes=VMEM_LIMIT)
LIGHT = pltpu.CompilerParams(vmem_limit_bytes=1024 * 1024)


def corrections(step_ref):
    one, two = lax.fori_loop(
        0, step_ref[0], lambda _, p: (p[0] * BETA_ONE, p[1] * BETA_TWO), (F32(1.0), F32(1.0))
    )
    rate = LEARN_RATE / (1.0 - jnp.full((1, TILE), one, F32))
    corr = 1.0 / (1.0 - jnp.full((1, TILE), two, F32))
    return rate, corr


def adamw_tile(w, m, v, g, rate, corr):
    g = g.astype(F32)
    m1 = BETA_ONE * m.astype(F32) + (1.0 - BETA_ONE) * g
    v1 = BETA_TWO * v.astype(F32) + (1.0 - BETA_TWO) * g * g
    x = v1 * corr
    inv = pl.reciprocal(x * lax.rsqrt(x) + ADAM_EPS, approx=True)
    w1 = (1.0 - LEARN_RATE * DECAY_RATE) * w - rate * m1 * inv
    return w1, m1.astype(BF16), v1.astype(BF16)


def sub_max(w1):
    return jnp.max(jnp.abs(w1).reshape(w1.shape[0] // 8, 8, TILE), axis=0)


def stack_max(parts):
    parts = parts + [parts[-1]] * (8 - len(parts))
    rows = [jnp.max(p, axis=0, keepdims=True) for p in parts]
    return jnp.max(jnp.concatenate(rows, axis=0), axis=1, keepdims=True)


def three_parts(x):
    high = x.astype(BF16).astype(F32)
    rest = x - high
    middle = rest.astype(BF16).astype(F32)
    return high, middle, rest - middle


def copy_all(copies):
    for c in copies:
        c.start()


def wait_all(copies):
    for c in copies:
        c.wait()


def expert_kernel(
    partners, per_dest, n_alias, n_carry, n_after, chunks, n_maxima,
    owner_ref, pos_ref, line_ref, step_ref, *refs
):
    maxima, refs = refs[:n_maxima], refs[n_maxima:]
    hbm, refs = refs[:4], refs[4 + n_alias + n_carry + n_after :]
    n_dest = len(partners)
    outs, q_refs, served_ref = refs[:3], refs[3 : 3 + n_dest], refs[3 + n_dest]
    w, m, v, g, extra, in_sem, out_sem, extra_sem = refs[-8:]
    bufs = (w, m, v, g)
    blocks = owner_ref.shape[0]
    rows = w.shape[1]
    tiles = rows // TILE
    pos = pos_ref[0]

    loads, stores = [], []
    for d, k in enumerate(partners):
        for j in range(per_dest):
            i = d * per_dest + j
            slot = (pos ^ k) * per_dest + j
            block = jnp.int32(0)
            for b in range(blocks):
                block = jnp.where(owner_ref[b] == slot, b, block)
            cols = pl.ds(pl.multiple_of(block * TILE, TILE), TILE)
            loads.append(
                [
                    pltpu.make_async_copy(hbm[a].at[:, cols], bufs[a].at[i], in_sem.at[i, a])
                    for a in range(4)
                ]
            )
            target = q_refs[d].at[pl.ds(j * rows, rows), :] if k else served_ref.at[j, pos]
            stores.append(
                [
                    pltpu.make_async_copy(bufs[a].at[i], outs[a].at[:, cols], out_sem.at[i, a])
                    for a in range(3)
                ]
                + [pltpu.make_async_copy(g.at[i], target, out_sem.at[i, 3])]
            )
            copy_all(loads[-1])
    rate, corr = corrections(step_ref)
    lane = lax.broadcasted_iota(jnp.int32, (8, TILE), 1)
    if chunks:
        tops_ref, ext = refs[3 + n_dest + n_carry], refs[-9]
        per_tile = TILE // CHUNK
        for s in range(n_maxima):
            peer = lax.rem(line_ref[0] + n_maxima - s, n_maxima)
            ext[pl.ds(peer * chunks, chunks), :] = maxima[s][0:chunks, :]
        tops_ref[...] = jnp.zeros_like(tops_ref)
        for t in range(n_maxima * chunks // per_tile):
            tops_ref[t : t + 1, :] = jnp.max(
                ext[t * per_tile : (t + 1) * per_tile, :], axis=0, keepdims=True
            )
        maxima = (tops_ref,)
    carried = jnp.zeros((8, TILE), F32)
    for p, value in enumerate(three_parts(maxima[0][...])):
        at = MAXIMA_AT + 16 * p
        carried = jnp.where((lane >= at) & (lane < at + 16), pltpu.roll(value, at, 1), carried)
    extras = []
    for d, k in enumerate(partners):
        side = carried
        for j in range(per_dest):
            i = d * per_dest + j
            wait_all(loads[i])
            parts = []
            for t in range(tiles):
                at = pl.ds(t * TILE, TILE)
                w1, m1, v1 = adamw_tile(w[i, at, :], m[i, at, :], v[i, at, :], g[i, at, :], rate, corr)
                w[i, at, :] = w1
                m[i, at, :] = m1
                v[i, at, :] = v1
                parts.append(sub_max(w1))
            copy_all(stores[i][:3])
            top = stack_max(parts)
            inv = 1.0 / (top + SCALE_EPS)
            for t in range(tiles):
                at = pl.ds(t * TILE, TILE)
                g[i, at, :] = (w[i, at, :] * inv[t : t + 1, :]).astype(BF16)
            stores[i][3].start()
            for p, value in enumerate(three_parts(top)):
                side = jnp.where(lane == 3 * j + p, value, side)
        extra[d] = jnp.concatenate([side, jnp.zeros_like(side)], axis=0).astype(BF16)
        first = per_dest * rows if k else 0
        extras.append(
            pltpu.make_async_copy(
                extra.at[d], q_refs[d].at[pl.ds(first, EXTRA), :], extra_sem.at[d]
            )
        )
        extras[-1].start()
    for group in stores:
        wait_all(group)
    wait_all(extras)


def expert_group(
    arrays, state, owner, pos, line, step, maxima, chunks, carry, after, partners, per_dest
):
    rows, cols = arrays[0].shape
    n_alias, n_maxima = len(state), len(maxima)
    n = len(partners) * per_dest
    elems = rows * TILE * n
    flat = [jax.ShapeDtypeStruct((8, TILE), F32)] * (chunks > 0)
    first = 8 + n_maxima
    aliases = {first + i: i for i in range(n_alias)}
    aliases.update({first + n_alias + i: 3 + len(partners) + i for i in range(len(carry))})
    out = pl.pallas_call(
        functools.partial(
            expert_kernel, partners, per_dest, n_alias, len(carry), len(after), chunks, n_maxima
        ),
        in_specs=[SMEM] * 4
        + [VMEM] * n_maxima
        + [ANY] * (4 + n_alias + len(carry) + len(after)),
        out_specs=[ANY] * (3 + len(partners) + len(carry)) + [VMEM] * len(flat),
        out_shape=[
            jax.ShapeDtypeStruct((rows, cols), F32),
            jax.ShapeDtypeStruct((rows, cols), BF16),
            jax.ShapeDtypeStruct((rows, cols), BF16),
        ]
        + [
            jax.ShapeDtypeStruct((per_dest * rows * (k > 0) + EXTRA, TILE), BF16)
            for k in partners
        ]
        + [jax.ShapeDtypeStruct(x.shape, x.dtype) for x in carry]
        + flat,
        scratch_shapes=[
            pltpu.VMEM((32, TILE), F32),
            pltpu.VMEM((n, rows, TILE), F32),
            pltpu.VMEM((n, rows, TILE), BF16),
            pltpu.VMEM((n, rows, TILE), BF16),
            pltpu.VMEM((n, rows, TILE), BF16),
            pltpu.VMEM((len(partners), EXTRA, TILE), BF16),
            pltpu.SemaphoreType.DMA((n, 4)),
            pltpu.SemaphoreType.DMA((n, 4)),
            pltpu.SemaphoreType.DMA((len(partners),)),
        ],
        input_output_aliases=aliases,
        compiler_params=PARAMS,
        cost_estimate=pl.CostEstimate(flops=elems, bytes_accessed=elems, transcendentals=0),
        name="expert_adamw",
    )(owner, pos, line, step, *maxima, *arrays, *state, *carry, *after)
    return out[:3], out[3 : 3 + len(partners)], out[3 + len(partners) :]


def block_copies(served, payloads, srcs, sem):
    per_dest, _, rows, _ = served.shape
    return [
        pltpu.make_async_copy(q.at[pl.ds(j * rows, rows), :], served.at[j, src], sem.at[i, j])
        for i, (q, src) in enumerate(zip(payloads, srcs))
        for j in range(per_dest)
    ]


def place_kernel(partners, pos_ref, *refs):
    n = len(partners)
    served, sem = refs[-2:]
    copies = block_copies(served, refs[:n], [pos_ref[0] ^ k for k in partners], sem)
    copy_all(copies)
    wait_all(copies)


def place_blocks(served, pos, payloads, partners, shape):
    n = len(partners)
    return pl.pallas_call(
        functools.partial(place_kernel, partners),
        in_specs=[SMEM] + [ANY] * (n + len(served)),
        out_specs=ANY,
        out_shape=jax.ShapeDtypeStruct(shape, BF16),
        scratch_shapes=[pltpu.SemaphoreType.DMA((n, shape[0]))],
        input_output_aliases={1 + n: 0} if served else {},
        compiler_params=LIGHT,
        cost_estimate=pl.CostEstimate(
            flops=0, bytes_accessed=4 * n * payloads[0].size, transcendentals=0
        ),
        name="place_served",
    )(pos, *payloads, *served)


def collect_kernel(order, tiles, lat_tiles, to_place, pos_ref, *refs):
    n = len(order)
    q_refs = refs[:n]
    served, _, exp_ref, lat_ref, extra, rows_ref, place_sem, sem = refs[n + 2 :]
    pos = pos_ref[0]
    per_dest = served.shape[0]
    blocks_copies = block_copies(
        served, [q_refs[i] for i in to_place], [pos ^ order[i] for i in to_place], place_sem
    )
    copies = [
        pltpu.make_async_copy(
            q.at[pl.ds(q.shape[0] - EXTRA, EXTRA), :], extra.at[i], sem.at[i]
        )
        for i, q in enumerate(q_refs)
    ]
    copy_all(copies)
    copy_all(blocks_copies)
    rows_ref[...] = jnp.zeros_like(rows_ref)
    flat = jnp.zeros((8, exp_ref.shape[1]), F32)
    wide = lax.broadcasted_iota(jnp.int32, flat.shape, 1)
    deep = lax.broadcasted_iota(jnp.int32, flat.shape, 0)
    for i, k in enumerate(order):
        copies[i].wait()
        src = pos ^ k
        x = extra[i].astype(F32)[0:8, :]
        lat = sum(pltpu.roll(x, TILE - MAXIMA_AT - 16 * p, 1) for p in range(3))
        rows_ref[pl.ds(src * lat_tiles, lat_tiles), :] = lat[0:lat_tiles, :]
        for j in range(per_dest):
            first = 3 * j
            top = x[:, first : first + 1] + x[:, first + 1 : first + 2] + x[:, first + 2 : first + 3]
            hit = (wide == (j * n + src) * tiles + deep) & (deep < tiles)
            flat = jnp.where(hit, top, flat)
    exp_ref[...] = jnp.max(flat, axis=0, keepdims=True)
    blocks, height = lat_ref.shape
    lat_ref[...] = jnp.transpose(rows_ref[...])[0:blocks, 0:height]
    wait_all(blocks_copies)


def collect(served, through, pos, received, groups, tiles, lat_tiles, lat_blocks):
    order = [k for partners in groups for k in partners]
    n = len(order)
    per_dest = served.shape[0]
    to_place = [i for i, k in enumerate(order) if k in groups[2] and k]
    served, through, expert, latent = pl.pallas_call(
        functools.partial(collect_kernel, order, tiles, lat_tiles, to_place),
        in_specs=[SMEM] + [ANY] * (n + 2),
        out_specs=[ANY, ANY, VMEM, VMEM],
        out_shape=[
            jax.ShapeDtypeStruct(served.shape, served.dtype),
            jax.ShapeDtypeStruct(through.shape, through.dtype),
            jax.ShapeDtypeStruct((1, per_dest * n * tiles), F32),
            jax.ShapeDtypeStruct((lat_blocks, n * lat_tiles), F32),
        ],
        scratch_shapes=[
            pltpu.VMEM((n, EXTRA, TILE), BF16),
            pltpu.VMEM((TILE, TILE), F32),
            pltpu.SemaphoreType.DMA((len(to_place), per_dest)),
            pltpu.SemaphoreType.DMA((n,)),
        ],
        input_output_aliases={1 + n: 0, 2 + n: 1},
        compiler_params=LIGHT,
        cost_estimate=pl.CostEstimate(flops=1000000, bytes_accessed=1000000, transcendentals=0),
        name="place_last",
    )(pos, *received, served, through)
    return served, through, expert, latent.T


def finish_kernel(deltas, rows, pos_ref, *refs):
    n = len(deltas)
    latent, buf, in_sem, out_sem = refs[n + 1 :]
    loads = [pltpu.make_async_copy(refs[i], buf.at[i], in_sem.at[i]) for i in range(n)]
    copy_all(loads)
    copies = []
    for i, delta in enumerate(deltas):
        loads[i].wait()
        group = rest_stores(buf, i, pos_ref[0] ^ delta, rows, latent, out_sem)
        copy_all(group)
        copies += group
    wait_all(copies)


def finish(latent, pos, rest, deltas):
    n = len(rest)
    span, cols = rest[0].shape
    return pl.pallas_call(
        functools.partial(finish_kernel, deltas, TILE + span),
        in_specs=[SMEM] + [ANY] * (n + 1),
        out_specs=ANY,
        out_shape=jax.ShapeDtypeStruct(latent.shape, latent.dtype),
        scratch_shapes=[
            pltpu.VMEM((n, span, cols), BF16),
            pltpu.SemaphoreType.DMA((n,)),
            pltpu.SemaphoreType.DMA((n, span // CHUNK)),
        ],
        input_output_aliases={1 + n: 0},
        compiler_params=pltpu.CompilerParams(vmem_limit_bytes=4 * 1024 * 1024),
        cost_estimate=pl.CostEstimate(flops=0, bytes_accessed=1000000, transcendentals=0),
        name="place_finish",
    )(pos, *rest, latent)


def whole_tile(pos, rows):
    return pl.multiple_of(lax.rem(pos * (TILE - rows % TILE), TILE), CHUNK)


def full_kernel(pieces, rows, pos_ref, x_ref, own_ref, *refs):
    out_ref, buf, own, in_sem, out_sem, own_in, own_out = refs[1:]
    loads, stores = [], []
    for i in range(pieces):
        lead = i * (TILE - rows % TILE) % TILE
        at = pl.ds(i * TILE, TILE)
        loads.append(pltpu.make_async_copy(x_ref.at[at, :], buf.at[at, :], in_sem.at[i]))
        stores.append(
            pltpu.make_async_copy(
                buf.at[at, :], out_ref.at[pl.ds(i * rows + lead, TILE), :], out_sem.at[i]
            )
        )
    loads.append(pltpu.make_async_copy(own_ref, own.at[0], own_in.at[0]))
    copy_all(loads)
    for i in range(pieces):
        loads[i].wait()
        stores[i].start()
    loads[pieces].wait()
    rest = rest_stores(own, 0, pos_ref[0], rows, out_ref, own_out)
    copy_all(rest)
    wait_all(stores + rest)


def place_full(out, pos, x, own, rows):
    pieces = x.shape[0] // TILE
    return pl.pallas_call(
        functools.partial(full_kernel, pieces, rows),
        in_specs=[SMEM] + [ANY] * 3,
        out_specs=ANY,
        out_shape=jax.ShapeDtypeStruct((pieces * rows, x.shape[1]), BF16),
        scratch_shapes=[
            pltpu.VMEM(x.shape, BF16),
            pltpu.VMEM((1,) + own.shape, BF16),
            pltpu.SemaphoreType.DMA((pieces,)),
            pltpu.SemaphoreType.DMA((pieces,)),
            pltpu.SemaphoreType.DMA((1,)),
            pltpu.SemaphoreType.DMA((1, own.shape[0] // CHUNK)),
        ],
        input_output_aliases={3: 0},
        compiler_params=PARAMS,
        cost_estimate=pl.CostEstimate(flops=0, bytes_accessed=4 * x.size, transcendentals=0),
        name="place_whole",
    )(pos, x, own, out)


def rest_stores(buf, i, peer, rows, out_ref, sem):
    lead = whole_tile(peer, rows)
    copies = []
    for c in range((rows - TILE) // CHUNK):
        at = peer * rows + c * CHUNK + jnp.where(c * CHUNK < lead, 0, TILE)
        copies.append(
            pltpu.make_async_copy(
                buf.at[i, pl.ds(c * CHUNK, CHUNK), :],
                out_ref.at[pl.ds(pl.multiple_of(at, CHUNK), CHUNK), :],
                sem.at[i, c],
            )
        )
    return copies


def hop_kernel(deltas, rows, pos_ref, *refs):
    n = len(deltas)
    out_ref, again_ref, _, buf, in_sem, out_sem = refs[-6:]
    loads = [pltpu.make_async_copy(refs[i], buf.at[i], in_sem.at[i]) for i in range(n)]
    copy_all(loads)
    copies = [pltpu.make_async_copy(buf.at[n - 1], again_ref, in_sem.at[n])]
    for i in reversed(range(n)):
        loads[i].wait()
        group = rest_stores(buf, i, pos_ref[0] ^ deltas[i], rows, out_ref, out_sem)
        copy_all(copies + group if i == n - 1 else group)
        copies += group
    wait_all(copies)


def place_and_pass(pos, xs, deltas, through, rows, peers):
    span, cols = xs[0].shape
    n = len(xs)
    return pl.pallas_call(
        functools.partial(hop_kernel, deltas, rows),
        in_specs=[SMEM] + [ANY] * (n + 1),
        out_specs=[ANY] * 3,
        out_shape=[
            jax.ShapeDtypeStruct((peers * rows, cols), BF16),
            jax.ShapeDtypeStruct((span, cols), BF16),
            jax.ShapeDtypeStruct(through.shape, through.dtype),
        ],
        input_output_aliases={1 + n: 2},
        scratch_shapes=[
            pltpu.VMEM((n, span, cols), BF16),
            pltpu.SemaphoreType.DMA((n + 1,)),
            pltpu.SemaphoreType.DMA((n, span // CHUNK)),
        ],
        compiler_params=pltpu.CompilerParams(vmem_limit_bytes=4 * 1024 * 1024),
        cost_estimate=pl.CostEstimate(flops=0, bytes_accessed=6 * span * cols, transcendentals=0),
        name="place_hop",
    )(pos, *xs, through)


SLABS = 4


def latent_kernel(chunks, step_ref, pos_ref, *refs):
    hbm, outs, top_ref = refs[:4], refs[4:8], refs[8]
    w, m, v, g, q, in_sem, out_sem = refs[9:]
    bufs = (w, m, v, g)
    width = w.shape[1] // SLABS
    loads, stores = [], []
    for i in range(SLABS):
        cols = pl.ds(i * width, width)
        loads.append(
            [
                pltpu.make_async_copy(hbm[a].at[:, cols], bufs[a].at[:, cols], in_sem.at[i, a])
                for a in range(4)
            ]
        )
        stores.append(
            [
                pltpu.make_async_copy(src.at[:, cols], outs[a].at[:, cols], out_sem.at[i, a])
                for a, src in enumerate((w, m, v, q))
            ]
        )
        copy_all(loads[i])
    rate, corr = corrections(step_ref)
    lane = lax.broadcasted_iota(jnp.int32, (8, TILE), 1)
    lead = whole_tile(pos_ref[0], w.shape[0])
    sub = lax.broadcasted_iota(jnp.int32, (8, 1), 0) * CHUNK
    inside = (sub >= lead) & (sub < lead + TILE)
    tops = jnp.zeros((8, TILE), F32)
    for i in range(SLABS):
        wait_all(loads[i])
        blocks = range(i * width // TILE, (i + 1) * width // TILE)
        slab_tops = []
        for b in blocks:
            cols = pl.ds(b * TILE, TILE)
            w1, m1, v1 = adamw_tile(w[:, cols], m[:, cols], v[:, cols], g[:, cols], rate, corr)
            w[:, cols] = w1
            m[:, cols] = m1
            v[:, cols] = v1
            slab_tops.append(stack_max([sub_max(w1[c * CHUNK : (c + 1) * CHUNK]) for c in range(chunks)]))
        for b, top in zip(blocks, slab_tops):
            cols = pl.ds(b * TILE, TILE)
            tops = jnp.where(lane == b, top, tops)
            whole = jnp.max(jnp.where(inside, top, 0.0), axis=0, keepdims=True)
            q[:, cols] = (w[pl.ds(lead, TILE), cols] * (1.0 / (whole + SCALE_EPS))).astype(BF16)
        copy_all(stores[i])
    top_ref[...] = tops
    for group in stores:
        wait_all(group)


def latent_update(arrays, step, pos):
    rows, cols = arrays[0].shape
    elems = rows * cols
    return pl.pallas_call(
        functools.partial(latent_kernel, rows // CHUNK),
        in_specs=[SMEM] * 2 + [ANY] * 4,
        out_specs=[ANY] * 4 + [VMEM],
        out_shape=[
            jax.ShapeDtypeStruct((rows, cols), F32),
            jax.ShapeDtypeStruct((rows, cols), BF16),
            jax.ShapeDtypeStruct((rows, cols), BF16),
            jax.ShapeDtypeStruct((TILE, cols), BF16),
            jax.ShapeDtypeStruct((8, TILE), F32),
        ],
        scratch_shapes=[
            pltpu.VMEM((rows, cols), F32),
            pltpu.VMEM((rows, cols), BF16),
            pltpu.VMEM((rows, cols), BF16),
            pltpu.VMEM((rows, cols), BF16),
            pltpu.VMEM((TILE, cols), BF16),
            pltpu.SemaphoreType.DMA((SLABS, 4)),
            pltpu.SemaphoreType.DMA((SLABS, 4)),
        ],
        compiler_params=PARAMS,
        cost_estimate=pl.CostEstimate(
            flops=30 * elems, bytes_accessed=18 * elems, transcendentals=2 * elems
        ),
        name="latent_adamw",
    )(step, pos, *arrays)


def latent_rest_kernel(
    chunks, pos_ref, w1_ref, own_ref, prev_ref, next_ref, after_ref, q_ref, w, q, ext, in_sem, out_sem
):
    per_tile = TILE // CHUNK
    rows, cols = w1_ref.shape
    width = cols // SLABS
    lead = whole_tile(pos_ref[0], rows)
    loads, stores = [], []
    for i in range(SLABS):
        at = pl.ds(i * width, width)
        group = []
        for c in range(chunks - per_tile):
            first = pl.multiple_of(c * CHUNK + jnp.where(c * CHUNK < lead, 0, TILE), CHUNK)
            group.append(
                pltpu.make_async_copy(
                    w1_ref.at[pl.ds(first, CHUNK), at],
                    w.at[pl.ds(c * CHUNK, CHUNK), at],
                    in_sem.at[i, c],
                )
            )
        copy_all(group)
        loads.append(group)
        stores.append(pltpu.make_async_copy(q.at[:, at], q_ref.at[:, at], out_sem.at[i]))
    ext[0:chunks, :] = prev_ref[0:chunks, :]
    ext[chunks : 2 * chunks, :] = own_ref[0:chunks, :]
    ext[2 * chunks : 3 * chunks, :] = next_ref[0:chunks, :]
    first = chunks + lead // CHUNK
    above = jnp.max(ext[pl.ds(first - per_tile, per_tile), :], axis=0, keepdims=True)
    below = jnp.max(ext[pl.ds(first + per_tile, per_tile), :], axis=0, keepdims=True)
    both = jnp.concatenate([above] * 4 + [below] * 4, axis=0)
    lane = lax.broadcasted_iota(jnp.int32, (8, TILE), 1)
    tops = [
        jnp.max(jnp.where(lane == b, both, 0.0), axis=1, keepdims=True) for b in range(cols // TILE)
    ]
    invs = [1.0 / (top + SCALE_EPS) for top in tops]
    for i in range(SLABS):
        wait_all(loads[i])
        for b in range(i * width // TILE, (i + 1) * width // TILE):
            at = pl.ds(b * TILE, TILE)
            for c in range(chunks - per_tile):
                span = pl.ds(c * CHUNK, CHUNK)
                inv = jnp.where(c * CHUNK < lead, invs[b][0:1, :], invs[b][4:5, :])
                q[span, at] = (w[span, at] * inv).astype(BF16)
        stores[i].start()
    wait_all(stores)


def latent_rest(w1, own, above, below, pos, after):
    rows, cols = w1.shape
    chunks = rows // CHUNK
    return pl.pallas_call(
        functools.partial(latent_rest_kernel, chunks),
        in_specs=[SMEM, ANY] + [VMEM] * 3 + [ANY],
        out_specs=ANY,
        out_shape=jax.ShapeDtypeStruct((rows - TILE, cols), BF16),
        scratch_shapes=[
            pltpu.VMEM((rows - TILE, cols), F32),
            pltpu.VMEM((rows - TILE, cols), BF16),
            pltpu.VMEM((24, TILE), F32),
            pltpu.SemaphoreType.DMA((SLABS, chunks)),
            pltpu.SemaphoreType.DMA((SLABS,)),
        ],
        compiler_params=PARAMS,
        cost_estimate=pl.CostEstimate(
            flops=rows * cols, bytes_accessed=3 * rows * cols, transcendentals=0
        ),
        name="latent_rest",
    )(pos, w1, own, above, below, after)


def fast_fits(expert_shape, latent_shape, dp_count, exp_axis):
    exp_count, rows, cols = expert_shape
    latent_rows, latent_cols = latent_shape
    return (
        exp_count == 1
        and rows % TILE == 0
        and rows <= 8 * TILE
        and cols % (TILE * dp_count) == 0
        and cols // TILE // dp_count <= 5
        and dp_count == 8
        and dp_count * latent_rows * exp_axis <= TILE * TILE
        and latent_rows % CHUNK == 0
        and 2 * TILE - CHUNK <= latent_rows < 2 * TILE
        and latent_rows * exp_axis % TILE == 0
        and latent_rows * exp_axis <= 8 * TILE
        and exp_axis == 4
        and latent_cols % (SLABS * TILE) == 0
        and latent_cols <= 16 * TILE
    )


def partner_groups(dp_count):
    hops = lambda k: bin(k >> 1).count("1")
    stage = lambda k: 2 if k & 1 and hops(k) < 2 else (3 if k == 0 else hops(k) - 1)
    order = sorted(range(dp_count), key=lambda k: (stage(k), -k))
    return [[k for k in order if stage(k) in n] for n in ((0,), (1,), (2, 3))]


def fast_body(
    expert_master,
    expert_first,
    expert_second,
    expert_grad,
    latent_master,
    latent_first,
    latent_second,
    latent_grad,
    step_count,
    column_owner,
):
    dp_count = lax.axis_size("dp")
    dp_pos = lax.axis_index("dp").astype(jnp.int32)
    exp_axis = lax.axis_size("expert")
    exp_pos = lax.axis_index("expert").astype(jnp.int32)
    _, rows, cols = expert_master.shape
    block_count = cols // TILE
    per_dest = block_count // dp_count
    tiles = rows // TILE

    expert_at, dp_at = exp_pos.reshape(1), dp_pos.reshape(1)
    latent_new, latent_one, latent_two, whole, chunk_top = latent_update(
        (latent_master, latent_first, latent_second, latent_grad), step_count, expert_at
    )
    latent_rows = latent_new.shape[0]
    whole = lax.all_gather(whole, "expert", axis=0, tiled=True)
    maxima = [chunk_top] + [
        lax.ppermute(chunk_top, "expert", [(i, (i + s) % exp_axis) for i in range(exp_axis)])
        for s in range(1, exp_axis)
    ]

    arrays = tuple(
        a.reshape(rows, cols) for a in (expert_master, expert_first, expert_second, expert_grad)
    )
    def swap(x, axis, k):
        return lax.ppermute(x, axis, [(i, i ^ k) for i in range(lax.axis_size(axis))])

    groups = partner_groups(dp_count)
    order = [k for partners in groups for k in partners]
    send = lambda sent, partners: [swap(q, "dp", k) if k else q for k, q in zip(partners, sent)]
    group = functools.partial(
        expert_group,
        arrays,
        owner=column_owner,
        pos=dp_at,
        line=expert_at,
        step=step_count,
        per_dest=per_dest,
    )
    chunks = latent_rows // CHUNK
    state, sent, (tops,) = group(
        state=(), maxima=maxima, chunks=chunks, carry=(), after=(), partners=groups[0]
    )
    received = send(sent, groups[0])
    state, sent, _ = group(
        state=state, maxima=(tops,), chunks=0, carry=(), after=(), partners=groups[1]
    )
    received += send(sent, groups[1])
    rest = latent_rest(latent_new, chunk_top, maxima[1], maxima[-1], expert_at, sent[0])
    far, near = swap(rest, "expert", 2), swap(rest, "expert", 1)
    first, count = len(groups[0]), len(received)
    served = place_blocks(
        (), dp_at, received[:first], groups[0], (per_dest, dp_count, rows, TILE)
    )
    state, sent, (served,) = group(
        state=state,
        maxima=(tops,),
        chunks=0,
        carry=(served,),
        after=(),
        partners=groups[2],
    )
    received += send(sent, groups[2])
    served = place_blocks(
        (served,), dp_at, received[first:count], groups[1], served.shape
    )
    latent_served, far_again, served = place_and_pass(
        expert_at, [near, far], [1, 2], served, latent_rows, exp_axis
    )
    last = swap(far_again, "expert", 1)
    latent_served = place_full(latent_served, expert_at, whole, rest, latent_rows)
    served, latent_served, expert_scales, latent_scales = collect(
        served,
        latent_served,
        dp_at,
        received,
        groups,
        tiles,
        latent_rows * exp_axis // TILE,
        latent_new.shape[1] // TILE,
    )
    latent_served = finish(latent_served, expert_at, [last], [3])
    expert_served = served.reshape(1, block_count * rows, TILE)

    return (
        state[0][None],
        state[1][None],
        state[2][None],
        expert_served,
        expert_scales,
        latent_new,
        latent_one,
        latent_two,
        latent_served,
        latent_scales,
    )


def body(*args):
    if fast_fits(args[0].shape, args[4].shape, lax.axis_size("dp"), lax.axis_size("expert")):
        return fast_body(*args)
    return general_body(*args)


def solution(mesh):
    placed = (
        P("expert", "dp", None),
        P("expert", "dp", None),
        P("expert", "dp", None),
        P("expert", "dp", None),
        P(("dp", "expert"), None),
        P(("dp", "expert"), None),
        P(("dp", "expert"), None),
        P(("dp", "expert"), None),
        P(),
        P(),
    )
    return jax.shard_map(
        body,
        mesh=mesh,
        in_specs=placed,
        out_specs=(
            P("expert", "dp", None),
            P("expert", "dp", None),
            P("expert", "dp", None),
            P("expert", "dp", None),
            P("expert", "dp"),
            P(("dp", "expert"), None),
            P(("dp", "expert"), None),
            P(("dp", "expert"), None),
            P("dp", None),
            P(),
        ),
        check_vma=False,
    )
```

```python
import functools
import math

import jax
import jax.numpy as jnp
from jax import lax
from jax.experimental import pallas as pl
from jax.experimental.pallas import tpu as pltpu
from jax.sharding import PartitionSpec as P

D = 7168
TILE = 128


BETA_ONE = 0.9
BETA_TWO = 0.95
LEARN_RATE = 0.2
DECAY_RATE = 0.1
ADAM_EPS = 1e-08
SCALE_EPS = 1e-06


def adamw_step(master, moment_one, moment_two, gradient, step_count):
    grad_value = gradient.astype(jnp.float32)
    first_new = BETA_ONE * moment_one.astype(jnp.float32) + (1.0 - BETA_ONE) * grad_value
    second_new = (
        BETA_TWO * moment_two.astype(jnp.float32) + (1.0 - BETA_TWO) * grad_value * grad_value
    )
    step_value = step_count[0].astype(jnp.float32)
    corr_one = 1.0 - jnp.power(jnp.float32(BETA_ONE), step_value)
    corr_two = 1.0 - jnp.power(jnp.float32(BETA_TWO), step_value)
    update = first_new / corr_one / (jnp.sqrt(second_new / corr_two) + ADAM_EPS)
    master_new = master - LEARN_RATE * (update + DECAY_RATE * master)
    return (master_new, first_new.astype(jnp.bfloat16), second_new.astype(jnp.bfloat16))


def row_maxima(weights):
    leading = weights.shape[:-1]
    tile_count = weights.shape[-1] // TILE
    return jnp.max(jnp.abs(weights).reshape(leading + (tile_count, TILE)), axis=-1)


def local_tiles(row_max, lead_rows):
    exp_count, row_count, tile_count = row_max.shape
    tile_span = row_count // TILE + 2
    buffer = jnp.zeros((exp_count, tile_span * TILE, tile_count), jnp.float32)
    buffer = lax.dynamic_update_slice(buffer, row_max, (jnp.int32(0), lead_rows, jnp.int32(0)))
    return jnp.max(buffer.reshape(exp_count, tile_span, TILE, tile_count), axis=2)


def place_tiles(tile_max, first_tile):
    exp_count, tile_span, tile_count = tile_max.shape
    global_map = jnp.zeros((exp_count, D // TILE + tile_span, tile_count), jnp.float32)
    return lax.dynamic_update_slice(global_map, tile_max, (jnp.int32(0), first_tile, jnp.int32(0)))


def quantized_rows(weights, tile_max, lead_rows):
    exp_count, row_count, col_count = weights.shape
    repeated = jnp.repeat(tile_max, TILE, axis=1)
    row_scale = lax.dynamic_slice_in_dim(repeated, lead_rows, row_count, 1)
    blocks = weights.reshape(exp_count, row_count, col_count // TILE, TILE)
    return (blocks / (row_scale[..., None] + SCALE_EPS)).reshape(weights.shape).astype(jnp.bfloat16)


def general_body(
    expert_master,
    expert_first,
    expert_second,
    expert_grad,
    latent_master,
    latent_first,
    latent_second,
    latent_grad,
    step_count,
    column_owner,
):
    master_new, first_new, second_new = adamw_step(
        expert_master, expert_first, expert_second, expert_grad, step_count
    )
    latent_new, latent_one, latent_two = adamw_step(
        latent_master, latent_first, latent_second, latent_grad, step_count
    )
    dp_count = lax.axis_size("dp")
    dp_pos = lax.axis_index("dp")
    exp_count, row_count, col_count = master_new.shape
    block_count = col_count // TILE
    slot_count = max(1, block_count // dp_count)
    total_tiles = D // TILE
    recv_rows = block_count * row_count
    recv_tiles = recv_rows // TILE
    positions = jnp.arange(block_count, dtype=jnp.int32)
    inverse = jnp.sum(
        positions[:, None] * (column_owner[:, None] == positions[None, :]).astype(jnp.int32), axis=0
    )
    receiver_ids = jnp.arange(dp_count, dtype=jnp.int32)[:, None]
    slot_ids = jnp.arange(slot_count, dtype=jnp.int32)[None, :]
    segment = (
        receiver_ids * block_count
        + jnp.mod(dp_pos - receiver_ids * block_count, dp_count)
        + slot_ids * dp_count
    )
    usable_slot = (segment < (receiver_ids + 1) * block_count).reshape(-1)
    send_block = jnp.take(inverse, jnp.minimum(segment // dp_count, block_count - 1)).reshape(-1)
    local_segments = jnp.arange(block_count, dtype=jnp.int32)
    source_dev = jnp.mod(dp_pos * block_count + local_segments, dp_count)
    pick_index = source_dev * slot_count + local_segments // dp_count
    blocks = master_new.reshape(exp_count, row_count, block_count, TILE)
    picked = jnp.take(blocks, send_block, axis=2)
    received = lax.all_to_all(
        jnp.where(usable_slot[None, None, :, None], picked, jnp.zeros((), picked.dtype)),
        "dp",
        split_axis=2,
        concat_axis=2,
        tiled=True,
    )
    ordered = jnp.take(received, pick_index, axis=2)
    tall = (
        jnp.transpose(ordered, (0, 2, 1, 3))
        .reshape(exp_count, recv_rows, TILE)
        .reshape(exp_count, recv_tiles, TILE, TILE)
    )
    expert_scales = jnp.max(jnp.abs(tall), axis=(2, 3))
    expert_served = (
        (tall / (expert_scales[:, :, None, None] + SCALE_EPS))
        .reshape(exp_count, recv_rows, TILE)
        .astype(jnp.bfloat16)
    )
    latent_block = lax.all_gather(latent_new, "expert", axis=0, tiled=True)
    block_rows = latent_block.shape[0]
    block_offset = dp_pos * block_rows
    block_lead = block_offset % TILE
    block_tiles = local_tiles(row_maxima(latent_block)[None], block_lead)
    block_map = lax.pmax(place_tiles(block_tiles, block_offset // TILE), "dp")
    latent_scales = block_map[0, :total_tiles]
    block_tiles = lax.dynamic_slice_in_dim(block_map, block_offset // TILE, block_tiles.shape[1], 1)
    latent_served = quantized_rows(latent_block[None], block_tiles, block_lead)[0]
    return (
        master_new,
        first_new,
        second_new,
        expert_served,
        expert_scales,
        latent_new,
        latent_one,
        latent_two,
        latent_served,
        latent_scales,
    )


CHUNK = 32
EXTRA = 16
MAXIMA_AT = 64
F32 = jnp.float32
BF16 = jnp.bfloat16
VMEM_LIMIT = 56 * 1024 * 1024
ANY = pl.BlockSpec(memory_space=pl.ANY)
SMEM = pl.BlockSpec(memory_space=pltpu.SMEM)
VMEM = pl.BlockSpec(memory_space=pltpu.VMEM)
PARAMS = pltpu.CompilerParams(vmem_limit_bytes=VMEM_LIMIT)
LIGHT = pltpu.CompilerParams(vmem_limit_bytes=1024 * 1024)


def corrections(step_ref):
    one, two = lax.fori_loop(
        0, step_ref[0], lambda _, p: (p[0] * BETA_ONE, p[1] * BETA_TWO), (F32(1.0), F32(1.0))
    )
    rate = LEARN_RATE / (1.0 - jnp.full((1, TILE), one, F32))
    corr = 1.0 / (1.0 - jnp.full((1, TILE), two, F32))
    return rate, corr


def adamw_tile(w, m, v, g, rate, corr):
    g = g.astype(F32)
    m1 = BETA_ONE * m.astype(F32) + (1.0 - BETA_ONE) * g
    v1 = BETA_TWO * v.astype(F32) + (1.0 - BETA_TWO) * g * g
    x = v1 * corr
    inv = pl.reciprocal(x * lax.rsqrt(x) + ADAM_EPS, approx=True)
    w1 = (1.0 - LEARN_RATE * DECAY_RATE) * w - rate * m1 * inv
    return w1, m1.astype(BF16), v1.astype(BF16)


def sub_max(w1):
    return jnp.max(jnp.abs(w1).reshape(w1.shape[0] // 8, 8, TILE), axis=0)


def stack_max(parts):
    parts = parts + [parts[-1]] * (8 - len(parts))
    rows = [jnp.max(p, axis=0, keepdims=True) for p in parts]
    return jnp.max(jnp.concatenate(rows, axis=0), axis=1, keepdims=True)


def three_parts(x):
    high = x.astype(BF16).astype(F32)
    rest = x - high
    middle = rest.astype(BF16).astype(F32)
    return high, middle, rest - middle


def copy_all(copies):
    for c in copies:
        c.start()


def wait_all(copies):
    for c in copies:
        c.wait()


def expert_kernel(
    partners, per_dest, n_alias, n_carry, n_after, chunks, n_maxima,
    owner_ref, pos_ref, line_ref, step_ref, *refs
):
    maxima, refs = refs[:n_maxima], refs[n_maxima:]
    hbm, refs = refs[:4], refs[4 + n_alias + n_carry + n_after :]
    n_dest = len(partners)
    outs, q_refs, served_ref = refs[:3], refs[3 : 3 + n_dest], refs[3 + n_dest]
    w, m, v, g, extra, in_sem, out_sem, extra_sem = refs[-8:]
    bufs = (w, m, v, g)
    blocks = owner_ref.shape[0]
    rows = w.shape[1]
    tiles = rows // TILE
    pos = pos_ref[0]

    loads, stores = [], []
    for d, k in enumerate(partners):
        for j in range(per_dest):
            i = d * per_dest + j
            slot = (pos ^ k) * per_dest + j
            block = jnp.int32(0)
            for b in range(blocks):
                block = jnp.where(owner_ref[b] == slot, b, block)
            cols = pl.ds(pl.multiple_of(block * TILE, TILE), TILE)
            loads.append(
                [
                    pltpu.make_async_copy(hbm[a].at[:, cols], bufs[a].at[i], in_sem.at[i, a])
                    for a in range(4)
                ]
            )
            target = q_refs[d].at[pl.ds(j * rows, rows), :] if k else served_ref.at[j, pos]
            stores.append(
                [
                    pltpu.make_async_copy(bufs[a].at[i], outs[a].at[:, cols], out_sem.at[i, a])
                    for a in range(3)
                ]
                + [pltpu.make_async_copy(g.at[i], target, out_sem.at[i, 3])]
            )
            copy_all(loads[-1])
    rate, corr = corrections(step_ref)
    lane = lax.broadcasted_iota(jnp.int32, (8, TILE), 1)
    extras = []
    for d, k in enumerate(partners):
        side = jnp.zeros((8, TILE), F32)
        for j in range(per_dest):
            i = d * per_dest + j
            wait_all(loads[i])
            parts = []
            for t in range(tiles):
                at = pl.ds(t * TILE, TILE)
                w1, m1, v1 = adamw_tile(w[i, at, :], m[i, at, :], v[i, at, :], g[i, at, :], rate, corr)
                w[i, at, :] = w1
                m[i, at, :] = m1
                v[i, at, :] = v1
                parts.append(sub_max(w1))
            copy_all(stores[i][:3])
            top = stack_max(parts)
            inv = 1.0 / (top + SCALE_EPS)
            for t in range(tiles):
                at = pl.ds(t * TILE, TILE)
                g[i, at, :] = (w[i, at, :] * inv[t : t + 1, :]).astype(BF16)
            stores[i][3].start()
            for p, value in enumerate(three_parts(top)):
                side = jnp.where(lane == 3 * j + p, value, side)
        if d == 0:
            if chunks:
                tops_ref, ext = refs[3 + n_dest + n_carry], refs[-9]
                per_tile = TILE // CHUNK
                for s in range(n_maxima):
                    peer = lax.rem(line_ref[0] + n_maxima - s, n_maxima)
                    ext[pl.ds(peer * chunks, chunks), :] = maxima[s][0:chunks, :]
                tops_ref[...] = jnp.zeros_like(tops_ref)
                for t in range(n_maxima * chunks // per_tile):
                    tops_ref[t : t + 1, :] = jnp.max(
                        ext[t * per_tile : (t + 1) * per_tile, :], axis=0, keepdims=True
                    )
                maxima = (tops_ref,)
            carried = jnp.zeros((8, TILE), F32)
            for p, value in enumerate(three_parts(maxima[0][...])):
                at = MAXIMA_AT + 16 * p
                carried = jnp.where((lane >= at) & (lane < at + 16), pltpu.roll(value, at, 1), carried)
        side += carried
        extra[d] = jnp.concatenate([side, jnp.zeros_like(side)], axis=0).astype(BF16)
        first = per_dest * rows if k else 0
        extras.append(
            pltpu.make_async_copy(
                extra.at[d], q_refs[d].at[pl.ds(first, EXTRA), :], extra_sem.at[d]
            )
        )
        extras[-1].start()
    for group in stores:
        wait_all(group)
    wait_all(extras)


def expert_group(
    arrays, state, owner, pos, line, step, maxima, chunks, carry, after, partners, per_dest
):
    rows, cols = arrays[0].shape
    n_alias, n_maxima = len(state), len(maxima)
    n = len(partners) * per_dest
    elems = rows * TILE * n
    flat = [jax.ShapeDtypeStruct((8, TILE), F32)] * (chunks > 0)
    first = 8 + n_maxima
    aliases = {first + i: i for i in range(n_alias)}
    aliases.update({first + n_alias + i: 3 + len(partners) + i for i in range(len(carry))})
    out = pl.pallas_call(
        functools.partial(
            expert_kernel, partners, per_dest, n_alias, len(carry), len(after), chunks, n_maxima
        ),
        in_specs=[SMEM] * 4
        + [VMEM] * n_maxima
        + [ANY] * (4 + n_alias + len(carry) + len(after)),
        out_specs=[ANY] * (3 + len(partners) + len(carry)) + [VMEM] * len(flat),
        out_shape=[
            jax.ShapeDtypeStruct((rows, cols), F32),
            jax.ShapeDtypeStruct((rows, cols), BF16),
            jax.ShapeDtypeStruct((rows, cols), BF16),
        ]
        + [
            jax.ShapeDtypeStruct((per_dest * rows * (k > 0) + EXTRA, TILE), BF16)
            for k in partners
        ]
        + [jax.ShapeDtypeStruct(x.shape, x.dtype) for x in carry]
        + flat,
        scratch_shapes=[
            pltpu.VMEM((32, TILE), F32),
            pltpu.VMEM((n, rows, TILE), F32),
            pltpu.VMEM((n, rows, TILE), BF16),
            pltpu.VMEM((n, rows, TILE), BF16),
            pltpu.VMEM((n, rows, TILE), BF16),
            pltpu.VMEM((len(partners), EXTRA, TILE), BF16),
            pltpu.SemaphoreType.DMA((n, 4)),
            pltpu.SemaphoreType.DMA((n, 4)),
            pltpu.SemaphoreType.DMA((len(partners),)),
        ],
        input_output_aliases=aliases,
        compiler_params=PARAMS,
        cost_estimate=pl.CostEstimate(flops=elems, bytes_accessed=elems, transcendentals=0),
        name="expert_adamw",
    )(owner, pos, line, step, *maxima, *arrays, *state, *carry, *after)
    return out[:3], out[3 : 3 + len(partners)], out[3 + len(partners) :]


def block_copies(served, payloads, srcs, sem):
    per_dest, _, rows, _ = served.shape
    return [
        pltpu.make_async_copy(q.at[pl.ds(j * rows, rows), :], served.at[j, src], sem.at[i, j])
        for i, (q, src) in enumerate(zip(payloads, srcs))
        for j in range(per_dest)
    ]


def place_kernel(partners, pos_ref, *refs):
    n = len(partners)
    served, sem = refs[-2:]
    copies = block_copies(served, refs[:n], [pos_ref[0] ^ k for k in partners], sem)
    copy_all(copies)
    wait_all(copies)


def place_blocks(served, pos, payloads, partners, shape):
    n = len(partners)
    return pl.pallas_call(
        functools.partial(place_kernel, partners),
        in_specs=[SMEM] + [ANY] * (n + len(served)),
        out_specs=ANY,
        out_shape=jax.ShapeDtypeStruct(shape, BF16),
        scratch_shapes=[pltpu.SemaphoreType.DMA((n, shape[0]))],
        input_output_aliases={1 + n: 0} if served else {},
        compiler_params=LIGHT,
        cost_estimate=pl.CostEstimate(
            flops=0, bytes_accessed=4 * n * payloads[0].size, transcendentals=0
        ),
        name="place_served",
    )(pos, *payloads, *served)


def collect_kernel(order, tiles, lat_tiles, to_place, pos_ref, *refs):
    n = len(order)
    q_refs = refs[:n]
    served, _, exp_ref, lat_ref, extra, rows_ref, place_sem, sem = refs[n + 2 :]
    pos = pos_ref[0]
    per_dest = served.shape[0]
    blocks_copies = block_copies(
        served, [q_refs[i] for i in to_place], [pos ^ order[i] for i in to_place], place_sem
    )
    copies = [
        pltpu.make_async_copy(
            q.at[pl.ds(q.shape[0] - EXTRA, EXTRA), :], extra.at[i], sem.at[i]
        )
        for i, q in enumerate(q_refs)
    ]
    copy_all(copies)
    copy_all(blocks_copies)
    rows_ref[...] = jnp.zeros_like(rows_ref)
    flat = jnp.zeros((8, exp_ref.shape[1]), F32)
    wide = lax.broadcasted_iota(jnp.int32, flat.shape, 1)
    deep = lax.broadcasted_iota(jnp.int32, flat.shape, 0)
    for i, k in enumerate(order):
        copies[i].wait()
        src = pos ^ k
        x = extra[i].astype(F32)[0:8, :]
        lat = sum(pltpu.roll(x, TILE - MAXIMA_AT - 16 * p, 1) for p in range(3))
        rows_ref[pl.ds(src * lat_tiles, lat_tiles), :] = lat[0:lat_tiles, :]
        for j in range(per_dest):
            first = 3 * j
            top = x[:, first : first + 1] + x[:, first + 1 : first + 2] + x[:, first + 2 : first + 3]
            hit = (wide == (j * n + src) * tiles + deep) & (deep < tiles)
            flat = jnp.where(hit, top, flat)
    exp_ref[...] = jnp.max(flat, axis=0, keepdims=True)
    blocks, height = lat_ref.shape
    lat_ref[...] = jnp.transpose(rows_ref[...])[0:blocks, 0:height]
    wait_all(blocks_copies)


def collect(served, through, pos, received, groups, tiles, lat_tiles, lat_blocks):
    order = [k for partners in groups for k in partners]
    n = len(order)
    per_dest = served.shape[0]
    to_place = [i for i, k in enumerate(order) if k in groups[2] and k]
    served, through, expert, latent = pl.pallas_call(
        functools.partial(collect_kernel, order, tiles, lat_tiles, to_place),
        in_specs=[SMEM] + [ANY] * (n + 2),
        out_specs=[ANY, ANY, VMEM, VMEM],
        out_shape=[
            jax.ShapeDtypeStruct(served.shape, served.dtype),
            jax.ShapeDtypeStruct(through.shape, through.dtype),
            jax.ShapeDtypeStruct((1, per_dest * n * tiles), F32),
            jax.ShapeDtypeStruct((lat_blocks, n * lat_tiles), F32),
        ],
        scratch_shapes=[
            pltpu.VMEM((n, EXTRA, TILE), BF16),
            pltpu.VMEM((TILE, TILE), F32),
            pltpu.SemaphoreType.DMA((len(to_place), per_dest)),
            pltpu.SemaphoreType.DMA((n,)),
        ],
        input_output_aliases={1 + n: 0, 2 + n: 1},
        compiler_params=LIGHT,
        cost_estimate=pl.CostEstimate(flops=1000000, bytes_accessed=1000000, transcendentals=0),
        name="place_last",
    )(pos, *received, served, through)
    return served, through, expert, latent.T


def rest_kernel(deltas, rows, pos_ref, *refs):
    n = len(deltas)
    latent, buf, in_sem, out_sem = refs[n + 1 :]
    loads = [pltpu.make_async_copy(refs[i], buf.at[i], in_sem.at[i]) for i in range(n)]
    copy_all(loads)
    copies = []
    for i, delta in enumerate(deltas):
        loads[i].wait()
        group = rest_stores(buf, i, pos_ref[0] ^ delta, rows, latent, out_sem)
        copy_all(group)
        copies += group
    wait_all(copies)


def place_rest(latent, pos, rest, deltas):
    n = len(rest)
    span, cols = rest[0].shape
    return pl.pallas_call(
        functools.partial(rest_kernel, deltas, TILE + span),
        in_specs=[SMEM] + [ANY] * (n + 1),
        out_specs=ANY,
        out_shape=jax.ShapeDtypeStruct(latent.shape, latent.dtype),
        scratch_shapes=[
            pltpu.VMEM((n, span, cols), BF16),
            pltpu.SemaphoreType.DMA((n,)),
            pltpu.SemaphoreType.DMA((n, span // CHUNK)),
        ],
        input_output_aliases={1 + n: 0},
        compiler_params=pltpu.CompilerParams(vmem_limit_bytes=4 * 1024 * 1024),
        cost_estimate=pl.CostEstimate(flops=0, bytes_accessed=1000000, transcendentals=0),
        name="place_rest",
    )(pos, *rest, latent)


def whole_tile(pos, rows):
    return pl.multiple_of(lax.rem(pos * (TILE - rows % TILE), TILE), CHUNK)


def full_kernel(pieces, rows, deltas, pos_ref, x_ref, *refs):
    n = len(deltas)
    out_ref, buf, rest, in_sem, out_sem, rest_in, rest_out = refs[n:]
    loads, stores = [], []
    for i in range(pieces):
        lead = i * (TILE - rows % TILE) % TILE
        at = pl.ds(i * TILE, TILE)
        loads.append(pltpu.make_async_copy(x_ref.at[at, :], buf.at[at, :], in_sem.at[i]))
        stores.append(
            pltpu.make_async_copy(
                buf.at[at, :], out_ref.at[pl.ds(i * rows + lead, TILE), :], out_sem.at[i]
            )
        )
    rest_loads = [pltpu.make_async_copy(refs[i], rest.at[i], rest_in.at[i]) for i in range(n)]
    copy_all(loads + rest_loads)
    for i in range(pieces):
        loads[i].wait()
        stores[i].start()
    for i, delta in enumerate(deltas):
        rest_loads[i].wait()
        group = rest_stores(rest, i, pos_ref[0] ^ delta, rows, out_ref, rest_out)
        copy_all(group)
        stores += group
    wait_all(stores)


def place_full(pos, x, xs, deltas, rows):
    pieces, n = x.shape[0] // TILE, len(xs)
    span, cols = xs[0].shape
    return pl.pallas_call(
        functools.partial(full_kernel, pieces, rows, deltas),
        in_specs=[SMEM] + [ANY] * (1 + n),
        out_specs=ANY,
        out_shape=jax.ShapeDtypeStruct((pieces * rows, cols), BF16),
        scratch_shapes=[
            pltpu.VMEM(x.shape, BF16),
            pltpu.VMEM((n, span, cols), BF16),
            pltpu.SemaphoreType.DMA((pieces,)),
            pltpu.SemaphoreType.DMA((pieces,)),
            pltpu.SemaphoreType.DMA((n,)),
            pltpu.SemaphoreType.DMA((n, span // CHUNK)),
        ],
        compiler_params=PARAMS,
        cost_estimate=pl.CostEstimate(flops=0, bytes_accessed=4 * x.size, transcendentals=0),
        name="place_whole",
    )(pos, x, *xs)


def rest_stores(buf, i, peer, rows, out_ref, sem):
    lead = whole_tile(peer, rows)
    copies = []
    for c in range((rows - TILE) // CHUNK):
        at = peer * rows + c * CHUNK + jnp.where(c * CHUNK < lead, 0, TILE)
        copies.append(
            pltpu.make_async_copy(
                buf.at[i, pl.ds(c * CHUNK, CHUNK), :],
                out_ref.at[pl.ds(pl.multiple_of(at, CHUNK), CHUNK), :],
                sem.at[i, c],
            )
        )
    return copies


def in_order(*arrays):
    return pl.pallas_call(
        lambda *refs: None,
        in_specs=[ANY] * len(arrays),
        out_specs=[ANY] * len(arrays),
        out_shape=[jax.ShapeDtypeStruct(x.shape, x.dtype) for x in arrays],
        input_output_aliases={i: i for i in range(len(arrays))},
        compiler_params=pltpu.CompilerParams(vmem_limit_bytes=1024 * 1024),
        cost_estimate=pl.CostEstimate(flops=1, bytes_accessed=1, transcendentals=0),
        name="in_order",
    )(*arrays)


SLABS = 4


def latent_kernel(chunks, step_ref, pos_ref, *refs):
    hbm, outs, top_ref = refs[:4], refs[4:8], refs[8]
    w, m, v, g, q, in_sem, out_sem = refs[9:]
    bufs = (w, m, v, g)
    width = w.shape[1] // SLABS
    loads, stores = [], []
    for i in range(SLABS):
        cols = pl.ds(i * width, width)
        loads.append(
            [
                pltpu.make_async_copy(hbm[a].at[:, cols], bufs[a].at[:, cols], in_sem.at[i, a])
                for a in range(4)
            ]
        )
        stores.append(
            [
                pltpu.make_async_copy(src.at[:, cols], outs[a].at[:, cols], out_sem.at[i, a])
                for a, src in enumerate((w, m, v, q))
            ]
        )
        copy_all(loads[i])
    rate, corr = corrections(step_ref)
    lane = lax.broadcasted_iota(jnp.int32, (8, TILE), 1)
    lead = whole_tile(pos_ref[0], w.shape[0])
    sub = lax.broadcasted_iota(jnp.int32, (8, 1), 0) * CHUNK
    inside = (sub >= lead) & (sub < lead + TILE)
    tops = jnp.zeros((8, TILE), F32)
    for i in range(SLABS):
        wait_all(loads[i])
        blocks = range(i * width // TILE, (i + 1) * width // TILE)
        slab_tops = []
        for b in blocks:
            cols = pl.ds(b * TILE, TILE)
            w1, m1, v1 = adamw_tile(w[:, cols], m[:, cols], v[:, cols], g[:, cols], rate, corr)
            w[:, cols] = w1
            m[:, cols] = m1
            v[:, cols] = v1
            slab_tops.append(stack_max([sub_max(w1[c * CHUNK : (c + 1) * CHUNK]) for c in range(chunks)]))
        for b, top in zip(blocks, slab_tops):
            cols = pl.ds(b * TILE, TILE)
            tops = jnp.where(lane == b, top, tops)
            whole = jnp.max(jnp.where(inside, top, 0.0), axis=0, keepdims=True)
            q[:, cols] = (w[pl.ds(lead, TILE), cols] * (1.0 / (whole + SCALE_EPS))).astype(BF16)
        copy_all(stores[i])
    top_ref[...] = tops
    for group in stores:
        wait_all(group)


def latent_update(arrays, step, pos):
    rows, cols = arrays[0].shape
    elems = rows * cols
    return pl.pallas_call(
        functools.partial(latent_kernel, rows // CHUNK),
        in_specs=[SMEM] * 2 + [ANY] * 4,
        out_specs=[ANY] * 4 + [VMEM],
        out_shape=[
            jax.ShapeDtypeStruct((rows, cols), F32),
            jax.ShapeDtypeStruct((rows, cols), BF16),
            jax.ShapeDtypeStruct((rows, cols), BF16),
            jax.ShapeDtypeStruct((TILE, cols), BF16),
            jax.ShapeDtypeStruct((8, TILE), F32),
        ],
        scratch_shapes=[
            pltpu.VMEM((rows, cols), F32),
            pltpu.VMEM((rows, cols), BF16),
            pltpu.VMEM((rows, cols), BF16),
            pltpu.VMEM((rows, cols), BF16),
            pltpu.VMEM((TILE, cols), BF16),
            pltpu.SemaphoreType.DMA((SLABS, 4)),
            pltpu.SemaphoreType.DMA((SLABS, 4)),
        ],
        compiler_params=PARAMS,
        cost_estimate=pl.CostEstimate(
            flops=30 * elems, bytes_accessed=18 * elems, transcendentals=2 * elems
        ),
        name="latent_adamw",
    )(step, pos, *arrays)


def latent_rest_kernel(
    chunks, pos_ref, w1_ref, own_ref, prev_ref, next_ref, after_ref, q_ref, w, q, ext, in_sem, out_sem
):
    per_tile = TILE // CHUNK
    rows, cols = w1_ref.shape
    width = cols // SLABS
    lead = whole_tile(pos_ref[0], rows)
    loads, stores = [], []
    for i in range(SLABS):
        at = pl.ds(i * width, width)
        group = []
        for c in range(chunks - per_tile):
            first = pl.multiple_of(c * CHUNK + jnp.where(c * CHUNK < lead, 0, TILE), CHUNK)
            group.append(
                pltpu.make_async_copy(
                    w1_ref.at[pl.ds(first, CHUNK), at],
                    w.at[pl.ds(c * CHUNK, CHUNK), at],
                    in_sem.at[i, c],
                )
            )
        copy_all(group)
        loads.append(group)
        stores.append(pltpu.make_async_copy(q.at[:, at], q_ref.at[:, at], out_sem.at[i]))
    ext[0:chunks, :] = prev_ref[0:chunks, :]
    ext[chunks : 2 * chunks, :] = own_ref[0:chunks, :]
    ext[2 * chunks : 3 * chunks, :] = next_ref[0:chunks, :]
    first = chunks + lead // CHUNK
    above = jnp.max(ext[pl.ds(first - per_tile, per_tile), :], axis=0, keepdims=True)
    below = jnp.max(ext[pl.ds(first + per_tile, per_tile), :], axis=0, keepdims=True)
    both = jnp.concatenate([above] * 4 + [below] * 4, axis=0)
    lane = lax.broadcasted_iota(jnp.int32, (8, TILE), 1)
    tops = [
        jnp.max(jnp.where(lane == b, both, 0.0), axis=1, keepdims=True) for b in range(cols // TILE)
    ]
    invs = [1.0 / (top + SCALE_EPS) for top in tops]
    for i in range(SLABS):
        wait_all(loads[i])
        for b in range(i * width // TILE, (i + 1) * width // TILE):
            at = pl.ds(b * TILE, TILE)
            for c in range(chunks - per_tile):
                span = pl.ds(c * CHUNK, CHUNK)
                inv = jnp.where(c * CHUNK < lead, invs[b][0:1, :], invs[b][4:5, :])
                q[span, at] = (w[span, at] * inv).astype(BF16)
        stores[i].start()
    wait_all(stores)


def latent_rest(w1, own, above, below, pos, after):
    rows, cols = w1.shape
    chunks = rows // CHUNK
    return pl.pallas_call(
        functools.partial(latent_rest_kernel, chunks),
        in_specs=[SMEM, ANY] + [VMEM] * 3 + [ANY],
        out_specs=ANY,
        out_shape=jax.ShapeDtypeStruct((rows - TILE, cols), BF16),
        scratch_shapes=[
            pltpu.VMEM((rows - TILE, cols), F32),
            pltpu.VMEM((rows - TILE, cols), BF16),
            pltpu.VMEM((24, TILE), F32),
            pltpu.SemaphoreType.DMA((SLABS, chunks)),
            pltpu.SemaphoreType.DMA((SLABS,)),
        ],
        compiler_params=PARAMS,
        cost_estimate=pl.CostEstimate(
            flops=rows * cols, bytes_accessed=3 * rows * cols, transcendentals=0
        ),
        name="latent_rest",
    )(pos, w1, own, above, below, after)


def fast_fits(expert_shape, latent_shape, dp_count, exp_axis):
    exp_count, rows, cols = expert_shape
    latent_rows, latent_cols = latent_shape
    return (
        exp_count == 1
        and rows % TILE == 0
        and rows <= 8 * TILE
        and cols % (TILE * dp_count) == 0
        and cols // TILE // dp_count <= 5
        and dp_count == 8
        and dp_count * latent_rows * exp_axis <= TILE * TILE
        and latent_rows % CHUNK == 0
        and 2 * TILE - CHUNK <= latent_rows < 2 * TILE
        and latent_rows * exp_axis % TILE == 0
        and latent_rows * exp_axis <= 8 * TILE
        and exp_axis == 4
        and latent_cols % (SLABS * TILE) == 0
        and latent_cols <= 16 * TILE
    )


def partner_groups(dp_count):
    hops = lambda k: bin(k >> 1).count("1")
    stage = lambda k: 2 if k & 1 and hops(k) < 2 else (3 if k == 0 else hops(k) - 1)
    order = sorted(range(dp_count), key=lambda k: (stage(k), -k))
    return [[k for k in order if stage(k) in n] for n in ((0,), (1,), (2, 3))]


def fast_body(
    expert_master,
    expert_first,
    expert_second,
    expert_grad,
    latent_master,
    latent_first,
    latent_second,
    latent_grad,
    step_count,
    column_owner,
):
    dp_count = lax.axis_size("dp")
    dp_pos = lax.axis_index("dp").astype(jnp.int32)
    exp_axis = lax.axis_size("expert")
    exp_pos = lax.axis_index("expert").astype(jnp.int32)
    _, rows, cols = expert_master.shape
    block_count = cols // TILE
    per_dest = block_count // dp_count
    tiles = rows // TILE

    expert_at, dp_at = exp_pos.reshape(1), dp_pos.reshape(1)
    latent_new, latent_one, latent_two, whole, chunk_top = latent_update(
        (latent_master, latent_first, latent_second, latent_grad), step_count, expert_at
    )
    latent_rows = latent_new.shape[0]
    whole = lax.all_gather(whole, "expert", axis=0, tiled=True)
    maxima = [chunk_top] + [
        lax.ppermute(chunk_top, "expert", [(i, (i + s) % exp_axis) for i in range(exp_axis)])
        for s in range(1, exp_axis)
    ]

    arrays = tuple(
        a.reshape(rows, cols) for a in (expert_master, expert_first, expert_second, expert_grad)
    )
    def swap(x, axis, k):
        return lax.ppermute(x, axis, [(i, i ^ k) for i in range(lax.axis_size(axis))])

    groups = partner_groups(dp_count)
    order = [k for partners in groups for k in partners]
    send = lambda sent, partners: [swap(q, "dp", k) if k else q for k, q in zip(partners, sent)]
    group = functools.partial(
        expert_group,
        arrays,
        owner=column_owner,
        pos=dp_at,
        line=expert_at,
        step=step_count,
        per_dest=per_dest,
    )
    chunks = latent_rows // CHUNK
    state, sent, (tops,) = group(
        state=(), maxima=maxima, chunks=chunks, carry=(), after=(), partners=groups[0]
    )
    received = send(sent, groups[0])
    state, sent, _ = group(
        state=state, maxima=(tops,), chunks=0, carry=(), after=(), partners=groups[1]
    )
    received += send(sent, groups[1])
    rest = latent_rest(latent_new, chunk_top, maxima[1], maxima[-1], expert_at, sent[0])
    far, near = swap(rest, "expert", 2), swap(rest, "expert", 1)
    first, count = len(groups[0]), len(received)
    served = place_blocks(
        (), dp_at, received[:first], groups[0], (per_dest, dp_count, rows, TILE)
    )
    state, sent, (served,) = group(
        state=state,
        maxima=(tops,),
        chunks=0,
        carry=(served,),
        after=(),
        partners=groups[2],
    )
    received += send(sent, groups[2])
    served = place_blocks(
        (served,), dp_at, received[first:count], groups[1], served.shape
    )
    near, far, served = in_order(near, far, served)
    last = swap(far, "expert", 1)
    latent_served = place_full(expert_at, whole, [rest], [0], latent_rows)
    latent_served = place_rest(latent_served, expert_at, [near, far], [1, 2])
    served, latent_served, expert_scales, latent_scales = collect(
        served,
        latent_served,
        dp_at,
        received,
        groups,
        tiles,
        latent_rows * exp_axis // TILE,
        latent_new.shape[1] // TILE,
    )
    latent_served = place_rest(latent_served, expert_at, [last], [3])
    expert_served = served.reshape(1, block_count * rows, TILE)

    return (
        state[0][None],
        state[1][None],
        state[2][None],
        expert_served,
        expert_scales,
        latent_new,
        latent_one,
        latent_two,
        latent_served,
        latent_scales,
    )


def body(*args):
    if fast_fits(args[0].shape, args[4].shape, lax.axis_size("dp"), lax.axis_size("expert")):
        return fast_body(*args)
    return general_body(*args)


def solution(mesh):
    placed = (
        P("expert", "dp", None),
        P("expert", "dp", None),
        P("expert", "dp", None),
        P("expert", "dp", None),
        P(("dp", "expert"), None),
        P(("dp", "expert"), None),
        P(("dp", "expert"), None),
        P(("dp", "expert"), None),
        P(),
        P(),
    )
    return jax.shard_map(
        body,
        mesh=mesh,
        in_specs=placed,
        out_specs=(
            P("expert", "dp", None),
            P("expert", "dp", None),
            P("expert", "dp", None),
            P("expert", "dp", None),
            P("expert", "dp"),
            P(("dp", "expert"), None),
            P(("dp", "expert"), None),
            P(("dp", "expert"), None),
            P("dp", None),
            P(),
        ),
        check_vma=False,
    )
```

```python
import functools
import math

import jax
import jax.numpy as jnp
from jax import lax
from jax.experimental import pallas as pl
from jax.experimental.pallas import tpu as pltpu
from jax.sharding import PartitionSpec as P

D = 7168
TILE = 128


BETA_ONE = 0.9
BETA_TWO = 0.95
LEARN_RATE = 0.2
DECAY_RATE = 0.1
ADAM_EPS = 1e-08
SCALE_EPS = 1e-06


def adamw_step(master, moment_one, moment_two, gradient, step_count):
    grad_value = gradient.astype(jnp.float32)
    first_new = BETA_ONE * moment_one.astype(jnp.float32) + (1.0 - BETA_ONE) * grad_value
    second_new = (
        BETA_TWO * moment_two.astype(jnp.float32) + (1.0 - BETA_TWO) * grad_value * grad_value
    )
    step_value = step_count[0].astype(jnp.float32)
    corr_one = 1.0 - jnp.power(jnp.float32(BETA_ONE), step_value)
    corr_two = 1.0 - jnp.power(jnp.float32(BETA_TWO), step_value)
    update = first_new / corr_one / (jnp.sqrt(second_new / corr_two) + ADAM_EPS)
    master_new = master - LEARN_RATE * (update + DECAY_RATE * master)
    return (master_new, first_new.astype(jnp.bfloat16), second_new.astype(jnp.bfloat16))


def row_maxima(weights):
    leading = weights.shape[:-1]
    tile_count = weights.shape[-1] // TILE
    return jnp.max(jnp.abs(weights).reshape(leading + (tile_count, TILE)), axis=-1)


def local_tiles(row_max, lead_rows):
    exp_count, row_count, tile_count = row_max.shape
    tile_span = row_count // TILE + 2
    buffer = jnp.zeros((exp_count, tile_span * TILE, tile_count), jnp.float32)
    buffer = lax.dynamic_update_slice(buffer, row_max, (jnp.int32(0), lead_rows, jnp.int32(0)))
    return jnp.max(buffer.reshape(exp_count, tile_span, TILE, tile_count), axis=2)


def place_tiles(tile_max, first_tile):
    exp_count, tile_span, tile_count = tile_max.shape
    global_map = jnp.zeros((exp_count, D // TILE + tile_span, tile_count), jnp.float32)
    return lax.dynamic_update_slice(global_map, tile_max, (jnp.int32(0), first_tile, jnp.int32(0)))


def quantized_rows(weights, tile_max, lead_rows):
    exp_count, row_count, col_count = weights.shape
    repeated = jnp.repeat(tile_max, TILE, axis=1)
    row_scale = lax.dynamic_slice_in_dim(repeated, lead_rows, row_count, 1)
    blocks = weights.reshape(exp_count, row_count, col_count // TILE, TILE)
    return (blocks / (row_scale[..., None] + SCALE_EPS)).reshape(weights.shape).astype(jnp.bfloat16)


def general_body(
    expert_master,
    expert_first,
    expert_second,
    expert_grad,
    latent_master,
    latent_first,
    latent_second,
    latent_grad,
    step_count,
    column_owner,
):
    master_new, first_new, second_new = adamw_step(
        expert_master, expert_first, expert_second, expert_grad, step_count
    )
    latent_new, latent_one, latent_two = adamw_step(
        latent_master, latent_first, latent_second, latent_grad, step_count
    )
    dp_count = lax.axis_size("dp")
    dp_pos = lax.axis_index("dp")
    exp_count, row_count, col_count = master_new.shape
    block_count = col_count // TILE
    slot_count = max(1, block_count // dp_count)
    total_tiles = D // TILE
    recv_rows = block_count * row_count
    recv_tiles = recv_rows // TILE
    positions = jnp.arange(block_count, dtype=jnp.int32)
    inverse = jnp.sum(
        positions[:, None] * (column_owner[:, None] == positions[None, :]).astype(jnp.int32), axis=0
    )
    receiver_ids = jnp.arange(dp_count, dtype=jnp.int32)[:, None]
    slot_ids = jnp.arange(slot_count, dtype=jnp.int32)[None, :]
    segment = (
        receiver_ids * block_count
        + jnp.mod(dp_pos - receiver_ids * block_count, dp_count)
        + slot_ids * dp_count
    )
    usable_slot = (segment < (receiver_ids + 1) * block_count).reshape(-1)
    send_block = jnp.take(inverse, jnp.minimum(segment // dp_count, block_count - 1)).reshape(-1)
    local_segments = jnp.arange(block_count, dtype=jnp.int32)
    source_dev = jnp.mod(dp_pos * block_count + local_segments, dp_count)
    pick_index = source_dev * slot_count + local_segments // dp_count
    blocks = master_new.reshape(exp_count, row_count, block_count, TILE)
    picked = jnp.take(blocks, send_block, axis=2)
    received = lax.all_to_all(
        jnp.where(usable_slot[None, None, :, None], picked, jnp.zeros((), picked.dtype)),
        "dp",
        split_axis=2,
        concat_axis=2,
        tiled=True,
    )
    ordered = jnp.take(received, pick_index, axis=2)
    tall = (
        jnp.transpose(ordered, (0, 2, 1, 3))
        .reshape(exp_count, recv_rows, TILE)
        .reshape(exp_count, recv_tiles, TILE, TILE)
    )
    expert_scales = jnp.max(jnp.abs(tall), axis=(2, 3))
    expert_served = (
        (tall / (expert_scales[:, :, None, None] + SCALE_EPS))
        .reshape(exp_count, recv_rows, TILE)
        .astype(jnp.bfloat16)
    )
    latent_block = lax.all_gather(latent_new, "expert", axis=0, tiled=True)
    block_rows = latent_block.shape[0]
    block_offset = dp_pos * block_rows
    block_lead = block_offset % TILE
    block_tiles = local_tiles(row_maxima(latent_block)[None], block_lead)
    block_map = lax.pmax(place_tiles(block_tiles, block_offset // TILE), "dp")
    latent_scales = block_map[0, :total_tiles]
    block_tiles = lax.dynamic_slice_in_dim(block_map, block_offset // TILE, block_tiles.shape[1], 1)
    latent_served = quantized_rows(latent_block[None], block_tiles, block_lead)[0]
    return (
        master_new,
        first_new,
        second_new,
        expert_served,
        expert_scales,
        latent_new,
        latent_one,
        latent_two,
        latent_served,
        latent_scales,
    )


CHUNK = 32
EXTRA = 16
MAXIMA_AT = 64
F32 = jnp.float32
BF16 = jnp.bfloat16
VMEM_LIMIT = 56 * 1024 * 1024
ANY = pl.BlockSpec(memory_space=pl.ANY)
SMEM = pl.BlockSpec(memory_space=pltpu.SMEM)
VMEM = pl.BlockSpec(memory_space=pltpu.VMEM)
PARAMS = pltpu.CompilerParams(vmem_limit_bytes=VMEM_LIMIT)
LIGHT = pltpu.CompilerParams(vmem_limit_bytes=4 * 1024 * 1024)


def corrections(step_ref):
    one, two = lax.fori_loop(
        0, step_ref[0], lambda _, p: (p[0] * BETA_ONE, p[1] * BETA_TWO), (F32(1.0), F32(1.0))
    )
    rate = LEARN_RATE / (1.0 - jnp.full((1, TILE), one, F32))
    corr = 1.0 / (1.0 - jnp.full((1, TILE), two, F32))
    return rate, corr


def adamw_tile(w, m, v, g, rate, corr):
    g = g.astype(F32)
    m1 = BETA_ONE * m.astype(F32) + (1.0 - BETA_ONE) * g
    v1 = BETA_TWO * v.astype(F32) + (1.0 - BETA_TWO) * g * g
    x = v1 * corr
    inv = pl.reciprocal(x * lax.rsqrt(x) + ADAM_EPS, approx=True)
    w1 = (1.0 - LEARN_RATE * DECAY_RATE) * w - rate * m1 * inv
    return w1, m1.astype(BF16), v1.astype(BF16)


def sub_max(w1):
    return jnp.max(jnp.abs(w1).reshape(w1.shape[0] // 8, 8, TILE), axis=0)


def stack_max(parts):
    parts = parts + [parts[-1]] * (8 - len(parts))
    rows = [jnp.max(p, axis=0, keepdims=True) for p in parts]
    return jnp.max(jnp.concatenate(rows, axis=0), axis=1, keepdims=True)


def three_parts(x):
    high = x.astype(BF16).astype(F32)
    rest = x - high
    middle = rest.astype(BF16).astype(F32)
    return high, middle, rest - middle


def copy_all(copies):
    for c in copies:
        c.start()


def wait_all(copies):
    for c in copies:
        c.wait()


def expert_kernel(
    partners, per_dest, n_alias, n_carry, n_after, chunks, n_maxima,
    owner_ref, pos_ref, line_ref, step_ref, *refs
):
    maxima, refs = refs[:n_maxima], refs[n_maxima:]
    hbm, refs = refs[:4], refs[4 + n_alias + n_carry + n_after :]
    n_dest = len(partners)
    outs, q_refs, served_ref = refs[:3], refs[3 : 3 + n_dest], refs[3 + n_dest]
    w, m, v, g, extra, in_sem, out_sem, extra_sem = refs[-8:]
    bufs = (w, m, v, g)
    blocks = owner_ref.shape[0]
    rows = w.shape[1]
    tiles = rows // TILE
    pos = pos_ref[0]

    loads, stores = [], []
    for d, k in enumerate(partners):
        for j in range(per_dest):
            i = d * per_dest + j
            slot = (pos ^ k) * per_dest + j
            block = jnp.int32(0)
            for b in range(blocks):
                block = jnp.where(owner_ref[b] == slot, b, block)
            cols = pl.ds(pl.multiple_of(block * TILE, TILE), TILE)
            loads.append(
                [
                    pltpu.make_async_copy(hbm[a].at[:, cols], bufs[a].at[i], in_sem.at[i, a])
                    for a in range(4)
                ]
            )
            target = q_refs[d].at[pl.ds(j * rows, rows), :] if k else served_ref.at[j, pos]
            stores.append(
                [
                    pltpu.make_async_copy(bufs[a].at[i], outs[a].at[:, cols], out_sem.at[i, a])
                    for a in range(3)
                ]
                + [pltpu.make_async_copy(g.at[i], target, out_sem.at[i, 3])]
            )
            copy_all(loads[-1])
    rate, corr = corrections(step_ref)
    lane = lax.broadcasted_iota(jnp.int32, (8, TILE), 1)
    extras = []
    for d, k in enumerate(partners):
        side = jnp.zeros((8, TILE), F32)
        for j in range(per_dest):
            i = d * per_dest + j
            wait_all(loads[i])
            parts = []
            for t in range(tiles):
                at = pl.ds(t * TILE, TILE)
                w1, m1, v1 = adamw_tile(w[i, at, :], m[i, at, :], v[i, at, :], g[i, at, :], rate, corr)
                w[i, at, :] = w1
                m[i, at, :] = m1
                v[i, at, :] = v1
                parts.append(sub_max(w1))
            copy_all(stores[i][:3])
            top = stack_max(parts)
            inv = 1.0 / (top + SCALE_EPS)
            for t in range(tiles):
                at = pl.ds(t * TILE, TILE)
                g[i, at, :] = (w[i, at, :] * inv[t : t + 1, :]).astype(BF16)
            stores[i][3].start()
            for p, value in enumerate(three_parts(top)):
                side = jnp.where(lane == 3 * j + p, value, side)
        if d == 0:
            if chunks:
                tops_ref, ext = refs[3 + n_dest + n_carry], refs[-9]
                per_tile = TILE // CHUNK
                for s in range(n_maxima):
                    peer = lax.rem(line_ref[0] + n_maxima - s, n_maxima)
                    ext[pl.ds(peer * chunks, chunks), :] = maxima[s][0:chunks, :]
                tops_ref[...] = jnp.zeros_like(tops_ref)
                for t in range(n_maxima * chunks // per_tile):
                    tops_ref[t : t + 1, :] = jnp.max(
                        ext[t * per_tile : (t + 1) * per_tile, :], axis=0, keepdims=True
                    )
                maxima = (tops_ref,)
            carried = jnp.zeros((8, TILE), F32)
            for p, value in enumerate(three_parts(maxima[0][...])):
                at = MAXIMA_AT + 16 * p
                carried = jnp.where((lane >= at) & (lane < at + 16), pltpu.roll(value, at, 1), carried)
        side += carried
        extra[d] = jnp.concatenate([side, jnp.zeros_like(side)], axis=0).astype(BF16)
        first = per_dest * rows if k else 0
        extras.append(
            pltpu.make_async_copy(
                extra.at[d], q_refs[d].at[pl.ds(first, EXTRA), :], extra_sem.at[d]
            )
        )
        extras[-1].start()
    for group in stores:
        wait_all(group)
    wait_all(extras)


def expert_group(
    arrays, state, owner, pos, line, step, maxima, chunks, carry, after, partners, per_dest
):
    rows, cols = arrays[0].shape
    n_alias, n_maxima = len(state), len(maxima)
    n = len(partners) * per_dest
    elems = rows * TILE * n
    flat = [jax.ShapeDtypeStruct((8, TILE), F32)] * (chunks > 0)
    first = 8 + n_maxima
    aliases = {first + i: i for i in range(n_alias)}
    aliases.update({first + n_alias + i: 3 + len(partners) + i for i in range(len(carry))})
    out = pl.pallas_call(
        functools.partial(
            expert_kernel, partners, per_dest, n_alias, len(carry), len(after), chunks, n_maxima
        ),
        in_specs=[SMEM] * 4
        + [VMEM] * n_maxima
        + [ANY] * (4 + n_alias + len(carry) + len(after)),
        out_specs=[ANY] * (3 + len(partners) + len(carry)) + [VMEM] * len(flat),
        out_shape=[
            jax.ShapeDtypeStruct((rows, cols), F32),
            jax.ShapeDtypeStruct((rows, cols), BF16),
            jax.ShapeDtypeStruct((rows, cols), BF16),
        ]
        + [
            jax.ShapeDtypeStruct((per_dest * rows * (k > 0) + EXTRA, TILE), BF16)
            for k in partners
        ]
        + [jax.ShapeDtypeStruct(x.shape, x.dtype) for x in carry]
        + flat,
        scratch_shapes=[
            pltpu.VMEM((32, TILE), F32),
            pltpu.VMEM((n, rows, TILE), F32),
            pltpu.VMEM((n, rows, TILE), BF16),
            pltpu.VMEM((n, rows, TILE), BF16),
            pltpu.VMEM((n, rows, TILE), BF16),
            pltpu.VMEM((len(partners), EXTRA, TILE), BF16),
            pltpu.SemaphoreType.DMA((n, 4)),
            pltpu.SemaphoreType.DMA((n, 4)),
            pltpu.SemaphoreType.DMA((len(partners),)),
        ],
        input_output_aliases=aliases,
        compiler_params=PARAMS,
        cost_estimate=pl.CostEstimate(flops=elems, bytes_accessed=elems, transcendentals=0),
        name="expert_adamw",
    )(owner, pos, line, step, *maxima, *arrays, *state, *carry, *after)
    return out[:3], out[3 : 3 + len(partners)], out[3 + len(partners) :]


def load_blocks(payloads, buf, sem):
    return [
        pltpu.make_async_copy(q.at[pl.ds(0, buf.shape[1]), :], buf.at[i], sem.at[i])
        for i, q in enumerate(payloads)
    ]


def store_blocks(served, buf, i, src, sem):
    per_dest, _, rows, _ = served.shape
    return [
        pltpu.make_async_copy(buf.at[i, pl.ds(j * rows, rows), :], served.at[j, src], sem.at[i, j])
        for j in range(per_dest)
    ]


def place_kernel(partners, pos_ref, *refs):
    n = len(partners)
    served, buf, in_sem, out_sem = refs[-4:]
    loads = load_blocks(refs[:n], buf, in_sem)
    copy_all(loads)
    stores = []
    for i, k in enumerate(partners):
        loads[i].wait()
        group = store_blocks(served, buf, i, pos_ref[0] ^ k, out_sem)
        copy_all(group)
        stores += group
    wait_all(stores)


def place_blocks(served, pos, payloads, partners, shape):
    n, per_dest = len(partners), shape[0]
    return pl.pallas_call(
        functools.partial(place_kernel, partners),
        in_specs=[SMEM] + [ANY] * (n + len(served)),
        out_specs=ANY,
        out_shape=jax.ShapeDtypeStruct(shape, BF16),
        scratch_shapes=[
            pltpu.VMEM((n, per_dest * shape[2], TILE), BF16),
            pltpu.SemaphoreType.DMA((n,)),
            pltpu.SemaphoreType.DMA((n, per_dest)),
        ],
        input_output_aliases={1 + n: 0} if served else {},
        compiler_params=LIGHT,
        cost_estimate=pl.CostEstimate(
            flops=0, bytes_accessed=4 * n * payloads[0].size, transcendentals=0
        ),
        name="place_served",
    )(pos, *payloads, *served)


def collect_kernel(order, tiles, lat_tiles, to_place, pos_ref, *refs):
    n = len(order)
    q_refs = refs[:n]
    served, _, exp_ref, lat_ref, extra, rows_ref, buf, in_sem, out_sem, sem = refs[n + 2 :]
    pos = pos_ref[0]
    per_dest = served.shape[0]
    loads = load_blocks([q_refs[i] for i in to_place], buf, in_sem)
    copy_all(loads)
    copies = [
        pltpu.make_async_copy(
            q.at[pl.ds(q.shape[0] - EXTRA, EXTRA), :], extra.at[i], sem.at[i]
        )
        for i, q in enumerate(q_refs)
    ]
    copy_all(copies)
    stores = []
    for i, at in enumerate(to_place):
        loads[i].wait()
        group = store_blocks(served, buf, i, pos ^ order[at], out_sem)
        copy_all(group)
        stores += group
    rows_ref[...] = jnp.zeros_like(rows_ref)
    flat = jnp.zeros((8, exp_ref.shape[1]), F32)
    wide = lax.broadcasted_iota(jnp.int32, flat.shape, 1)
    deep = lax.broadcasted_iota(jnp.int32, flat.shape, 0)
    for i, k in enumerate(order):
        copies[i].wait()
        src = pos ^ k
        x = extra[i].astype(F32)[0:8, :]
        lat = sum(pltpu.roll(x, TILE - MAXIMA_AT - 16 * p, 1) for p in range(3))
        rows_ref[pl.ds(src * lat_tiles, lat_tiles), :] = lat[0:lat_tiles, :]
        for j in range(per_dest):
            first = 3 * j
            top = x[:, first : first + 1] + x[:, first + 1 : first + 2] + x[:, first + 2 : first + 3]
            hit = (wide == (j * n + src) * tiles + deep) & (deep < tiles)
            flat = jnp.where(hit, top, flat)
    exp_ref[...] = jnp.max(flat, axis=0, keepdims=True)
    blocks, height = lat_ref.shape
    lat_ref[...] = jnp.transpose(rows_ref[...])[0:blocks, 0:height]
    wait_all(stores)


def collect(served, through, pos, received, groups, tiles, lat_tiles, lat_blocks):
    order = [k for partners in groups for k in partners]
    n = len(order)
    per_dest = served.shape[0]
    to_place = [i for i, k in enumerate(order) if k in groups[2] and k]
    served, through, expert, latent = pl.pallas_call(
        functools.partial(collect_kernel, order, tiles, lat_tiles, to_place),
        in_specs=[SMEM] + [ANY] * (n + 2),
        out_specs=[ANY, ANY, VMEM, VMEM],
        out_shape=[
            jax.ShapeDtypeStruct(served.shape, served.dtype),
            jax.ShapeDtypeStruct(through.shape, through.dtype),
            jax.ShapeDtypeStruct((1, per_dest * n * tiles), F32),
            jax.ShapeDtypeStruct((lat_blocks, n * lat_tiles), F32),
        ],
        scratch_shapes=[
            pltpu.VMEM((n, EXTRA, TILE), BF16),
            pltpu.VMEM((TILE, TILE), F32),
            pltpu.VMEM((len(to_place), per_dest * served.shape[2], TILE), BF16),
            pltpu.SemaphoreType.DMA((len(to_place),)),
            pltpu.SemaphoreType.DMA((len(to_place), per_dest)),
            pltpu.SemaphoreType.DMA((n,)),
        ],
        input_output_aliases={1 + n: 0, 2 + n: 1},
        compiler_params=LIGHT,
        cost_estimate=pl.CostEstimate(flops=1000000, bytes_accessed=1000000, transcendentals=0),
        name="place_last",
    )(pos, *received, served, through)
    return served, through, expert, latent.T


def rest_kernel(deltas, rows, pos_ref, *refs):
    n = len(deltas)
    latent, buf, in_sem, out_sem = refs[n + 1 :]
    loads = [pltpu.make_async_copy(refs[i], buf.at[i], in_sem.at[i]) for i in range(n)]
    copy_all(loads)
    copies = []
    for i, delta in enumerate(deltas):
        loads[i].wait()
        group = rest_stores(buf, i, pos_ref[0] ^ delta, rows, latent, out_sem)
        copy_all(group)
        copies += group
    wait_all(copies)


def place_rest(latent, pos, rest, deltas):
    n = len(rest)
    span, cols = rest[0].shape
    return pl.pallas_call(
        functools.partial(rest_kernel, deltas, TILE + span),
        in_specs=[SMEM] + [ANY] * (n + 1),
        out_specs=ANY,
        out_shape=jax.ShapeDtypeStruct(latent.shape, latent.dtype),
        scratch_shapes=[
            pltpu.VMEM((n, span, cols), BF16),
            pltpu.SemaphoreType.DMA((n,)),
            pltpu.SemaphoreType.DMA((n, span // CHUNK)),
        ],
        input_output_aliases={1 + n: 0},
        compiler_params=pltpu.CompilerParams(vmem_limit_bytes=4 * 1024 * 1024),
        cost_estimate=pl.CostEstimate(flops=0, bytes_accessed=1000000, transcendentals=0),
        name="place_rest",
    )(pos, *rest, latent)


def whole_tile(pos, rows):
    return pl.multiple_of(lax.rem(pos * (TILE - rows % TILE), TILE), CHUNK)


def full_kernel(pieces, rows, deltas, pos_ref, x_ref, *refs):
    n = len(deltas)
    out_ref, buf, rest, in_sem, out_sem, rest_in, rest_out = refs[n:]
    loads, stores = [], []
    for i in range(pieces):
        lead = i * (TILE - rows % TILE) % TILE
        at = pl.ds(i * TILE, TILE)
        loads.append(pltpu.make_async_copy(x_ref.at[at, :], buf.at[at, :], in_sem.at[i]))
        stores.append(
            pltpu.make_async_copy(
                buf.at[at, :], out_ref.at[pl.ds(i * rows + lead, TILE), :], out_sem.at[i]
            )
        )
    rest_loads = [pltpu.make_async_copy(refs[i], rest.at[i], rest_in.at[i]) for i in range(n)]
    copy_all(loads + rest_loads)
    for i in range(pieces):
        loads[i].wait()
        stores[i].start()
    for i, delta in enumerate(deltas):
        rest_loads[i].wait()
        group = rest_stores(rest, i, pos_ref[0] ^ delta, rows, out_ref, rest_out)
        copy_all(group)
        stores += group
    wait_all(stores)


def place_full(pos, x, xs, deltas, rows):
    pieces, n = x.shape[0] // TILE, len(xs)
    span, cols = xs[0].shape
    return pl.pallas_call(
        functools.partial(full_kernel, pieces, rows, deltas),
        in_specs=[SMEM] + [ANY] * (1 + n),
        out_specs=ANY,
        out_shape=jax.ShapeDtypeStruct((pieces * rows, cols), BF16),
        scratch_shapes=[
            pltpu.VMEM(x.shape, BF16),
            pltpu.VMEM((n, span, cols), BF16),
            pltpu.SemaphoreType.DMA((pieces,)),
            pltpu.SemaphoreType.DMA((pieces,)),
            pltpu.SemaphoreType.DMA((n,)),
            pltpu.SemaphoreType.DMA((n, span // CHUNK)),
        ],
        compiler_params=PARAMS,
        cost_estimate=pl.CostEstimate(flops=0, bytes_accessed=4 * x.size, transcendentals=0),
        name="place_whole",
    )(pos, x, *xs)


def rest_stores(buf, i, peer, rows, out_ref, sem):
    lead = whole_tile(peer, rows)
    copies = []
    for c in range((rows - TILE) // CHUNK):
        at = peer * rows + c * CHUNK + jnp.where(c * CHUNK < lead, 0, TILE)
        copies.append(
            pltpu.make_async_copy(
                buf.at[i, pl.ds(c * CHUNK, CHUNK), :],
                out_ref.at[pl.ds(pl.multiple_of(at, CHUNK), CHUNK), :],
                sem.at[i, c],
            )
        )
    return copies


def in_order(*arrays):
    return pl.pallas_call(
        lambda *refs: None,
        in_specs=[ANY] * len(arrays),
        out_specs=[ANY] * len(arrays),
        out_shape=[jax.ShapeDtypeStruct(x.shape, x.dtype) for x in arrays],
        input_output_aliases={i: i for i in range(len(arrays))},
        compiler_params=pltpu.CompilerParams(vmem_limit_bytes=1024 * 1024),
        cost_estimate=pl.CostEstimate(flops=1, bytes_accessed=1, transcendentals=0),
        name="in_order",
    )(*arrays)


SLABS = 4


def latent_kernel(chunks, step_ref, pos_ref, *refs):
    hbm, outs, top_ref = refs[:4], refs[4:8], refs[8]
    w, m, v, g, q, in_sem, out_sem = refs[9:]
    bufs = (w, m, v, g)
    width = w.shape[1] // SLABS
    loads, stores = [], []
    for i in range(SLABS):
        cols = pl.ds(i * width, width)
        loads.append(
            [
                pltpu.make_async_copy(hbm[a].at[:, cols], bufs[a].at[:, cols], in_sem.at[i, a])
                for a in range(4)
            ]
        )
        stores.append(
            [
                pltpu.make_async_copy(src.at[:, cols], outs[a].at[:, cols], out_sem.at[i, a])
                for a, src in enumerate((w, m, v, q))
            ]
        )
        copy_all(loads[i])
    rate, corr = corrections(step_ref)
    lane = lax.broadcasted_iota(jnp.int32, (8, TILE), 1)
    lead = whole_tile(pos_ref[0], w.shape[0])
    sub = lax.broadcasted_iota(jnp.int32, (8, 1), 0) * CHUNK
    inside = (sub >= lead) & (sub < lead + TILE)
    tops = jnp.zeros((8, TILE), F32)
    for i in range(SLABS):
        wait_all(loads[i])
        blocks = range(i * width // TILE, (i + 1) * width // TILE)
        slab_tops = []
        for b in blocks:
            cols = pl.ds(b * TILE, TILE)
            w1, m1, v1 = adamw_tile(w[:, cols], m[:, cols], v[:, cols], g[:, cols], rate, corr)
            w[:, cols] = w1
            m[:, cols] = m1
            v[:, cols] = v1
            slab_tops.append(stack_max([sub_max(w1[c * CHUNK : (c + 1) * CHUNK]) for c in range(chunks)]))
        for b, top in zip(blocks, slab_tops):
            cols = pl.ds(b * TILE, TILE)
            tops = jnp.where(lane == b, top, tops)
            whole = jnp.max(jnp.where(inside, top, 0.0), axis=0, keepdims=True)
            q[:, cols] = (w[pl.ds(lead, TILE), cols] * (1.0 / (whole + SCALE_EPS))).astype(BF16)
        copy_all(stores[i])
    top_ref[...] = tops
    for group in stores:
        wait_all(group)


def latent_update(arrays, step, pos):
    rows, cols = arrays[0].shape
    elems = rows * cols
    return pl.pallas_call(
        functools.partial(latent_kernel, rows // CHUNK),
        in_specs=[SMEM] * 2 + [ANY] * 4,
        out_specs=[ANY] * 4 + [VMEM],
        out_shape=[
            jax.ShapeDtypeStruct((rows, cols), F32),
            jax.ShapeDtypeStruct((rows, cols), BF16),
            jax.ShapeDtypeStruct((rows, cols), BF16),
            jax.ShapeDtypeStruct((TILE, cols), BF16),
            jax.ShapeDtypeStruct((8, TILE), F32),
        ],
        scratch_shapes=[
            pltpu.VMEM((rows, cols), F32),
            pltpu.VMEM((rows, cols), BF16),
            pltpu.VMEM((rows, cols), BF16),
            pltpu.VMEM((rows, cols), BF16),
            pltpu.VMEM((TILE, cols), BF16),
            pltpu.SemaphoreType.DMA((SLABS, 4)),
            pltpu.SemaphoreType.DMA((SLABS, 4)),
        ],
        compiler_params=PARAMS,
        cost_estimate=pl.CostEstimate(
            flops=30 * elems, bytes_accessed=18 * elems, transcendentals=2 * elems
        ),
        name="latent_adamw",
    )(step, pos, *arrays)


def latent_rest_kernel(
    chunks, pos_ref, w1_ref, own_ref, prev_ref, next_ref, after_ref, q_ref, w, q, ext, in_sem, out_sem
):
    per_tile = TILE // CHUNK
    rows, cols = w1_ref.shape
    width = cols // SLABS
    lead = whole_tile(pos_ref[0], rows)
    loads, stores = [], []
    for i in range(SLABS):
        at = pl.ds(i * width, width)
        group = []
        for c in range(chunks - per_tile):
            first = pl.multiple_of(c * CHUNK + jnp.where(c * CHUNK < lead, 0, TILE), CHUNK)
            group.append(
                pltpu.make_async_copy(
                    w1_ref.at[pl.ds(first, CHUNK), at],
                    w.at[pl.ds(c * CHUNK, CHUNK), at],
                    in_sem.at[i, c],
                )
            )
        copy_all(group)
        loads.append(group)
        stores.append(pltpu.make_async_copy(q.at[:, at], q_ref.at[:, at], out_sem.at[i]))
    ext[0:chunks, :] = prev_ref[0:chunks, :]
    ext[chunks : 2 * chunks, :] = own_ref[0:chunks, :]
    ext[2 * chunks : 3 * chunks, :] = next_ref[0:chunks, :]
    first = chunks + lead // CHUNK
    above = jnp.max(ext[pl.ds(first - per_tile, per_tile), :], axis=0, keepdims=True)
    below = jnp.max(ext[pl.ds(first + per_tile, per_tile), :], axis=0, keepdims=True)
    both = jnp.concatenate([above] * 4 + [below] * 4, axis=0)
    lane = lax.broadcasted_iota(jnp.int32, (8, TILE), 1)
    tops = [
        jnp.max(jnp.where(lane == b, both, 0.0), axis=1, keepdims=True) for b in range(cols // TILE)
    ]
    invs = [1.0 / (top + SCALE_EPS) for top in tops]
    for i in range(SLABS):
        wait_all(loads[i])
        for b in range(i * width // TILE, (i + 1) * width // TILE):
            at = pl.ds(b * TILE, TILE)
            for c in range(chunks - per_tile):
                span = pl.ds(c * CHUNK, CHUNK)
                inv = jnp.where(c * CHUNK < lead, invs[b][0:1, :], invs[b][4:5, :])
                q[span, at] = (w[span, at] * inv).astype(BF16)
        stores[i].start()
    wait_all(stores)


def latent_rest(w1, own, above, below, pos, after):
    rows, cols = w1.shape
    chunks = rows // CHUNK
    return pl.pallas_call(
        functools.partial(latent_rest_kernel, chunks),
        in_specs=[SMEM, ANY] + [VMEM] * 3 + [ANY],
        out_specs=ANY,
        out_shape=jax.ShapeDtypeStruct((rows - TILE, cols), BF16),
        scratch_shapes=[
            pltpu.VMEM((rows - TILE, cols), F32),
            pltpu.VMEM((rows - TILE, cols), BF16),
            pltpu.VMEM((24, TILE), F32),
            pltpu.SemaphoreType.DMA((SLABS, chunks)),
            pltpu.SemaphoreType.DMA((SLABS,)),
        ],
        compiler_params=PARAMS,
        cost_estimate=pl.CostEstimate(
            flops=rows * cols, bytes_accessed=3 * rows * cols, transcendentals=0
        ),
        name="latent_rest",
    )(pos, w1, own, above, below, after)


def fast_fits(expert_shape, latent_shape, dp_count, exp_axis):
    exp_count, rows, cols = expert_shape
    latent_rows, latent_cols = latent_shape
    return (
        exp_count == 1
        and rows % TILE == 0
        and rows <= 8 * TILE
        and cols % (TILE * dp_count) == 0
        and cols // TILE // dp_count <= 5
        and dp_count == 8
        and dp_count * latent_rows * exp_axis <= TILE * TILE
        and latent_rows % CHUNK == 0
        and 2 * TILE - CHUNK <= latent_rows < 2 * TILE
        and latent_rows * exp_axis % TILE == 0
        and latent_rows * exp_axis <= 8 * TILE
        and exp_axis == 4
        and latent_cols % (SLABS * TILE) == 0
        and latent_cols <= 16 * TILE
    )


def partner_groups(dp_count):
    hops = lambda k: bin(k >> 1).count("1")
    stage = lambda k: 2 if k & 1 and hops(k) < 2 else (3 if k == 0 else hops(k) - 1)
    order = sorted(range(dp_count), key=lambda k: (stage(k), -k))
    return [[k for k in order if stage(k) in n] for n in ((0,), (1,), (2, 3))]


def fast_body(
    expert_master,
    expert_first,
    expert_second,
    expert_grad,
    latent_master,
    latent_first,
    latent_second,
    latent_grad,
    step_count,
    column_owner,
):
    dp_count = lax.axis_size("dp")
    dp_pos = lax.axis_index("dp").astype(jnp.int32)
    exp_axis = lax.axis_size("expert")
    exp_pos = lax.axis_index("expert").astype(jnp.int32)
    _, rows, cols = expert_master.shape
    block_count = cols // TILE
    per_dest = block_count // dp_count
    tiles = rows // TILE

    expert_at, dp_at = exp_pos.reshape(1), dp_pos.reshape(1)
    latent_new, latent_one, latent_two, whole, chunk_top = latent_update(
        (latent_master, latent_first, latent_second, latent_grad), step_count, expert_at
    )
    latent_rows = latent_new.shape[0]
    whole = lax.all_gather(whole, "expert", axis=0, tiled=True)
    maxima = [chunk_top] + [
        lax.ppermute(chunk_top, "expert", [(i, (i + s) % exp_axis) for i in range(exp_axis)])
        for s in range(1, exp_axis)
    ]

    arrays = tuple(
        a.reshape(rows, cols) for a in (expert_master, expert_first, expert_second, expert_grad)
    )
    def swap(x, axis, k):
        return lax.ppermute(x, axis, [(i, i ^ k) for i in range(lax.axis_size(axis))])

    groups = partner_groups(dp_count)
    order = [k for partners in groups for k in partners]
    send = lambda sent, partners: [swap(q, "dp", k) if k else q for k, q in zip(partners, sent)]
    group = functools.partial(
        expert_group,
        arrays,
        owner=column_owner,
        pos=dp_at,
        line=expert_at,
        step=step_count,
        per_dest=per_dest,
    )
    chunks = latent_rows // CHUNK
    state, sent, (tops,) = group(
        state=(), maxima=maxima, chunks=chunks, carry=(), after=(), partners=groups[0]
    )
    received = send(sent, groups[0])
    state, sent, _ = group(
        state=state, maxima=(tops,), chunks=0, carry=(), after=(), partners=groups[1]
    )
    received += send(sent, groups[1])
    rest = latent_rest(latent_new, chunk_top, maxima[1], maxima[-1], expert_at, sent[0])
    far, near = swap(rest, "expert", 2), swap(rest, "expert", 1)
    first, count = len(groups[0]), len(received)
    served = place_blocks(
        (), dp_at, received[:first], groups[0], (per_dest, dp_count, rows, TILE)
    )
    state, sent, (served,) = group(
        state=state,
        maxima=(tops,),
        chunks=0,
        carry=(served,),
        after=(),
        partners=groups[2],
    )
    received += send(sent, groups[2])
    served = place_blocks(
        (served,), dp_at, received[first:count], groups[1], served.shape
    )
    near, far, served = in_order(near, far, served)
    last = swap(far, "expert", 1)
    latent_served = place_full(expert_at, whole, [rest], [0], latent_rows)
    latent_served = place_rest(latent_served, expert_at, [near, far], [1, 2])
    served, latent_served, expert_scales, latent_scales = collect(
        served,
        latent_served,
        dp_at,
        received,
        groups,
        tiles,
        latent_rows * exp_axis // TILE,
        latent_new.shape[1] // TILE,
    )
    latent_served = place_rest(latent_served, expert_at, [last], [3])
    expert_served = served.reshape(1, block_count * rows, TILE)

    return (
        state[0][None],
        state[1][None],
        state[2][None],
        expert_served,
        expert_scales,
        latent_new,
        latent_one,
        latent_two,
        latent_served,
        latent_scales,
    )


def body(*args):
    if fast_fits(args[0].shape, args[4].shape, lax.axis_size("dp"), lax.axis_size("expert")):
        return fast_body(*args)
    return general_body(*args)


def solution(mesh):
    placed = (
        P("expert", "dp", None),
        P("expert", "dp", None),
        P("expert", "dp", None),
        P("expert", "dp", None),
        P(("dp", "expert"), None),
        P(("dp", "expert"), None),
        P(("dp", "expert"), None),
        P(("dp", "expert"), None),
        P(),
        P(),
    )
    return jax.shard_map(
        body,
        mesh=mesh,
        in_specs=placed,
        out_specs=(
            P("expert", "dp", None),
            P("expert", "dp", None),
            P("expert", "dp", None),
            P("expert", "dp", None),
            P("expert", "dp"),
            P(("dp", "expert"), None),
            P(("dp", "expert"), None),
            P(("dp", "expert"), None),
            P("dp", None),
            P(),
        ),
        check_vma=False,
    )
```

```python
import functools
import math

import jax
import jax.numpy as jnp
from jax import lax
from jax.experimental import pallas as pl
from jax.experimental.pallas import tpu as pltpu
from jax.sharding import PartitionSpec as P

D = 7168
TILE = 128


BETA_ONE = 0.9
BETA_TWO = 0.95
LEARN_RATE = 0.2
DECAY_RATE = 0.1
ADAM_EPS = 1e-08
SCALE_EPS = 1e-06


def adamw_step(master, moment_one, moment_two, gradient, step_count):
    grad_value = gradient.astype(jnp.float32)
    first_new = BETA_ONE * moment_one.astype(jnp.float32) + (1.0 - BETA_ONE) * grad_value
    second_new = (
        BETA_TWO * moment_two.astype(jnp.float32) + (1.0 - BETA_TWO) * grad_value * grad_value
    )
    step_value = step_count[0].astype(jnp.float32)
    corr_one = 1.0 - jnp.power(jnp.float32(BETA_ONE), step_value)
    corr_two = 1.0 - jnp.power(jnp.float32(BETA_TWO), step_value)
    update = first_new / corr_one / (jnp.sqrt(second_new / corr_two) + ADAM_EPS)
    master_new = master - LEARN_RATE * (update + DECAY_RATE * master)
    return (master_new, first_new.astype(jnp.bfloat16), second_new.astype(jnp.bfloat16))


def row_maxima(weights):
    leading = weights.shape[:-1]
    tile_count = weights.shape[-1] // TILE
    return jnp.max(jnp.abs(weights).reshape(leading + (tile_count, TILE)), axis=-1)


def local_tiles(row_max, lead_rows):
    exp_count, row_count, tile_count = row_max.shape
    tile_span = row_count // TILE + 2
    buffer = jnp.zeros((exp_count, tile_span * TILE, tile_count), jnp.float32)
    buffer = lax.dynamic_update_slice(buffer, row_max, (jnp.int32(0), lead_rows, jnp.int32(0)))
    return jnp.max(buffer.reshape(exp_count, tile_span, TILE, tile_count), axis=2)


def place_tiles(tile_max, first_tile):
    exp_count, tile_span, tile_count = tile_max.shape
    global_map = jnp.zeros((exp_count, D // TILE + tile_span, tile_count), jnp.float32)
    return lax.dynamic_update_slice(global_map, tile_max, (jnp.int32(0), first_tile, jnp.int32(0)))


def quantized_rows(weights, tile_max, lead_rows):
    exp_count, row_count, col_count = weights.shape
    repeated = jnp.repeat(tile_max, TILE, axis=1)
    row_scale = lax.dynamic_slice_in_dim(repeated, lead_rows, row_count, 1)
    blocks = weights.reshape(exp_count, row_count, col_count // TILE, TILE)
    return (blocks / (row_scale[..., None] + SCALE_EPS)).reshape(weights.shape).astype(jnp.bfloat16)


def general_body(
    expert_master,
    expert_first,
    expert_second,
    expert_grad,
    latent_master,
    latent_first,
    latent_second,
    latent_grad,
    step_count,
    column_owner,
):
    master_new, first_new, second_new = adamw_step(
        expert_master, expert_first, expert_second, expert_grad, step_count
    )
    latent_new, latent_one, latent_two = adamw_step(
        latent_master, latent_first, latent_second, latent_grad, step_count
    )
    dp_count = lax.axis_size("dp")
    dp_pos = lax.axis_index("dp")
    exp_count, row_count, col_count = master_new.shape
    block_count = col_count // TILE
    slot_count = max(1, block_count // dp_count)
    total_tiles = D // TILE
    recv_rows = block_count * row_count
    recv_tiles = recv_rows // TILE
    positions = jnp.arange(block_count, dtype=jnp.int32)
    inverse = jnp.sum(
        positions[:, None] * (column_owner[:, None] == positions[None, :]).astype(jnp.int32), axis=0
    )
    receiver_ids = jnp.arange(dp_count, dtype=jnp.int32)[:, None]
    slot_ids = jnp.arange(slot_count, dtype=jnp.int32)[None, :]
    segment = (
        receiver_ids * block_count
        + jnp.mod(dp_pos - receiver_ids * block_count, dp_count)
        + slot_ids * dp_count
    )
    usable_slot = (segment < (receiver_ids + 1) * block_count).reshape(-1)
    send_block = jnp.take(inverse, jnp.minimum(segment // dp_count, block_count - 1)).reshape(-1)
    local_segments = jnp.arange(block_count, dtype=jnp.int32)
    source_dev = jnp.mod(dp_pos * block_count + local_segments, dp_count)
    pick_index = source_dev * slot_count + local_segments // dp_count
    blocks = master_new.reshape(exp_count, row_count, block_count, TILE)
    picked = jnp.take(blocks, send_block, axis=2)
    received = lax.all_to_all(
        jnp.where(usable_slot[None, None, :, None], picked, jnp.zeros((), picked.dtype)),
        "dp",
        split_axis=2,
        concat_axis=2,
        tiled=True,
    )
    ordered = jnp.take(received, pick_index, axis=2)
    tall = (
        jnp.transpose(ordered, (0, 2, 1, 3))
        .reshape(exp_count, recv_rows, TILE)
        .reshape(exp_count, recv_tiles, TILE, TILE)
    )
    expert_scales = jnp.max(jnp.abs(tall), axis=(2, 3))
    expert_served = (
        (tall / (expert_scales[:, :, None, None] + SCALE_EPS))
        .reshape(exp_count, recv_rows, TILE)
        .astype(jnp.bfloat16)
    )
    latent_block = lax.all_gather(latent_new, "expert", axis=0, tiled=True)
    block_rows = latent_block.shape[0]
    block_offset = dp_pos * block_rows
    block_lead = block_offset % TILE
    block_tiles = local_tiles(row_maxima(latent_block)[None], block_lead)
    block_map = lax.pmax(place_tiles(block_tiles, block_offset // TILE), "dp")
    latent_scales = block_map[0, :total_tiles]
    block_tiles = lax.dynamic_slice_in_dim(block_map, block_offset // TILE, block_tiles.shape[1], 1)
    latent_served = quantized_rows(latent_block[None], block_tiles, block_lead)[0]
    return (
        master_new,
        first_new,
        second_new,
        expert_served,
        expert_scales,
        latent_new,
        latent_one,
        latent_two,
        latent_served,
        latent_scales,
    )


CHUNK = 32
EXTRA = 16
MAXIMA_AT = 64
F32 = jnp.float32
BF16 = jnp.bfloat16
VMEM_LIMIT = 56 * 1024 * 1024
ANY = pl.BlockSpec(memory_space=pl.ANY)
SMEM = pl.BlockSpec(memory_space=pltpu.SMEM)
VMEM = pl.BlockSpec(memory_space=pltpu.VMEM)
PARAMS = pltpu.CompilerParams(vmem_limit_bytes=VMEM_LIMIT)
LIGHT = pltpu.CompilerParams(vmem_limit_bytes=1024 * 1024)


def corrections(step_ref):
    one, two = lax.fori_loop(
        0, step_ref[0], lambda _, p: (p[0] * BETA_ONE, p[1] * BETA_TWO), (F32(1.0), F32(1.0))
    )
    rate = LEARN_RATE / (1.0 - jnp.full((1, TILE), one, F32))
    corr = 1.0 / (1.0 - jnp.full((1, TILE), two, F32))
    return rate, corr


def adamw_tile(w, m, v, g, rate, corr):
    g = g.astype(F32)
    m1 = BETA_ONE * m.astype(F32) + (1.0 - BETA_ONE) * g
    v1 = BETA_TWO * v.astype(F32) + (1.0 - BETA_TWO) * g * g
    x = v1 * corr
    inv = pl.reciprocal(x * lax.rsqrt(x) + ADAM_EPS, approx=True)
    w1 = (1.0 - LEARN_RATE * DECAY_RATE) * w - rate * m1 * inv
    return w1, m1.astype(BF16), v1.astype(BF16)


def sub_max(w1):
    return jnp.max(jnp.abs(w1).reshape(w1.shape[0] // 8, 8, TILE), axis=0)


def stack_max(parts):
    parts = parts + [parts[-1]] * (8 - len(parts))
    rows = [jnp.max(p, axis=0, keepdims=True) for p in parts]
    return jnp.max(jnp.concatenate(rows, axis=0), axis=1, keepdims=True)


def three_parts(x):
    high = x.astype(BF16).astype(F32)
    rest = x - high
    middle = rest.astype(BF16).astype(F32)
    return high, middle, rest - middle


def copy_all(copies):
    for c in copies:
        c.start()


def wait_all(copies):
    for c in copies:
        c.wait()


def expert_kernel(
    partners, per_dest, n_alias, n_carry, n_after, chunks, n_maxima,
    owner_ref, pos_ref, line_ref, step_ref, *refs
):
    maxima, refs = refs[:n_maxima], refs[n_maxima:]
    hbm, refs = refs[:4], refs[4 + n_alias + n_carry + n_after :]
    n_dest = len(partners)
    outs, q_refs, served_ref = refs[:3], refs[3 : 3 + n_dest], refs[3 + n_dest]
    w, m, v, g, extra, in_sem, out_sem, extra_sem = refs[-8:]
    bufs = (w, m, v, g)
    blocks = owner_ref.shape[0]
    rows = w.shape[1]
    tiles = rows // TILE
    pos = pos_ref[0]

    loads, stores = [], []
    for d, k in enumerate(partners):
        for j in range(per_dest):
            i = d * per_dest + j
            slot = (pos ^ k) * per_dest + j
            block = jnp.int32(0)
            for b in range(blocks):
                block = jnp.where(owner_ref[b] == slot, b, block)
            cols = pl.ds(pl.multiple_of(block * TILE, TILE), TILE)
            loads.append(
                [
                    pltpu.make_async_copy(hbm[a].at[:, cols], bufs[a].at[i], in_sem.at[i, a])
                    for a in range(4)
                ]
            )
            target = q_refs[d].at[pl.ds(j * rows, rows), :] if k else served_ref.at[j, pos]
            stores.append(
                [
                    pltpu.make_async_copy(bufs[a].at[i], outs[a].at[:, cols], out_sem.at[i, a])
                    for a in range(3)
                ]
                + [pltpu.make_async_copy(g.at[i], target, out_sem.at[i, 3])]
            )
            copy_all(loads[-1])
    rate, corr = corrections(step_ref)
    lane = lax.broadcasted_iota(jnp.int32, (8, TILE), 1)
    extras = []
    for d, k in enumerate(partners):
        side = jnp.zeros((8, TILE), F32)
        for j in range(per_dest):
            i = d * per_dest + j
            wait_all(loads[i])
            parts = []
            for t in range(tiles):
                at = pl.ds(t * TILE, TILE)
                w1, m1, v1 = adamw_tile(w[i, at, :], m[i, at, :], v[i, at, :], g[i, at, :], rate, corr)
                w[i, at, :] = w1
                m[i, at, :] = m1
                v[i, at, :] = v1
                parts.append(sub_max(w1))
            copy_all(stores[i][:3])
            top = stack_max(parts)
            inv = 1.0 / (top + SCALE_EPS)
            for t in range(tiles):
                at = pl.ds(t * TILE, TILE)
                g[i, at, :] = (w[i, at, :] * inv[t : t + 1, :]).astype(BF16)
            stores[i][3].start()
            for p, value in enumerate(three_parts(top)):
                side = jnp.where(lane == 3 * j + p, value, side)
        if d == 0:
            if chunks:
                tops_ref, ext = refs[3 + n_dest + n_carry], refs[-9]
                per_tile = TILE // CHUNK
                for s in range(n_maxima):
                    peer = lax.rem(line_ref[0] + n_maxima - s, n_maxima)
                    ext[pl.ds(peer * chunks, chunks), :] = maxima[s][0:chunks, :]
                tops_ref[...] = jnp.zeros_like(tops_ref)
                for t in range(n_maxima * chunks // per_tile):
                    tops_ref[t : t + 1, :] = jnp.max(
                        ext[t * per_tile : (t + 1) * per_tile, :], axis=0, keepdims=True
                    )
                maxima = (tops_ref,)
            carried = jnp.zeros((8, TILE), F32)
            for p, value in enumerate(three_parts(maxima[0][...])):
                at = MAXIMA_AT + 16 * p
                carried = jnp.where((lane >= at) & (lane < at + 16), pltpu.roll(value, at, 1), carried)
        side += carried
        extra[d] = jnp.concatenate([side, jnp.zeros_like(side)], axis=0).astype(BF16)
        first = per_dest * rows if k else 0
        extras.append(
            pltpu.make_async_copy(
                extra.at[d], q_refs[d].at[pl.ds(first, EXTRA), :], extra_sem.at[d]
            )
        )
        extras[-1].start()
    for group in stores:
        wait_all(group)
    wait_all(extras)


def expert_group(
    arrays, state, owner, pos, line, step, maxima, chunks, carry, after, partners, per_dest
):
    rows, cols = arrays[0].shape
    n_alias, n_maxima = len(state), len(maxima)
    n = len(partners) * per_dest
    elems = rows * TILE * n
    flat = [jax.ShapeDtypeStruct((8, TILE), F32)] * (chunks > 0)
    first = 8 + n_maxima
    aliases = {first + i: i for i in range(n_alias)}
    aliases.update({first + n_alias + i: 3 + len(partners) + i for i in range(len(carry))})
    out = pl.pallas_call(
        functools.partial(
            expert_kernel, partners, per_dest, n_alias, len(carry), len(after), chunks, n_maxima
        ),
        in_specs=[SMEM] * 4
        + [VMEM] * n_maxima
        + [ANY] * (4 + n_alias + len(carry) + len(after)),
        out_specs=[ANY] * (3 + len(partners) + len(carry)) + [VMEM] * len(flat),
        out_shape=[
            jax.ShapeDtypeStruct((rows, cols), F32),
            jax.ShapeDtypeStruct((rows, cols), BF16),
            jax.ShapeDtypeStruct((rows, cols), BF16),
        ]
        + [
            jax.ShapeDtypeStruct((per_dest * rows * (k > 0) + EXTRA, TILE), BF16)
            for k in partners
        ]
        + [jax.ShapeDtypeStruct(x.shape, x.dtype) for x in carry]
        + flat,
        scratch_shapes=[
            pltpu.VMEM((32, TILE), F32),
            pltpu.VMEM((n, rows, TILE), F32),
            pltpu.VMEM((n, rows, TILE), BF16),
            pltpu.VMEM((n, rows, TILE), BF16),
            pltpu.VMEM((n, rows, TILE), BF16),
            pltpu.VMEM((len(partners), EXTRA, TILE), BF16),
            pltpu.SemaphoreType.DMA((n, 4)),
            pltpu.SemaphoreType.DMA((n, 4)),
            pltpu.SemaphoreType.DMA((len(partners),)),
        ],
        input_output_aliases=aliases,
        compiler_params=PARAMS,
        cost_estimate=pl.CostEstimate(flops=elems, bytes_accessed=elems, transcendentals=0),
        name="expert_adamw",
    )(owner, pos, line, step, *maxima, *arrays, *state, *carry, *after)
    return out[:3], out[3 : 3 + len(partners)], out[3 + len(partners) :]


def block_copies(served, payloads, srcs, sem):
    per_dest, _, rows, _ = served.shape
    return [
        pltpu.make_async_copy(q.at[pl.ds(j * rows, rows), :], served.at[j, src], sem.at[i, j])
        for i, (q, src) in enumerate(zip(payloads, srcs))
        for j in range(per_dest)
    ]


def place_kernel(partners, pos_ref, *refs):
    n = len(partners)
    served, sem = refs[-2:]
    copies = block_copies(served, refs[:n], [pos_ref[0] ^ k for k in partners], sem)
    copy_all(copies)
    wait_all(copies)


def place_blocks(served, pos, payloads, partners, shape):
    n = len(partners)
    return pl.pallas_call(
        functools.partial(place_kernel, partners),
        in_specs=[SMEM] + [ANY] * (n + len(served)),
        out_specs=ANY,
        out_shape=jax.ShapeDtypeStruct(shape, BF16),
        scratch_shapes=[pltpu.SemaphoreType.DMA((n, shape[0]))],
        input_output_aliases={1 + n: 0} if served else {},
        compiler_params=LIGHT,
        cost_estimate=pl.CostEstimate(
            flops=0, bytes_accessed=4 * n * payloads[0].size, transcendentals=0
        ),
        name="place_served",
    )(pos, *payloads, *served)


def collect_kernel(order, tiles, lat_tiles, to_place, pos_ref, *refs):
    n = len(order)
    q_refs = refs[:n]
    served, _, exp_ref, lat_ref, extra, rows_ref, place_sem, sem = refs[n + 2 :]
    pos = pos_ref[0]
    per_dest = served.shape[0]
    blocks_copies = block_copies(
        served, [q_refs[i] for i in to_place], [pos ^ order[i] for i in to_place], place_sem
    )
    copies = [
        pltpu.make_async_copy(
            q.at[pl.ds(q.shape[0] - EXTRA, EXTRA), :], extra.at[i], sem.at[i]
        )
        for i, q in enumerate(q_refs)
    ]
    copy_all(copies)
    copy_all(blocks_copies)
    rows_ref[...] = jnp.zeros_like(rows_ref)
    flat = jnp.zeros((8, exp_ref.shape[1]), F32)
    wide = lax.broadcasted_iota(jnp.int32, flat.shape, 1)
    deep = lax.broadcasted_iota(jnp.int32, flat.shape, 0)
    for i, k in enumerate(order):
        copies[i].wait()
        src = pos ^ k
        x = extra[i].astype(F32)[0:8, :]
        lat = sum(pltpu.roll(x, TILE - MAXIMA_AT - 16 * p, 1) for p in range(3))
        rows_ref[pl.ds(src * lat_tiles, lat_tiles), :] = lat[0:lat_tiles, :]
        for j in range(per_dest):
            first = 3 * j
            top = x[:, first : first + 1] + x[:, first + 1 : first + 2] + x[:, first + 2 : first + 3]
            hit = (wide == (j * n + src) * tiles + deep) & (deep < tiles)
            flat = jnp.where(hit, top, flat)
    exp_ref[...] = jnp.max(flat, axis=0, keepdims=True)
    blocks, height = lat_ref.shape
    lat_ref[...] = jnp.transpose(rows_ref[...])[0:blocks, 0:height]
    wait_all(blocks_copies)


def collect(served, through, pos, received, groups, tiles, lat_tiles, lat_blocks):
    order = [k for partners in groups for k in partners]
    n = len(order)
    per_dest = served.shape[0]
    to_place = [i for i, k in enumerate(order) if k in groups[2] and k]
    served, through, expert, latent = pl.pallas_call(
        functools.partial(collect_kernel, order, tiles, lat_tiles, to_place),
        in_specs=[SMEM] + [ANY] * (n + 2),
        out_specs=[ANY, ANY, VMEM, VMEM],
        out_shape=[
            jax.ShapeDtypeStruct(served.shape, served.dtype),
            jax.ShapeDtypeStruct(through.shape, through.dtype),
            jax.ShapeDtypeStruct((1, per_dest * n * tiles), F32),
            jax.ShapeDtypeStruct((lat_blocks, n * lat_tiles), F32),
        ],
        scratch_shapes=[
            pltpu.VMEM((n, EXTRA, TILE), BF16),
            pltpu.VMEM((TILE, TILE), F32),
            pltpu.SemaphoreType.DMA((len(to_place), per_dest)),
            pltpu.SemaphoreType.DMA((n,)),
        ],
        input_output_aliases={1 + n: 0, 2 + n: 1},
        compiler_params=LIGHT,
        cost_estimate=pl.CostEstimate(flops=1000000, bytes_accessed=1000000, transcendentals=0),
        name="place_last",
    )(pos, *received, served, through)
    return served, through, expert, latent.T


def rest_kernel(deltas, rows, pos_ref, *refs):
    n = len(deltas)
    latent, buf, in_sem, out_sem = refs[-4:]
    loads = [pltpu.make_async_copy(refs[i], buf.at[i], in_sem.at[i]) for i in range(n)]
    copy_all(loads)
    copies = []
    for i, delta in enumerate(deltas):
        loads[i].wait()
        group = rest_stores(buf, i, pos_ref[0] ^ delta, rows, latent, out_sem)
        copy_all(group)
        copies += group
    wait_all(copies)


def place_rest(out, pos, rest, deltas, rows, peers):
    n = len(rest)
    span, cols = rest[0].shape
    return pl.pallas_call(
        functools.partial(rest_kernel, deltas, rows),
        in_specs=[SMEM] + [ANY] * (n + len(out)),
        out_specs=ANY,
        out_shape=jax.ShapeDtypeStruct((peers * rows, cols), BF16),
        scratch_shapes=[
            pltpu.VMEM((n, span, cols), BF16),
            pltpu.SemaphoreType.DMA((n,)),
            pltpu.SemaphoreType.DMA((n, span // CHUNK)),
        ],
        input_output_aliases={1 + n: 0} if out else {},
        compiler_params=pltpu.CompilerParams(vmem_limit_bytes=4 * 1024 * 1024),
        cost_estimate=pl.CostEstimate(flops=0, bytes_accessed=1000000, transcendentals=0),
        name="place_rest",
    )(pos, *rest, *out)


def whole_tile(pos, rows):
    return pl.multiple_of(lax.rem(pos * (TILE - rows % TILE), TILE), CHUNK)


def full_kernel(pieces, rows, deltas, pos_ref, x_ref, *refs):
    n = len(deltas)
    out_ref, buf, rest, in_sem, out_sem, rest_in, rest_out = refs[n + 1 :]
    loads, stores = [], []
    for i in range(pieces):
        lead = i * (TILE - rows % TILE) % TILE
        at = pl.ds(i * TILE, TILE)
        loads.append(pltpu.make_async_copy(x_ref.at[at, :], buf.at[at, :], in_sem.at[i]))
        stores.append(
            pltpu.make_async_copy(
                buf.at[at, :], out_ref.at[pl.ds(i * rows + lead, TILE), :], out_sem.at[i]
            )
        )
    rest_loads = [pltpu.make_async_copy(refs[i], rest.at[i], rest_in.at[i]) for i in range(n)]
    copy_all(loads + rest_loads)
    for i in range(pieces):
        loads[i].wait()
        stores[i].start()
    for i, delta in enumerate(deltas):
        rest_loads[i].wait()
        group = rest_stores(rest, i, pos_ref[0] ^ delta, rows, out_ref, rest_out)
        copy_all(group)
        stores += group
    wait_all(stores)


def place_full(out, pos, x, xs, deltas, rows):
    pieces, n = x.shape[0] // TILE, len(xs)
    span, cols = xs[0].shape
    return pl.pallas_call(
        functools.partial(full_kernel, pieces, rows, deltas),
        in_specs=[SMEM] + [ANY] * (2 + n),
        out_specs=ANY,
        out_shape=jax.ShapeDtypeStruct((pieces * rows, cols), BF16),
        scratch_shapes=[
            pltpu.VMEM(x.shape, BF16),
            pltpu.VMEM((n, span, cols), BF16),
            pltpu.SemaphoreType.DMA((pieces,)),
            pltpu.SemaphoreType.DMA((pieces,)),
            pltpu.SemaphoreType.DMA((n,)),
            pltpu.SemaphoreType.DMA((n, span // CHUNK)),
        ],
        input_output_aliases={2 + n: 0},
        compiler_params=PARAMS,
        cost_estimate=pl.CostEstimate(flops=0, bytes_accessed=4 * x.size, transcendentals=0),
        name="place_whole",
    )(pos, x, *xs, out)


def rest_stores(buf, i, peer, rows, out_ref, sem):
    lead = whole_tile(peer, rows)
    copies = []
    for c in range((rows - TILE) // CHUNK):
        at = peer * rows + c * CHUNK + jnp.where(c * CHUNK < lead, 0, TILE)
        copies.append(
            pltpu.make_async_copy(
                buf.at[i, pl.ds(c * CHUNK, CHUNK), :],
                out_ref.at[pl.ds(pl.multiple_of(at, CHUNK), CHUNK), :],
                sem.at[i, c],
            )
        )
    return copies


def in_order(*arrays):
    return pl.pallas_call(
        lambda *refs: None,
        in_specs=[ANY] * len(arrays),
        out_specs=[ANY] * len(arrays),
        out_shape=[jax.ShapeDtypeStruct(x.shape, x.dtype) for x in arrays],
        input_output_aliases={i: i for i in range(len(arrays))},
        compiler_params=pltpu.CompilerParams(vmem_limit_bytes=1024 * 1024),
        cost_estimate=pl.CostEstimate(flops=1, bytes_accessed=1, transcendentals=0),
        name="in_order",
    )(*arrays)


SLABS = 4


def latent_kernel(chunks, step_ref, pos_ref, *refs):
    hbm, outs, top_ref = refs[:4], refs[4:8], refs[8]
    w, m, v, g, q, in_sem, out_sem = refs[9:]
    bufs = (w, m, v, g)
    width = w.shape[1] // SLABS
    loads, stores = [], []
    for i in range(SLABS):
        cols = pl.ds(i * width, width)
        loads.append(
            [
                pltpu.make_async_copy(hbm[a].at[:, cols], bufs[a].at[:, cols], in_sem.at[i, a])
                for a in range(4)
            ]
        )
        stores.append(
            [
                pltpu.make_async_copy(src.at[:, cols], outs[a].at[:, cols], out_sem.at[i, a])
                for a, src in enumerate((w, m, v, q))
            ]
        )
        copy_all(loads[i])
    rate, corr = corrections(step_ref)
    lane = lax.broadcasted_iota(jnp.int32, (8, TILE), 1)
    lead = whole_tile(pos_ref[0], w.shape[0])
    sub = lax.broadcasted_iota(jnp.int32, (8, 1), 0) * CHUNK
    inside = (sub >= lead) & (sub < lead + TILE)
    tops = jnp.zeros((8, TILE), F32)
    for i in range(SLABS):
        wait_all(loads[i])
        blocks = range(i * width // TILE, (i + 1) * width // TILE)
        slab_tops = []
        for b in blocks:
            cols = pl.ds(b * TILE, TILE)
            w1, m1, v1 = adamw_tile(w[:, cols], m[:, cols], v[:, cols], g[:, cols], rate, corr)
            w[:, cols] = w1
            m[:, cols] = m1
            v[:, cols] = v1
            slab_tops.append(stack_max([sub_max(w1[c * CHUNK : (c + 1) * CHUNK]) for c in range(chunks)]))
        for b, top in zip(blocks, slab_tops):
            cols = pl.ds(b * TILE, TILE)
            tops = jnp.where(lane == b, top, tops)
            whole = jnp.max(jnp.where(inside, top, 0.0), axis=0, keepdims=True)
            q[:, cols] = (w[pl.ds(lead, TILE), cols] * (1.0 / (whole + SCALE_EPS))).astype(BF16)
        copy_all(stores[i])
    top_ref[...] = tops
    for group in stores:
        wait_all(group)


def latent_update(arrays, step, pos):
    rows, cols = arrays[0].shape
    elems = rows * cols
    return pl.pallas_call(
        functools.partial(latent_kernel, rows // CHUNK),
        in_specs=[SMEM] * 2 + [ANY] * 4,
        out_specs=[ANY] * 4 + [VMEM],
        out_shape=[
            jax.ShapeDtypeStruct((rows, cols), F32),
            jax.ShapeDtypeStruct((rows, cols), BF16),
            jax.ShapeDtypeStruct((rows, cols), BF16),
            jax.ShapeDtypeStruct((TILE, cols), BF16),
            jax.ShapeDtypeStruct((8, TILE), F32),
        ],
        scratch_shapes=[
            pltpu.VMEM((rows, cols), F32),
            pltpu.VMEM((rows, cols), BF16),
            pltpu.VMEM((rows, cols), BF16),
            pltpu.VMEM((rows, cols), BF16),
            pltpu.VMEM((TILE, cols), BF16),
            pltpu.SemaphoreType.DMA((SLABS, 4)),
            pltpu.SemaphoreType.DMA((SLABS, 4)),
        ],
        compiler_params=PARAMS,
        cost_estimate=pl.CostEstimate(
            flops=30 * elems, bytes_accessed=18 * elems, transcendentals=2 * elems
        ),
        name="latent_adamw",
    )(step, pos, *arrays)


def latent_rest_kernel(
    chunks, pos_ref, w1_ref, own_ref, prev_ref, next_ref, after_ref, q_ref, w, q, ext, in_sem, out_sem
):
    per_tile = TILE // CHUNK
    rows, cols = w1_ref.shape
    width = cols // SLABS
    lead = whole_tile(pos_ref[0], rows)
    loads, stores = [], []
    for i in range(SLABS):
        at = pl.ds(i * width, width)
        group = []
        for c in range(chunks - per_tile):
            first = pl.multiple_of(c * CHUNK + jnp.where(c * CHUNK < lead, 0, TILE), CHUNK)
            group.append(
                pltpu.make_async_copy(
                    w1_ref.at[pl.ds(first, CHUNK), at],
                    w.at[pl.ds(c * CHUNK, CHUNK), at],
                    in_sem.at[i, c],
                )
            )
        copy_all(group)
        loads.append(group)
        stores.append(pltpu.make_async_copy(q.at[:, at], q_ref.at[:, at], out_sem.at[i]))
    ext[0:chunks, :] = prev_ref[0:chunks, :]
    ext[chunks : 2 * chunks, :] = own_ref[0:chunks, :]
    ext[2 * chunks : 3 * chunks, :] = next_ref[0:chunks, :]
    first = chunks + lead // CHUNK
    above = jnp.max(ext[pl.ds(first - per_tile, per_tile), :], axis=0, keepdims=True)
    below = jnp.max(ext[pl.ds(first + per_tile, per_tile), :], axis=0, keepdims=True)
    both = jnp.concatenate([above] * 4 + [below] * 4, axis=0)
    lane = lax.broadcasted_iota(jnp.int32, (8, TILE), 1)
    tops = [
        jnp.max(jnp.where(lane == b, both, 0.0), axis=1, keepdims=True) for b in range(cols // TILE)
    ]
    invs = [1.0 / (top + SCALE_EPS) for top in tops]
    for i in range(SLABS):
        wait_all(loads[i])
        for b in range(i * width // TILE, (i + 1) * width // TILE):
            at = pl.ds(b * TILE, TILE)
            for c in range(chunks - per_tile):
                span = pl.ds(c * CHUNK, CHUNK)
                inv = jnp.where(c * CHUNK < lead, invs[b][0:1, :], invs[b][4:5, :])
                q[span, at] = (w[span, at] * inv).astype(BF16)
        stores[i].start()
    wait_all(stores)


def latent_rest(w1, own, above, below, pos, after):
    rows, cols = w1.shape
    chunks = rows // CHUNK
    return pl.pallas_call(
        functools.partial(latent_rest_kernel, chunks),
        in_specs=[SMEM, ANY] + [VMEM] * 3 + [ANY],
        out_specs=ANY,
        out_shape=jax.ShapeDtypeStruct((rows - TILE, cols), BF16),
        scratch_shapes=[
            pltpu.VMEM((rows - TILE, cols), F32),
            pltpu.VMEM((rows - TILE, cols), BF16),
            pltpu.VMEM((24, TILE), F32),
            pltpu.SemaphoreType.DMA((SLABS, chunks)),
            pltpu.SemaphoreType.DMA((SLABS,)),
        ],
        compiler_params=PARAMS,
        cost_estimate=pl.CostEstimate(
            flops=rows * cols, bytes_accessed=3 * rows * cols, transcendentals=0
        ),
        name="latent_rest",
    )(pos, w1, own, above, below, after)


def fast_fits(expert_shape, latent_shape, dp_count, exp_axis):
    exp_count, rows, cols = expert_shape
    latent_rows, latent_cols = latent_shape
    return (
        exp_count == 1
        and rows % TILE == 0
        and rows <= 8 * TILE
        and cols % (TILE * dp_count) == 0
        and cols // TILE // dp_count <= 5
        and dp_count == 8
        and dp_count * latent_rows * exp_axis <= TILE * TILE
        and latent_rows % CHUNK == 0
        and 2 * TILE - CHUNK <= latent_rows < 2 * TILE
        and latent_rows * exp_axis % TILE == 0
        and latent_rows * exp_axis <= 8 * TILE
        and exp_axis == 4
        and latent_cols % (SLABS * TILE) == 0
        and latent_cols <= 16 * TILE
    )


def partner_groups(dp_count):
    hops = lambda k: bin(k >> 1).count("1")
    stage = lambda k: 2 if k & 1 and hops(k) < 2 else (3 if k == 0 else hops(k) - 1)
    order = sorted(range(dp_count), key=lambda k: (stage(k), -k))
    return [[k for k in order if stage(k) in n] for n in ((0,), (1,), (2, 3))]


def fast_body(
    expert_master,
    expert_first,
    expert_second,
    expert_grad,
    latent_master,
    latent_first,
    latent_second,
    latent_grad,
    step_count,
    column_owner,
):
    dp_count = lax.axis_size("dp")
    dp_pos = lax.axis_index("dp").astype(jnp.int32)
    exp_axis = lax.axis_size("expert")
    exp_pos = lax.axis_index("expert").astype(jnp.int32)
    _, rows, cols = expert_master.shape
    block_count = cols // TILE
    per_dest = block_count // dp_count
    tiles = rows // TILE

    expert_at, dp_at = exp_pos.reshape(1), dp_pos.reshape(1)
    latent_new, latent_one, latent_two, whole, chunk_top = latent_update(
        (latent_master, latent_first, latent_second, latent_grad), step_count, expert_at
    )
    latent_rows = latent_new.shape[0]
    whole = lax.all_gather(whole, "expert", axis=0, tiled=True)
    maxima = [chunk_top] + [
        lax.ppermute(chunk_top, "expert", [(i, (i + s) % exp_axis) for i in range(exp_axis)])
        for s in range(1, exp_axis)
    ]

    arrays = tuple(
        a.reshape(rows, cols) for a in (expert_master, expert_first, expert_second, expert_grad)
    )
    def swap(x, axis, k):
        return lax.ppermute(x, axis, [(i, i ^ k) for i in range(lax.axis_size(axis))])

    groups = partner_groups(dp_count)
    order = [k for partners in groups for k in partners]
    send = lambda sent, partners: [swap(q, "dp", k) if k else q for k, q in zip(partners, sent)]
    group = functools.partial(
        expert_group,
        arrays,
        owner=column_owner,
        pos=dp_at,
        line=expert_at,
        step=step_count,
        per_dest=per_dest,
    )
    chunks = latent_rows // CHUNK
    state, sent, (tops,) = group(
        state=(), maxima=maxima, chunks=chunks, carry=(), after=(), partners=groups[0]
    )
    received = send(sent, groups[0])
    state, sent, _ = group(
        state=state, maxima=(tops,), chunks=0, carry=(), after=(), partners=groups[1]
    )
    received += send(sent, groups[1])
    rest = latent_rest(latent_new, chunk_top, maxima[1], maxima[-1], expert_at, sent[0])
    far, near = swap(rest, "expert", 2), swap(rest, "expert", 1)
    first, count = len(groups[0]), len(received)
    served = place_blocks(
        (), dp_at, received[:first], groups[0], (per_dest, dp_count, rows, TILE)
    )
    state, sent, (served,) = group(
        state=state,
        maxima=(tops,),
        chunks=0,
        carry=(served,),
        after=(),
        partners=groups[2],
    )
    received += send(sent, groups[2])
    served = place_blocks(
        (served,), dp_at, received[first:count], groups[1], served.shape
    )
    near, far, served = in_order(near, far, served)
    last = swap(far, "expert", 1)
    latent_served = place_rest((), expert_at, [near, far], [1, 2], latent_rows, exp_axis)
    latent_served = place_full(latent_served, expert_at, whole, [rest], [0], latent_rows)
    served, latent_served, expert_scales, latent_scales = collect(
        served,
        latent_served,
        dp_at,
        received,
        groups,
        tiles,
        latent_rows * exp_axis // TILE,
        latent_new.shape[1] // TILE,
    )
    latent_served = place_rest(
        (latent_served,), expert_at, [last], [3], latent_rows, exp_axis
    )
    expert_served = served.reshape(1, block_count * rows, TILE)

    return (
        state[0][None],
        state[1][None],
        state[2][None],
        expert_served,
        expert_scales,
        latent_new,
        latent_one,
        latent_two,
        latent_served,
        latent_scales,
    )


def body(*args):
    if fast_fits(args[0].shape, args[4].shape, lax.axis_size("dp"), lax.axis_size("expert")):
        return fast_body(*args)
    return general_body(*args)


def solution(mesh):
    placed = (
        P("expert", "dp", None),
        P("expert", "dp", None),
        P("expert", "dp", None),
        P("expert", "dp", None),
        P(("dp", "expert"), None),
        P(("dp", "expert"), None),
        P(("dp", "expert"), None),
        P(("dp", "expert"), None),
        P(),
        P(),
    )
    return jax.shard_map(
        body,
        mesh=mesh,
        in_specs=placed,
        out_specs=(
            P("expert", "dp", None),
            P("expert", "dp", None),
            P("expert", "dp", None),
            P("expert", "dp", None),
            P("expert", "dp"),
            P(("dp", "expert"), None),
            P(("dp", "expert"), None),
            P(("dp", "expert"), None),
            P("dp", None),
            P(),
        ),
        check_vma=False,
    )
```

```python
import functools
import math

import jax
import jax.numpy as jnp
from jax import lax
from jax.experimental import pallas as pl
from jax.experimental.pallas import tpu as pltpu
from jax.sharding import PartitionSpec as P

D = 7168
TILE = 128


BETA_ONE = 0.9
BETA_TWO = 0.95
LEARN_RATE = 0.2
DECAY_RATE = 0.1
ADAM_EPS = 1e-08
SCALE_EPS = 1e-06


def adamw_step(master, moment_one, moment_two, gradient, step_count):
    grad_value = gradient.astype(jnp.float32)
    first_new = BETA_ONE * moment_one.astype(jnp.float32) + (1.0 - BETA_ONE) * grad_value
    second_new = (
        BETA_TWO * moment_two.astype(jnp.float32) + (1.0 - BETA_TWO) * grad_value * grad_value
    )
    step_value = step_count[0].astype(jnp.float32)
    corr_one = 1.0 - jnp.power(jnp.float32(BETA_ONE), step_value)
    corr_two = 1.0 - jnp.power(jnp.float32(BETA_TWO), step_value)
    update = first_new / corr_one / (jnp.sqrt(second_new / corr_two) + ADAM_EPS)
    master_new = master - LEARN_RATE * (update + DECAY_RATE * master)
    return (master_new, first_new.astype(jnp.bfloat16), second_new.astype(jnp.bfloat16))


def row_maxima(weights):
    leading = weights.shape[:-1]
    tile_count = weights.shape[-1] // TILE
    return jnp.max(jnp.abs(weights).reshape(leading + (tile_count, TILE)), axis=-1)


def local_tiles(row_max, lead_rows):
    exp_count, row_count, tile_count = row_max.shape
    tile_span = row_count // TILE + 2
    buffer = jnp.zeros((exp_count, tile_span * TILE, tile_count), jnp.float32)
    buffer = lax.dynamic_update_slice(buffer, row_max, (jnp.int32(0), lead_rows, jnp.int32(0)))
    return jnp.max(buffer.reshape(exp_count, tile_span, TILE, tile_count), axis=2)


def place_tiles(tile_max, first_tile):
    exp_count, tile_span, tile_count = tile_max.shape
    global_map = jnp.zeros((exp_count, D // TILE + tile_span, tile_count), jnp.float32)
    return lax.dynamic_update_slice(global_map, tile_max, (jnp.int32(0), first_tile, jnp.int32(0)))


def quantized_rows(weights, tile_max, lead_rows):
    exp_count, row_count, col_count = weights.shape
    repeated = jnp.repeat(tile_max, TILE, axis=1)
    row_scale = lax.dynamic_slice_in_dim(repeated, lead_rows, row_count, 1)
    blocks = weights.reshape(exp_count, row_count, col_count // TILE, TILE)
    return (blocks / (row_scale[..., None] + SCALE_EPS)).reshape(weights.shape).astype(jnp.bfloat16)


def general_body(
    expert_master,
    expert_first,
    expert_second,
    expert_grad,
    latent_master,
    latent_first,
    latent_second,
    latent_grad,
    step_count,
    column_owner,
):
    master_new, first_new, second_new = adamw_step(
        expert_master, expert_first, expert_second, expert_grad, step_count
    )
    latent_new, latent_one, latent_two = adamw_step(
        latent_master, latent_first, latent_second, latent_grad, step_count
    )
    dp_count = lax.axis_size("dp")
    dp_pos = lax.axis_index("dp")
    exp_count, row_count, col_count = master_new.shape
    block_count = col_count // TILE
    slot_count = max(1, block_count // dp_count)
    total_tiles = D // TILE
    recv_rows = block_count * row_count
    recv_tiles = recv_rows // TILE
    positions = jnp.arange(block_count, dtype=jnp.int32)
    inverse = jnp.sum(
        positions[:, None] * (column_owner[:, None] == positions[None, :]).astype(jnp.int32), axis=0
    )
    receiver_ids = jnp.arange(dp_count, dtype=jnp.int32)[:, None]
    slot_ids = jnp.arange(slot_count, dtype=jnp.int32)[None, :]
    segment = (
        receiver_ids * block_count
        + jnp.mod(dp_pos - receiver_ids * block_count, dp_count)
        + slot_ids * dp_count
    )
    usable_slot = (segment < (receiver_ids + 1) * block_count).reshape(-1)
    send_block = jnp.take(inverse, jnp.minimum(segment // dp_count, block_count - 1)).reshape(-1)
    local_segments = jnp.arange(block_count, dtype=jnp.int32)
    source_dev = jnp.mod(dp_pos * block_count + local_segments, dp_count)
    pick_index = source_dev * slot_count + local_segments // dp_count
    blocks = master_new.reshape(exp_count, row_count, block_count, TILE)
    picked = jnp.take(blocks, send_block, axis=2)
    received = lax.all_to_all(
        jnp.where(usable_slot[None, None, :, None], picked, jnp.zeros((), picked.dtype)),
        "dp",
        split_axis=2,
        concat_axis=2,
        tiled=True,
    )
    ordered = jnp.take(received, pick_index, axis=2)
    tall = (
        jnp.transpose(ordered, (0, 2, 1, 3))
        .reshape(exp_count, recv_rows, TILE)
        .reshape(exp_count, recv_tiles, TILE, TILE)
    )
    expert_scales = jnp.max(jnp.abs(tall), axis=(2, 3))
    expert_served = (
        (tall / (expert_scales[:, :, None, None] + SCALE_EPS))
        .reshape(exp_count, recv_rows, TILE)
        .astype(jnp.bfloat16)
    )
    latent_block = lax.all_gather(latent_new, "expert", axis=0, tiled=True)
    block_rows = latent_block.shape[0]
    block_offset = dp_pos * block_rows
    block_lead = block_offset % TILE
    block_tiles = local_tiles(row_maxima(latent_block)[None], block_lead)
    block_map = lax.pmax(place_tiles(block_tiles, block_offset // TILE), "dp")
    latent_scales = block_map[0, :total_tiles]
    block_tiles = lax.dynamic_slice_in_dim(block_map, block_offset // TILE, block_tiles.shape[1], 1)
    latent_served = quantized_rows(latent_block[None], block_tiles, block_lead)[0]
    return (
        master_new,
        first_new,
        second_new,
        expert_served,
        expert_scales,
        latent_new,
        latent_one,
        latent_two,
        latent_served,
        latent_scales,
    )


CHUNK = 32
EXTRA = 16
MAXIMA_AT = 64
F32 = jnp.float32
BF16 = jnp.bfloat16
VMEM_LIMIT = 56 * 1024 * 1024
ANY = pl.BlockSpec(memory_space=pl.ANY)
SMEM = pl.BlockSpec(memory_space=pltpu.SMEM)
VMEM = pl.BlockSpec(memory_space=pltpu.VMEM)
PARAMS = pltpu.CompilerParams(vmem_limit_bytes=VMEM_LIMIT)
LIGHT = pltpu.CompilerParams(vmem_limit_bytes=1024 * 1024)


def corrections(step_ref):
    one, two = lax.fori_loop(
        0, step_ref[0], lambda _, p: (p[0] * BETA_ONE, p[1] * BETA_TWO), (F32(1.0), F32(1.0))
    )
    rate = LEARN_RATE / (1.0 - jnp.full((1, TILE), one, F32))
    corr = 1.0 / (1.0 - jnp.full((1, TILE), two, F32))
    return rate, corr


def adamw_tile(w, m, v, g, rate, corr):
    g = g.astype(F32)
    m1 = BETA_ONE * m.astype(F32) + (1.0 - BETA_ONE) * g
    v1 = BETA_TWO * v.astype(F32) + (1.0 - BETA_TWO) * g * g
    x = v1 * corr
    inv = pl.reciprocal(x * lax.rsqrt(x) + ADAM_EPS, approx=True)
    w1 = (1.0 - LEARN_RATE * DECAY_RATE) * w - rate * m1 * inv
    return w1, m1.astype(BF16), v1.astype(BF16)


def sub_max(w1):
    return jnp.max(jnp.abs(w1).reshape(w1.shape[0] // 8, 8, TILE), axis=0)


def stack_max(parts):
    parts = parts + [parts[-1]] * (8 - len(parts))
    rows = [jnp.max(p, axis=0, keepdims=True) for p in parts]
    return jnp.max(jnp.concatenate(rows, axis=0), axis=1, keepdims=True)


def three_parts(x):
    high = x.astype(BF16).astype(F32)
    rest = x - high
    middle = rest.astype(BF16).astype(F32)
    return high, middle, rest - middle


def copy_all(copies):
    for c in copies:
        c.start()


def wait_all(copies):
    for c in copies:
        c.wait()


def expert_kernel(
    partners, per_dest, n_alias, n_carry, n_after, chunks, n_maxima,
    owner_ref, pos_ref, line_ref, step_ref, *refs
):
    maxima, refs = refs[:n_maxima], refs[n_maxima:]
    hbm, refs = refs[:4], refs[4 + n_alias + n_carry + n_after :]
    n_dest = len(partners)
    outs, q_refs, served_ref = refs[:3], refs[3 : 3 + n_dest], refs[3 + n_dest]
    w, m, v, g, extra, in_sem, out_sem, extra_sem = refs[-8:]
    bufs = (w, m, v, g)
    blocks = owner_ref.shape[0]
    rows = w.shape[1]
    tiles = rows // TILE
    pos = pos_ref[0]

    loads, stores = [], []
    for d, k in enumerate(partners):
        for j in range(per_dest):
            i = d * per_dest + j
            slot = (pos ^ k) * per_dest + j
            block = jnp.int32(0)
            for b in range(blocks):
                block = jnp.where(owner_ref[b] == slot, b, block)
            cols = pl.ds(pl.multiple_of(block * TILE, TILE), TILE)
            loads.append(
                [
                    pltpu.make_async_copy(hbm[a].at[:, cols], bufs[a].at[i], in_sem.at[i, a])
                    for a in range(4)
                ]
            )
            target = q_refs[d].at[pl.ds(j * rows, rows), :] if k else served_ref.at[j, pos]
            stores.append(
                [
                    pltpu.make_async_copy(bufs[a].at[i], outs[a].at[:, cols], out_sem.at[i, a])
                    for a in range(3)
                ]
                + [pltpu.make_async_copy(g.at[i], target, out_sem.at[i, 3])]
            )
            copy_all(loads[-1])
    rate, corr = corrections(step_ref)
    lane = lax.broadcasted_iota(jnp.int32, (8, TILE), 1)
    extras = []
    for d, k in enumerate(partners):
        side = jnp.zeros((8, TILE), F32)
        for j in range(per_dest):
            i = d * per_dest + j
            wait_all(loads[i])
            parts = []
            for t in range(tiles):
                at = pl.ds(t * TILE, TILE)
                w1, m1, v1 = adamw_tile(w[i, at, :], m[i, at, :], v[i, at, :], g[i, at, :], rate, corr)
                w[i, at, :] = w1
                m[i, at, :] = m1
                v[i, at, :] = v1
                parts.append(sub_max(w1))
            copy_all(stores[i][:3])
            top = stack_max(parts)
            inv = 1.0 / (top + SCALE_EPS)
            for t in range(tiles):
                at = pl.ds(t * TILE, TILE)
                g[i, at, :] = (w[i, at, :] * inv[t : t + 1, :]).astype(BF16)
            stores[i][3].start()
            for p, value in enumerate(three_parts(top)):
                side = jnp.where(lane == 3 * j + p, value, side)
        if d == 0:
            if chunks:
                tops_ref, ext = refs[3 + n_dest + n_carry], refs[-9]
                per_tile = TILE // CHUNK
                for s in range(n_maxima):
                    peer = lax.rem(line_ref[0] + n_maxima - s, n_maxima)
                    ext[pl.ds(peer * chunks, chunks), :] = maxima[s][0:chunks, :]
                tops_ref[...] = jnp.zeros_like(tops_ref)
                for t in range(n_maxima * chunks // per_tile):
                    tops_ref[t : t + 1, :] = jnp.max(
                        ext[t * per_tile : (t + 1) * per_tile, :], axis=0, keepdims=True
                    )
                maxima = (tops_ref,)
            carried = jnp.zeros((8, TILE), F32)
            for p, value in enumerate(three_parts(maxima[0][...])):
                at = MAXIMA_AT + 16 * p
                carried = jnp.where((lane >= at) & (lane < at + 16), pltpu.roll(value, at, 1), carried)
        side += carried
        extra[d] = jnp.concatenate([side, jnp.zeros_like(side)], axis=0).astype(BF16)
        first = per_dest * rows if k else 0
        extras.append(
            pltpu.make_async_copy(
                extra.at[d], q_refs[d].at[pl.ds(first, EXTRA), :], extra_sem.at[d]
            )
        )
        extras[-1].start()
    for group in stores:
        wait_all(group)
    wait_all(extras)


def expert_group(
    arrays, state, owner, pos, line, step, maxima, chunks, carry, after, partners, per_dest
):
    rows, cols = arrays[0].shape
    n_alias, n_maxima = len(state), len(maxima)
    n = len(partners) * per_dest
    elems = rows * TILE * n
    flat = [jax.ShapeDtypeStruct((8, TILE), F32)] * (chunks > 0)
    first = 8 + n_maxima
    aliases = {first + i: i for i in range(n_alias)}
    aliases.update({first + n_alias + i: 3 + len(partners) + i for i in range(len(carry))})
    out = pl.pallas_call(
        functools.partial(
            expert_kernel, partners, per_dest, n_alias, len(carry), len(after), chunks, n_maxima
        ),
        in_specs=[SMEM] * 4
        + [VMEM] * n_maxima
        + [ANY] * (4 + n_alias + len(carry) + len(after)),
        out_specs=[ANY] * (3 + len(partners) + len(carry)) + [VMEM] * len(flat),
        out_shape=[
            jax.ShapeDtypeStruct((rows, cols), F32),
            jax.ShapeDtypeStruct((rows, cols), BF16),
            jax.ShapeDtypeStruct((rows, cols), BF16),
        ]
        + [
            jax.ShapeDtypeStruct((per_dest * rows * (k > 0) + EXTRA, TILE), BF16)
            for k in partners
        ]
        + [jax.ShapeDtypeStruct(x.shape, x.dtype) for x in carry]
        + flat,
        scratch_shapes=[
            pltpu.VMEM((32, TILE), F32),
            pltpu.VMEM((n, rows, TILE), F32),
            pltpu.VMEM((n, rows, TILE), BF16),
            pltpu.VMEM((n, rows, TILE), BF16),
            pltpu.VMEM((n, rows, TILE), BF16),
            pltpu.VMEM((len(partners), EXTRA, TILE), BF16),
            pltpu.SemaphoreType.DMA((n, 4)),
            pltpu.SemaphoreType.DMA((n, 4)),
            pltpu.SemaphoreType.DMA((len(partners),)),
        ],
        input_output_aliases=aliases,
        compiler_params=PARAMS,
        cost_estimate=pl.CostEstimate(flops=elems, bytes_accessed=elems, transcendentals=0),
        name="expert_adamw",
    )(owner, pos, line, step, *maxima, *arrays, *state, *carry, *after)
    return out[:3], out[3 : 3 + len(partners)], out[3 + len(partners) :]


def block_copies(served, payloads, srcs, sem):
    per_dest, _, rows, _ = served.shape
    return [
        pltpu.make_async_copy(q.at[pl.ds(j * rows, rows), :], served.at[j, src], sem.at[i, j])
        for i, (q, src) in enumerate(zip(payloads, srcs))
        for j in range(per_dest)
    ]


def place_kernel(partners, pos_ref, *refs):
    n = len(partners)
    served, sem = refs[-2:]
    copies = block_copies(served, refs[:n], [pos_ref[0] ^ k for k in partners], sem)
    copy_all(copies)
    wait_all(copies)


def place_blocks(served, pos, payloads, partners, shape):
    n = len(partners)
    return pl.pallas_call(
        functools.partial(place_kernel, partners),
        in_specs=[SMEM] + [ANY] * (n + len(served)),
        out_specs=ANY,
        out_shape=jax.ShapeDtypeStruct(shape, BF16),
        scratch_shapes=[pltpu.SemaphoreType.DMA((n, shape[0]))],
        input_output_aliases={1 + n: 0} if served else {},
        compiler_params=LIGHT,
        cost_estimate=pl.CostEstimate(
            flops=0, bytes_accessed=4 * n * payloads[0].size, transcendentals=0
        ),
        name="place_served",
    )(pos, *payloads, *served)


def collect_kernel(order, tiles, lat_tiles, to_place, pos_ref, *refs):
    n = len(order)
    q_refs = refs[:n]
    served, _, exp_ref, lat_ref, extra, rows_ref, place_sem, sem = refs[n + 2 :]
    pos = pos_ref[0]
    per_dest = served.shape[0]
    blocks_copies = block_copies(
        served, [q_refs[i] for i in to_place], [pos ^ order[i] for i in to_place], place_sem
    )
    copies = [
        pltpu.make_async_copy(
            q.at[pl.ds(q.shape[0] - EXTRA, EXTRA), :], extra.at[i], sem.at[i]
        )
        for i, q in enumerate(q_refs)
    ]
    copy_all(copies)
    copy_all(blocks_copies)
    rows_ref[...] = jnp.zeros_like(rows_ref)
    flat = jnp.zeros((8, exp_ref.shape[1]), F32)
    wide = lax.broadcasted_iota(jnp.int32, flat.shape, 1)
    deep = lax.broadcasted_iota(jnp.int32, flat.shape, 0)
    for i, k in enumerate(order):
        copies[i].wait()
        src = pos ^ k
        x = extra[i].astype(F32)[0:8, :]
        lat = sum(pltpu.roll(x, TILE - MAXIMA_AT - 16 * p, 1) for p in range(3))
        rows_ref[pl.ds(src * lat_tiles, lat_tiles), :] = lat[0:lat_tiles, :]
        for j in range(per_dest):
            first = 3 * j
            top = x[:, first : first + 1] + x[:, first + 1 : first + 2] + x[:, first + 2 : first + 3]
            hit = (wide == (j * n + src) * tiles + deep) & (deep < tiles)
            flat = jnp.where(hit, top, flat)
    exp_ref[...] = jnp.max(flat, axis=0, keepdims=True)
    blocks, height = lat_ref.shape
    lat_ref[...] = jnp.transpose(rows_ref[...])[0:blocks, 0:height]
    wait_all(blocks_copies)


def collect(served, through, pos, received, groups, tiles, lat_tiles, lat_blocks):
    order = [k for partners in groups for k in partners]
    n = len(order)
    per_dest = served.shape[0]
    to_place = [i for i, k in enumerate(order) if k in groups[2] and k]
    served, through, expert, latent = pl.pallas_call(
        functools.partial(collect_kernel, order, tiles, lat_tiles, to_place),
        in_specs=[SMEM] + [ANY] * (n + 2),
        out_specs=[ANY, ANY, VMEM, VMEM],
        out_shape=[
            jax.ShapeDtypeStruct(served.shape, served.dtype),
            jax.ShapeDtypeStruct(through.shape, through.dtype),
            jax.ShapeDtypeStruct((1, per_dest * n * tiles), F32),
            jax.ShapeDtypeStruct((lat_blocks, n * lat_tiles), F32),
        ],
        scratch_shapes=[
            pltpu.VMEM((n, EXTRA, TILE), BF16),
            pltpu.VMEM((TILE, TILE), F32),
            pltpu.SemaphoreType.DMA((len(to_place), per_dest)),
            pltpu.SemaphoreType.DMA((n,)),
        ],
        input_output_aliases={1 + n: 0, 2 + n: 1},
        compiler_params=LIGHT,
        cost_estimate=pl.CostEstimate(flops=1000000, bytes_accessed=1000000, transcendentals=0),
        name="place_last",
    )(pos, *received, served, through)
    return served, through, expert, latent.T


def rest_kernel(deltas, rows, pos_ref, *refs):
    n = len(deltas)
    latent, buf, in_sem, out_sem = refs[-4:]
    spans = [pl.ds(c * CHUNK, CHUNK) for c in range(buf.shape[1] // CHUNK)]
    loads = [
        pltpu.make_async_copy(refs[i].at[at, :], buf.at[i, at, :], in_sem.at[i, c])
        for i in range(n)
        for c, at in enumerate(spans)
    ]
    copy_all(loads)
    copies = []
    for i, delta in enumerate(deltas):
        copies += rest_stores(buf, i, pos_ref[0] ^ delta, rows, latent, out_sem)
    for load, copy in zip(loads, copies):
        load.wait()
        copy.start()
    wait_all(copies)


def place_rest(out, pos, rest, deltas, rows, peers):
    n = len(rest)
    span, cols = rest[0].shape
    return pl.pallas_call(
        functools.partial(rest_kernel, deltas, rows),
        in_specs=[SMEM] + [ANY] * (n + len(out)),
        out_specs=ANY,
        out_shape=jax.ShapeDtypeStruct((peers * rows, cols), BF16),
        scratch_shapes=[
            pltpu.VMEM((n, span, cols), BF16),
            pltpu.SemaphoreType.DMA((n, span // CHUNK)),
            pltpu.SemaphoreType.DMA((n, span // CHUNK)),
        ],
        input_output_aliases={1 + n: 0} if out else {},
        compiler_params=pltpu.CompilerParams(vmem_limit_bytes=4 * 1024 * 1024),
        cost_estimate=pl.CostEstimate(flops=0, bytes_accessed=1000000, transcendentals=0),
        name="place_rest",
    )(pos, *rest, *out)


def whole_tile(pos, rows):
    return pl.multiple_of(lax.rem(pos * (TILE - rows % TILE), TILE), CHUNK)


def full_kernel(pieces, rows, deltas, pos_ref, x_ref, *refs):
    n = len(deltas)
    out_ref, buf, rest, in_sem, out_sem, rest_in, rest_out = refs[n + 1 :]
    loads, stores = [], []
    for i in range(pieces):
        lead = i * (TILE - rows % TILE) % TILE
        at = pl.ds(i * TILE, TILE)
        loads.append(pltpu.make_async_copy(x_ref.at[at, :], buf.at[at, :], in_sem.at[i]))
        stores.append(
            pltpu.make_async_copy(
                buf.at[at, :], out_ref.at[pl.ds(i * rows + lead, TILE), :], out_sem.at[i]
            )
        )
    rest_loads = [pltpu.make_async_copy(refs[i], rest.at[i], rest_in.at[i]) for i in range(n)]
    copy_all(loads + rest_loads)
    for i in range(pieces):
        loads[i].wait()
        stores[i].start()
    for i, delta in enumerate(deltas):
        rest_loads[i].wait()
        group = rest_stores(rest, i, pos_ref[0] ^ delta, rows, out_ref, rest_out)
        copy_all(group)
        stores += group
    wait_all(stores)


def place_full(out, pos, x, xs, deltas, rows):
    pieces, n = x.shape[0] // TILE, len(xs)
    span, cols = xs[0].shape
    return pl.pallas_call(
        functools.partial(full_kernel, pieces, rows, deltas),
        in_specs=[SMEM] + [ANY] * (2 + n),
        out_specs=ANY,
        out_shape=jax.ShapeDtypeStruct((pieces * rows, cols), BF16),
        scratch_shapes=[
            pltpu.VMEM(x.shape, BF16),
            pltpu.VMEM((n, span, cols), BF16),
            pltpu.SemaphoreType.DMA((pieces,)),
            pltpu.SemaphoreType.DMA((pieces,)),
            pltpu.SemaphoreType.DMA((n,)),
            pltpu.SemaphoreType.DMA((n, span // CHUNK)),
        ],
        input_output_aliases={2 + n: 0},
        compiler_params=pltpu.CompilerParams(vmem_limit_bytes=VMEM_LIMIT - 4 * 1024 * 1024),
        cost_estimate=pl.CostEstimate(flops=0, bytes_accessed=4 * x.size, transcendentals=0),
        name="place_whole",
    )(pos, x, *xs, out)


def rest_stores(buf, i, peer, rows, out_ref, sem):
    lead = whole_tile(peer, rows)
    copies = []
    for c in range((rows - TILE) // CHUNK):
        at = peer * rows + c * CHUNK + jnp.where(c * CHUNK < lead, 0, TILE)
        copies.append(
            pltpu.make_async_copy(
                buf.at[i, pl.ds(c * CHUNK, CHUNK), :],
                out_ref.at[pl.ds(pl.multiple_of(at, CHUNK), CHUNK), :],
                sem.at[i, c],
            )
        )
    return copies


def in_order(*arrays):
    return pl.pallas_call(
        lambda *refs: None,
        in_specs=[ANY] * len(arrays),
        out_specs=[ANY] * len(arrays),
        out_shape=[jax.ShapeDtypeStruct(x.shape, x.dtype) for x in arrays],
        input_output_aliases={i: i for i in range(len(arrays))},
        compiler_params=pltpu.CompilerParams(vmem_limit_bytes=1024 * 1024),
        cost_estimate=pl.CostEstimate(flops=1, bytes_accessed=1, transcendentals=0),
        name="in_order",
    )(*arrays)


SLABS = 4


def latent_kernel(chunks, step_ref, pos_ref, *refs):
    hbm, outs, top_ref = refs[:4], refs[4:8], refs[8]
    w, m, v, g, q, in_sem, out_sem = refs[9:]
    bufs = (w, m, v, g)
    width = w.shape[1] // SLABS
    loads, stores = [], []
    for i in range(SLABS):
        cols = pl.ds(i * width, width)
        loads.append(
            [
                pltpu.make_async_copy(hbm[a].at[:, cols], bufs[a].at[:, cols], in_sem.at[i, a])
                for a in range(4)
            ]
        )
        stores.append(
            [
                pltpu.make_async_copy(src.at[:, cols], outs[a].at[:, cols], out_sem.at[i, a])
                for a, src in enumerate((w, m, v, q))
            ]
        )
        copy_all(loads[i])
    rate, corr = corrections(step_ref)
    lane = lax.broadcasted_iota(jnp.int32, (8, TILE), 1)
    lead = whole_tile(pos_ref[0], w.shape[0])
    sub = lax.broadcasted_iota(jnp.int32, (8, 1), 0) * CHUNK
    inside = (sub >= lead) & (sub < lead + TILE)
    tops = jnp.zeros((8, TILE), F32)
    for i in range(SLABS):
        wait_all(loads[i])
        blocks = range(i * width // TILE, (i + 1) * width // TILE)
        slab_tops = []
        for b in blocks:
            cols = pl.ds(b * TILE, TILE)
            w1, m1, v1 = adamw_tile(w[:, cols], m[:, cols], v[:, cols], g[:, cols], rate, corr)
            w[:, cols] = w1
            m[:, cols] = m1
            v[:, cols] = v1
            slab_tops.append(stack_max([sub_max(w1[c * CHUNK : (c + 1) * CHUNK]) for c in range(chunks)]))
        for b, top in zip(blocks, slab_tops):
            cols = pl.ds(b * TILE, TILE)
            tops = jnp.where(lane == b, top, tops)
            whole = jnp.max(jnp.where(inside, top, 0.0), axis=0, keepdims=True)
            q[:, cols] = (w[pl.ds(lead, TILE), cols] * (1.0 / (whole + SCALE_EPS))).astype(BF16)
        copy_all(stores[i])
    top_ref[...] = tops
    for group in stores:
        wait_all(group)


def latent_update(arrays, step, pos):
    rows, cols = arrays[0].shape
    elems = rows * cols
    return pl.pallas_call(
        functools.partial(latent_kernel, rows // CHUNK),
        in_specs=[SMEM] * 2 + [ANY] * 4,
        out_specs=[ANY] * 4 + [VMEM],
        out_shape=[
            jax.ShapeDtypeStruct((rows, cols), F32),
            jax.ShapeDtypeStruct((rows, cols), BF16),
            jax.ShapeDtypeStruct((rows, cols), BF16),
            jax.ShapeDtypeStruct((TILE, cols), BF16),
            jax.ShapeDtypeStruct((8, TILE), F32),
        ],
        scratch_shapes=[
            pltpu.VMEM((rows, cols), F32),
            pltpu.VMEM((rows, cols), BF16),
            pltpu.VMEM((rows, cols), BF16),
            pltpu.VMEM((rows, cols), BF16),
            pltpu.VMEM((TILE, cols), BF16),
            pltpu.SemaphoreType.DMA((SLABS, 4)),
            pltpu.SemaphoreType.DMA((SLABS, 4)),
        ],
        compiler_params=PARAMS,
        cost_estimate=pl.CostEstimate(
            flops=30 * elems, bytes_accessed=18 * elems, transcendentals=2 * elems
        ),
        name="latent_adamw",
    )(step, pos, *arrays)


def latent_rest_kernel(
    chunks, pos_ref, w1_ref, own_ref, prev_ref, next_ref, after_ref, q_ref, w, q, ext, in_sem, out_sem
):
    per_tile = TILE // CHUNK
    rows, cols = w1_ref.shape
    width = cols // SLABS
    lead = whole_tile(pos_ref[0], rows)
    loads, stores = [], []
    for i in range(SLABS):
        at = pl.ds(i * width, width)
        group = []
        for c in range(chunks - per_tile):
            first = pl.multiple_of(c * CHUNK + jnp.where(c * CHUNK < lead, 0, TILE), CHUNK)
            group.append(
                pltpu.make_async_copy(
                    w1_ref.at[pl.ds(first, CHUNK), at],
                    w.at[pl.ds(c * CHUNK, CHUNK), at],
                    in_sem.at[i, c],
                )
            )
        copy_all(group)
        loads.append(group)
        stores.append(pltpu.make_async_copy(q.at[:, at], q_ref.at[:, at], out_sem.at[i]))
    ext[0:chunks, :] = prev_ref[0:chunks, :]
    ext[chunks : 2 * chunks, :] = own_ref[0:chunks, :]
    ext[2 * chunks : 3 * chunks, :] = next_ref[0:chunks, :]
    first = chunks + lead // CHUNK
    above = jnp.max(ext[pl.ds(first - per_tile, per_tile), :], axis=0, keepdims=True)
    below = jnp.max(ext[pl.ds(first + per_tile, per_tile), :], axis=0, keepdims=True)
    both = jnp.concatenate([above] * 4 + [below] * 4, axis=0)
    lane = lax.broadcasted_iota(jnp.int32, (8, TILE), 1)
    tops = [
        jnp.max(jnp.where(lane == b, both, 0.0), axis=1, keepdims=True) for b in range(cols // TILE)
    ]
    invs = [1.0 / (top + SCALE_EPS) for top in tops]
    for i in range(SLABS):
        wait_all(loads[i])
        for b in range(i * width // TILE, (i + 1) * width // TILE):
            at = pl.ds(b * TILE, TILE)
            for c in range(chunks - per_tile):
                span = pl.ds(c * CHUNK, CHUNK)
                inv = jnp.where(c * CHUNK < lead, invs[b][0:1, :], invs[b][4:5, :])
                q[span, at] = (w[span, at] * inv).astype(BF16)
        stores[i].start()
    wait_all(stores)


def latent_rest(w1, own, above, below, pos, after):
    rows, cols = w1.shape
    chunks = rows // CHUNK
    return pl.pallas_call(
        functools.partial(latent_rest_kernel, chunks),
        in_specs=[SMEM, ANY] + [VMEM] * 3 + [ANY],
        out_specs=ANY,
        out_shape=jax.ShapeDtypeStruct((rows - TILE, cols), BF16),
        scratch_shapes=[
            pltpu.VMEM((rows - TILE, cols), F32),
            pltpu.VMEM((rows - TILE, cols), BF16),
            pltpu.VMEM((24, TILE), F32),
            pltpu.SemaphoreType.DMA((SLABS, chunks)),
            pltpu.SemaphoreType.DMA((SLABS,)),
        ],
        compiler_params=PARAMS,
        cost_estimate=pl.CostEstimate(
            flops=rows * cols, bytes_accessed=3 * rows * cols, transcendentals=0
        ),
        name="latent_rest",
    )(pos, w1, own, above, below, after)


def fast_fits(expert_shape, latent_shape, dp_count, exp_axis):
    exp_count, rows, cols = expert_shape
    latent_rows, latent_cols = latent_shape
    return (
        exp_count == 1
        and rows % TILE == 0
        and rows <= 8 * TILE
        and cols % (TILE * dp_count) == 0
        and cols // TILE // dp_count <= 5
        and dp_count == 8
        and dp_count * latent_rows * exp_axis <= TILE * TILE
        and latent_rows % CHUNK == 0
        and 2 * TILE - CHUNK <= latent_rows < 2 * TILE
        and latent_rows * exp_axis % TILE == 0
        and latent_rows * exp_axis <= 8 * TILE
        and exp_axis == 4
        and latent_cols % (SLABS * TILE) == 0
        and latent_cols <= 16 * TILE
    )


def partner_groups(dp_count):
    hops = lambda k: bin(k >> 1).count("1")
    stage = lambda k: 2 if k & 1 and hops(k) < 2 else (3 if k == 0 else hops(k) - 1)
    order = sorted(range(dp_count), key=lambda k: (stage(k), -k))
    return [[k for k in order if stage(k) in n] for n in ((0,), (1,), (2, 3))]


def fast_body(
    expert_master,
    expert_first,
    expert_second,
    expert_grad,
    latent_master,
    latent_first,
    latent_second,
    latent_grad,
    step_count,
    column_owner,
):
    dp_count = lax.axis_size("dp")
    dp_pos = lax.axis_index("dp").astype(jnp.int32)
    exp_axis = lax.axis_size("expert")
    exp_pos = lax.axis_index("expert").astype(jnp.int32)
    _, rows, cols = expert_master.shape
    block_count = cols // TILE
    per_dest = block_count // dp_count
    tiles = rows // TILE

    expert_at, dp_at = exp_pos.reshape(1), dp_pos.reshape(1)
    latent_new, latent_one, latent_two, whole, chunk_top = latent_update(
        (latent_master, latent_first, latent_second, latent_grad), step_count, expert_at
    )
    latent_rows = latent_new.shape[0]
    whole = lax.all_gather(whole, "expert", axis=0, tiled=True)
    maxima = [chunk_top] + [
        lax.ppermute(chunk_top, "expert", [(i, (i + s) % exp_axis) for i in range(exp_axis)])
        for s in range(1, exp_axis)
    ]

    arrays = tuple(
        a.reshape(rows, cols) for a in (expert_master, expert_first, expert_second, expert_grad)
    )
    def swap(x, axis, k):
        return lax.ppermute(x, axis, [(i, i ^ k) for i in range(lax.axis_size(axis))])

    groups = partner_groups(dp_count)
    order = [k for partners in groups for k in partners]
    send = lambda sent, partners: [swap(q, "dp", k) if k else q for k, q in zip(partners, sent)]
    group = functools.partial(
        expert_group,
        arrays,
        owner=column_owner,
        pos=dp_at,
        line=expert_at,
        step=step_count,
        per_dest=per_dest,
    )
    chunks = latent_rows // CHUNK
    state, sent, (tops,) = group(
        state=(), maxima=maxima, chunks=chunks, carry=(), after=(), partners=groups[0]
    )
    received = send(sent, groups[0])
    state, sent, _ = group(
        state=state, maxima=(tops,), chunks=0, carry=(), after=(), partners=groups[1]
    )
    received += send(sent, groups[1])
    rest = latent_rest(latent_new, chunk_top, maxima[1], maxima[-1], expert_at, sent[0])
    far, near = swap(rest, "expert", 2), swap(rest, "expert", 1)
    first, count = len(groups[0]), len(received)
    served = place_blocks(
        (), dp_at, received[:first], groups[0], (per_dest, dp_count, rows, TILE)
    )
    state, sent, (served,) = group(
        state=state,
        maxima=(tops,),
        chunks=0,
        carry=(served,),
        after=(),
        partners=groups[2],
    )
    received += send(sent, groups[2])
    served = place_blocks(
        (served,), dp_at, received[first:count], groups[1], served.shape
    )
    near, far, served = in_order(near, far, served)
    last = swap(far, "expert", 1)
    latent_served = place_rest((), expert_at, [near, far], [1, 2], latent_rows, exp_axis)
    latent_served = place_full(latent_served, expert_at, whole, [rest], [0], latent_rows)
    served, latent_served, expert_scales, latent_scales = collect(
        served,
        latent_served,
        dp_at,
        received,
        groups,
        tiles,
        latent_rows * exp_axis // TILE,
        latent_new.shape[1] // TILE,
    )
    latent_served = place_rest(
        (latent_served,), expert_at, [last], [3], latent_rows, exp_axis
    )
    expert_served = served.reshape(1, block_count * rows, TILE)

    return (
        state[0][None],
        state[1][None],
        state[2][None],
        expert_served,
        expert_scales,
        latent_new,
        latent_one,
        latent_two,
        latent_served,
        latent_scales,
    )


def body(*args):
    if fast_fits(args[0].shape, args[4].shape, lax.axis_size("dp"), lax.axis_size("expert")):
        return fast_body(*args)
    return general_body(*args)


def solution(mesh):
    placed = (
        P("expert", "dp", None),
        P("expert", "dp", None),
        P("expert", "dp", None),
        P("expert", "dp", None),
        P(("dp", "expert"), None),
        P(("dp", "expert"), None),
        P(("dp", "expert"), None),
        P(("dp", "expert"), None),
        P(),
        P(),
    )
    return jax.shard_map(
        body,
        mesh=mesh,
        in_specs=placed,
        out_specs=(
            P("expert", "dp", None),
            P("expert", "dp", None),
            P("expert", "dp", None),
            P("expert", "dp", None),
            P("expert", "dp"),
            P(("dp", "expert"), None),
            P(("dp", "expert"), None),
            P(("dp", "expert"), None),
            P("dp", None),
            P(),
        ),
        check_vma=False,
    )
```
